32 devices in a mesh: groups: 2 (over y), slab: 16 (over z, x, core).
Axes of the slice: x: 2, y: 2, z: 4, core: 2. Of those that a mesh axis runs over, the one named last changes fastest.
Arguments:
- volume: bfloat16 [4096, 32, 2048], P(('groups', 'slab')), parts along dimension 0, may hold values from 0 to 2
- measured: bfloat16 [32, 512, 2048], P(('groups', 'slab')), parts along dimension 0, may hold values from 0 to 80
- path_weights: bfloat16 [16, 32], replicated, may hold values from 0.25 to 1
- fractions: float32 [16, 2048], replicated, may hold values from 0.1 to 0.5
- bases: int32 [16], replicated, may hold values from 1 to 1536, as said below
Outputs:
- new_volume: float32 [4096, 32, 2048], P(('groups', 'slab')), parts along dimension 0
The draws below stay inside these ranges and needn't reach their ends.
There are 2 independent parts, one for each index of `groups`. The reference program is written for one: setup_inputs(seed, part) draws one part's arguments, and reference() takes and returns one part's arrays. A program takes and returns all parts, laid end to end along the dimension named above; an argument that names none is the same for every part. Nothing has to cross between parts.
Inputs may be any that keep to these rules, and one draw needn't show every extreme that they name: `bases`: the entries, taken in increasing order, begin with 1 and end with 1536, and consecutive ones differ by less than 512; every slice lies within, or directly before, the rows of some projection. The order of the projections along the subset is not that of the helix.
All inputs are finite; a program needn't handle non-finite values.
Results may differ from the reference program's by a relative error of at most 0.002.
Values may be sent and summed in bfloat16 or wider, within the bound.
No kernel may reach another device: no remote copies, remote signals or barrier semaphores. Data moves between devices by JAX's collectives and lax.ppermute only.
A program may use at most 192 MiB of HBM per device.

```python
import jax
import jax.numpy as jnp
from jax import lax

NZ = 2048
DEPTH = 32
COLS = 2048
ROWS = 512
SL = 128
ANGLES = 16
N_SLAB = 16


def draw_bases(key, part):
    key = jax.random.fold_in(key, 7)
    order_key = jax.random.fold_in(key, 11)
    jitter_key = jax.random.fold_in(key, 13)
    span = NZ - ROWS - 1
    middle = ANGLES // 2
    order = jax.random.permutation(order_key, ANGLES).astype(jnp.int32)
    where_mid = jnp.argmax(order == middle).astype(jnp.int32)
    first_val = order[0]
    order = order.at[where_mid].set(first_val)
    order = order.at[0].set(middle)
    centre = 1 + order * span // (ANGLES - 1)
    jitter = jax.random.randint(jitter_key, (ANGLES,), -SL, SL + 1, dtype=jnp.int32)
    inner = (order > 0) & (order < ANGLES - 1) & (order != middle)
    moved = jnp.clip(centre + jitter, 1, NZ - ROWS)
    return jnp.where(inner, moved, centre).astype(jnp.int32)


def steps_of(stream_key, shape, shards, low, high):
    gain = 1.0
    for axis_at, shards_of in shards:
        draws = jax.random.uniform(jax.random.fold_in(jax.random.fold_in(stream_key, 6), axis_at), (shards_of,), jnp.float32, low / len(shards), high / len(shards))
        gain = gain * jnp.repeat(jnp.exp(draws), shape[axis_at] // shards_of).reshape((-1,) + (1,) * (len(shape) - 1 - axis_at))
    return gain


def setup_inputs(seed: int = 0, part: int = 0) -> dict:
    key_of = jax.random.split(jax.random.key(seed), 6)
    part_keys = jax.random.split(jax.random.fold_in(key_of[5], part), 6)
    return {
        "volume": jnp.clip(2.0 * jax.random.uniform(part_keys[0], (NZ, DEPTH, COLS), jnp.float32) ** steps_of(part_keys[0], (NZ, DEPTH, COLS), ((0, 16),), -0.2, 0.2), 0.0, 2.0).astype(jnp.bfloat16),
        "measured": jnp.clip(80.0 * jax.random.uniform(part_keys[1], (ANGLES, ROWS, COLS), jnp.float32) ** steps_of(part_keys[1], (ANGLES, ROWS, COLS), ((0, 16),), -0.2, 0.2), 0.0, 80.0).astype(jnp.bfloat16),
        "path_weights": jnp.clip(jax.random.uniform(key_of[2], (ANGLES, DEPTH), jnp.float32, 0.25, 1.0), 0.25, 1.0).astype(jnp.bfloat16),
        "fractions": jnp.clip(jax.random.uniform(key_of[3], (ANGLES, NZ), jnp.float32, 0.1, 0.5), 0.1, 0.5),
        "bases": draw_bases(jax.random.fold_in(key_of[5], 71), part),
    }


RELAX = 1.0


def reference(volume, measured, path_weights, fractions, bases):
    weights = path_weights.astype(jnp.float32)
    ray_total = jnp.sum(weights, axis=1)

    def project(angle):
        base = bases[angle]
        window = lax.dynamic_slice_in_dim(volume, base - 1, ROWS + 1, 0).astype(jnp.float32)
        image = jnp.einsum("d,zdc->zc", weights[angle], window, precision=lax.Precision.HIGHEST)
        share = lax.dynamic_slice_in_dim(fractions[angle], base - 1, ROWS + 1, 0)
        forward = (1.0 - share[1:])[:, None] * image[1:] + share[:-1][:, None] * image[:-1]
        ray_norm = ray_total[angle] * ((1.0 - share[1:]) + share[:-1])
        return ((measured[angle].astype(jnp.float32) - forward) / ray_norm[:, None]).astype(jnp.bfloat16)

    residual = lax.map(project, jnp.arange(ANGLES, dtype=jnp.int32))

    def correct(block):
        first = block * SL
        slices = first + jnp.arange(SL, dtype=jnp.int32)
        row_now = slices[None, :] - bases[:, None]
        valid_now = (row_now >= 0) & (row_now < ROWS)
        valid_next = (row_now + 1 >= 0) & (row_now + 1 < ROWS)
        share = lax.dynamic_slice_in_dim(fractions, first, SL, 1)
        w_now = jnp.where(valid_now, 1.0 - share, 0.0)
        w_next = jnp.where(valid_next, share, 0.0)
        pick = jax.vmap(lambda res, idx: res[idx])
        take_now = pick(residual, jnp.clip(row_now, 0, ROWS - 1)).astype(jnp.float32)
        take_next = pick(residual, jnp.clip(row_now + 1, 0, ROWS - 1)).astype(jnp.float32)
        blend = (w_now[:, :, None] * take_now + w_next[:, :, None] * take_next).astype(jnp.bfloat16)
        spread = jnp.einsum("ad,azc->zdc", weights, blend.astype(jnp.float32), precision=lax.Precision.HIGHEST)
        column_norm = jnp.einsum("ad,az->zd", weights, w_now + w_next, precision=lax.Precision.HIGHEST)
        piece = lax.dynamic_slice_in_dim(volume, first, SL, 0).astype(jnp.float32)
        return piece + RELAX * spread / column_norm[:, :, None]

    result = lax.map(correct, jnp.arange(N_SLAB, dtype=jnp.int32))
    return result.reshape(NZ, DEPTH, COLS)
```

```python
import jax
import jax.numpy as jnp
from jax import lax
from jax.experimental import pallas as pl
from jax.experimental.pallas import tpu as pltpu
from jax.sharding import PartitionSpec as P

RELAX = 1.0
BLOCK = 16
HALF = 8
LANES = 128
WIDE = 256


def update_kernel(
    vol_ref, next_ref, left_ref, right_ref, seen_ref, edge_ref, now_ref, prev_ref, inv_ref,
    edge_now_ref, edge_prev_ref, edge_inv_ref, image_w_ref, weight_ref, spread_ref, carry_w_ref,
    out_ref, carry_ref, slab_ref,
):
    block = pl.program_id(1)
    last = pl.num_programs(1) - 1
    depth, width = vol_ref.shape[1:]
    angles = weight_ref.shape[0]
    slab_ref[0 : BLOCK * depth] = vol_ref[...].reshape(BLOCK * depth, width)

    @pl.when(block < last)
    def _():
        slab_ref[BLOCK * depth :] = next_ref[0]

    @pl.when(block == last)
    def _():
        slab_ref[BLOCK * depth :] = right_ref[0]

    def wide(coef):
        return jnp.concatenate([coef] * (WIDE // LANES), axis=1)

    def dot(a, b):
        return jnp.dot(a, b, preferred_element_type=jnp.float32)

    @pl.loop(0, width // WIDE)
    def _(chunk):
        at = pl.ds(pl.multiple_of(chunk * WIDE, WIDE), WIDE)

        @pl.when(block == 0)
        def _():
            weights = weight_ref[...]
            mine = dot(weights, slab_ref[0:depth, at])
            before = dot(weights, left_ref[0, :, at])
            carry_ref[:, at] = (
                edge_ref[:, at].astype(jnp.float32) * wide(edge_inv_ref[...])
                - mine * wide(edge_now_ref[...])
                - before * wide(edge_prev_ref[...])
            ).astype(jnp.bfloat16)

        seen = seen_ref[:, :, at].astype(jnp.float32)
        parts = []
        for half in range(BLOCK // HALF):
            start = half * HALF * depth
            prev = dot(image_w_ref[...], slab_ref[start : start + HALF * depth, at])
            now = dot(image_w_ref[...], slab_ref[start + depth : start + (HALF + 1) * depth, at])
            got = seen[:, half * HALF : (half + 1) * HALF].reshape(angles * HALF, WIDE)
            resid = got * wide(inv_ref[0, half]) - now * wide(now_ref[0, half]) - prev * wide(prev_ref[0, half])
            parts.append(resid.reshape(angles, HALF, WIDE))
        resid = jnp.concatenate(parts, axis=1)
        spread = dot(spread_ref[0], resid.astype(jnp.bfloat16).reshape(angles * BLOCK, WIDE))
        extra = dot(carry_w_ref[0], carry_ref[:, at])
        carry_ref[:, at] = resid[:, BLOCK - 1].astype(jnp.bfloat16)
        volume = slab_ref[0 : BLOCK * depth, at].astype(jnp.float32)
        result = volume + spread
        out_ref[0, :, at] = result[:depth] + extra
        out_ref[1:, :, at] = result[depth:].reshape(BLOCK - 1, depth, WIDE)


def update(volume, left, right, seen, edge, coefs, edge_coefs, image_w, weights, spread_w, carry_w):
    slices, depth, cols = volume.shape
    angles = weights.shape[0]
    blocks = slices // BLOCK
    width = 1024 if angles <= 16 else WIDE
    half_spec = pl.BlockSpec((1, BLOCK // HALF, angles * HALF, LANES), lambda c, b: (b, 0, 0, 0))
    whole2 = lambda shape: pl.BlockSpec(shape, lambda c, b: (0,) * len(shape))
    return pl.pallas_call(
        update_kernel,
        grid=(cols // width, blocks),
        in_specs=[
            pl.BlockSpec((BLOCK, depth, width), lambda c, b: (b, 0, c)),
            pl.BlockSpec((1, depth, width), lambda c, b: (jnp.minimum((b + 1) * BLOCK, slices - 1), 0, c)),
            pl.BlockSpec((1, depth, width), lambda c, b: (0, 0, c)),
            pl.BlockSpec((1, depth, width), lambda c, b: (0, 0, c)),
            pl.BlockSpec((angles, BLOCK, width), lambda c, b: (0, b, c)),
            pl.BlockSpec((angles, width), lambda c, b: (0, c)),
            half_spec, half_spec, half_spec,
            whole2((angles, LANES)), whole2((angles, LANES)), whole2((angles, LANES)),
            whole2(image_w.shape), whole2(weights.shape),
            pl.BlockSpec((1,) + spread_w.shape[1:], lambda c, b: (b, 0, 0)),
            pl.BlockSpec((1,) + carry_w.shape[1:], lambda c, b: (b, 0, 0)),
        ],
        out_specs=pl.BlockSpec((BLOCK, depth, width), lambda c, b: (b, 0, c)),
        out_shape=jax.ShapeDtypeStruct(volume.shape, jnp.float32),
        scratch_shapes=[
            pltpu.VMEM((angles, width), jnp.bfloat16),
            pltpu.VMEM(((BLOCK + 1) * depth, width), jnp.bfloat16),
        ],
        compiler_params=pltpu.CompilerParams(
            dimension_semantics=("arbitrary", "arbitrary"), vmem_limit_bytes=48 * 2**20
        ),
        cost_estimate=pl.CostEstimate(
            flops=4 * slices * depth * cols * angles, bytes_accessed=volume.size * 6 + seen.size * 2, transcendentals=0
        ),
        name="slab_update",
    )(volume, volume, left, right, seen, edge, *coefs, *edge_coefs, image_w, weights, spread_w, carry_w)


def on_device(volume, measured, path_weights, fractions, bases):
    slices, depth, cols = volume.shape
    local, rows = measured.shape[:2]
    nslab = lax.axis_size("slab")
    device = lax.axis_index("slab")
    angles = local * nslab
    first = device * slices
    classes = rows // slices
    planes = nslab // classes
    blocks = slices // BLOCK

    my_bases = lax.dynamic_slice_in_dim(bases, device * local, local, 0)
    turned = jax.vmap(lambda m, b: jnp.roll(m, b - 1, axis=0))(measured, my_bases)
    by_class = turned.reshape(local, classes, slices, cols).transpose(1, 0, 2, 3)
    outgoing = jnp.tile(by_class, (planes, 1, 1, 1)).reshape(nslab * local, slices, cols)
    seen = lax.all_to_all(outgoing, "slab", split_axis=0, concat_axis=0, tiled=True)
    ends = jnp.roll(by_class[:, :, slices - 1], 1, axis=0)
    ends = jnp.tile(ends, (planes, 1, 1)).reshape(nslab * local, cols // LANES, LANES)
    edge = lax.all_to_all(ends, "slab", split_axis=0, concat_axis=0, tiled=True).reshape(angles, cols)
    left = lax.ppermute(volume[slices - 1 :], "slab", [(i, i + 1) for i in range(nslab - 1)])
    right = lax.ppermute(volume[:1], "slab", [(i + 1, i) for i in range(nslab - 1)])

    weights = path_weights.astype(jnp.float32)
    ray_total = jnp.sum(weights, axis=1)[:, None]
    share = lax.dynamic_slice_in_dim(jnp.pad(fractions, ((0, 0), (1, 1))), first, slices + 2, 1)
    norm = 1.0 / (ray_total * ((1.0 - share[:, 1:]) + share[:, :-1]))
    coef_now = (1.0 - share[:, 1:]) * norm
    coef_prev = share[:, :-1] * norm

    def by_block(coef):
        coef = coef[:, 1:].reshape(angles, blocks, BLOCK // HALF, HALF).transpose(1, 2, 0, 3)
        return jnp.broadcast_to(coef.reshape(blocks, BLOCK // HALF, angles * HALF, 1), (blocks, BLOCK // HALF, angles * HALF, LANES))

    def at_edge(coef):
        return jnp.broadcast_to(coef[:, :1], (angles, LANES))

    coefs = [by_block(c) for c in (coef_now, coef_prev, norm)]
    edge_coefs = [at_edge(c) for c in (coef_now, coef_prev, norm)]

    share_own = share[:, 1:-1]
    row_now = (first - bases)[:, None] + jnp.arange(slices, dtype=jnp.int32)[None, :]
    w_now = jnp.where((row_now >= 0) & (row_now < rows), 1.0 - share_own, 0.0)
    w_next = jnp.where((row_now + 1 >= 0) & (row_now + 1 < rows), share_own, 0.0)
    column_norm = jnp.einsum("ad,az->zd", weights, w_now + w_next, precision=lax.Precision.HIGHEST)
    scale = RELAX / column_norm

    eye = jnp.eye(HALF, dtype=jnp.float32)
    image_w = jnp.einsum("ad,yz->ayzd", weights, eye).reshape(angles * HALF, HALF * depth).astype(jnp.bfloat16)
    same = jnp.eye(BLOCK, dtype=jnp.float32)
    later = jnp.eye(BLOCK, k=-1, dtype=jnp.float32)
    pair = (
        w_next.T.reshape(blocks, BLOCK, 1, angles, 1) * same[None, :, None, None, :]
        + w_now.T.reshape(blocks, BLOCK, 1, angles, 1) * later[None, :, None, None, :]
    )
    spread_w = pair * weights.T[None, None, :, :, None] * scale.reshape(blocks, BLOCK, depth, 1, 1)
    spread_w = spread_w.reshape(blocks, BLOCK * depth, angles * BLOCK).astype(jnp.bfloat16)
    carry_w = (
        w_now.T.reshape(blocks, BLOCK, 1, angles)[:, 0] * weights.T[None] * scale.reshape(blocks, BLOCK, depth, 1)[:, 0]
    ).astype(jnp.bfloat16)
    return update(volume, left, right, seen, edge, coefs, edge_coefs, image_w, path_weights, spread_w, carry_w)


def solution(mesh):
    placed = (P(("groups", "slab"), None, None), P(("groups", "slab"), None, None), P(), P(), P())
    return jax.shard_map(
        on_device,
        mesh=mesh,
        in_specs=placed,
        out_specs=P(("groups", "slab"), None, None),
        check_vma=False,
    )
```

```python
import functools

import jax
import jax.numpy as jnp
from jax import lax
from jax.experimental import pallas as pl
from jax.experimental.pallas import tpu as pltpu
from jax.sharding import PartitionSpec as P

RELAX = 1.0
BLOCK = 16
HALF = 8
LANES = 128
WIDE = 256
CHUNKS = 2
ROUTED_CLASSES = 4
STEADY = 5
CODE = 256


def update_kernel(
    dense, first_width, ids_ref, vol_ref, next_ref, left_ref, right_ref, edge_ref, now_ref, prev_ref, inv_ref,
    edge_now_ref, edge_prev_ref, edge_inv_ref, image_w_ref, weight_ref, wide_w_ref, turned_w_ref,
    pick_next_ref, pick_now_ref, pick_carry_ref, *rest,
):
    out_ref, carry_ref, slab_ref, spread_ref, carry_w_ref, seen_ref, sems = rest[-7:]
    packets = rest[: -8]
    block = pl.program_id(1)
    column = pl.program_id(0)
    blocks = pl.num_programs(1)
    depth, width = vol_ref.shape[1:]
    angles = weight_ref.shape[0]
    step = column * blocks + block
    steps = pl.num_programs(0) * blocks

    def fetch(at_step, act):
        slot = at_step % 2
        rows = pl.ds(pl.multiple_of((at_step % blocks) * BLOCK, BLOCK), BLOCK)
        cols = pl.ds(pl.multiple_of((at_step // blocks) * width, width), width)
        if dense:
            act(pltpu.make_async_copy(packets[0].at[:, rows, cols], seen_ref.at[slot], sems.at[slot, 0]))
            return
        for n, packet in enumerate(packets):

            @pl.when(ids_ref[n] >= 0)
            def _():
                act(pltpu.make_async_copy(packet.at[rows, cols], seen_ref.at[slot, ids_ref[n]], sems.at[slot, n]))

    @pl.when(step == 0)
    def _():
        seen_ref[...] = jnp.zeros_like(seen_ref)
        fetch(step, lambda copy: copy.start())

    @pl.when(step + 1 < steps)
    def _():
        fetch(step + 1, lambda copy: copy.start())

    slab_ref[0 : BLOCK * depth] = vol_ref[...].reshape(BLOCK * depth, width)

    @pl.when(block < blocks - 1)
    def _():
        slab_ref[BLOCK * depth :] = next_ref[0]

    @pl.when(block == blocks - 1)
    def _():
        slab_ref[BLOCK * depth :] = right_ref[0]

    place = lax.broadcasted_iota(jnp.int32, (depth, angles * BLOCK), 1) % BLOCK
    from_next = wide_w_ref[...] * pick_next_ref[0]
    from_now = wide_w_ref[...] * pick_now_ref[0]
    from_carry = turned_w_ref[...] * pick_carry_ref[0]
    for z in range(BLOCK):
        row = jnp.where(place == z, from_next, jnp.where(place == z - 1, from_now, 0.0))
        total = jnp.sum(row, axis=1, keepdims=True)
        if z == 0:
            total = total + jnp.sum(from_carry, axis=1, keepdims=True)
            carry_w_ref[...] = (from_carry * (RELAX / total)).astype(jnp.bfloat16)
        spread_ref[z * depth : (z + 1) * depth] = (row * (RELAX / total)).astype(jnp.bfloat16)

    def wide(coef):
        return jnp.concatenate([coef] * (WIDE // LANES), axis=1)

    def dot(a, b):
        return jnp.dot(a, b, preferred_element_type=jnp.float32)

    @pl.when(block == 0)
    def _():
        for chunk in range(width // WIDE):
            at = pl.ds(chunk * WIDE, WIDE)
            mine = dot(weight_ref[...], slab_ref[0:depth, at])
            before = dot(weight_ref[...], left_ref[0, :, at])
            carry_ref[:, at] = (
                edge_ref[:, at].astype(jnp.float32) * wide(edge_inv_ref[...])
                - mine * wide(edge_now_ref[...])
                - before * wide(edge_prev_ref[...])
            ).astype(jnp.bfloat16)

    fetch(step, lambda copy: copy.wait())
    slot = step % 2
    for chunk in range(width // WIDE):
        at = pl.ds(chunk * WIDE, WIDE)
        seen = seen_ref[slot, :, :, at].astype(jnp.float32)
        parts = []
        for half in range(BLOCK // HALF):
            start = half * HALF * depth
            prev = dot(image_w_ref[...], slab_ref[start : start + HALF * depth, at])
            now = dot(image_w_ref[...], slab_ref[start + depth : start + (HALF + 1) * depth, at])
            got = seen[:, half * HALF : (half + 1) * HALF].reshape(angles * HALF, WIDE)
            resid = got * wide(inv_ref[0, half]) - now * wide(now_ref[0, half]) - prev * wide(prev_ref[0, half])
            parts.append(resid.reshape(angles, HALF, WIDE))
        resid = jnp.concatenate(parts, axis=1)
        spread = dot(spread_ref[...], resid.astype(jnp.bfloat16).reshape(angles * BLOCK, WIDE))
        extra = dot(carry_w_ref[...], carry_ref[:, at])
        carry_ref[:, at] = resid[:, BLOCK - 1].astype(jnp.bfloat16)
        volume = slab_ref[0 : BLOCK * depth, at].astype(jnp.float32)
        result = volume + spread
        out_ref[0, :, at] = result[:depth] + extra
        out_ref[1:, :, at] = result[depth:].reshape(BLOCK - 1, depth, WIDE)


def update(volume, left, right, edge, tables, packets, ids, before, part, parts, dense):
    slices, depth, cols = volume.shape
    angles = edge.shape[0]
    blocks = slices // BLOCK
    width = min(1024 if angles <= 16 else WIDE, cols // parts)
    steps = cols // parts // width
    off = part * steps
    half_spec = pl.BlockSpec((1, BLOCK // HALF, angles * HALF, LANES), lambda c, b, i: (b, 0, 0, 0))
    by_block = lambda n: pl.BlockSpec((1, 1, n), lambda c, b, i: (b, 0, 0))
    whole = lambda x: pl.BlockSpec(x.shape, lambda c, b, i: (0,) * x.ndim)
    anywhere = pl.BlockSpec(memory_space=pl.ANY)
    now, prev, inv, edge_now, edge_prev, edge_inv, image_w, weights, wide_w, turned_w, pick_next, pick_now, pick_carry = tables
    if before is None:
        before = edge
        aliases = {}
    else:
        aliases = {19 + len(packets): 0}
    one = (1, depth, width)
    return pl.pallas_call(
        functools.partial(update_kernel, dense, width),
        grid_spec=pltpu.PrefetchScalarGridSpec(
            num_scalar_prefetch=1,
            grid=(steps, blocks),
            in_specs=[
                pl.BlockSpec((BLOCK, depth, width), lambda c, b, i: (b, 0, c + off)),
                pl.BlockSpec(one, lambda c, b, i: (jnp.minimum((b + 1) * BLOCK, slices - 1), 0, c + off)),
                pl.BlockSpec(one, lambda c, b, i: (0, 0, c + off)),
                pl.BlockSpec(one, lambda c, b, i: (0, 0, c + off)),
                pl.BlockSpec((angles, width), lambda c, b, i: (0, c + off)),
                half_spec, half_spec, half_spec,
                whole(edge_now), whole(edge_prev), whole(edge_inv),
                whole(image_w), whole(weights), whole(wide_w), whole(turned_w),
                by_block(angles * BLOCK), by_block(angles * BLOCK), by_block(angles),
            ]
            + [anywhere] * (len(packets) + 1),
            out_specs=pl.BlockSpec((BLOCK, depth, width), lambda c, b, i: (b, 0, c + off)),
            scratch_shapes=[
                pltpu.VMEM((angles, width), jnp.bfloat16),
                pltpu.VMEM(((BLOCK + 1) * depth, width), jnp.bfloat16),
                pltpu.VMEM((BLOCK * depth, angles * BLOCK), jnp.bfloat16),
                pltpu.VMEM((depth, angles), jnp.bfloat16),
                pltpu.VMEM((2, angles, BLOCK, width), jnp.bfloat16),
                pltpu.SemaphoreType.DMA((2, len(packets))),
            ],
        ),
        out_shape=jax.ShapeDtypeStruct(volume.shape, jnp.float32),
        input_output_aliases=aliases,
        compiler_params=pltpu.CompilerParams(
            dimension_semantics=("arbitrary", "arbitrary"), vmem_limit_bytes=48 * 2**20
        ),
        cost_estimate=pl.CostEstimate(
            flops=4 * slices * depth * cols * angles // parts, bytes_accessed=volume.size * 7 // parts, transcendentals=0
        ),
        name="slab_update",
    )(
        ids, volume, volume, left, right, edge, now, prev, inv, edge_now, edge_prev, edge_inv,
        image_w, weights, wide_w, turned_w, pick_next, pick_now, pick_carry, *packets, before,
    )


def plan_kernel(slots, planes, at_ref, to_ref, sent_ref):
    at = at_ref[...]
    to = to_ref[...]
    lane = lax.broadcasted_iota(jnp.int32, at.shape, 1)
    key = to * CODE + (CODE - 1 - lane)
    sent = [jnp.full(at.shape, -1, jnp.int32) for _ in range(planes - 1)]
    for slot in range(slots):
        for link in reversed(range(planes - 1)):
            ready = (at == link) & (to > link)
            best = jnp.max(jnp.where(ready, key, -1), axis=1, keepdims=True)
            at = jnp.where(ready & (key == best), link + 1, at)
            which = jnp.where(best >= 0, CODE - 1 - best % CODE, -1)
            sent[link] = jnp.where(lane == slot, which, sent[link])
    for link in range(planes - 1):
        sent_ref[link] = sent[link]


def choose_kernel(slot, ups, downs, index_ref, *refs):
    up_from, down_from = refs[:ups], refs[ups : ups + downs]
    up_out, down_out, sems = refs[ups + downs :]
    pairs = ((index_ref[0, slot], up_from, up_out), (index_ref[1, slot], down_from, down_out))
    for n, (index, sources, out) in enumerate(pairs):
        for m, source in enumerate(sources):

            @pl.when(index == m)
            def _():
                pltpu.make_async_copy(source, out, sems.at[n]).start()

    for n, (index, sources, out) in enumerate(pairs):
        pltpu.make_async_copy(sources[0], out, sems.at[n]).wait()


def choose(slot, index, own, ups, downs):
    up_from, down_from = own + ups, own + downs
    anywhere = pl.BlockSpec(memory_space=pl.ANY)
    shape = jax.ShapeDtypeStruct(own[0].shape, own[0].dtype)
    return pl.pallas_call(
        functools.partial(choose_kernel, slot, len(up_from), len(down_from)),
        in_specs=[pl.BlockSpec(memory_space=pltpu.SMEM)] + [anywhere] * (len(up_from) + len(down_from)),
        out_specs=[anywhere, anywhere],
        out_shape=[shape, shape],
        scratch_shapes=[pltpu.SemaphoreType.DMA((2,))],
        cost_estimate=pl.CostEstimate(flops=0, bytes_accessed=4 * own[0].size * 2, transcendentals=0),
        name="choose_packet",
    )(index, *up_from, *down_from)


def make_tables(share, first, rows, path_weights, bases, slices):
    angles, depth = path_weights.shape
    blocks = slices // BLOCK
    weights = path_weights.astype(jnp.float32)
    ray_total = jnp.sum(weights, axis=1)[:, None]
    norm = 1.0 / (ray_total * ((1.0 - share[:, 1:]) + share[:, :-1]))
    coefs = ((1.0 - share[:, 1:]) * norm, share[:, :-1] * norm, norm)

    def by_block(coef):
        coef = coef[:, 1:].reshape(angles, blocks, BLOCK // HALF, HALF).transpose(1, 2, 0, 3)
        coef = coef.reshape(blocks, BLOCK // HALF, angles * HALF, 1)
        return jnp.broadcast_to(coef, coef.shape[:3] + (LANES,))

    def at_edge(coef):
        return jnp.broadcast_to(coef[:, :1], (angles, LANES))

    share_own = share[:, 1:-1]
    row_now = (first - bases)[:, None] + jnp.arange(slices, dtype=jnp.int32)[None, :]
    w_now = jnp.where((row_now >= 0) & (row_now < rows), 1.0 - share_own, 0.0)
    w_next = jnp.where((row_now + 1 >= 0) & (row_now + 1 < rows), share_own, 0.0)
    flat = lambda w: w.reshape(angles, blocks, BLOCK).transpose(1, 0, 2).reshape(blocks, 1, angles * BLOCK)
    pick_next = flat(w_next)
    pick_now = flat(jnp.pad(w_now[:, 1:], ((0, 0), (0, 1))))
    pick_carry = w_now[:, ::BLOCK].T[:, None, :]
    eye = jnp.eye(HALF, dtype=jnp.float32)
    image_w = jnp.einsum("ad,yz->ayzd", weights, eye).reshape(angles * HALF, HALF * depth).astype(jnp.bfloat16)
    wide_w = jnp.repeat(weights.T, BLOCK, axis=1)
    return (
        *[by_block(c) for c in coefs], *[at_edge(c) for c in coefs],
        image_w, path_weights, wide_w, weights.T, pick_next, pick_now, pick_carry,
    )


def on_device(volume, measured, path_weights, fractions, bases):
    slices, depth, cols = volume.shape
    local, rows = measured.shape[:2]
    nslab = lax.axis_size("slab")
    device = lax.axis_index("slab")
    angles = local * nslab
    first = device * slices
    classes = rows // slices
    planes = nslab // classes
    my_class = device % classes
    plane = device // classes

    share = lax.dynamic_slice_in_dim(jnp.pad(fractions, ((0, 0), (1, 1))), first, slices + 2, 1)
    tables = make_tables(share, first, rows, path_weights, bases, slices)
    left = lax.ppermute(volume[slices - 1 :], "slab", [(i, i + 1) for i in range(nslab - 1)])
    right = lax.ppermute(volume[:1], "slab", [(i + 1, i) for i in range(nslab - 1)])
    my_bases = lax.dynamic_slice_in_dim(bases, device * local, local, 0)

    if local > 1 or classes != ROUTED_CLASSES:
        turned = jax.vmap(lambda m, b: jnp.roll(m, b - 1, axis=0))(measured, my_bases)
        by_class = turned.reshape(local, classes, slices, cols).transpose(1, 0, 2, 3)
        outgoing = jnp.tile(by_class, (planes, 1, 1, 1)).reshape(angles, slices, cols)
        seen = lax.all_to_all(outgoing, "slab", split_axis=0, concat_axis=0, tiled=True)
        ends = jnp.roll(by_class[:, :, slices - 1], 1, axis=0)
        ends = jnp.tile(ends, (planes, 1, 1)).reshape(angles, cols // LANES, LANES)
        edge = lax.all_to_all(ends, "slab", split_axis=0, concat_axis=0, tiled=True).reshape(angles, cols)
        return update(volume, left, right, edge, tables, [seen], jnp.zeros((1,), jnp.int32), None, 0, 1, True)

    base = my_bases[0]
    mine = measured[0]
    end_rows = (jnp.arange(classes, dtype=jnp.int32) * slices - base) % rows
    ends = lax.all_gather(mine[end_rows], "slab")
    edge = lax.dynamic_index_in_dim(ends, my_class, 1, keepdims=False)

    doubled = jnp.concatenate([mine, mine], axis=0)
    width = cols // CHUNKS

    def quarter(which, part):
        start = (which * slices - (base - 1)) % rows
        return lax.dynamic_slice(doubled, (start, part * width), (slices, width))

    own = [
        [
            quarter(my_class ^ d, part)
            if d == 0
            else lax.ppermute(quarter(my_class ^ d, part), "slab", [(i, i ^ d) for i in range(nslab)])
            for d in range(classes)
        ]
        for part in range(CHUNKS)
    ]

    most = classes * (planes - 1) + planes - 2
    source = jnp.arange(angles, dtype=jnp.int32) // classes
    low_plane = (bases - 1) // rows
    turn = (bases - 1) % rows
    starts = jnp.arange(classes, dtype=jnp.int32)[:, None] * slices
    highest = low_plane[None] + (starts < turn[None])
    lowest = low_plane[None] + (starts + slices - 1 < turn[None])
    at = jnp.stack([jnp.broadcast_to(source, highest.shape), jnp.broadcast_to(planes - 1 - source, highest.shape)], 1)
    to = jnp.stack([highest, planes - 1 - lowest], 1)
    flat = lambda x: jnp.pad(x.reshape(2 * classes, angles), ((0, 0), (0, LANES - angles)), constant_values=-1)
    sent = pl.pallas_call(
        functools.partial(plan_kernel, most, planes),
        out_shape=jax.ShapeDtypeStruct((planes - 1, 2 * classes, LANES), jnp.int32),
        name="plan_slots",
    )(flat(at), flat(to))
    sent = sent[:, :, :most]
    slots = jnp.sum(jnp.any(sent >= 0, axis=(0, 1)).astype(jnp.int32))
    sent = jnp.pad(sent.reshape(planes - 1, classes, 2, most), ((1, 1), (0, 0), (0, 0), (0, 0)), constant_values=-1)
    line = lax.dynamic_index_in_dim(sent, my_class, 1, keepdims=False)
    pick = lambda index, way: lax.dynamic_index_in_dim(line[:, way], index, 0, keepdims=False)
    sends = jnp.stack([pick(plane + 1, 0), pick(planes - plane, 1)])
    gets = jnp.stack([pick(plane, 0), pick(planes - 1 - plane, 1)])
    arrived = jnp.argmax(gets[:, None, :] == sends[:, :, None], axis=2).astype(jnp.int32)
    index = jnp.where(sends // classes == plane, (sends % classes) ^ my_class, classes + arrived)
    index = jnp.where(sends < 0, 0, index)
    high_here = lax.dynamic_index_in_dim(highest, my_class, 0, keepdims=False)
    low_here = lax.dynamic_index_in_dim(lowest, my_class, 0, keepdims=False)
    wanted = (plane >= low_here) & (plane <= high_here)
    held = plane * classes + (my_class ^ jnp.arange(classes, dtype=jnp.int32))
    keep = lambda ids: jnp.where((ids >= 0) & wanted[jnp.maximum(ids, 0)], ids, -1)
    held, gets = keep(held), keep(gets)

    step = classes
    up = [(i, i + step) for i in range(nslab - step)]
    down = [(i + step, i) for i in range(nslab - step)]

    def run_slots(begin, end, ups, downs):
        ups, downs = [list(u) for u in ups], [list(d) for d in downs]
        for slot in range(begin, end):
            for part in range(CHUNKS):
                go_up, go_down = choose(slot, index, own[part], ups[part], downs[part])
                ups[part].append(lax.ppermute(go_up, "slab", up))
                downs[part].append(lax.ppermute(go_down, "slab", down))
        return ups, downs

    ups, downs = run_slots(0, STEADY, [[] for _ in range(CHUNKS)], [[] for _ in range(CHUNKS)])

    def finish(end):
        def branch(ups, downs):
            ups, downs = run_slots(STEADY, end, ups, downs)
            ids = jnp.concatenate([held, gets[0, :end], gets[1, :end]])
            out = None
            for part in range(CHUNKS):
                packets = own[part] + ups[part] + downs[part]
                out = update(volume, left, right, edge, tables, packets, ids, out, part, CHUNKS, False)
            return out

        return branch

    ends_at = [STEADY, STEADY + 1, STEADY + 2, STEADY + 3, most]
    which = jnp.sum(jnp.array([slots > e for e in ends_at[:-1]]).astype(jnp.int32))
    return lax.switch(which, [finish(e) for e in ends_at], ups, downs)


def solution(mesh):
    placed = (P(("groups", "slab"), None, None), P(("groups", "slab"), None, None), P(), P(), P())
    return jax.shard_map(
        on_device,
        mesh=mesh,
        in_specs=placed,
        out_specs=P(("groups", "slab"), None, None),
        check_vma=False,
    )
```

```python
import functools

import jax
import jax.numpy as jnp
from jax import lax
from jax.experimental import pallas as pl
from jax.experimental.pallas import tpu as pltpu
from jax.sharding import PartitionSpec as P

RELAX = 1.0
BLOCK = 16
HALF = 8
LANES = 128
WIDE = 256
CHUNKS = 2
ROUTED_CLASSES = 4
LOAD = 2
STEADY = 2
CODE = 256


def update_kernel(
    dense, ids_ref, vol_ref, next_ref, left_ref, right_ref, edge_ref, coef_ref, edge_coef_ref,
    image_w_ref, weight_ref, wide_w_ref, turned_w_ref, pick_ref, pick_carry_ref, *rest,
):
    out_ref, carry_ref, spread_ref, carry_w_ref, seen_ref, sems = rest[-6:]
    packets = rest[:-7]
    if not dense:
        packets = [r for p in packets for r in ([p] if p.ndim == 2 else [p.at[n] for n in range(LOAD)])]
    block = pl.program_id(1)
    column = pl.program_id(0)
    blocks = pl.num_programs(1)
    depth, width = vol_ref.shape[1:]
    angles = weight_ref.shape[0]
    step = column * blocks + block
    steps = pl.num_programs(0) * blocks

    def fetch(at_step, act):
        slot = at_step % 2
        rows = pl.ds(pl.multiple_of((at_step % blocks) * BLOCK, BLOCK), BLOCK)
        cols = pl.ds(pl.multiple_of((at_step // blocks) * width, width), width)
        if dense:
            act(pltpu.make_async_copy(packets[0].at[:, rows, cols], seen_ref.at[slot], sems.at[slot, 0]))
            return
        for n, packet in enumerate(packets):

            @pl.when(ids_ref[n] >= 0)
            def _():
                act(pltpu.make_async_copy(packet.at[rows, cols], seen_ref.at[slot, ids_ref[n]], sems.at[slot, n]))

    @pl.when(step == 0)
    def _():
        seen_ref[...] = jnp.zeros_like(seen_ref)
        fetch(step, lambda copy: copy.start())

    @pl.when(step + 1 < steps)
    def _():
        fetch(step + 1, lambda copy: copy.start())

    place = lax.broadcasted_iota(jnp.int32, (depth, angles * BLOCK), 1) % BLOCK
    from_next = wide_w_ref[...] * pick_ref[0, 0:1]
    from_now = wide_w_ref[...] * pick_ref[0, 1:2]
    from_carry = turned_w_ref[...] * pick_carry_ref[0]
    for z in range(BLOCK):
        row = jnp.where(place == z, from_next, jnp.where(place == z - 1, from_now, 0.0))
        total = jnp.sum(row, axis=1, keepdims=True)
        if z == 0:
            total = total + jnp.sum(from_carry, axis=1, keepdims=True)
            carry_w_ref[...] = (from_carry * (RELAX / total)).astype(jnp.bfloat16)
        spread_ref[z * depth : (z + 1) * depth] = (row * (RELAX / total)).astype(jnp.bfloat16)

    def wide(coef):
        return jnp.concatenate([coef] * (WIDE // LANES), axis=1)

    def dot(a, b):
        return jnp.dot(a, b, preferred_element_type=jnp.float32)

    @pl.when(block == 0)
    def _():
        for chunk in range(width // WIDE):
            at = pl.ds(chunk * WIDE, WIDE)
            mine = dot(weight_ref[...], vol_ref[0, :, at])
            before = dot(weight_ref[...], left_ref[0, :, at])
            carry_ref[:, at] = (
                edge_ref[:, at].astype(jnp.float32) * wide(edge_coef_ref[2])
                - mine * wide(edge_coef_ref[0])
                - before * wide(edge_coef_ref[1])
            ).astype(jnp.bfloat16)

    fetch(step, lambda copy: copy.wait())
    slot = step % 2
    final = block == blocks - 1
    count = BLOCK // HALF
    for chunk in range(width // WIDE):
        at = pl.ds(chunk * WIDE, WIDE)
        seen = seen_ref[slot, :, :, at].astype(jnp.float32)
        images = [
            dot(image_w_ref[...], vol_ref[half * HALF : (half + 1) * HALF, :, at].reshape(HALF * depth, WIDE))
            for half in range(count)
        ]
        after = dot(image_w_ref[:, :depth], jnp.where(final, right_ref[0, :, at], next_ref[0, :, at]))
        ahead = [pltpu.roll(x.reshape(angles, HALF, WIDE), HALF - 1, 1) for x in images + [after]]
        tail = lax.broadcasted_iota(jnp.int32, (angles, HALF, WIDE), 1) == HALF - 1
        parts = []
        for half in range(count):
            now = jnp.where(tail, ahead[half + 1], ahead[half]).reshape(angles * HALF, WIDE)
            got = seen[:, half * HALF : (half + 1) * HALF].reshape(angles * HALF, WIDE)
            coef = [wide(coef_ref[0, half, n]) for n in range(3)]
            resid = got * coef[2] - now * coef[0] - images[half] * coef[1]
            parts.append(resid.reshape(angles, HALF, WIDE))
        resid = jnp.concatenate(parts, axis=1)
        spread = dot(spread_ref[...], resid.astype(jnp.bfloat16).reshape(angles * BLOCK, WIDE))
        extra = dot(carry_w_ref[...], carry_ref[:, at])
        carry_ref[:, at] = resid[:, BLOCK - 1].astype(jnp.bfloat16)
        volume = vol_ref[:, :, at].astype(jnp.float32)
        out_ref[0, :, at] = volume[0] + spread[:depth] + extra
        out_ref[1:, :, at] = volume[1:] + spread[depth:].reshape(BLOCK - 1, depth, WIDE)


def update(volume, left, right, edge, tables, packets, ids, before, part, parts, dense):
    slices, depth, cols = volume.shape
    angles = edge.shape[0]
    blocks = slices // BLOCK
    width = min(1024 if angles <= 16 else WIDE, cols // parts)
    steps = cols // parts // width
    off = part * steps
    by_block = lambda x: pl.BlockSpec((1,) + x.shape[1:], lambda c, b, i: (b,) + (0,) * (x.ndim - 1))
    whole = lambda x: pl.BlockSpec(x.shape, lambda c, b, i: (0,) * x.ndim)
    anywhere = pl.BlockSpec(memory_space=pl.ANY)
    coef, edge_coef, image_w, weights, wide_w, turned_w, pick, pick_carry = tables
    if before is None:
        before = edge
        aliases = {}
    else:
        aliases = {14 + len(packets): 0}
    one = (1, depth, width)
    return pl.pallas_call(
        functools.partial(update_kernel, dense),
        grid_spec=pltpu.PrefetchScalarGridSpec(
            num_scalar_prefetch=1,
            grid=(steps, blocks),
            in_specs=[
                pl.BlockSpec((BLOCK, depth, width), lambda c, b, i: (b, 0, c + off)),
                pl.BlockSpec(one, lambda c, b, i: (jnp.minimum((b + 1) * BLOCK, slices - 1), 0, c + off)),
                pl.BlockSpec(one, lambda c, b, i: (0, 0, c + off)),
                pl.BlockSpec(one, lambda c, b, i: (0, 0, c + off)),
                pl.BlockSpec((angles, width), lambda c, b, i: (0, c + off)),
                by_block(coef), whole(edge_coef), whole(image_w), whole(weights), whole(wide_w), whole(turned_w),
                by_block(pick), by_block(pick_carry),
            ]
            + [anywhere] * (len(packets) + 1),
            out_specs=pl.BlockSpec((BLOCK, depth, width), lambda c, b, i: (b, 0, c + off)),
            scratch_shapes=[
                pltpu.VMEM((angles, width), jnp.bfloat16),
                pltpu.VMEM((BLOCK * depth, angles * BLOCK), jnp.bfloat16),
                pltpu.VMEM((depth, angles), jnp.bfloat16),
                pltpu.VMEM((2, angles, BLOCK, width), jnp.bfloat16),
                pltpu.SemaphoreType.DMA((2, ids.shape[0])),
            ],
        ),
        out_shape=jax.ShapeDtypeStruct(volume.shape, jnp.float32),
        input_output_aliases=aliases,
        compiler_params=pltpu.CompilerParams(
            dimension_semantics=("arbitrary", "arbitrary"), vmem_limit_bytes=48 * 2**20
        ),
        cost_estimate=pl.CostEstimate(
            flops=4 * slices * depth * cols * angles // parts, bytes_accessed=volume.size * 7 // parts, transcendentals=0
        ),
        name="slab_update",
    )(
        ids, volume, volume, left, right, edge, coef, edge_coef,
        image_w, weights, wide_w, turned_w, pick, pick_carry, *packets, before,
    )


def plan_kernel(slots, planes, at_ref, to_ref, sent_ref):
    at = at_ref[...]
    to = to_ref[...]
    lane = lax.broadcasted_iota(jnp.int32, at.shape, 1)
    key = to * CODE + (CODE - 1 - lane)
    sent = [jnp.full(at.shape, -1, jnp.int32) for _ in range(planes - 1)]
    for slot in range(slots):
        for link in reversed(range(planes - 1)):
            for n in range(LOAD):
                ready = (at == link) & (to > link)
                best = jnp.max(jnp.where(ready, key, -1), axis=1, keepdims=True)
                at = jnp.where(ready & (key == best), link + 1, at)
                which = jnp.where(best >= 0, CODE - 1 - best % CODE, -1)
                sent[link] = jnp.where(lane == slot * LOAD + n, which, sent[link])
    for link in range(planes - 1):
        sent_ref[link] = sent[link]


def choose_kernel(slot, ups, downs, index_ref, *refs):
    sources = refs[:ups], refs[ups : ups + downs]
    outs = refs[ups + downs : ups + downs + 2]
    held, sems = refs[ups + downs + 2 :]
    views = [[r for p in side for r in ([p] if p.ndim == 2 else [p.at[n] for n in range(LOAD)])] for side in sources]
    for way in range(2):
        for n in range(LOAD):
            for m, view in enumerate(views[way]):

                @pl.when(index_ref[way, slot * LOAD + n] == m)
                def _():
                    pltpu.make_async_copy(view, held.at[way, n], sems.at[0, way, n]).start()

    for way in range(2):
        for n in range(LOAD):
            pltpu.make_async_copy(views[way][0], held.at[way, n], sems.at[0, way, n]).wait()
            pltpu.make_async_copy(held.at[way, n], outs[way].at[n], sems.at[1, way, n]).start()
    for way in range(2):
        for n in range(LOAD):
            pltpu.make_async_copy(held.at[way, n], outs[way].at[n], sems.at[1, way, n]).wait()


def choose(slot, index, own, ups, downs):
    up_from, down_from = own + ups, own + downs
    anywhere = pl.BlockSpec(memory_space=pl.ANY)
    shape = jax.ShapeDtypeStruct((LOAD,) + own[0].shape, own[0].dtype)
    return pl.pallas_call(
        functools.partial(choose_kernel, slot, len(up_from), len(down_from)),
        in_specs=[pl.BlockSpec(memory_space=pltpu.SMEM)] + [anywhere] * (len(up_from) + len(down_from)),
        out_specs=[anywhere, anywhere],
        out_shape=[shape, shape],
        scratch_shapes=[
            pltpu.VMEM((2, LOAD) + own[0].shape, own[0].dtype),
            pltpu.SemaphoreType.DMA((2, 2, LOAD)),
        ],
        cost_estimate=pl.CostEstimate(flops=0, bytes_accessed=4 * LOAD * own[0].size * 2, transcendentals=0),
        name="choose_packet",
    )(index, *up_from, *down_from)


def make_tables(share, first, rows, path_weights, bases, slices):
    angles, depth = path_weights.shape
    blocks = slices // BLOCK
    weights = path_weights.astype(jnp.float32)
    ray_total = jnp.sum(weights, axis=1)[:, None]
    norm = 1.0 / (ray_total * ((1.0 - share[:, 1:]) + share[:, :-1]))
    coefs = jnp.stack([(1.0 - share[:, 1:]) * norm, share[:, :-1] * norm, norm])
    coef = coefs[:, :, 1:].reshape(3, angles, blocks, BLOCK // HALF, HALF).transpose(2, 3, 0, 1, 4)
    coef = coef.reshape(blocks, BLOCK // HALF, 3, angles * HALF, 1)
    coef = jnp.broadcast_to(coef, coef.shape[:4] + (LANES,))
    edge_coef = jnp.broadcast_to(coefs[:, :, :1], (3, angles, LANES))
    share_own = share[:, 1:-1]
    row_now = (first - bases)[:, None] + jnp.arange(slices, dtype=jnp.int32)[None, :]
    w_now = jnp.where((row_now >= 0) & (row_now < rows), 1.0 - share_own, 0.0)
    w_next = jnp.where((row_now + 1 >= 0) & (row_now + 1 < rows), share_own, 0.0)
    pick = jnp.stack([w_next, jnp.pad(w_now[:, 1:], ((0, 0), (0, 1)))]).reshape(2, angles, blocks, BLOCK)
    pick = pick.transpose(2, 0, 1, 3).reshape(blocks, 2, angles * BLOCK)
    pick_carry = w_now[:, ::BLOCK].T[:, None, :]
    eye = jnp.eye(HALF, dtype=jnp.float32)
    image_w = jnp.einsum("ad,yz->ayzd", weights, eye).reshape(angles * HALF, HALF * depth).astype(jnp.bfloat16)
    wide_w = jnp.repeat(weights.T, BLOCK, axis=1)
    return coef, edge_coef, image_w, path_weights, wide_w, weights.T, pick, pick_carry


def on_device(volume, measured, path_weights, fractions, bases):
    slices, depth, cols = volume.shape
    local, rows = measured.shape[:2]
    nslab = lax.axis_size("slab")
    device = lax.axis_index("slab")
    angles = local * nslab
    first = device * slices
    classes = rows // slices
    planes = nslab // classes
    my_class = device % classes
    plane = device // classes

    share = lax.dynamic_slice_in_dim(jnp.pad(fractions, ((0, 0), (1, 1))), first, slices + 2, 1)
    tables = make_tables(share, first, rows, path_weights, bases, slices)
    left = lax.ppermute(volume[slices - 1 :], "slab", [(i, i + 1) for i in range(nslab - 1)])
    right = lax.ppermute(volume[:1], "slab", [(i + 1, i) for i in range(nslab - 1)])
    my_bases = lax.dynamic_slice_in_dim(bases, device * local, local, 0)

    if local > 1 or classes != ROUTED_CLASSES:
        turned = jax.vmap(lambda m, b: jnp.roll(m, b - 1, axis=0))(measured, my_bases)
        by_class = turned.reshape(local, classes, slices, cols).transpose(1, 0, 2, 3)
        outgoing = jnp.tile(by_class, (planes, 1, 1, 1)).reshape(angles, slices, cols)
        seen = lax.all_to_all(outgoing, "slab", split_axis=0, concat_axis=0, tiled=True)
        ends = jnp.roll(by_class[:, :, slices - 1], 1, axis=0)
        ends = jnp.tile(ends, (planes, 1, 1)).reshape(angles, cols // LANES, LANES)
        edge = lax.all_to_all(ends, "slab", split_axis=0, concat_axis=0, tiled=True).reshape(angles, cols)
        return update(volume, left, right, edge, tables, [seen], jnp.zeros((1,), jnp.int32), None, 0, 1, True)

    base = my_bases[0]
    mine = measured[0]
    end_rows = (jnp.arange(classes, dtype=jnp.int32) * slices - base) % rows
    ends = jnp.concatenate([lax.dynamic_slice_in_dim(mine, end_rows[c], 1, 0) for c in range(classes)])

    doubled = jnp.concatenate([mine, mine], axis=0)
    width = cols // CHUNKS

    def quarter(which, part):
        start = (which * slices - (base - 1)) % rows
        return lax.dynamic_slice(doubled, (start, part * width), (slices, width))

    own = [
        [
            quarter(my_class ^ d, part)
            if d == 0
            else lax.ppermute(quarter(my_class ^ d, part), "slab", [(i, i ^ d) for i in range(nslab)])
            for d in range(classes)
        ]
        for part in range(CHUNKS)
    ]

    most = -(-classes * (planes - 1) // LOAD) + planes - 2
    room = most * LOAD
    source = jnp.arange(angles, dtype=jnp.int32) // classes
    low_plane = (bases - 1) // rows
    turn = (bases - 1) % rows
    starts = jnp.arange(classes, dtype=jnp.int32)[:, None] * slices
    highest = low_plane[None] + (starts < turn[None])
    lowest = low_plane[None] + (starts + slices - 1 < turn[None])
    at = jnp.stack([jnp.broadcast_to(source, highest.shape), jnp.broadcast_to(planes - 1 - source, highest.shape)], 1)
    to = jnp.stack([highest, planes - 1 - lowest], 1)
    flat = lambda x: jnp.pad(x.reshape(2 * classes, angles), ((0, 0), (0, LANES - angles)), constant_values=-1)
    sent = pl.pallas_call(
        functools.partial(plan_kernel, most, planes),
        out_shape=jax.ShapeDtypeStruct((planes - 1, 2 * classes, LANES), jnp.int32),
        name="plan_slots",
    )(flat(at), flat(to))
    sent, ends = lax.optimization_barrier((sent, ends))
    ends = jnp.tile(ends[None], (planes, 1, 1)).reshape(angles, cols // LANES, LANES)
    edge = lax.all_to_all(ends, "slab", split_axis=0, concat_axis=0, tiled=True).reshape(angles, cols)
    sent = sent[:, :, :room]
    slots = jnp.sum(jnp.any(sent[:, :, ::LOAD] >= 0, axis=(0, 1)).astype(jnp.int32))
    sent = jnp.pad(sent.reshape(planes - 1, classes, 2, room), ((1, 1), (0, 0), (0, 0), (0, 0)), constant_values=-1)
    line = lax.dynamic_index_in_dim(sent, my_class, 1, keepdims=False)
    pick = lambda index, way: lax.dynamic_index_in_dim(line[:, way], index, 0, keepdims=False)
    sends = jnp.stack([pick(plane + 1, 0), pick(planes - plane, 1)])
    gets = jnp.stack([pick(plane, 0), pick(planes - 1 - plane, 1)])
    arrived = jnp.argmax(gets[:, None, :] == sends[:, :, None], axis=2).astype(jnp.int32)
    index = jnp.where(sends // classes == plane, (sends % classes) ^ my_class, classes + arrived)
    index = jnp.where(sends < 0, 0, index)
    high_here = lax.dynamic_index_in_dim(highest, my_class, 0, keepdims=False)
    low_here = lax.dynamic_index_in_dim(lowest, my_class, 0, keepdims=False)
    wanted = (plane >= low_here) & (plane <= high_here)
    held = plane * classes + (my_class ^ jnp.arange(classes, dtype=jnp.int32))
    keep = lambda ids: jnp.where((ids >= 0) & wanted[jnp.maximum(ids, 0)], ids, -1)
    held, gets = keep(held), keep(gets)
    index, edge = lax.optimization_barrier((index, edge))

    step = classes
    up = [(i, i + step) for i in range(nslab - step)]
    down = [(i + step, i) for i in range(nslab - step)]

    def run_slots(begin, end, ups, downs):
        ups, downs = [list(u) for u in ups], [list(d) for d in downs]
        for slot in range(begin, end):
            for part in range(CHUNKS):
                go_up, go_down = choose(slot, index, own[part], ups[part], downs[part])
                ups[part].append(lax.ppermute(go_up, "slab", up))
                downs[part].append(lax.ppermute(go_down, "slab", down))
        return ups, downs

    ups, downs = run_slots(0, STEADY, [[] for _ in range(CHUNKS)], [[] for _ in range(CHUNKS)])

    def finish(end):
        def branch(ups, downs):
            ups, downs = run_slots(STEADY, end, ups, downs)
            ids = jnp.concatenate([held, gets[0, : end * LOAD], gets[1, : end * LOAD]])
            out = None
            for part in range(CHUNKS):
                packets = own[part] + ups[part] + downs[part]
                out = update(volume, left, right, edge, tables, packets, ids, out, part, CHUNKS, False)
            return out

        return branch

    ends_at = [STEADY + 1, STEADY + 2, most]
    which = jnp.sum(jnp.array([slots > e for e in ends_at[:-1]]).astype(jnp.int32))
    return lax.switch(which, [finish(e) for e in ends_at], ups, downs)


def solution(mesh):
    placed = (P(("groups", "slab"), None, None), P(("groups", "slab"), None, None), P(), P(), P())
    return jax.shard_map(
        on_device,
        mesh=mesh,
        in_specs=placed,
        out_specs=P(("groups", "slab"), None, None),
        check_vma=False,
    )
```

```python
import functools

import jax
import jax.numpy as jnp
from jax import lax
from jax.experimental import pallas as pl
from jax.experimental.pallas import tpu as pltpu
from jax.sharding import PartitionSpec as P

RELAX = 1.0
BLOCK = 16
HALF = 8
LANES = 128
WIDE = 512
CHUNKS = 2
ROUTED_CLASSES = 4
LOAD = 2
STEADY = 2
CODE = 256


def update_kernel(
    dense, ids_ref, vol_ref, next_ref, left_ref, right_ref, edge_ref, coef_ref, edge_coef_ref,
    image_w_ref, weight_ref, spread_ref, carry_w_ref, *rest,
):
    out_ref, carry_ref, seen_ref, sems = rest[-4:]
    packets = rest[:-5]
    if not dense:
        packets = [r for p in packets for r in ([p] if p.ndim == 2 else [p.at[n] for n in range(LOAD)])]
    block = pl.program_id(1)
    column = pl.program_id(0)
    blocks = pl.num_programs(1)
    depth, width = vol_ref.shape[1:]
    angles = weight_ref.shape[0]
    step = column * blocks + block
    steps = pl.num_programs(0) * blocks

    def fetch(at_step, act):
        slot = at_step % 2
        rows = pl.ds(pl.multiple_of((at_step % blocks) * BLOCK, BLOCK), BLOCK)
        cols = pl.ds(pl.multiple_of((at_step // blocks) * width, width), width)
        if dense:
            act(pltpu.make_async_copy(packets[0].at[:, rows, cols], seen_ref.at[slot], sems.at[slot, 0]))
            return
        arrived = (len(packets) - ROUTED_CLASSES) // 2
        names = [(4, n) for n in range(ROUTED_CLASSES)] + [(way, n) for way in (2, 3) for n in range(arrived)]
        for n, (packet, name) in enumerate(zip(packets, names)):

            @pl.when(ids_ref[name] >= 0)
            def _():
                act(pltpu.make_async_copy(packet.at[rows, cols], seen_ref.at[slot, ids_ref[name]], sems.at[slot, n]))

    @pl.when(step == 0)
    def _():
        seen_ref[...] = jnp.zeros_like(seen_ref)
        fetch(step, lambda copy: copy.start())

    @pl.when(step + 1 < steps)
    def _():
        fetch(step + 1, lambda copy: copy.start())

    def wide(coef):
        return jnp.concatenate([coef] * (WIDE // LANES), axis=1)

    def dot(a, b):
        return jnp.dot(a, b, preferred_element_type=jnp.float32)

    @pl.when(block == 0)
    def _():
        for chunk in range(width // WIDE):
            at = pl.ds(chunk * WIDE, WIDE)
            mine = dot(weight_ref[...], vol_ref[0, :, at])
            before = dot(weight_ref[...], left_ref[0, :, at])
            carry_ref[:, at] = (
                edge_ref[:, at].astype(jnp.float32) * wide(edge_coef_ref[2])
                - mine * wide(edge_coef_ref[0])
                - before * wide(edge_coef_ref[1])
            ).astype(jnp.bfloat16)

    fetch(step, lambda copy: copy.wait())
    slot = step % 2
    final = block == blocks - 1
    count = BLOCK // HALF
    for chunk in range(width // WIDE):
        at = pl.ds(chunk * WIDE, WIDE)
        seen = seen_ref[slot, :, :, at].astype(jnp.float32)
        images = [
            dot(image_w_ref[...], vol_ref[half * HALF : (half + 1) * HALF, :, at].reshape(HALF * depth, WIDE))
            for half in range(count)
        ]
        after = dot(weight_ref[...], jnp.where(final, right_ref[0, :, at], next_ref[0, :, at]))
        ahead = [pltpu.roll(x.reshape(angles, HALF, WIDE), HALF - 1, 1) for x in images]
        ahead.append(jnp.broadcast_to(after.reshape(angles, 1, WIDE), (angles, HALF, WIDE)))
        tail = lax.broadcasted_iota(jnp.int32, (angles, HALF, WIDE), 1) == HALF - 1
        parts = []
        for half in range(count):
            now = jnp.where(tail, ahead[half + 1], ahead[half]).reshape(angles * HALF, WIDE)
            got = seen[:, half * HALF : (half + 1) * HALF].reshape(angles * HALF, WIDE)
            coef = [wide(coef_ref[0, half, n]) for n in range(3)]
            resid = got * coef[2] - now * coef[0] - images[half] * coef[1]
            parts.append(resid.reshape(angles, HALF, WIDE))
        resid = jnp.concatenate(parts, axis=1)
        spread = dot(spread_ref[0], resid.astype(jnp.bfloat16).reshape(angles * BLOCK, WIDE))
        extra = dot(carry_w_ref[0], carry_ref[:, at])
        carry_ref[:, at] = resid[:, BLOCK - 1].astype(jnp.bfloat16)
        volume = vol_ref[:, :, at].astype(jnp.float32)
        out_ref[0, :, at] = volume[0] + spread[:depth] + extra
        out_ref[1:, :, at] = volume[1:] + spread[depth:].reshape(BLOCK - 1, depth, WIDE)


def update(volume, left, right, edge, tables, packets, ids, before, part, parts, dense):
    slices, depth, cols = volume.shape
    angles = edge.shape[0]
    blocks = slices // BLOCK
    width = min(1024 if angles <= 16 else WIDE, cols // parts)
    steps = cols // parts // width
    off = part * steps
    by_block = lambda x: pl.BlockSpec((1,) + x.shape[1:], lambda c, b, i: (b,) + (0,) * (x.ndim - 1))
    whole = lambda x: pl.BlockSpec(x.shape, lambda c, b, i: (0,) * x.ndim)
    anywhere = pl.BlockSpec(memory_space=pl.ANY)
    coef, edge_coef, image_w, weights, spread_w, carry_w = tables
    if before is None:
        before = edge
        aliases = {}
    else:
        aliases = {12 + len(packets): 0}
    one = (1, depth, width)
    return pl.pallas_call(
        functools.partial(update_kernel, dense),
        grid_spec=pltpu.PrefetchScalarGridSpec(
            num_scalar_prefetch=1,
            grid=(steps, blocks),
            in_specs=[
                pl.BlockSpec((BLOCK, depth, width), lambda c, b, i: (b, 0, c + off)),
                pl.BlockSpec(one, lambda c, b, i: (jnp.minimum((b + 1) * BLOCK, slices - 1), 0, c + off)),
                pl.BlockSpec(one, lambda c, b, i: (0, 0, c + off)),
                pl.BlockSpec(one, lambda c, b, i: (0, 0, c + off)),
                pl.BlockSpec((angles, width), lambda c, b, i: (0, c + off)),
                by_block(coef), whole(edge_coef), whole(image_w), whole(weights), by_block(spread_w), by_block(carry_w),
            ]
            + [anywhere] * (len(packets) + 1),
            out_specs=pl.BlockSpec((BLOCK, depth, width), lambda c, b, i: (b, 0, c + off)),
            scratch_shapes=[
                pltpu.VMEM((angles, width), jnp.bfloat16),
                pltpu.VMEM((2, angles, BLOCK, width), jnp.bfloat16),
                pltpu.SemaphoreType.DMA((2, 1 if dense else ROUTED_CLASSES + LOAD * (len(packets) - ROUTED_CLASSES))),
            ],
        ),
        out_shape=jax.ShapeDtypeStruct(volume.shape, jnp.float32),
        input_output_aliases=aliases,
        compiler_params=pltpu.CompilerParams(
            dimension_semantics=("arbitrary", "arbitrary"), vmem_limit_bytes=48 * 2**20
        ),
        cost_estimate=pl.CostEstimate(
            flops=4 * slices * depth * cols * angles // parts, bytes_accessed=volume.size * 7 // parts, transcendentals=0
        ),
        name="slab_update",
    )(
        ids, volume, volume, left, right, edge, coef, edge_coef,
        image_w, weights, spread_w, carry_w, *packets, before,
    )


def weights_kernel(wide_w_ref, turned_w_ref, pick_ref, pick_carry_ref, spread_ref, carry_w_ref):
    depth, columns = wide_w_ref.shape
    place = lax.broadcasted_iota(jnp.int32, (depth, columns), 1) % BLOCK
    from_next = wide_w_ref[...] * pick_ref[0, 0:1]
    from_now = wide_w_ref[...] * pick_ref[0, 1:2]
    from_carry = turned_w_ref[...] * pick_carry_ref[0]
    for z in range(BLOCK):
        row = jnp.where(place == z, from_next, jnp.where(place == z - 1, from_now, 0.0))
        total = jnp.sum(row, axis=1, keepdims=True)
        if z == 0:
            total = total + jnp.sum(from_carry, axis=1, keepdims=True)
            carry_w_ref[0] = (from_carry * (RELAX / total)).astype(jnp.bfloat16)
        spread_ref[0, z * depth : (z + 1) * depth] = (row * (RELAX / total)).astype(jnp.bfloat16)


def make_weights(wide_w, turned_w, pick, pick_carry):
    blocks = pick.shape[0]
    depth, angles = turned_w.shape
    by_block = lambda shape: pl.BlockSpec((1,) + shape, lambda b: (b,) + (0,) * len(shape))
    whole = lambda x: pl.BlockSpec(x.shape, lambda b: (0,) * x.ndim)
    spread = (BLOCK * depth, angles * BLOCK)
    carry = (depth, angles)
    return pl.pallas_call(
        weights_kernel,
        grid=(blocks,),
        in_specs=[whole(wide_w), whole(turned_w), by_block(pick.shape[1:]), by_block(pick_carry.shape[1:])],
        out_specs=[by_block(spread), by_block(carry)],
        out_shape=[
            jax.ShapeDtypeStruct((blocks,) + spread, jnp.bfloat16),
            jax.ShapeDtypeStruct((blocks,) + carry, jnp.bfloat16),
        ],
        name="spread_weights",
    )(wide_w, turned_w, pick, pick_carry)


def plan_kernel(slots, planes, classes, angles, slices, rows, device_ref, bases_ref, table_ref):
    shape = (2 * classes, LANES)
    lane = lax.broadcasted_iota(jnp.int32, shape, 1)
    row = lax.broadcasted_iota(jnp.int32, shape, 0)
    class_shift = classes.bit_length() - 1
    base = jnp.broadcast_to(bases_ref[...], shape) - 1
    low_plane = base >> (rows.bit_length() - 1)
    turn = base & (rows - 1)

    def reach(which):
        lowest = low_plane + jnp.where(which * slices + slices - 1 < turn, 1, 0)
        highest = low_plane + jnp.where(which * slices < turn, 1, 0)
        return lowest, highest

    lowest, highest = reach(row >> 1)
    upward = (row & 1) == 0
    source = lane >> class_shift
    at = jnp.where(upward, source, planes - 1 - source)
    to = jnp.where(lane < angles, jnp.where(upward, highest, planes - 1 - lowest), -1)
    key = to * CODE + (CODE - 1 - lane)
    sent = [jnp.full(shape, -1, jnp.int32) for _ in range(planes - 1)]
    for slot in range(slots):
        begin = at
        for link in range(planes - 1):
            ready = (begin == link) & (to > link)
            for n in range(LOAD):
                best = jnp.max(jnp.where(ready, key, -1), axis=1, keepdims=True)
                taken = ready & (key == best)
                at = jnp.where(taken, link + 1, at)
                ready = ready & (key != best)
                which = jnp.where(best >= 0, CODE - 1 - (best & (CODE - 1)), -1)
                sent[link] = jnp.where(lane == slot * LOAD + n, which, sent[link])

    me = device_ref[0]
    my_class = me & (classes - 1)
    plane = me >> class_shift
    none = jnp.full(shape, -1, jnp.int32)
    used = none
    for link in range(planes - 1):
        used = jnp.maximum(used, sent[link])
    used = jnp.max(used, axis=0, keepdims=True)
    head = lane[:1]
    count = jnp.sum(jnp.where((used >= 0) & (head % LOAD == 0), 1, 0), axis=1, keepdims=True)

    tall = -(-max(slots * LOAD, angles) // 8) * 8
    sub = lax.broadcasted_iota(jnp.int32, (tall, LANES), 0)
    wide = lax.broadcasted_iota(jnp.int32, (tall, LANES), 1)
    column = lambda x: jnp.max(jnp.where(sub == wide, x, -1), axis=1, keepdims=True)
    low_here, high_here = reach(my_class)
    wanted = (plane >= low_here) & (plane <= high_here) & (lane < angles)
    wanted = column(jnp.where(wanted, 1, 0)[:1]) > 0
    keep = lambda ids: jnp.max(jnp.where((sub == ids) & wanted, ids, -1), axis=0, keepdims=True)

    indices, kept = [], []
    for way, spot in ((0, plane), (1, planes - 1 - plane)):
        sends, gets = none, none
        for link in range(planes - 1):
            sends = jnp.where(spot == link, sent[link], sends)
            gets = jnp.where(spot == link + 1, sent[link], gets)
        mine = row == 2 * my_class + way
        sends = jnp.max(jnp.where(mine, sends, -1), axis=0, keepdims=True)
        gets = jnp.max(jnp.where(mine, gets, -1), axis=0, keepdims=True)
        arrived = jnp.max(jnp.where((column(gets) == sends) & (sends >= 0), sub, 0), axis=0, keepdims=True)
        own = (sends >> class_shift) == plane
        index = jnp.where(own, (sends & (classes - 1)) ^ my_class, classes + arrived)
        indices.append(jnp.where(sends >= 0, index, 0))
        kept.append(keep(gets))
    held = jnp.where(head < classes, plane * classes + (head ^ my_class), -1)
    for n, line in enumerate(indices + kept + [keep(held), jnp.broadcast_to(count, held.shape)]):
        table_ref[n : n + 1] = line


def choose_kernel(slot, ups, downs, index_ref, *refs):
    sources = refs[:ups], refs[ups : ups + downs]
    outs = refs[ups + downs : ups + downs + 2]
    held, sems = refs[ups + downs + 2 :]
    views = [[r for p in side for r in ([p] if p.ndim == 2 else [p.at[n] for n in range(LOAD)])] for side in sources]
    for way in range(2):
        for n in range(LOAD):
            for m, view in enumerate(views[way]):

                @pl.when(index_ref[way, slot * LOAD + n] == m)
                def _():
                    pltpu.make_async_copy(view, held.at[way, n], sems.at[0, way, n]).start()

    for way in range(2):
        for n in range(LOAD):
            pltpu.make_async_copy(views[way][0], held.at[way, n], sems.at[0, way, n]).wait()
            pltpu.make_async_copy(held.at[way, n], outs[way].at[n], sems.at[1, way, n]).start()
    for way in range(2):
        for n in range(LOAD):
            pltpu.make_async_copy(held.at[way, n], outs[way].at[n], sems.at[1, way, n]).wait()


def choose(slot, index, own, ups, downs):
    up_from, down_from = own + ups, own + downs
    anywhere = pl.BlockSpec(memory_space=pl.ANY)
    shape = jax.ShapeDtypeStruct((LOAD,) + own[0].shape, own[0].dtype)
    return pl.pallas_call(
        functools.partial(choose_kernel, slot, len(up_from), len(down_from)),
        in_specs=[pl.BlockSpec(memory_space=pltpu.SMEM)] + [anywhere] * (len(up_from) + len(down_from)),
        out_specs=[anywhere, anywhere],
        out_shape=[shape, shape],
        scratch_shapes=[
            pltpu.VMEM((2, LOAD) + own[0].shape, own[0].dtype),
            pltpu.SemaphoreType.DMA((2, 2, LOAD)),
        ],
        cost_estimate=pl.CostEstimate(flops=0, bytes_accessed=4 * LOAD * own[0].size * 2, transcendentals=0),
        name="choose_packet",
    )(index, *up_from, *down_from)


def make_tables(share, first, rows, path_weights, bases, slices):
    angles, depth = path_weights.shape
    blocks = slices // BLOCK
    weights = path_weights.astype(jnp.float32)
    ray_total = jnp.sum(weights, axis=1)[:, None]
    norm = 1.0 / (ray_total * ((1.0 - share[:, 1:]) + share[:, :-1]))
    coefs = jnp.stack([(1.0 - share[:, 1:]) * norm, share[:, :-1] * norm, norm])
    coef = coefs[:, :, 1:].reshape(3, angles, blocks, BLOCK // HALF, HALF).transpose(2, 3, 0, 1, 4)
    coef = coef.reshape(blocks, BLOCK // HALF, 3, angles * HALF, 1)
    coef = jnp.broadcast_to(coef, coef.shape[:4] + (LANES,))
    edge_coef = jnp.broadcast_to(coefs[:, :, :1], (3, angles, LANES))
    share_own = share[:, 1:-1]
    row_now = (first - bases)[:, None] + jnp.arange(slices, dtype=jnp.int32)[None, :]
    w_now = jnp.where((row_now >= 0) & (row_now < rows), 1.0 - share_own, 0.0)
    w_next = jnp.where((row_now + 1 >= 0) & (row_now + 1 < rows), share_own, 0.0)
    pick = jnp.stack([w_next, jnp.pad(w_now[:, 1:], ((0, 0), (0, 1)))]).reshape(2, angles, blocks, BLOCK)
    pick = pick.transpose(2, 0, 1, 3).reshape(blocks, 2, angles * BLOCK)
    pick_carry = w_now[:, ::BLOCK].T[:, None, :]
    eye = jnp.eye(HALF, dtype=jnp.float32)
    image_w = jnp.einsum("ad,yz->ayzd", weights, eye).reshape(angles * HALF, HALF * depth).astype(jnp.bfloat16)
    wide_w = jnp.repeat(weights.T, BLOCK, axis=1)
    return coef, edge_coef, image_w, path_weights, *make_weights(wide_w, weights.T, pick, pick_carry)


def on_device(volume, measured, path_weights, fractions, bases):
    slices, depth, cols = volume.shape
    local, rows = measured.shape[:2]
    nslab = lax.axis_size("slab")
    device = lax.axis_index("slab")
    angles = local * nslab
    first = device * slices
    classes = rows // slices
    planes = nslab // classes
    my_class = device % classes
    plane = device // classes

    halos = (volume[slices - 1 :], volume[:1])

    def prepare(fractions, halos):
        share = lax.dynamic_slice_in_dim(jnp.pad(fractions, ((0, 0), (1, 1))), first, slices + 2, 1)
        tables = make_tables(share, first, rows, path_weights, bases, slices)
        left = lax.ppermute(halos[0], "slab", [(i, i + 1) for i in range(nslab - 1)])
        right = lax.ppermute(halos[1], "slab", [(i + 1, i) for i in range(nslab - 1)])
        return left, right, tables

    my_bases = lax.dynamic_slice_in_dim(bases, device * local, local, 0)

    if local > 1 or classes != ROUTED_CLASSES or rows & (rows - 1) or angles > LANES:
        turned = jax.vmap(lambda m, b: jnp.roll(m, b - 1, axis=0))(measured, my_bases)
        by_class = turned.reshape(local, classes, slices, cols).transpose(1, 0, 2, 3)
        outgoing = jnp.tile(by_class, (planes, 1, 1, 1)).reshape(angles, slices, cols)
        seen = lax.all_to_all(outgoing, "slab", split_axis=0, concat_axis=0, tiled=True)
        ends = jnp.roll(by_class[:, :, slices - 1], 1, axis=0)
        ends = jnp.tile(ends, (planes, 1, 1)).reshape(angles, cols // LANES, LANES)
        edge = lax.all_to_all(ends, "slab", split_axis=0, concat_axis=0, tiled=True).reshape(angles, cols)
        left, right, tables = prepare(fractions, halos)
        return update(volume, left, right, edge, tables, [seen], jnp.zeros((8, LANES), jnp.int32), None, 0, 1, True)

    base = my_bases[0]
    mine = measured[0]
    end_rows = (jnp.arange(classes, dtype=jnp.int32) * slices - base) % rows
    ends = jnp.concatenate([lax.dynamic_slice_in_dim(mine, end_rows[c], 1, 0) for c in range(classes)])

    doubled = jnp.concatenate([mine, mine], axis=0)
    width = cols // CHUNKS

    def quarter(which, part):
        start = (which * slices - (base - 1)) % rows
        return lax.dynamic_slice(doubled, (start, part * width), (slices, width))

    quarters = [[quarter(my_class ^ d, part) for d in range(classes)] for part in range(CHUNKS)]
    row_of_bases = jnp.pad(bases, (0, LANES - angles), constant_values=1)[None]
    quarters[0], row_of_bases = lax.optimization_barrier((quarters[0], row_of_bases))
    own = []
    for part in range(CHUNKS):
        if part:
            quarters[part], own[-1] = lax.optimization_barrier((quarters[part], own[-1]))
        own.append(
            [quarters[part][0]]
            + [lax.ppermute(quarters[part][d], "slab", [(i, i ^ d) for i in range(nslab)]) for d in range(1, classes)]
        )

    most = -(-classes * (planes - 1) // LOAD) + planes - 2
    table = pl.pallas_call(
        functools.partial(plan_kernel, most, planes, classes, angles, slices, rows),
        in_specs=[pl.BlockSpec(memory_space=pltpu.SMEM), pl.BlockSpec(memory_space=pltpu.VMEM)],
        out_shape=jax.ShapeDtypeStruct((8, LANES), jnp.int32),
        name="plan_slots",
    )(device.astype(jnp.int32)[None], row_of_bases)
    table, ends = lax.optimization_barrier((table, ends))
    ends = jnp.tile(ends[None], (planes, 1, 1)).reshape(angles, cols // LANES, LANES)
    edge = lax.all_to_all(ends, "slab", split_axis=0, concat_axis=0, tiled=True).reshape(angles, cols)
    table, edge = lax.optimization_barrier((table, edge))
    slots = table[5, 0]

    step = classes
    up = [(i, i + step) for i in range(nslab - step)]
    down = [(i + step, i) for i in range(nslab - step)]

    def run_slots(begin, end, ups, downs):
        ups, downs = [list(u) for u in ups], [list(d) for d in downs]
        for slot in range(begin, end):
            for part in range(CHUNKS):
                go_up, go_down = choose(slot, table, own[part], ups[part], downs[part])
                if slot == 0 and part == CHUNKS - 1:
                    go_up, *late = lax.optimization_barrier((go_up, fractions, halos))
                    extras.extend(late)
                ups[part].append(lax.ppermute(go_up, "slab", up))
                downs[part].append(lax.ppermute(go_down, "slab", down))
        return ups, downs

    extras = []
    ups, downs = run_slots(0, STEADY, [[] for _ in range(CHUNKS)], [[] for _ in range(CHUNKS)])
    left, right, tables = lax.optimization_barrier(prepare(*extras))

    def finish(end):
        def branch(ups, downs):
            ups, downs = run_slots(STEADY, end, ups, downs)
            out = None
            for part in range(CHUNKS):
                packets = own[part] + ups[part] + downs[part]
                out = update(volume, left, right, edge, tables, packets, table, out, part, CHUNKS, False)
            return out

        return branch

    ends_at = [STEADY + 1, STEADY + 2, most]
    which = jnp.sum(jnp.array([slots > e for e in ends_at[:-1]]).astype(jnp.int32))
    return lax.switch(which, [finish(e) for e in ends_at], ups, downs)


def solution(mesh):
    placed = (P(("groups", "slab"), None, None), P(("groups", "slab"), None, None), P(), P(), P())
    return jax.shard_map(
        on_device,
        mesh=mesh,
        in_specs=placed,
        out_specs=P(("groups", "slab"), None, None),
        check_vma=False,
    )
```

```python
import functools

import jax
import jax.numpy as jnp
from jax import lax
from jax.experimental import pallas as pl
from jax.experimental.pallas import tpu as pltpu
from jax.sharding import PartitionSpec as P

RELAX = 1.0
BLOCK = 16
HALF = 8
LANES = 128
WIDE = 256
PIECES = 4
PARTS = 2
ROUTED_CLASSES = 4
LOAD = 2
STEADY = 2
CODE = 256
LINES = 5
VMEM_LIMIT = 56 * 2**20


def dot(a, b):
    return jnp.dot(a, b, preferred_element_type=jnp.float32)


def widen(coef):
    return jnp.concatenate([coef] * (WIDE // LANES), axis=1)


def spread_out(packets):
    return [r for p in packets for r in ([p] if p.ndim == 2 else [p.at[n] for n in range(LOAD)])]


def update_kernel(
    dense, part, table_ref, lower_ref, upper_ref, next_ref, left_ref, right_ref, edge_ref, coef_ref, edge_coef_ref,
    image_w_ref, weight_ref, spread_ref, carry_w_ref, *rest,
):
    out_ref, carry_ref, seen_ref, result_ref, sems, out_sems = rest[-6:]
    packets = rest[:-7]
    block = pl.program_id(0)
    blocks = pl.num_programs(0)
    depth, width = lower_ref.shape[1:]
    angles = weight_ref.shape[0]
    first = part * blocks * BLOCK

    def fetch(at_block, act):
        slot = at_block % 2
        rows = pl.ds(pl.multiple_of(at_block * BLOCK, BLOCK), BLOCK)
        if dense:
            act(pltpu.make_async_copy(packets[0].at[:, rows], seen_ref.at[slot], sems.at[slot, 0]))
            return
        views = spread_out(packets)
        arrived = (len(views) - ROUTED_CLASSES) // 2
        names = [(4, n) for n in range(ROUTED_CLASSES)] + [(way, n) for way in (2, 3) for n in range(arrived)]
        for n, (view, (line, spot)) in enumerate(zip(views, names)):
            name = table_ref[part * LINES + line, spot]

            @pl.when(name >= 0)
            def _():
                act(pltpu.make_async_copy(view.at[rows], seen_ref.at[slot, name], sems.at[slot, n]))

    def deliver(at_block, act):
        slot = at_block % 2
        size = BLOCK // PIECES
        for n in range(PIECES):
            source = result_ref.at[slot, pl.ds(n * size, size)]
            act(pltpu.make_async_copy(source, out_ref.at[pl.ds(first + at_block * BLOCK + n * size, size)], out_sems.at[slot, n]))

    @pl.when(block == 0)
    def _():
        seen_ref[...] = jnp.zeros_like(seen_ref)
        fetch(block, lambda copy: copy.start())

    @pl.when(block + 1 < blocks)
    def _():
        fetch(block + 1, lambda copy: copy.start())

    @pl.when(block == 0)
    def _():
        if part:
            carry_ref[...] = edge_ref[...]
            return
        for chunk in range(width // WIDE):
            at = pl.ds(chunk * WIDE, WIDE)
            mine = dot(weight_ref[...], lower_ref[0, :, at])
            before = dot(weight_ref[...], left_ref[0, :, at])
            carry_ref[:, at] = (
                edge_ref[:, at].astype(jnp.float32) * widen(edge_coef_ref[2])
                - mine * widen(edge_coef_ref[0])
                - before * widen(edge_coef_ref[1])
            ).astype(jnp.bfloat16)

    @pl.when(block >= 2)
    def _():
        deliver(block - 2, lambda copy: copy.wait())

    fetch(block, lambda copy: copy.wait())
    slot = block % 2
    final = (block == blocks - 1) & (part == PARTS - 1 or dense)

    def work(chunk):
        at = pl.ds(pl.multiple_of(chunk * WIDE, WIDE), WIDE)
        seen = seen_ref[slot, :, :, at].astype(jnp.float32)
        slabs = [lower_ref[:, :, at], upper_ref[:, :, at]]
        images = [dot(image_w_ref[...], slab.reshape(HALF * depth, WIDE)) for slab in slabs]
        after = dot(weight_ref[...], jnp.where(final, right_ref[0, :, at], next_ref[0, :, at]))
        ahead = [pltpu.roll(x.reshape(angles, HALF, WIDE), HALF - 1, 1) for x in images]
        ahead.append(jnp.broadcast_to(after.reshape(angles, 1, WIDE), (angles, HALF, WIDE)))
        tail = lax.broadcasted_iota(jnp.int32, (angles, HALF, WIDE), 1) == HALF - 1
        parts = []
        for half in range(2):
            now = jnp.where(tail, ahead[half + 1], ahead[half]).reshape(angles * HALF, WIDE)
            got = seen[:, half * HALF : (half + 1) * HALF].reshape(angles * HALF, WIDE)
            coef = [widen(coef_ref[0, half, n]) for n in range(3)]
            resid = got * coef[2] - now * coef[0] - images[half] * coef[1]
            parts.append(resid.reshape(angles, HALF, WIDE))
        resid = jnp.concatenate(parts, axis=1)
        spread = dot(spread_ref[0], resid.astype(jnp.bfloat16).reshape(angles * BLOCK, WIDE))
        extra = dot(carry_w_ref[0], carry_ref[:, at])
        carry_ref[:, at] = resid[:, BLOCK - 1].astype(jnp.bfloat16)
        spread = spread.reshape(BLOCK, depth, WIDE)
        for half in range(2):
            here = slice(half * HALF, (half + 1) * HALF)
            result_ref[slot, here, :, at] = slabs[half].astype(jnp.float32) + spread[here]
        result_ref[slot, 0, :, at] += extra

    if dense:
        pl.loop(0, width // WIDE)(work)
    else:
        for chunk in range(width // WIDE):
            work(chunk)
    deliver(block, lambda copy: copy.start())

    @pl.when(block == blocks - 1)
    def _():
        @pl.when(block >= 1)
        def _():
            deliver(block - 1, lambda copy: copy.wait())

        deliver(block, lambda copy: copy.wait())


def update(volume, left, right, edge, tables, packets, table, before, part, parts, dense):
    slices, depth, cols = volume.shape
    angles = edge.shape[0]
    blocks = slices // BLOCK // parts
    off = part * blocks
    by_block = lambda x: pl.BlockSpec((1,) + x.shape[1:], lambda b, i: (b + off,) + (0,) * (x.ndim - 1))
    whole = lambda x: pl.BlockSpec(x.shape, lambda b, i: (0,) * x.ndim)
    anywhere = pl.BlockSpec(memory_space=pl.ANY)
    coef, edge_coef, image_w, weights, spread_w, carry_w = tables
    aliases = {} if before is None else {13 + len(packets): 0}
    copies = 1 if dense else ROUTED_CLASSES + LOAD * (len(packets) - ROUTED_CLASSES)
    one = (1, depth, cols)
    return pl.pallas_call(
        functools.partial(update_kernel, dense, part),
        grid_spec=pltpu.PrefetchScalarGridSpec(
            num_scalar_prefetch=1,
            grid=(blocks,),
            in_specs=[
                pl.BlockSpec((HALF, depth, cols), lambda b, i: (2 * (b + off), 0, 0)),
                pl.BlockSpec((HALF, depth, cols), lambda b, i: (2 * (b + off) + 1, 0, 0)),
                pl.BlockSpec(one, lambda b, i: (jnp.minimum((b + off + 1) * BLOCK, slices - 1), 0, 0)),
                pl.BlockSpec(one, lambda b, i: (0, 0, 0)),
                pl.BlockSpec(one, lambda b, i: (0, 0, 0)),
                whole(edge), by_block(coef), whole(edge_coef), whole(image_w), whole(weights),
                by_block(spread_w), by_block(carry_w),
            ]
            + [anywhere] * (len(packets) + 1),
            out_specs=[anywhere, whole(edge)],
            scratch_shapes=[
                pltpu.VMEM((2, angles, BLOCK, cols), jnp.bfloat16),
                pltpu.VMEM((2, BLOCK, depth, cols), jnp.float32),
                pltpu.SemaphoreType.DMA((2, copies)),
                pltpu.SemaphoreType.DMA((2, PIECES)),
            ],
        ),
        out_shape=[jax.ShapeDtypeStruct(volume.shape, jnp.float32), jax.ShapeDtypeStruct(edge.shape, edge.dtype)],
        input_output_aliases=aliases,
        compiler_params=pltpu.CompilerParams(dimension_semantics=("arbitrary",), vmem_limit_bytes=VMEM_LIMIT),
        cost_estimate=pl.CostEstimate(
            flops=4 * slices * depth * cols * angles // parts, bytes_accessed=volume.size * 7 // parts, transcendentals=0
        ),
        name="slab_update",
    )(
        table, volume, volume, volume, left, right, edge, coef, edge_coef, image_w, weights, spread_w, carry_w,
        *packets, edge if before is None else before,
    )


def fill_weights(wide_w, turned_w, pick_next, pick_now, pick_carry, spread_ref, carry_w_ref):
    depth, columns = wide_w.shape
    place = lax.broadcasted_iota(jnp.int32, (depth, columns), 1) % BLOCK
    from_next = wide_w * pick_next
    from_now = wide_w * pick_now
    from_carry = turned_w * pick_carry
    for z in range(BLOCK):
        row = jnp.where(place == z, from_next, jnp.where(place == z - 1, from_now, 0.0))
        total = jnp.sum(row, axis=1, keepdims=True)
        if z == 0:
            total = total + jnp.sum(from_carry, axis=1, keepdims=True)
            carry_w_ref[0] = (from_carry * (RELAX / total)).astype(jnp.bfloat16)
        spread_ref[0, z * depth : (z + 1) * depth] = (row * (RELAX / total)).astype(jnp.bfloat16)


def weights_kernel(wide_w_ref, turned_w_ref, pick_ref, pick_carry_ref, spread_ref, carry_w_ref):
    picks = pick_ref[0, 0:1], pick_ref[0, 1:2], pick_carry_ref[0]
    fill_weights(wide_w_ref[...], turned_w_ref[...], *picks, spread_ref, carry_w_ref)


def make_weights(wide_w, turned_w, pick, pick_carry):
    blocks = pick.shape[0]
    depth, angles = turned_w.shape
    by_block = lambda shape: pl.BlockSpec((1,) + shape, lambda b: (b,) + (0,) * len(shape))
    whole = lambda x: pl.BlockSpec(x.shape, lambda b: (0,) * x.ndim)
    spread = (BLOCK * depth, angles * BLOCK)
    carry = (depth, angles)
    return pl.pallas_call(
        weights_kernel,
        grid=(blocks,),
        in_specs=[whole(wide_w), whole(turned_w), by_block(pick.shape[1:]), by_block(pick_carry.shape[1:])],
        out_specs=[by_block(spread), by_block(carry)],
        out_shape=[
            jax.ShapeDtypeStruct((blocks,) + spread, jnp.bfloat16),
            jax.ShapeDtypeStruct((blocks,) + carry, jnp.bfloat16),
        ],
        name="spread_weights",
    )(wide_w, turned_w, pick, pick_carry)


def make_tables(share, first, rows, path_weights, bases, slices):
    angles, depth = path_weights.shape
    blocks = slices // BLOCK
    weights = path_weights.astype(jnp.float32)
    ray_total = jnp.sum(weights, axis=1)[:, None]
    norm = 1.0 / (ray_total * ((1.0 - share[:, 1:]) + share[:, :-1]))
    coefs = jnp.stack([(1.0 - share[:, 1:]) * norm, share[:, :-1] * norm, norm])
    coef = coefs[:, :, 1:].reshape(3, angles, blocks, BLOCK // HALF, HALF).transpose(2, 3, 0, 1, 4)
    coef = coef.reshape(blocks, BLOCK // HALF, 3, angles * HALF, 1)
    coef = jnp.broadcast_to(coef, coef.shape[:4] + (LANES,))
    edge_coef = jnp.broadcast_to(coefs[:, :, :1], (3, angles, LANES))
    share_own = share[:, 1:-1]
    row_now = (first - bases)[:, None] + jnp.arange(slices, dtype=jnp.int32)[None, :]
    w_now = jnp.where((row_now >= 0) & (row_now < rows), 1.0 - share_own, 0.0)
    w_next = jnp.where((row_now + 1 >= 0) & (row_now + 1 < rows), share_own, 0.0)
    pick = jnp.stack([w_next, jnp.pad(w_now[:, 1:], ((0, 0), (0, 1)))]).reshape(2, angles, blocks, BLOCK)
    pick = pick.transpose(2, 0, 1, 3).reshape(blocks, 2, angles * BLOCK)
    pick_carry = w_now[:, ::BLOCK].T[:, None, :]
    eye = jnp.eye(HALF, dtype=jnp.float32)
    image_w = jnp.einsum("ad,yz->ayzd", weights, eye).reshape(angles * HALF, HALF * depth).astype(jnp.bfloat16)
    wide_w = jnp.repeat(weights.T, BLOCK, axis=1)
    return coef, edge_coef, image_w, path_weights, *make_weights(wide_w, weights.T, pick, pick_carry)


def column_of(line, tall):
    sub = lax.broadcasted_iota(jnp.int32, (tall, LANES), 0)
    lane = lax.broadcasted_iota(jnp.int32, (tall, LANES), 1)
    return jnp.max(jnp.where(sub == lane, line, -1), axis=1, keepdims=True)


def tables_kernel(
    rows, device_ref, bases_ref, before_ref, own_ref, after_ref, weight_ref,
    coef_ref, edge_coef_ref, image_w_ref, spread_ref, carry_w_ref,
):
    block = pl.program_id(0)
    angles, depth = weight_ref.shape
    first = device_ref[0] * LANES
    shape = (angles, LANES)
    lane = lax.broadcasted_iota(jnp.int32, shape, 1)
    sub = lax.broadcasted_iota(jnp.int32, shape, 0)
    weights = weight_ref[...].astype(jnp.float32)
    ray_total = jnp.sum(weights, axis=1, keepdims=True)
    own = own_ref[...]
    ahead = jnp.where(lane == LANES - 1, pltpu.roll(after_ref[...], LANES - 1, 1), pltpu.roll(own, LANES - 1, 1))
    norm = 1.0 / (ray_total * ((1.0 - ahead) + own))
    coefs = ((1.0 - ahead) * norm, own * norm, norm)
    spots = lax.broadcasted_iota(jnp.int32, (angles, HALF, LANES), 2) - lax.broadcasted_iota(jnp.int32, (angles, HALF, LANES), 1)
    for half in range(BLOCK // HALF):
        here = spots == block * BLOCK + half * HALF
        for n, coef in enumerate(coefs):
            tall = jnp.broadcast_to(coef.reshape(angles, 1, LANES), (angles, HALF, LANES))
            tall = jnp.sum(jnp.where(here, tall, 0.0), axis=2, keepdims=True)
            coef_ref[0, half, n] = jnp.broadcast_to(tall, (angles, HALF, LANES)).reshape(angles * HALF, LANES)

    @pl.when(block == 0)
    def _():
        edge_own = jnp.sum(jnp.where(lane == 0, own, 0.0), axis=1, keepdims=True)
        edge_before = jnp.sum(jnp.where(lane == LANES - 1, before_ref[...], 0.0), axis=1, keepdims=True)
        edge_norm = 1.0 / (ray_total * ((1.0 - edge_own) + edge_before))
        for n, coef in enumerate(((1.0 - edge_own) * edge_norm, edge_before * edge_norm, edge_norm)):
            edge_coef_ref[n] = jnp.broadcast_to(coef, shape)
        across = (HALF * depth)
        repeat = lax.broadcasted_iota(jnp.int32, (depth, across), 1) % depth
        repeat = jnp.where(repeat == lax.broadcasted_iota(jnp.int32, (depth, across), 0), 1.0, 0.0)
        wide = dot(weight_ref[...], repeat.astype(jnp.bfloat16)).astype(jnp.bfloat16)
        down = angles * HALF
        expand = lax.broadcasted_iota(jnp.int32, (down, angles), 0) // HALF
        expand = jnp.where(expand == lax.broadcasted_iota(jnp.int32, (down, angles), 1), 1.0, 0.0)
        wide = dot(expand.astype(jnp.bfloat16), wide)
        at = lax.broadcasted_iota(jnp.int32, (down, across), 0) % HALF
        same = lax.broadcasted_iota(jnp.int32, (down, across), 1) // depth == at
        image_w_ref[...] = jnp.where(same, wide, 0.0).astype(jnp.bfloat16)

    row_now = first + lane - column_of(bases_ref[...], angles)
    w_now = jnp.where((row_now >= 0) & (row_now < rows), 1.0 - own, 0.0)
    w_next = jnp.where((row_now + 1 >= 0) & (row_now + 1 < rows), own, 0.0)
    columns = angles * BLOCK
    place = lax.broadcasted_iota(jnp.int32, (LANES, columns), 1) % BLOCK
    z = lax.broadcasted_iota(jnp.int32, (LANES, columns), 0) - block * BLOCK
    mine = lax.broadcasted_iota(jnp.int32, (angles, columns), 1) // BLOCK
    mine = mine == lax.broadcasted_iota(jnp.int32, (angles, columns), 0)

    def gather(values, wanted):
        picked = jnp.dot(
            values, jnp.where(wanted, 1.0, 0.0), precision=lax.Precision.HIGHEST, preferred_element_type=jnp.float32
        )
        return jnp.sum(jnp.where(mine, picked, 0.0), axis=0, keepdims=True)

    pick_next = gather(w_next, z == place)
    pick_now = gather(w_now, (z == place + 1) & (place < BLOCK - 1))
    carry = jnp.sum(jnp.where(lane == block * BLOCK, w_now, 0.0), axis=1, keepdims=True)
    square = lax.broadcasted_iota(jnp.int32, (angles, angles), 0) == lax.broadcasted_iota(jnp.int32, (angles, angles), 1)
    pick_carry = jnp.sum(jnp.where(square, carry, 0.0), axis=0, keepdims=True)
    turn = lambda other: lax.dot_general(
        weights, other, (((0,), (0,)), ((), ())), precision=lax.Precision.HIGHEST, preferred_element_type=jnp.float32
    )
    wide_w = turn(jnp.where(mine, 1.0, 0.0))
    turned_w = turn(jnp.where(square, 1.0, 0.0))
    fill_weights(wide_w, turned_w, pick_next, pick_now, pick_carry, spread_ref, carry_w_ref)


def device_tables(device, row_of_bases, fractions, path_weights, rows):
    angles, depth = path_weights.shape
    blocks = LANES // BLOCK
    last = fractions.shape[1] // LANES - 1
    column = lambda by: pl.BlockSpec((angles, LANES), lambda b, d: (0, jnp.clip(d[0] + by, 0, last)))
    whole = lambda shape: pl.BlockSpec(shape, lambda b, d: (0,) * len(shape))
    by_block = lambda shape: pl.BlockSpec((1,) + shape, lambda b, d: (b,) + (0,) * len(shape))
    coef = (BLOCK // HALF, 3, angles * HALF, LANES)
    edge_coef = (3, angles, LANES)
    image_w = (angles * HALF, HALF * depth)
    spread = (BLOCK * depth, angles * BLOCK)
    carry = (depth, angles)
    made = pl.pallas_call(
        functools.partial(tables_kernel, rows),
        grid_spec=pltpu.PrefetchScalarGridSpec(
            num_scalar_prefetch=1,
            grid=(blocks,),
            in_specs=[whole((1, LANES)), column(-1), column(0), column(1), whole(path_weights.shape)],
            out_specs=[by_block(coef), whole(edge_coef), whole(image_w), by_block(spread), by_block(carry)],
        ),
        out_shape=[
            jax.ShapeDtypeStruct((blocks,) + coef, jnp.float32),
            jax.ShapeDtypeStruct(edge_coef, jnp.float32),
            jax.ShapeDtypeStruct(image_w, jnp.bfloat16),
            jax.ShapeDtypeStruct((blocks,) + spread, jnp.bfloat16),
            jax.ShapeDtypeStruct((blocks,) + carry, jnp.bfloat16),
        ],
        name="make_tables",
    )(device, row_of_bases, fractions, fractions, fractions, path_weights)
    return made[0], made[1], made[2], path_weights, made[3], made[4]


def turn_kernel(classes, count, device_ref, bases_ref, seen_ref, *refs):
    outs, ends_ref, twice_ref, sems = refs[:-3], refs[-3], refs[-2], refs[-1]
    rows, cols = seen_ref.shape
    more = twice_ref.shape[0] - rows
    copies = [
        pltpu.make_async_copy(seen_ref, twice_ref.at[pl.ds(0, rows)], sems.at[0]),
        pltpu.make_async_copy(seen_ref.at[pl.ds(0, more)], twice_ref.at[pl.ds(rows, more)], sems.at[1]),
    ]
    for copy in copies:
        copy.start()
    for copy in copies:
        copy.wait()
    device = device_ref[0]
    base = bases_ref[device]
    my_class = device & (classes - 1)
    slices = count * PARTS

    def window(place, size, at):
        start = (place - base + 1 + rows) & (rows - 1)
        begin = pl.multiple_of(start & ~(BLOCK - 1), BLOCK)
        tall = size + BLOCK
        wide = twice_ref[pl.ds(begin, tall), at].astype(jnp.float32)
        return pltpu.roll(wide, (tall - (start - begin)) % tall, 0)

    for d in range(classes):
        for part in range(PARTS):
            out = outs[d * PARTS + part]
            place = (my_class ^ d) * slices + part * count

            @pl.loop(0, cols // WIDE)
            def _(chunk):
                at = pl.ds(pl.multiple_of(chunk * WIDE, WIDE), WIDE)
                out[:, at] = window(place, count, at)[:count].astype(jnp.bfloat16)

    @pl.loop(0, cols // WIDE)
    def _(chunk):
        at = pl.ds(pl.multiple_of(chunk * WIDE, WIDE), WIDE)
        for c in range(classes):
            ends_ref[c : c + 1, at] = window(c * slices - 1, BLOCK, at)[:1]


def turn(device, bases, seen, classes):
    rows, cols = seen.shape
    count = rows // classes // PARTS
    runs = classes * PARTS
    return pl.pallas_call(
        functools.partial(turn_kernel, classes, count),
        in_specs=[
            pl.BlockSpec(memory_space=pltpu.SMEM),
            pl.BlockSpec(memory_space=pltpu.SMEM),
            pl.BlockSpec(memory_space=pl.ANY),
        ],
        out_specs=[pl.BlockSpec(memory_space=pltpu.VMEM)] * (runs + 1),
        out_shape=[jax.ShapeDtypeStruct((count, cols), seen.dtype)] * runs + [jax.ShapeDtypeStruct((classes, cols), jnp.float32)],
        scratch_shapes=[pltpu.VMEM((rows + count + BLOCK, cols), seen.dtype), pltpu.SemaphoreType.DMA((2,))],
        compiler_params=pltpu.CompilerParams(vmem_limit_bytes=32 * 2**20),
        name="turn_rows",
    )(device, bases, seen)


def plan_kernel(slots, planes, classes, angles, count, rows, device_ref, bases_ref, table_ref):
    shape = (2 * PARTS * classes, LANES)
    lane = lax.broadcasted_iota(jnp.int32, shape, 1)
    row = lax.broadcasted_iota(jnp.int32, shape, 0)
    class_shift = classes.bit_length() - 1
    base = jnp.broadcast_to(bases_ref[...], shape) - 1
    low_plane = base >> (rows.bit_length() - 1)
    turned = base & (rows - 1)

    def reach(which):
        lowest = low_plane + jnp.where(which * count + count - 1 < turned, 1, 0)
        highest = low_plane + jnp.where(which * count < turned, 1, 0)
        return lowest, highest

    lowest, highest = reach(row >> 1)
    upward = (row & 1) == 0
    source = lane >> class_shift
    at = jnp.where(upward, source, planes - 1 - source)
    to = jnp.where(lane < angles, jnp.where(upward, highest, planes - 1 - lowest), -1)
    key = to * CODE + (CODE - 1 - lane)
    sent = [jnp.full(shape, -1, jnp.int32) for _ in range(planes - 1)]
    for slot in range(slots):
        begin = at
        for link in range(planes - 1):
            ready = (begin == link) & (to > link)
            for n in range(LOAD):
                best = jnp.max(jnp.where(ready, key, -1), axis=1, keepdims=True)
                taken = ready & (key == best)
                at = jnp.where(taken, link + 1, at)
                ready = ready & (key != best)
                which = jnp.where(best >= 0, CODE - 1 - (best & (CODE - 1)), -1)
                sent[link] = jnp.where(lane == slot * LOAD + n, which, sent[link])

    me = device_ref[0]
    my_class = me & (classes - 1)
    plane = me >> class_shift
    none = jnp.full(shape, -1, jnp.int32)
    used = none
    for link in range(planes - 1):
        used = jnp.maximum(used, sent[link])
    used = jnp.max(used, axis=0, keepdims=True)
    head = lane[:1]
    total = jnp.sum(jnp.where((used >= 0) & (head % LOAD == 0), 1, 0), axis=1, keepdims=True)

    tall = -(-max(slots * LOAD, angles) // 8) * 8
    sub = lax.broadcasted_iota(jnp.int32, (tall, LANES), 0)
    held = jnp.where(head < classes, plane * classes + (head ^ my_class), -1)
    for part in range(PARTS):
        low_here, high_here = reach(my_class * PARTS + part)
        wanted = (plane >= low_here) & (plane <= high_here) & (lane < angles)
        wanted = column_of(jnp.where(wanted, 1, 0)[:1], tall) > 0
        keep = lambda ids: jnp.max(jnp.where((sub == ids) & wanted, ids, -1), axis=0, keepdims=True)
        for way, spot in ((0, plane), (1, planes - 1 - plane)):
            sends, gets = none, none
            for link in range(planes - 1):
                sends = jnp.where(spot == link, sent[link], sends)
                gets = jnp.where(spot == link + 1, sent[link], gets)
            mine = row == 2 * (my_class * PARTS + part) + way
            sends = jnp.max(jnp.where(mine, sends, -1), axis=0, keepdims=True)
            gets = jnp.max(jnp.where(mine, gets, -1), axis=0, keepdims=True)
            arrived = jnp.max(jnp.where((column_of(gets, tall) == sends) & (sends >= 0), sub, 0), axis=0, keepdims=True)
            own = (sends >> class_shift) == plane
            index = jnp.where(own, (sends & (classes - 1)) ^ my_class, classes + arrived)
            line = part * LINES + way
            table_ref[line : line + 1] = jnp.where(sends >= 0, index, 0)
            table_ref[line + 2 : line + 3] = keep(gets)
        line = part * LINES + 4
        table_ref[line : line + 1] = keep(held)
    table_ref[PARTS * LINES : PARTS * LINES + 1] = jnp.broadcast_to(total, head.shape)


def choose_kernel(slot, part, ups, downs, table_ref, *refs):
    sources = refs[:ups], refs[ups : ups + downs]
    outs = refs[ups + downs : ups + downs + 2]
    held, sems = refs[ups + downs + 2 :]
    views = [spread_out(side) for side in sources]
    for way in range(2):
        for n in range(LOAD):
            for m, view in enumerate(views[way]):

                @pl.when(table_ref[part * LINES + way, slot * LOAD + n] == m)
                def _():
                    pltpu.make_async_copy(view, held.at[way, n], sems.at[0, way, n]).start()

    for way in range(2):
        for n in range(LOAD):
            pltpu.make_async_copy(views[way][0], held.at[way, n], sems.at[0, way, n]).wait()
            pltpu.make_async_copy(held.at[way, n], outs[way].at[n], sems.at[1, way, n]).start()
    for way in range(2):
        for n in range(LOAD):
            pltpu.make_async_copy(held.at[way, n], outs[way].at[n], sems.at[1, way, n]).wait()


def choose(slot, part, table, own, ups, downs):
    up_from, down_from = own + ups, own + downs
    anywhere = pl.BlockSpec(memory_space=pl.ANY)
    shape = jax.ShapeDtypeStruct((LOAD,) + own[0].shape, own[0].dtype)
    return pl.pallas_call(
        functools.partial(choose_kernel, slot, part, len(up_from), len(down_from)),
        in_specs=[pl.BlockSpec(memory_space=pltpu.SMEM)] + [anywhere] * (len(up_from) + len(down_from)),
        out_specs=[anywhere, anywhere],
        out_shape=[shape, shape],
        scratch_shapes=[
            pltpu.VMEM((2, LOAD) + own[0].shape, own[0].dtype),
            pltpu.SemaphoreType.DMA((2, 2, LOAD)),
        ],
        cost_estimate=pl.CostEstimate(flops=0, bytes_accessed=4 * LOAD * own[0].size * 2, transcendentals=0),
        name="choose_packet",
    )(table, *up_from, *down_from)


def on_device(volume, measured, path_weights, fractions, bases):
    slices, depth, cols = volume.shape
    local, rows = measured.shape[:2]
    nslab = lax.axis_size("slab")
    device = lax.axis_index("slab")
    angles = local * nslab
    first = device * slices
    classes = rows // slices
    planes = nslab // classes
    ups_of = lambda step: [(i, i + step) for i in range(nslab - step)]
    downs_of = lambda step: [(i + step, i) for i in range(nslab - step)]

    routed = local == 1 and classes == ROUTED_CLASSES and slices == LANES and rows & (rows - 1) == 0 and angles <= LANES
    if not routed:
        left = lax.ppermute(volume[slices - 1 :], "slab", ups_of(1))
        right = lax.ppermute(volume[:1], "slab", downs_of(1))
        share = lax.dynamic_slice_in_dim(jnp.pad(fractions, ((0, 0), (1, 1))), first, slices + 2, 1)
        tables = make_tables(share, first, rows, path_weights, bases, slices)
        my_bases = lax.dynamic_slice_in_dim(bases, device * local, local, 0)
        turned = jax.vmap(lambda m, b: jnp.roll(m, b - 1, axis=0))(measured, my_bases)
        by_class = turned.reshape(local, classes, slices, cols).transpose(1, 0, 2, 3)
        outgoing = jnp.tile(by_class, (planes, 1, 1, 1)).reshape(angles, slices, cols)
        seen = lax.all_to_all(outgoing, "slab", split_axis=0, concat_axis=0, tiled=True)
        ends = jnp.roll(by_class[:, :, slices - 1], 1, axis=0)
        ends = jnp.tile(ends, (planes, 1, 1)).reshape(angles, cols // LANES, LANES)
        edge = lax.all_to_all(ends, "slab", split_axis=0, concat_axis=0, tiled=True).reshape(angles, cols)
        return update(volume, left, right, edge, tables, [seen], jnp.zeros((8, LANES), jnp.int32), None, 0, 1, True)[0]

    number = device.astype(jnp.int32)[None]
    *runs, ends = turn(number, bases, measured[0], classes)
    row_of_bases = jnp.pad(bases, (0, LANES - angles), constant_values=1)[None]
    runs, row_of_bases = lax.optimization_barrier((runs, row_of_bases))
    own = []
    for part in range(PARTS):
        mine = [runs[d * PARTS + part] for d in range(classes)]
        if part:
            mine, own[-1] = lax.optimization_barrier((mine, own[-1]))
        own.append(
            mine[:1] + [lax.ppermute(mine[d], "slab", [(i, i ^ d) for i in range(nslab)]) for d in range(1, classes)]
        )

    most = -(-classes * (planes - 1) // LOAD) + planes - 2
    table = pl.pallas_call(
        functools.partial(plan_kernel, most, planes, classes, angles, slices // PARTS, rows),
        in_specs=[pl.BlockSpec(memory_space=pltpu.SMEM), pl.BlockSpec(memory_space=pltpu.VMEM)],
        out_shape=jax.ShapeDtypeStruct((16, LANES), jnp.int32),
        name="plan_slots",
    )(number, row_of_bases)
    slots = table[PARTS * LINES, 0]
    late = (ends, fractions, volume[slices - 1 :], volume[:1])

    def run_slots(begin, end, ups, downs):
        nonlocal late
        ups, downs = [list(u) for u in ups], [list(d) for d in downs]
        for slot in range(begin, end):
            for part in range(PARTS):
                go_up, go_down = choose(slot, part, table, own[part], ups[part], downs[part])
                if slot == 0 and part == PARTS - 1:
                    go_up, *late = lax.optimization_barrier((go_up, *late))
                ups[part].append(lax.ppermute(go_up, "slab", ups_of(classes)))
                downs[part].append(lax.ppermute(go_down, "slab", downs_of(classes)))
        return ups, downs

    ups, downs = run_slots(0, STEADY, [[] for _ in range(PARTS)], [[] for _ in range(PARTS)])
    ends, late_fractions, low, high = late
    tables = device_tables(number, row_of_bases, late_fractions, path_weights, rows)
    left = lax.ppermute(low, "slab", ups_of(1))
    right = lax.ppermute(high, "slab", downs_of(1))
    ends = jnp.tile(ends.astype(jnp.bfloat16)[None], (planes, 1, 1)).reshape(angles, cols // LANES, LANES)
    edge = lax.all_to_all(ends, "slab", split_axis=0, concat_axis=0, tiled=True).reshape(angles, cols)
    left, right, edge, tables = lax.optimization_barrier((left, right, edge, tables))

    def finish(end):
        def branch(ups, downs):
            ups, downs = run_slots(STEADY, end, ups, downs)
            out, carry = None, edge
            for part in range(PARTS):
                packets = own[part] + ups[part] + downs[part]
                out, carry = update(volume, left, right, carry, tables, packets, table, out, part, PARTS, False)
            return out

        return branch

    ends_at = [STEADY + 1, STEADY + 2, most]
    which = jnp.sum(jnp.array([slots > e for e in ends_at[:-1]]).astype(jnp.int32))
    return lax.switch(which, [finish(e) for e in ends_at], ups, downs)


def solution(mesh):
    placed = (P(("groups", "slab"), None, None), P(("groups", "slab"), None, None), P(), P(), P())
    return jax.shard_map(
        on_device,
        mesh=mesh,
        in_specs=placed,
        out_specs=P(("groups", "slab"), None, None),
        check_vma=False,
    )
```

```python
import functools

import jax
import jax.numpy as jnp
from jax import lax
from jax.experimental import pallas as pl
from jax.experimental.pallas import tpu as pltpu
from jax.sharding import PartitionSpec as P

RELAX = 1.0
BLOCK = 16
HALF = 8
LANES = 128
WIDE = 256
PIECES = 4
PARTS = 2
ROUTED_CLASSES = 4
LOAD = 2
STEADY = 2
CODE = 256
LINES = 5
VMEM_LIMIT = 56 * 2**20


def dot(a, b):
    return jnp.dot(a, b, preferred_element_type=jnp.float32)


def widen(coef):
    return jnp.concatenate([coef] * (WIDE // LANES), axis=1)


def spread_out(packets):
    return [r for p in packets for r in ([p] if p.ndim == 2 else [p.at[n] for n in range(LOAD)])]


def update_kernel(
    dense, part, table_ref, lower_ref, upper_ref, next_ref, left_ref, right_ref, edge_ref, coef_ref, edge_coef_ref,
    image_w_ref, weight_ref, spread_ref, carry_w_ref, *rest,
):
    out_ref, carry_ref, seen_ref, result_ref, sems, out_sems = rest[-6:]
    packets = rest[:-7]
    block = pl.program_id(0)
    blocks = pl.num_programs(0)
    depth, width = lower_ref.shape[1:]
    angles = weight_ref.shape[0]
    first = part * blocks * BLOCK

    def fetch(at_block, act):
        slot = at_block % 2
        rows = pl.ds(pl.multiple_of(at_block * BLOCK, BLOCK), BLOCK)
        if dense:
            act(pltpu.make_async_copy(packets[0].at[:, rows], seen_ref.at[slot], sems.at[slot, 0]))
            return
        views = spread_out(packets)
        arrived = (len(views) - ROUTED_CLASSES) // 2
        names = [(4, n) for n in range(ROUTED_CLASSES)] + [(way, n) for way in (2, 3) for n in range(arrived)]
        for n, (view, (line, spot)) in enumerate(zip(views, names)):
            name = table_ref[part * LINES + line, spot]

            @pl.when(name >= 0)
            def _():
                act(pltpu.make_async_copy(view.at[rows], seen_ref.at[slot, name], sems.at[slot, n]))

    def deliver(at_block, act):
        slot = at_block % 2
        size = BLOCK // PIECES
        for n in range(PIECES):
            source = result_ref.at[slot, pl.ds(n * size, size)]
            act(pltpu.make_async_copy(source, out_ref.at[pl.ds(first + at_block * BLOCK + n * size, size)], out_sems.at[slot, n]))

    @pl.when(block == 0)
    def _():
        seen_ref[...] = jnp.zeros_like(seen_ref)
        fetch(block, lambda copy: copy.start())

    @pl.when(block + 1 < blocks)
    def _():
        fetch(block + 1, lambda copy: copy.start())

    @pl.when(block == 0)
    def _():
        if part:
            carry_ref[...] = edge_ref[...]
            return
        for chunk in range(width // WIDE):
            at = pl.ds(chunk * WIDE, WIDE)
            mine = dot(weight_ref[...], lower_ref[0, :, at])
            before = dot(weight_ref[...], left_ref[0, :, at])
            carry_ref[:, at] = (
                edge_ref[:, at].astype(jnp.float32) * widen(edge_coef_ref[2])
                - mine * widen(edge_coef_ref[0])
                - before * widen(edge_coef_ref[1])
            ).astype(jnp.bfloat16)

    @pl.when(block >= 2)
    def _():
        deliver(block - 2, lambda copy: copy.wait())

    fetch(block, lambda copy: copy.wait())
    slot = block % 2
    final = (block == blocks - 1) & (part == PARTS - 1 or dense)

    def work(chunk):
        at = pl.ds(pl.multiple_of(chunk * WIDE, WIDE), WIDE)
        seen = seen_ref[slot, :, :, at].astype(jnp.float32)
        slabs = [lower_ref[:, :, at], upper_ref[:, :, at]]
        images = [dot(image_w_ref[...], slab.reshape(HALF * depth, WIDE)) for slab in slabs]
        after = dot(weight_ref[...], jnp.where(final, right_ref[0, :, at], next_ref[0, :, at]))
        ahead = [pltpu.roll(x.reshape(angles, HALF, WIDE), HALF - 1, 1) for x in images]
        ahead.append(jnp.broadcast_to(after.reshape(angles, 1, WIDE), (angles, HALF, WIDE)))
        tail = lax.broadcasted_iota(jnp.int32, (angles, HALF, WIDE), 1) == HALF - 1
        parts = []
        for half in range(2):
            now = jnp.where(tail, ahead[half + 1], ahead[half]).reshape(angles * HALF, WIDE)
            got = seen[:, half * HALF : (half + 1) * HALF].reshape(angles * HALF, WIDE)
            coef = [widen(coef_ref[0, half, n]) for n in range(3)]
            resid = got * coef[2] - now * coef[0] - images[half] * coef[1]
            parts.append(resid.reshape(angles, HALF, WIDE))
        resid = jnp.concatenate(parts, axis=1)
        spread = dot(spread_ref[0], resid.astype(jnp.bfloat16).reshape(angles * BLOCK, WIDE))
        extra = dot(carry_w_ref[0], carry_ref[:, at])
        carry_ref[:, at] = resid[:, BLOCK - 1].astype(jnp.bfloat16)
        spread = spread.reshape(BLOCK, depth, WIDE)
        for half in range(2):
            here = slice(half * HALF, (half + 1) * HALF)
            result_ref[slot, here, :, at] = slabs[half].astype(jnp.float32) + spread[here]
        result_ref[slot, 0, :, at] += extra

    if dense:
        pl.loop(0, width // WIDE)(work)
    else:
        for chunk in range(width // WIDE):
            work(chunk)
    deliver(block, lambda copy: copy.start())

    @pl.when(block == blocks - 1)
    def _():
        @pl.when(block >= 1)
        def _():
            deliver(block - 1, lambda copy: copy.wait())

        deliver(block, lambda copy: copy.wait())


def update(volume, left, right, edge, tables, packets, table, before, part, parts, dense):
    slices, depth, cols = volume.shape
    angles = edge.shape[0]
    blocks = slices // BLOCK // parts
    off = part * blocks
    by_block = lambda x: pl.BlockSpec((1,) + x.shape[1:], lambda b, i: (b + off,) + (0,) * (x.ndim - 1))
    whole = lambda x: pl.BlockSpec(x.shape, lambda b, i: (0,) * x.ndim)
    anywhere = pl.BlockSpec(memory_space=pl.ANY)
    coef, edge_coef, image_w, weights, spread_w, carry_w = tables
    aliases = {} if before is None else {13 + len(packets): 0}
    copies = 1 if dense else ROUTED_CLASSES + LOAD * (len(packets) - ROUTED_CLASSES)
    one = (1, depth, cols)
    return pl.pallas_call(
        functools.partial(update_kernel, dense, part),
        grid_spec=pltpu.PrefetchScalarGridSpec(
            num_scalar_prefetch=1,
            grid=(blocks,),
            in_specs=[
                pl.BlockSpec((HALF, depth, cols), lambda b, i: (2 * (b + off), 0, 0)),
                pl.BlockSpec((HALF, depth, cols), lambda b, i: (2 * (b + off) + 1, 0, 0)),
                pl.BlockSpec(one, lambda b, i: (jnp.minimum((b + off + 1) * BLOCK, slices - 1), 0, 0)),
                pl.BlockSpec(one, lambda b, i: (0, 0, 0)),
                pl.BlockSpec(one, lambda b, i: (0, 0, 0)),
                whole(edge), by_block(coef), whole(edge_coef), whole(image_w), whole(weights),
                by_block(spread_w), by_block(carry_w),
            ]
            + [anywhere] * (len(packets) + 1),
            out_specs=[anywhere, whole(edge)],
            scratch_shapes=[
                pltpu.VMEM((2, angles, BLOCK, cols), jnp.bfloat16),
                pltpu.VMEM((2, BLOCK, depth, cols), jnp.float32),
                pltpu.SemaphoreType.DMA((2, copies)),
                pltpu.SemaphoreType.DMA((2, PIECES)),
            ],
        ),
        out_shape=[jax.ShapeDtypeStruct(volume.shape, jnp.float32), jax.ShapeDtypeStruct(edge.shape, edge.dtype)],
        input_output_aliases=aliases,
        compiler_params=pltpu.CompilerParams(dimension_semantics=("arbitrary",), vmem_limit_bytes=VMEM_LIMIT),
        cost_estimate=pl.CostEstimate(
            flops=4 * slices * depth * cols * angles // parts, bytes_accessed=volume.size * 7 // parts, transcendentals=0
        ),
        name="slab_update",
    )(
        table, volume, volume, volume, left, right, edge, coef, edge_coef, image_w, weights, spread_w, carry_w,
        *packets, edge if before is None else before,
    )


def fill_weights(wide_w, turned_w, pick_next, pick_now, pick_carry, spread_ref, carry_w_ref):
    depth, columns = wide_w.shape
    place = lax.broadcasted_iota(jnp.int32, (depth, columns), 1) % BLOCK
    from_next = wide_w * pick_next
    from_now = wide_w * pick_now
    from_carry = turned_w * pick_carry
    for z in range(BLOCK):
        row = jnp.where(place == z, from_next, jnp.where(place == z - 1, from_now, 0.0))
        total = jnp.sum(row, axis=1, keepdims=True)
        if z == 0:
            total = total + jnp.sum(from_carry, axis=1, keepdims=True)
            carry_w_ref[0] = (from_carry * (RELAX / total)).astype(jnp.bfloat16)
        spread_ref[0, z * depth : (z + 1) * depth] = (row * (RELAX / total)).astype(jnp.bfloat16)


def weights_kernel(wide_w_ref, turned_w_ref, pick_ref, pick_carry_ref, spread_ref, carry_w_ref):
    picks = pick_ref[0, 0:1], pick_ref[0, 1:2], pick_carry_ref[0]
    fill_weights(wide_w_ref[...], turned_w_ref[...], *picks, spread_ref, carry_w_ref)


def make_weights(wide_w, turned_w, pick, pick_carry):
    blocks = pick.shape[0]
    depth, angles = turned_w.shape
    by_block = lambda shape: pl.BlockSpec((1,) + shape, lambda b: (b,) + (0,) * len(shape))
    whole = lambda x: pl.BlockSpec(x.shape, lambda b: (0,) * x.ndim)
    spread = (BLOCK * depth, angles * BLOCK)
    carry = (depth, angles)
    return pl.pallas_call(
        weights_kernel,
        grid=(blocks,),
        in_specs=[whole(wide_w), whole(turned_w), by_block(pick.shape[1:]), by_block(pick_carry.shape[1:])],
        out_specs=[by_block(spread), by_block(carry)],
        out_shape=[
            jax.ShapeDtypeStruct((blocks,) + spread, jnp.bfloat16),
            jax.ShapeDtypeStruct((blocks,) + carry, jnp.bfloat16),
        ],
        name="spread_weights",
    )(wide_w, turned_w, pick, pick_carry)


def make_tables(share, first, rows, path_weights, bases, slices):
    angles, depth = path_weights.shape
    blocks = slices // BLOCK
    weights = path_weights.astype(jnp.float32)
    ray_total = jnp.sum(weights, axis=1)[:, None]
    norm = 1.0 / (ray_total * ((1.0 - share[:, 1:]) + share[:, :-1]))
    coefs = jnp.stack([(1.0 - share[:, 1:]) * norm, share[:, :-1] * norm, norm])
    coef = coefs[:, :, 1:].reshape(3, angles, blocks, BLOCK // HALF, HALF).transpose(2, 3, 0, 1, 4)
    coef = coef.reshape(blocks, BLOCK // HALF, 3, angles * HALF, 1)
    coef = jnp.broadcast_to(coef, coef.shape[:4] + (LANES,))
    edge_coef = jnp.broadcast_to(coefs[:, :, :1], (3, angles, LANES))
    share_own = share[:, 1:-1]
    row_now = (first - bases)[:, None] + jnp.arange(slices, dtype=jnp.int32)[None, :]
    w_now = jnp.where((row_now >= 0) & (row_now < rows), 1.0 - share_own, 0.0)
    w_next = jnp.where((row_now + 1 >= 0) & (row_now + 1 < rows), share_own, 0.0)
    pick = jnp.stack([w_next, jnp.pad(w_now[:, 1:], ((0, 0), (0, 1)))]).reshape(2, angles, blocks, BLOCK)
    pick = pick.transpose(2, 0, 1, 3).reshape(blocks, 2, angles * BLOCK)
    pick_carry = w_now[:, ::BLOCK].T[:, None, :]
    eye = jnp.eye(HALF, dtype=jnp.float32)
    image_w = jnp.einsum("ad,yz->ayzd", weights, eye).reshape(angles * HALF, HALF * depth).astype(jnp.bfloat16)
    wide_w = jnp.repeat(weights.T, BLOCK, axis=1)
    return coef, edge_coef, image_w, path_weights, *make_weights(wide_w, weights.T, pick, pick_carry)


def column_of(line, tall):
    sub = lax.broadcasted_iota(jnp.int32, (tall, LANES), 0)
    lane = lax.broadcasted_iota(jnp.int32, (tall, LANES), 1)
    return jnp.max(jnp.where(sub == lane, line, -1), axis=1, keepdims=True)


def tables_kernel(
    rows, device_ref, bases_ref, before_ref, own_ref, after_ref, weight_ref,
    coef_ref, edge_coef_ref, image_w_ref, spread_ref, carry_w_ref,
):
    block = pl.program_id(0)
    angles, depth = weight_ref.shape
    first = device_ref[0] * LANES
    shape = (angles, LANES)
    lane = lax.broadcasted_iota(jnp.int32, shape, 1)
    sub = lax.broadcasted_iota(jnp.int32, shape, 0)
    weights = weight_ref[...].astype(jnp.float32)
    ray_total = jnp.sum(weights, axis=1, keepdims=True)
    own = own_ref[...]
    ahead = jnp.where(lane == LANES - 1, pltpu.roll(after_ref[...], LANES - 1, 1), pltpu.roll(own, LANES - 1, 1))
    norm = 1.0 / (ray_total * ((1.0 - ahead) + own))
    coefs = ((1.0 - ahead) * norm, own * norm, norm)
    spots = lax.broadcasted_iota(jnp.int32, (angles, HALF, LANES), 2) - lax.broadcasted_iota(jnp.int32, (angles, HALF, LANES), 1)
    for half in range(BLOCK // HALF):
        here = spots == block * BLOCK + half * HALF
        for n, coef in enumerate(coefs):
            tall = jnp.broadcast_to(coef.reshape(angles, 1, LANES), (angles, HALF, LANES))
            tall = jnp.sum(jnp.where(here, tall, 0.0), axis=2, keepdims=True)
            coef_ref[0, half, n] = jnp.broadcast_to(tall, (angles, HALF, LANES)).reshape(angles * HALF, LANES)

    @pl.when(block == 0)
    def _():
        edge_own = jnp.sum(jnp.where(lane == 0, own, 0.0), axis=1, keepdims=True)
        edge_before = jnp.sum(jnp.where(lane == LANES - 1, before_ref[...], 0.0), axis=1, keepdims=True)
        edge_norm = 1.0 / (ray_total * ((1.0 - edge_own) + edge_before))
        for n, coef in enumerate(((1.0 - edge_own) * edge_norm, edge_before * edge_norm, edge_norm)):
            edge_coef_ref[n] = jnp.broadcast_to(coef, shape)
        across = (HALF * depth)
        repeat = lax.broadcasted_iota(jnp.int32, (depth, across), 1) % depth
        repeat = jnp.where(repeat == lax.broadcasted_iota(jnp.int32, (depth, across), 0), 1.0, 0.0)
        wide = dot(weight_ref[...], repeat.astype(jnp.bfloat16)).astype(jnp.bfloat16)
        down = angles * HALF
        expand = lax.broadcasted_iota(jnp.int32, (down, angles), 0) // HALF
        expand = jnp.where(expand == lax.broadcasted_iota(jnp.int32, (down, angles), 1), 1.0, 0.0)
        wide = dot(expand.astype(jnp.bfloat16), wide)
        at = lax.broadcasted_iota(jnp.int32, (down, across), 0) % HALF
        same = lax.broadcasted_iota(jnp.int32, (down, across), 1) // depth == at
        image_w_ref[...] = jnp.where(same, wide, 0.0).astype(jnp.bfloat16)

    row_now = first + lane - column_of(bases_ref[...], angles)
    w_now = jnp.where((row_now >= 0) & (row_now < rows), 1.0 - own, 0.0)
    w_next = jnp.where((row_now + 1 >= 0) & (row_now + 1 < rows), own, 0.0)
    columns = angles * BLOCK
    place = lax.broadcasted_iota(jnp.int32, (LANES, columns), 1) % BLOCK
    z = lax.broadcasted_iota(jnp.int32, (LANES, columns), 0) - block * BLOCK
    mine = lax.broadcasted_iota(jnp.int32, (angles, columns), 1) // BLOCK
    mine = mine == lax.broadcasted_iota(jnp.int32, (angles, columns), 0)

    def gather(values, wanted):
        picked = jnp.dot(
            values, jnp.where(wanted, 1.0, 0.0), precision=lax.Precision.HIGHEST, preferred_element_type=jnp.float32
        )
        return jnp.sum(jnp.where(mine, picked, 0.0), axis=0, keepdims=True)

    pick_next = gather(w_next, z == place)
    pick_now = gather(w_now, (z == place + 1) & (place < BLOCK - 1))
    carry = jnp.sum(jnp.where(lane == block * BLOCK, w_now, 0.0), axis=1, keepdims=True)
    square = lax.broadcasted_iota(jnp.int32, (angles, angles), 0) == lax.broadcasted_iota(jnp.int32, (angles, angles), 1)
    pick_carry = jnp.sum(jnp.where(square, carry, 0.0), axis=0, keepdims=True)
    turn = lambda other: lax.dot_general(
        weights, other, (((0,), (0,)), ((), ())), precision=lax.Precision.HIGHEST, preferred_element_type=jnp.float32
    )
    wide_w = turn(jnp.where(mine, 1.0, 0.0))
    turned_w = turn(jnp.where(square, 1.0, 0.0))
    fill_weights(wide_w, turned_w, pick_next, pick_now, pick_carry, spread_ref, carry_w_ref)


def device_tables(device, row_of_bases, fractions, path_weights, rows):
    angles, depth = path_weights.shape
    blocks = LANES // BLOCK
    last = fractions.shape[1] // LANES - 1
    column = lambda by: pl.BlockSpec((angles, LANES), lambda b, d: (0, jnp.clip(d[0] + by, 0, last)))
    whole = lambda shape: pl.BlockSpec(shape, lambda b, d: (0,) * len(shape))
    by_block = lambda shape: pl.BlockSpec((1,) + shape, lambda b, d: (b,) + (0,) * len(shape))
    coef = (BLOCK // HALF, 3, angles * HALF, LANES)
    edge_coef = (3, angles, LANES)
    image_w = (angles * HALF, HALF * depth)
    spread = (BLOCK * depth, angles * BLOCK)
    carry = (depth, angles)
    made = pl.pallas_call(
        functools.partial(tables_kernel, rows),
        grid_spec=pltpu.PrefetchScalarGridSpec(
            num_scalar_prefetch=1,
            grid=(blocks,),
            in_specs=[whole((1, LANES)), column(-1), column(0), column(1), whole(path_weights.shape)],
            out_specs=[by_block(coef), whole(edge_coef), whole(image_w), by_block(spread), by_block(carry)],
        ),
        out_shape=[
            jax.ShapeDtypeStruct((blocks,) + coef, jnp.float32),
            jax.ShapeDtypeStruct(edge_coef, jnp.float32),
            jax.ShapeDtypeStruct(image_w, jnp.bfloat16),
            jax.ShapeDtypeStruct((blocks,) + spread, jnp.bfloat16),
            jax.ShapeDtypeStruct((blocks,) + carry, jnp.bfloat16),
        ],
        name="make_tables",
    )(device, row_of_bases, fractions, fractions, fractions, path_weights)
    return made[0], made[1], made[2], path_weights, made[3], made[4]


def turn_kernel(classes, count, device_ref, bases_ref, seen_ref, *refs):
    outs, ends_ref, twice_ref, sems = refs[:-3], refs[-3], refs[-2], refs[-1]
    rows, cols = seen_ref.shape
    more = twice_ref.shape[0] - rows
    copies = [
        pltpu.make_async_copy(seen_ref, twice_ref.at[pl.ds(0, rows)], sems.at[0]),
        pltpu.make_async_copy(seen_ref.at[pl.ds(0, more)], twice_ref.at[pl.ds(rows, more)], sems.at[1]),
    ]
    for copy in copies:
        copy.start()
    for copy in copies:
        copy.wait()
    device = device_ref[0]
    base = bases_ref[device]
    my_class = device & (classes - 1)
    slices = count * PARTS

    def window(place, size, at):
        start = (place - base + 1 + rows) & (rows - 1)
        begin = pl.multiple_of(start & ~(BLOCK - 1), BLOCK)
        tall = size + BLOCK
        wide = twice_ref[pl.ds(begin, tall), at].astype(jnp.float32)
        return pltpu.roll(wide, (tall - (start - begin)) % tall, 0)

    for d in range(classes):
        for part in range(PARTS):
            out = outs[d * PARTS + part]
            place = (my_class ^ d) * slices + part * count

            @pl.loop(0, cols // WIDE)
            def _(chunk):
                at = pl.ds(pl.multiple_of(chunk * WIDE, WIDE), WIDE)
                out[:, at] = window(place, count, at)[:count].astype(jnp.bfloat16)

    @pl.loop(0, cols // WIDE)
    def _(chunk):
        at = pl.ds(pl.multiple_of(chunk * WIDE, WIDE), WIDE)
        for c in range(classes):
            ends_ref[c : c + 1, at] = window(c * slices - 1, BLOCK, at)[:1]


def turn(device, bases, seen, classes):
    rows, cols = seen.shape
    count = rows // classes // PARTS
    runs = classes * PARTS
    return pl.pallas_call(
        functools.partial(turn_kernel, classes, count),
        in_specs=[
            pl.BlockSpec(memory_space=pltpu.SMEM),
            pl.BlockSpec(memory_space=pltpu.SMEM),
            pl.BlockSpec(memory_space=pl.ANY),
        ],
        out_specs=[pl.BlockSpec(memory_space=pltpu.VMEM)] * (runs + 1),
        out_shape=[jax.ShapeDtypeStruct((count, cols), seen.dtype)] * runs + [jax.ShapeDtypeStruct((classes, cols), jnp.float32)],
        scratch_shapes=[pltpu.VMEM((rows + count + BLOCK, cols), seen.dtype), pltpu.SemaphoreType.DMA((2,))],
        compiler_params=pltpu.CompilerParams(vmem_limit_bytes=32 * 2**20),
        name="turn_rows",
    )(device, bases, seen)


def plan_kernel(slots, planes, classes, angles, count, rows, device_ref, bases_ref, table_ref):
    shape = (2 * PARTS * classes, LANES)
    lane = lax.broadcasted_iota(jnp.int32, shape, 1)
    row = lax.broadcasted_iota(jnp.int32, shape, 0)
    class_shift = classes.bit_length() - 1
    base = jnp.broadcast_to(bases_ref[...], shape) - 1
    low_plane = base >> (rows.bit_length() - 1)
    turned = base & (rows - 1)

    def reach(which):
        lowest = low_plane + jnp.where(which * count + count - 1 < turned, 1, 0)
        highest = low_plane + jnp.where(which * count < turned, 1, 0)
        return lowest, highest

    lowest, highest = reach(row >> 1)
    upward = (row & 1) == 0
    source = lane >> class_shift
    at = jnp.where(upward, source, planes - 1 - source)
    to = jnp.where(lane < angles, jnp.where(upward, highest, planes - 1 - lowest), -1)
    key = to * CODE + (CODE - 1 - lane)
    sent = [jnp.full(shape, -1, jnp.int32) for _ in range(planes - 1)]
    for slot in range(slots):
        begin = at
        for link in range(planes - 1):
            ready = (begin == link) & (to > link)
            for n in range(LOAD):
                best = jnp.max(jnp.where(ready, key, -1), axis=1, keepdims=True)
                taken = ready & (key == best)
                at = jnp.where(taken, link + 1, at)
                ready = ready & (key != best)
                which = jnp.where(best >= 0, CODE - 1 - (best & (CODE - 1)), -1)
                sent[link] = jnp.where(lane == slot * LOAD + n, which, sent[link])

    me = device_ref[0]
    my_class = me & (classes - 1)
    plane = me >> class_shift
    none = jnp.full(shape, -1, jnp.int32)
    used = none
    for link in range(planes - 1):
        used = jnp.maximum(used, sent[link])
    used = jnp.max(used, axis=0, keepdims=True)
    head = lane[:1]
    total = jnp.sum(jnp.where((used >= 0) & (head % LOAD == 0), 1, 0), axis=1, keepdims=True)

    tall = -(-max(slots * LOAD, angles) // 8) * 8
    sub = lax.broadcasted_iota(jnp.int32, (tall, LANES), 0)
    held = jnp.where(head < classes, plane * classes + (head ^ my_class), -1)
    for part in range(PARTS):
        low_here, high_here = reach(my_class * PARTS + part)
        wanted = (plane >= low_here) & (plane <= high_here) & (lane < angles)
        wanted = column_of(jnp.where(wanted, 1, 0)[:1], tall) > 0
        keep = lambda ids: jnp.max(jnp.where((sub == ids) & wanted, ids, -1), axis=0, keepdims=True)
        for way, spot in ((0, plane), (1, planes - 1 - plane)):
            sends, gets = none, none
            for link in range(planes - 1):
                sends = jnp.where(spot == link, sent[link], sends)
                gets = jnp.where(spot == link + 1, sent[link], gets)
            mine = row == 2 * (my_class * PARTS + part) + way
            sends = jnp.max(jnp.where(mine, sends, -1), axis=0, keepdims=True)
            gets = jnp.max(jnp.where(mine, gets, -1), axis=0, keepdims=True)
            arrived = jnp.max(jnp.where((column_of(gets, tall) == sends) & (sends >= 0), sub, 0), axis=0, keepdims=True)
            own = (sends >> class_shift) == plane
            index = jnp.where(own, (sends & (classes - 1)) ^ my_class, classes + arrived)
            line = part * LINES + way
            table_ref[line : line + 1] = jnp.where(sends >= 0, index, 0)
            table_ref[line + 2 : line + 3] = keep(gets)
        line = part * LINES + 4
        table_ref[line : line + 1] = keep(held)
    table_ref[PARTS * LINES : PARTS * LINES + 1] = jnp.broadcast_to(total, head.shape)


def choose_kernel(slot, part, ups, downs, table_ref, *refs):
    sources = refs[:ups], refs[ups : ups + downs]
    outs = refs[ups + downs : ups + downs + 2]
    held, sems = refs[ups + downs + 2 :]
    views = [spread_out(side) for side in sources]
    for way in range(2):
        for n in range(LOAD):
            for m, view in enumerate(views[way]):

                @pl.when(table_ref[part * LINES + way, slot * LOAD + n] == m)
                def _():
                    pltpu.make_async_copy(view, held.at[way, n], sems.at[0, way, n]).start()

    for way in range(2):
        for n in range(LOAD):
            pltpu.make_async_copy(views[way][0], held.at[way, n], sems.at[0, way, n]).wait()
            pltpu.make_async_copy(held.at[way, n], outs[way].at[n], sems.at[1, way, n]).start()
    for way in range(2):
        for n in range(LOAD):
            pltpu.make_async_copy(held.at[way, n], outs[way].at[n], sems.at[1, way, n]).wait()


def choose(slot, part, table, own, ups, downs):
    up_from, down_from = own + ups, own + downs
    anywhere = pl.BlockSpec(memory_space=pl.ANY)
    shape = jax.ShapeDtypeStruct((LOAD,) + own[0].shape, own[0].dtype)
    return pl.pallas_call(
        functools.partial(choose_kernel, slot, part, len(up_from), len(down_from)),
        in_specs=[pl.BlockSpec(memory_space=pltpu.SMEM)] + [anywhere] * (len(up_from) + len(down_from)),
        out_specs=[anywhere, anywhere],
        out_shape=[shape, shape],
        scratch_shapes=[
            pltpu.VMEM((2, LOAD) + own[0].shape, own[0].dtype),
            pltpu.SemaphoreType.DMA((2, 2, LOAD)),
        ],
        cost_estimate=pl.CostEstimate(flops=0, bytes_accessed=4 * LOAD * own[0].size * 2, transcendentals=0),
        name="choose_packet",
    )(table, *up_from, *down_from)


def on_device(volume, measured, path_weights, fractions, bases):
    slices, depth, cols = volume.shape
    local, rows = measured.shape[:2]
    nslab = lax.axis_size("slab")
    device = lax.axis_index("slab")
    angles = local * nslab
    first = device * slices
    classes = rows // slices
    planes = nslab // classes
    ups_of = lambda step: [(i, i + step) for i in range(nslab - step)]
    downs_of = lambda step: [(i + step, i) for i in range(nslab - step)]

    routed = local == 1 and classes == ROUTED_CLASSES and slices == LANES and rows & (rows - 1) == 0 and angles <= LANES
    if not routed:
        left = lax.ppermute(volume[slices - 1 :], "slab", ups_of(1))
        right = lax.ppermute(volume[:1], "slab", downs_of(1))
        share = lax.dynamic_slice_in_dim(jnp.pad(fractions, ((0, 0), (1, 1))), first, slices + 2, 1)
        tables = make_tables(share, first, rows, path_weights, bases, slices)
        my_bases = lax.dynamic_slice_in_dim(bases, device * local, local, 0)
        turned = jax.vmap(lambda m, b: jnp.roll(m, b - 1, axis=0))(measured, my_bases)
        by_class = turned.reshape(local, classes, slices, cols).transpose(1, 0, 2, 3)
        outgoing = jnp.tile(by_class, (planes, 1, 1, 1)).reshape(angles, slices, cols)
        seen = lax.all_to_all(outgoing, "slab", split_axis=0, concat_axis=0, tiled=True)
        ends = jnp.roll(by_class[:, :, slices - 1], 1, axis=0)
        ends = jnp.tile(ends, (planes, 1, 1)).reshape(angles, cols // LANES, LANES)
        edge = lax.all_to_all(ends, "slab", split_axis=0, concat_axis=0, tiled=True).reshape(angles, cols)
        return update(volume, left, right, edge, tables, [seen], jnp.zeros((8, LANES), jnp.int32), None, 0, 1, True)[0]

    number = device.astype(jnp.int32)[None]
    left = lax.ppermute(volume[slices - 1 :], "slab", ups_of(1))
    right = lax.ppermute(volume[:1], "slab", downs_of(1))
    *runs, ends = turn(number, bases, measured[0], classes)
    row_of_bases = jnp.pad(bases, (0, LANES - angles), constant_values=1)[None]
    runs, row_of_bases = lax.optimization_barrier((runs, row_of_bases))

    def share_out(part):
        mine = [runs[d * PARTS + part] for d in range(classes)]
        return mine[:1] + [
            lax.ppermute(mine[d], "slab", [(i, i ^ d) for i in range(nslab)]) for d in range(1, classes)
        ]

    own = [share_out(0)]

    most = -(-classes * (planes - 1) // LOAD) + planes - 2
    table = pl.pallas_call(
        functools.partial(plan_kernel, most, planes, classes, angles, slices // PARTS, rows),
        in_specs=[pl.BlockSpec(memory_space=pltpu.SMEM), pl.BlockSpec(memory_space=pltpu.VMEM)],
        out_shape=jax.ShapeDtypeStruct((16, LANES), jnp.int32),
        name="plan_slots",
    )(number, row_of_bases)
    tables = device_tables(number, row_of_bases, fractions, path_weights, rows)
    runs, own, table, tables, left, right = lax.optimization_barrier((runs, own, table, tables, left, right))
    own += [share_out(part) for part in range(1, PARTS)]
    slots = table[PARTS * LINES, 0]

    def run_slots(begin, end, ups, downs, ends=None):
        nonlocal table
        ups, downs = [list(u) for u in ups], [list(d) for d in downs]
        edge = None
        for slot in range(begin, end):
            for part in range(PARTS):
                go_up, go_down = choose(slot, part, table, own[part], ups[part], downs[part])
                if slot == 0 and part == PARTS - 1:
                    go_up, ends = lax.optimization_barrier((go_up, ends))
                    ends = jnp.tile(ends.astype(jnp.bfloat16)[None], (planes, 1, 1)).reshape(angles, cols // LANES, LANES)
                    edge = lax.all_to_all(ends, "slab", split_axis=0, concat_axis=0, tiled=True).reshape(angles, cols)
                    table, edge = lax.optimization_barrier((table, edge))
                ups[part].append(lax.ppermute(go_up, "slab", ups_of(classes)))
                downs[part].append(lax.ppermute(go_down, "slab", downs_of(classes)))
        return ups, downs, edge

    ups, downs, edge = run_slots(0, STEADY, [[] for _ in range(PARTS)], [[] for _ in range(PARTS)], ends)

    def finish(end):
        def branch(ups, downs):
            ups, downs, _ = run_slots(STEADY, end, ups, downs)
            out, carry = None, edge
            for part in range(PARTS):
                packets = own[part] + ups[part] + downs[part]
                out, carry = update(volume, left, right, carry, tables, packets, table, out, part, PARTS, False)
            return out

        return branch

    ends_at = [STEADY + 1, STEADY + 2, most]
    which = jnp.sum(jnp.array([slots > e for e in ends_at[:-1]]).astype(jnp.int32))
    return lax.switch(which, [finish(e) for e in ends_at], ups, downs)


def solution(mesh):
    placed = (P(("groups", "slab"), None, None), P(("groups", "slab"), None, None), P(), P(), P())
    return jax.shard_map(
        on_device,
        mesh=mesh,
        in_specs=placed,
        out_specs=P(("groups", "slab"), None, None),
        check_vma=False,
    )
```

```python
import functools

import jax
import jax.numpy as jnp
from jax import lax
from jax.experimental import pallas as pl
from jax.experimental.pallas import tpu as pltpu
from jax.sharding import PartitionSpec as P

RELAX = 1.0
BLOCK = 16
HALF = 8
LANES = 128
WIDE = 256
PIECES = 4
PARTS = 2
ROUTED_CLASSES = 4
LOAD = 2
STEADY = 2
CODE = 256
LINES = 5
VMEM_LIMIT = 56 * 2**20


def dot(a, b):
    return jnp.dot(a, b, preferred_element_type=jnp.float32)


def widen(coef):
    return jnp.concatenate([coef] * (WIDE // LANES), axis=1)


def spread_out(packets):
    return [r for p in packets for r in ([p] if p.ndim == 2 else [p.at[n] for n in range(LOAD)])]


def update_kernel(
    dense, part, table_ref, lower_ref, upper_ref, next_ref, left_ref, right_ref, edge_ref, coef_ref, edge_coef_ref,
    image_w_ref, weight_ref, spread_ref, carry_w_ref, *rest,
):
    out_ref, carry_ref, seen_ref, result_ref, sems, out_sems = rest[-6:]
    packets = rest[:-7]
    block = pl.program_id(0)
    blocks = pl.num_programs(0)
    depth, width = lower_ref.shape[1:]
    angles = weight_ref.shape[0]
    first = part * blocks * BLOCK

    def fetch(at_block, act):
        slot = at_block % 2
        rows = pl.ds(pl.multiple_of(at_block * BLOCK, BLOCK), BLOCK)
        if dense:
            act(pltpu.make_async_copy(packets[0].at[:, rows], seen_ref.at[slot], sems.at[slot, 0]))
            return
        views = spread_out(packets)
        arrived = (len(views) - ROUTED_CLASSES) // 2
        names = [(4, n) for n in range(ROUTED_CLASSES)] + [(way, n) for way in (2, 3) for n in range(arrived)]
        for n, (view, (line, spot)) in enumerate(zip(views, names)):
            name = table_ref[part * LINES + line, spot]

            @pl.when(name >= 0)
            def _():
                act(pltpu.make_async_copy(view.at[rows], seen_ref.at[slot, name], sems.at[slot, n]))

    def deliver(at_block, act):
        slot = at_block % 2
        size = BLOCK // PIECES
        for n in range(PIECES):
            source = result_ref.at[slot, pl.ds(n * size, size)]
            act(pltpu.make_async_copy(source, out_ref.at[pl.ds(first + at_block * BLOCK + n * size, size)], out_sems.at[slot, n]))

    @pl.when(block == 0)
    def _():
        seen_ref[...] = jnp.zeros_like(seen_ref)
        fetch(block, lambda copy: copy.start())

    @pl.when(block + 1 < blocks)
    def _():
        fetch(block + 1, lambda copy: copy.start())

    @pl.when(block == 0)
    def _():
        if part:
            carry_ref[...] = edge_ref[...]
            return
        for chunk in range(width // WIDE):
            at = pl.ds(chunk * WIDE, WIDE)
            mine = dot(weight_ref[...], lower_ref[0, :, at])
            before = dot(weight_ref[...], left_ref[0, :, at])
            carry_ref[:, at] = (
                edge_ref[:, at].astype(jnp.float32) * widen(edge_coef_ref[2])
                - mine * widen(edge_coef_ref[0])
                - before * widen(edge_coef_ref[1])
            ).astype(jnp.bfloat16)

    @pl.when(block >= 2)
    def _():
        deliver(block - 2, lambda copy: copy.wait())

    fetch(block, lambda copy: copy.wait())
    slot = block % 2
    final = (block == blocks - 1) & (part == PARTS - 1 or dense)

    def columns(chunk):
        if dense:
            return pl.ds(pl.multiple_of(chunk * WIDE, WIDE), WIDE)
        return slice(chunk * WIDE, (chunk + 1) * WIDE)

    def image(chunk):
        at = columns(chunk)
        images = [dot(image_w_ref[...], r[:, :, at].reshape(HALF * depth, WIDE)) for r in (lower_ref, upper_ref)]
        after = dot(weight_ref[...], jnp.where(final, right_ref[0, :, at], next_ref[0, :, at]))
        return images, after

    def residual(chunk, images, after):
        at = columns(chunk)
        seen = seen_ref[slot, :, :, at].astype(jnp.float32)
        ahead = [pltpu.roll(x.reshape(angles, HALF, WIDE), HALF - 1, 1) for x in images]
        ahead.append(jnp.broadcast_to(after.reshape(angles, 1, WIDE), (angles, HALF, WIDE)))
        tail = lax.broadcasted_iota(jnp.int32, (angles, HALF, WIDE), 1) == HALF - 1
        parts = []
        for half in range(2):
            now = jnp.where(tail, ahead[half + 1], ahead[half]).reshape(angles * HALF, WIDE)
            got = seen[:, half * HALF : (half + 1) * HALF].reshape(angles * HALF, WIDE)
            coef = [widen(coef_ref[0, half, n]) for n in range(3)]
            resid = got * coef[2] - now * coef[0] - images[half] * coef[1]
            parts.append(resid.reshape(angles, HALF, WIDE))
        resid = jnp.concatenate(parts, axis=1)
        return resid.astype(jnp.bfloat16).reshape(angles * BLOCK, WIDE), resid[:, BLOCK - 1].astype(jnp.bfloat16)

    def result(chunk, resid, last):
        at = columns(chunk)
        spread = dot(spread_ref[0], resid).reshape(BLOCK, depth, WIDE)
        extra = dot(carry_w_ref[0], carry_ref[:, at])
        carry_ref[:, at] = last
        for half, r in enumerate((lower_ref, upper_ref)):
            volume = r[:, :, at].astype(jnp.float32)
            here = half * HALF
            if half == 0:
                result_ref[slot, 0, :, at] = volume[0] + spread[0] + extra
                result_ref[slot, 1:HALF, :, at] = volume[1:] + spread[1:HALF]
            else:
                result_ref[slot, here : here + HALF, :, at] = volume + spread[here : here + HALF]

    chunks = width // WIDE
    if dense:
        pl.loop(0, chunks)(lambda chunk: result(chunk, *residual(chunk, *image(chunk))))
    else:
        images, resids = {}, {}
        for n in range(chunks + 2):
            if n < chunks:
                images[n] = image(n)
            if 1 <= n <= chunks:
                resids[n - 1] = residual(n - 1, *images.pop(n - 1))
            if n >= 2:
                result(n - 2, *resids.pop(n - 2))
    deliver(block, lambda copy: copy.start())

    @pl.when(block == blocks - 1)
    def _():
        @pl.when(block >= 1)
        def _():
            deliver(block - 1, lambda copy: copy.wait())

        deliver(block, lambda copy: copy.wait())


def update(volume, left, right, edge, tables, packets, table, before, part, parts, dense):
    slices, depth, cols = volume.shape
    angles = edge.shape[0]
    blocks = slices // BLOCK // parts
    off = part * blocks
    by_block = lambda x: pl.BlockSpec((1,) + x.shape[1:], lambda b, i: (b,) + (0,) * (x.ndim - 1))
    whole = lambda x: pl.BlockSpec(x.shape, lambda b, i: (0,) * x.ndim)
    anywhere = pl.BlockSpec(memory_space=pl.ANY)
    coef, edge_coef, image_w, weights, spread_w, carry_w = tables
    aliases = {} if before is None else {13 + len(packets): 0}
    copies = 1 if dense else ROUTED_CLASSES + LOAD * (len(packets) - ROUTED_CLASSES)
    one = (1, depth, cols)
    return pl.pallas_call(
        functools.partial(update_kernel, dense, part),
        grid_spec=pltpu.PrefetchScalarGridSpec(
            num_scalar_prefetch=1,
            grid=(blocks,),
            in_specs=[
                pl.BlockSpec((HALF, depth, cols), lambda b, i: (2 * (b + off), 0, 0)),
                pl.BlockSpec((HALF, depth, cols), lambda b, i: (2 * (b + off) + 1, 0, 0)),
                pl.BlockSpec(one, lambda b, i: (jnp.minimum((b + off + 1) * BLOCK, slices - 1), 0, 0)),
                pl.BlockSpec(one, lambda b, i: (0, 0, 0)),
                pl.BlockSpec(one, lambda b, i: (0, 0, 0)),
                whole(edge), by_block(coef), whole(edge_coef), whole(image_w), whole(weights),
                by_block(spread_w), by_block(carry_w),
            ]
            + [anywhere] * (len(packets) + 1),
            out_specs=[anywhere, whole(edge)],
            scratch_shapes=[
                pltpu.VMEM((2, angles, BLOCK, cols), jnp.bfloat16),
                pltpu.VMEM((2, BLOCK, depth, cols), jnp.float32),
                pltpu.SemaphoreType.DMA((2, copies)),
                pltpu.SemaphoreType.DMA((2, PIECES)),
            ],
        ),
        out_shape=[jax.ShapeDtypeStruct(volume.shape, jnp.float32), jax.ShapeDtypeStruct(edge.shape, edge.dtype)],
        input_output_aliases=aliases,
        compiler_params=pltpu.CompilerParams(dimension_semantics=("arbitrary",), vmem_limit_bytes=VMEM_LIMIT),
        cost_estimate=pl.CostEstimate(
            flops=4 * slices * depth * cols * angles // parts, bytes_accessed=volume.size * 7 // parts, transcendentals=0
        ),
        name="slab_update",
    )(
        table, volume, volume, volume, left, right, edge, coef, edge_coef, image_w, weights, spread_w, carry_w,
        *packets, edge if before is None else before,
    )


def fill_weights(wide_w, turned_w, pick_next, pick_now, pick_carry, spread_ref, carry_w_ref):
    depth, columns = wide_w.shape
    place = lax.broadcasted_iota(jnp.int32, (depth, columns), 1) % BLOCK
    from_next = wide_w * pick_next
    from_now = wide_w * pick_now
    from_carry = turned_w * pick_carry
    for z in range(BLOCK):
        row = jnp.where(place == z, from_next, jnp.where(place == z - 1, from_now, 0.0))
        total = jnp.sum(row, axis=1, keepdims=True)
        if z == 0:
            total = total + jnp.sum(from_carry, axis=1, keepdims=True)
            carry_w_ref[0] = (from_carry * (RELAX / total)).astype(jnp.bfloat16)
        spread_ref[0, z * depth : (z + 1) * depth] = (row * (RELAX / total)).astype(jnp.bfloat16)


def weights_kernel(wide_w_ref, turned_w_ref, pick_ref, pick_carry_ref, spread_ref, carry_w_ref):
    picks = pick_ref[0, 0:1], pick_ref[0, 1:2], pick_carry_ref[0]
    fill_weights(wide_w_ref[...], turned_w_ref[...], *picks, spread_ref, carry_w_ref)


def make_weights(wide_w, turned_w, pick, pick_carry):
    blocks = pick.shape[0]
    depth, angles = turned_w.shape
    by_block = lambda shape: pl.BlockSpec((1,) + shape, lambda b: (b,) + (0,) * len(shape))
    whole = lambda x: pl.BlockSpec(x.shape, lambda b: (0,) * x.ndim)
    spread = (BLOCK * depth, angles * BLOCK)
    carry = (depth, angles)
    return pl.pallas_call(
        weights_kernel,
        grid=(blocks,),
        in_specs=[whole(wide_w), whole(turned_w), by_block(pick.shape[1:]), by_block(pick_carry.shape[1:])],
        out_specs=[by_block(spread), by_block(carry)],
        out_shape=[
            jax.ShapeDtypeStruct((blocks,) + spread, jnp.bfloat16),
            jax.ShapeDtypeStruct((blocks,) + carry, jnp.bfloat16),
        ],
        name="spread_weights",
    )(wide_w, turned_w, pick, pick_carry)


def make_tables(share, first, rows, path_weights, bases, slices):
    angles, depth = path_weights.shape
    blocks = slices // BLOCK
    weights = path_weights.astype(jnp.float32)
    ray_total = jnp.sum(weights, axis=1)[:, None]
    norm = 1.0 / (ray_total * ((1.0 - share[:, 1:]) + share[:, :-1]))
    coefs = jnp.stack([(1.0 - share[:, 1:]) * norm, share[:, :-1] * norm, norm])
    coef = coefs[:, :, 1:].reshape(3, angles, blocks, BLOCK // HALF, HALF).transpose(2, 3, 0, 1, 4)
    coef = coef.reshape(blocks, BLOCK // HALF, 3, angles * HALF, 1)
    coef = jnp.broadcast_to(coef, coef.shape[:4] + (LANES,))
    edge_coef = jnp.broadcast_to(coefs[:, :, :1], (3, angles, LANES))
    share_own = share[:, 1:-1]
    row_now = (first - bases)[:, None] + jnp.arange(slices, dtype=jnp.int32)[None, :]
    w_now = jnp.where((row_now >= 0) & (row_now < rows), 1.0 - share_own, 0.0)
    w_next = jnp.where((row_now + 1 >= 0) & (row_now + 1 < rows), share_own, 0.0)
    pick = jnp.stack([w_next, jnp.pad(w_now[:, 1:], ((0, 0), (0, 1)))]).reshape(2, angles, blocks, BLOCK)
    pick = pick.transpose(2, 0, 1, 3).reshape(blocks, 2, angles * BLOCK)
    pick_carry = w_now[:, ::BLOCK].T[:, None, :]
    eye = jnp.eye(HALF, dtype=jnp.float32)
    image_w = jnp.einsum("ad,yz->ayzd", weights, eye).reshape(angles * HALF, HALF * depth).astype(jnp.bfloat16)
    wide_w = jnp.repeat(weights.T, BLOCK, axis=1)
    return coef, edge_coef, image_w, path_weights, *make_weights(wide_w, weights.T, pick, pick_carry)


def column_of(line, tall):
    sub = lax.broadcasted_iota(jnp.int32, (tall, LANES), 0)
    lane = lax.broadcasted_iota(jnp.int32, (tall, LANES), 1)
    return jnp.max(jnp.where(sub == lane, line, -1), axis=1, keepdims=True)


def tables_kernel(
    rows, off, device_ref, bases_ref, before_ref, own_ref, after_ref, weight_ref,
    coef_ref, edge_coef_ref, image_w_ref, spread_ref, carry_w_ref, wide_ref, turned_ref,
):
    block = pl.program_id(0) + off
    angles, depth = weight_ref.shape
    first = device_ref[0] * LANES
    shape = (angles, LANES)
    lane = lax.broadcasted_iota(jnp.int32, shape, 1)
    sub = lax.broadcasted_iota(jnp.int32, shape, 0)
    weights = weight_ref[...].astype(jnp.float32)
    ray_total = jnp.sum(weights, axis=1, keepdims=True)
    own = own_ref[...]
    ahead = jnp.where(lane == LANES - 1, pltpu.roll(after_ref[...], LANES - 1, 1), pltpu.roll(own, LANES - 1, 1))
    norm = 1.0 / (ray_total * ((1.0 - ahead) + own))
    coefs = ((1.0 - ahead) * norm, own * norm, norm)
    spots = lax.broadcasted_iota(jnp.int32, (angles, HALF, LANES), 2) - lax.broadcasted_iota(jnp.int32, (angles, HALF, LANES), 1)
    for half in range(BLOCK // HALF):
        here = spots == block * BLOCK + half * HALF
        for n, coef in enumerate(coefs):
            tall = jnp.broadcast_to(coef.reshape(angles, 1, LANES), (angles, HALF, LANES))
            tall = jnp.sum(jnp.where(here, tall, 0.0), axis=2, keepdims=True)
            coef_ref[0, half, n] = jnp.broadcast_to(tall, (angles, HALF, LANES)).reshape(angles * HALF, LANES)

    @pl.when(block == off)
    def _():
        edge_own = jnp.sum(jnp.where(lane == 0, own, 0.0), axis=1, keepdims=True)
        edge_before = jnp.sum(jnp.where(lane == LANES - 1, before_ref[...], 0.0), axis=1, keepdims=True)
        edge_norm = 1.0 / (ray_total * ((1.0 - edge_own) + edge_before))
        for n, coef in enumerate(((1.0 - edge_own) * edge_norm, edge_before * edge_norm, edge_norm)):
            edge_coef_ref[n] = jnp.broadcast_to(coef, shape)
        across = (HALF * depth)
        repeat = lax.broadcasted_iota(jnp.int32, (depth, across), 1) % depth
        repeat = jnp.where(repeat == lax.broadcasted_iota(jnp.int32, (depth, across), 0), 1.0, 0.0)
        wide = dot(weight_ref[...], repeat.astype(jnp.bfloat16)).astype(jnp.bfloat16)
        down = angles * HALF
        expand = lax.broadcasted_iota(jnp.int32, (down, angles), 0) // HALF
        expand = jnp.where(expand == lax.broadcasted_iota(jnp.int32, (down, angles), 1), 1.0, 0.0)
        wide = dot(expand.astype(jnp.bfloat16), wide)
        at = lax.broadcasted_iota(jnp.int32, (down, across), 0) % HALF
        same = lax.broadcasted_iota(jnp.int32, (down, across), 1) // depth == at
        image_w_ref[...] = jnp.where(same, wide, 0.0).astype(jnp.bfloat16)

    row_now = first + lane - column_of(bases_ref[...], angles)
    w_now = jnp.where((row_now >= 0) & (row_now < rows), 1.0 - own, 0.0)
    w_next = jnp.where((row_now + 1 >= 0) & (row_now + 1 < rows), own, 0.0)
    columns = angles * BLOCK
    place = lax.broadcasted_iota(jnp.int32, (LANES, columns), 1) % BLOCK
    z = lax.broadcasted_iota(jnp.int32, (LANES, columns), 0) - block * BLOCK
    mine = lax.broadcasted_iota(jnp.int32, (angles, columns), 1) // BLOCK
    mine = mine == lax.broadcasted_iota(jnp.int32, (angles, columns), 0)

    def gather(values, wanted):
        picked = jnp.dot(
            values, jnp.where(wanted, 1.0, 0.0), precision=lax.Precision.HIGHEST, preferred_element_type=jnp.float32
        )
        return jnp.sum(jnp.where(mine, picked, 0.0), axis=0, keepdims=True)

    pick_next = gather(w_next, z == place)
    pick_now = gather(w_now, (z == place + 1) & (place < BLOCK - 1))
    carry = jnp.sum(jnp.where(lane == block * BLOCK, w_now, 0.0), axis=1, keepdims=True)
    square = lax.broadcasted_iota(jnp.int32, (angles, angles), 0) == lax.broadcasted_iota(jnp.int32, (angles, angles), 1)
    pick_carry = jnp.sum(jnp.where(square, carry, 0.0), axis=0, keepdims=True)
    turned = lambda other: lax.dot_general(
        weights, other, (((0,), (0,)), ((), ())), precision=lax.Precision.HIGHEST, preferred_element_type=jnp.float32
    )

    @pl.when(block == off)
    def _():
        wide_ref[...] = turned(jnp.where(mine, 1.0, 0.0))
        turned_ref[...] = turned(jnp.where(square, 1.0, 0.0))

    fill_weights(wide_ref[...], turned_ref[...], pick_next, pick_now, pick_carry, spread_ref, carry_w_ref)


def device_tables(device, row_of_bases, fractions, path_weights, rows, part):
    angles, depth = path_weights.shape
    blocks = LANES // BLOCK // PARTS
    last = fractions.shape[1] // LANES - 1
    column = lambda by: pl.BlockSpec((angles, LANES), lambda b, d: (0, jnp.clip(d[0] + by, 0, last)))
    whole = lambda shape: pl.BlockSpec(shape, lambda b, d: (0,) * len(shape))
    by_block = lambda shape: pl.BlockSpec((1,) + shape, lambda b, d: (b,) + (0,) * len(shape))
    coef = (BLOCK // HALF, 3, angles * HALF, LANES)
    edge_coef = (3, angles, LANES)
    image_w = (angles * HALF, HALF * depth)
    spread = (BLOCK * depth, angles * BLOCK)
    carry = (depth, angles)
    made = pl.pallas_call(
        functools.partial(tables_kernel, rows, part * blocks),
        grid_spec=pltpu.PrefetchScalarGridSpec(
            num_scalar_prefetch=1,
            grid=(blocks,),
            in_specs=[whole((1, LANES)), column(-1), column(0), column(1), whole(path_weights.shape)],
            out_specs=[by_block(coef), whole(edge_coef), whole(image_w), by_block(spread), by_block(carry)],
            scratch_shapes=[
                pltpu.VMEM((depth, angles * BLOCK), jnp.float32),
                pltpu.VMEM((depth, angles), jnp.float32),
            ],
        ),
        out_shape=[
            jax.ShapeDtypeStruct((blocks,) + coef, jnp.float32),
            jax.ShapeDtypeStruct(edge_coef, jnp.float32),
            jax.ShapeDtypeStruct(image_w, jnp.bfloat16),
            jax.ShapeDtypeStruct((blocks,) + spread, jnp.bfloat16),
            jax.ShapeDtypeStruct((blocks,) + carry, jnp.bfloat16),
        ],
        name="make_tables",
    )(device, row_of_bases, fractions, fractions, fractions, path_weights)
    return made[0], made[1], made[2], path_weights, made[3], made[4]


def turn_kernel(classes, count, device_ref, bases_ref, seen_ref, *refs):
    outs, ends_ref, twice_ref, sems = refs[:-3], refs[-3], refs[-2], refs[-1]
    rows, cols = seen_ref.shape
    more = twice_ref.shape[0] - rows
    copies = [
        pltpu.make_async_copy(seen_ref, twice_ref.at[pl.ds(0, rows)], sems.at[0]),
        pltpu.make_async_copy(seen_ref.at[pl.ds(0, more)], twice_ref.at[pl.ds(rows, more)], sems.at[1]),
    ]
    for copy in copies:
        copy.start()
    for copy in copies:
        copy.wait()
    device = device_ref[0]
    base = bases_ref[device]
    my_class = device & (classes - 1)
    slices = count * PARTS

    def window(place, size, at):
        start = (place - base + 1 + rows) & (rows - 1)
        begin = pl.multiple_of(start & ~(BLOCK - 1), BLOCK)
        tall = size + BLOCK
        wide = twice_ref[pl.ds(begin, tall), at].astype(jnp.float32)
        return pltpu.roll(wide, (tall - (start - begin)) % tall, 0)

    for d in range(classes):
        for part in range(PARTS):
            out = outs[d * PARTS + part]
            place = (my_class ^ d) * slices + part * count

            @pl.loop(0, cols // WIDE)
            def _(chunk):
                at = pl.ds(pl.multiple_of(chunk * WIDE, WIDE), WIDE)
                out[:, at] = window(place, count, at)[:count].astype(jnp.bfloat16)

    @pl.loop(0, cols // WIDE)
    def _(chunk):
        at = pl.ds(pl.multiple_of(chunk * WIDE, WIDE), WIDE)
        for c in range(classes):
            ends_ref[c : c + 1, at] = window(c * slices - 1, BLOCK, at)[:1]


def turn(device, bases, seen, classes):
    rows, cols = seen.shape
    count = rows // classes // PARTS
    runs = classes * PARTS
    return pl.pallas_call(
        functools.partial(turn_kernel, classes, count),
        in_specs=[
            pl.BlockSpec(memory_space=pltpu.SMEM),
            pl.BlockSpec(memory_space=pltpu.SMEM),
            pl.BlockSpec(memory_space=pl.ANY),
        ],
        out_specs=[pl.BlockSpec(memory_space=pltpu.VMEM)] * (runs + 1),
        out_shape=[jax.ShapeDtypeStruct((count, cols), seen.dtype)] * runs + [jax.ShapeDtypeStruct((classes, cols), jnp.float32)],
        scratch_shapes=[pltpu.VMEM((rows + count + BLOCK, cols), seen.dtype), pltpu.SemaphoreType.DMA((2,))],
        compiler_params=pltpu.CompilerParams(vmem_limit_bytes=32 * 2**20),
        name="turn_rows",
    )(device, bases, seen)


def plan_kernel(slots, planes, classes, angles, count, rows, device_ref, bases_ref, table_ref):
    shape = (2 * PARTS * classes, LANES)
    lane = lax.broadcasted_iota(jnp.int32, shape, 1)
    row = lax.broadcasted_iota(jnp.int32, shape, 0)
    class_shift = classes.bit_length() - 1
    base = jnp.broadcast_to(bases_ref[...], shape) - 1
    low_plane = base >> (rows.bit_length() - 1)
    turned = base & (rows - 1)

    def reach(which):
        lowest = low_plane + jnp.where(which * count + count - 1 < turned, 1, 0)
        highest = low_plane + jnp.where(which * count < turned, 1, 0)
        return lowest, highest

    lowest, highest = reach(row >> 1)
    upward = (row & 1) == 0
    source = lane >> class_shift
    at = jnp.where(upward, source, planes - 1 - source)
    to = jnp.where(lane < angles, jnp.where(upward, highest, planes - 1 - lowest), -1)
    key = to * CODE + (CODE - 1 - lane)
    sent = [jnp.full(shape, -1, jnp.int32) for _ in range(planes - 1)]
    for slot in range(slots):
        begin = at
        for link in range(planes - 1):
            ready = (begin == link) & (to > link)
            for n in range(LOAD):
                best = jnp.max(jnp.where(ready, key, -1), axis=1, keepdims=True)
                taken = ready & (key == best)
                at = jnp.where(taken, link + 1, at)
                ready = ready & (key != best)
                which = jnp.where(best >= 0, CODE - 1 - (best & (CODE - 1)), -1)
                sent[link] = jnp.where(lane == slot * LOAD + n, which, sent[link])

    me = device_ref[0]
    my_class = me & (classes - 1)
    plane = me >> class_shift
    none = jnp.full(shape, -1, jnp.int32)
    used = none
    for link in range(planes - 1):
        used = jnp.maximum(used, sent[link])
    used = jnp.max(used, axis=0, keepdims=True)
    head = lane[:1]
    total = jnp.sum(jnp.where((used >= 0) & (head % LOAD == 0), 1, 0), axis=1, keepdims=True)

    tall = -(-max(slots * LOAD, angles) // 8) * 8
    sub = lax.broadcasted_iota(jnp.int32, (tall, LANES), 0)
    held = jnp.where(head < classes, plane * classes + (head ^ my_class), -1)
    for part in range(PARTS):
        low_here, high_here = reach(my_class * PARTS + part)
        wanted = (plane >= low_here) & (plane <= high_here) & (lane < angles)
        wanted = column_of(jnp.where(wanted, 1, 0)[:1], tall) > 0
        keep = lambda ids: jnp.max(jnp.where((sub == ids) & wanted, ids, -1), axis=0, keepdims=True)
        for way, spot in ((0, plane), (1, planes - 1 - plane)):
            sends, gets = none, none
            for link in range(planes - 1):
                sends = jnp.where(spot == link, sent[link], sends)
                gets = jnp.where(spot == link + 1, sent[link], gets)
            mine = row == 2 * (my_class * PARTS + part) + way
            sends = jnp.max(jnp.where(mine, sends, -1), axis=0, keepdims=True)
            gets = jnp.max(jnp.where(mine, gets, -1), axis=0, keepdims=True)
            arrived = jnp.max(jnp.where((column_of(gets, tall) == sends) & (sends >= 0), sub, 0), axis=0, keepdims=True)
            own = (sends >> class_shift) == plane
            index = jnp.where(own, (sends & (classes - 1)) ^ my_class, classes + arrived)
            line = part * LINES + way
            table_ref[line : line + 1] = jnp.where(sends >= 0, index, 0)
            table_ref[line + 2 : line + 3] = keep(gets)
        line = part * LINES + 4
        table_ref[line : line + 1] = keep(held)
    table_ref[PARTS * LINES : PARTS * LINES + 1] = jnp.broadcast_to(total, head.shape)


def choose_kernel(slot, part, ups, downs, table_ref, *refs):
    sources = refs[:ups], refs[ups : ups + downs]
    outs = refs[ups + downs : ups + downs + 2]
    held, sems = refs[ups + downs + 2 :]
    views = [spread_out(side) for side in sources]
    for way in range(2):
        for n in range(LOAD):
            for m, view in enumerate(views[way]):

                @pl.when(table_ref[part * LINES + way, slot * LOAD + n] == m)
                def _():
                    pltpu.make_async_copy(view, held.at[way, n], sems.at[0, way, n]).start()

    for way in range(2):
        for n in range(LOAD):
            pltpu.make_async_copy(views[way][0], held.at[way, n], sems.at[0, way, n]).wait()
            pltpu.make_async_copy(held.at[way, n], outs[way].at[n], sems.at[1, way, n]).start()
    for way in range(2):
        for n in range(LOAD):
            pltpu.make_async_copy(held.at[way, n], outs[way].at[n], sems.at[1, way, n]).wait()


def choose(slot, part, table, own, ups, downs):
    up_from, down_from = own + ups, own + downs
    anywhere = pl.BlockSpec(memory_space=pl.ANY)
    shape = jax.ShapeDtypeStruct((LOAD,) + own[0].shape, own[0].dtype)
    return pl.pallas_call(
        functools.partial(choose_kernel, slot, part, len(up_from), len(down_from)),
        in_specs=[pl.BlockSpec(memory_space=pltpu.SMEM)] + [anywhere] * (len(up_from) + len(down_from)),
        out_specs=[anywhere, anywhere],
        out_shape=[shape, shape],
        scratch_shapes=[
            pltpu.VMEM((2, LOAD) + own[0].shape, own[0].dtype),
            pltpu.SemaphoreType.DMA((2, 2, LOAD)),
        ],
        cost_estimate=pl.CostEstimate(flops=0, bytes_accessed=4 * LOAD * own[0].size * 2, transcendentals=0),
        name="choose_packet",
    )(table, *up_from, *down_from)


def on_device(volume, measured, path_weights, fractions, bases):
    slices, depth, cols = volume.shape
    local, rows = measured.shape[:2]
    nslab = lax.axis_size("slab")
    device = lax.axis_index("slab")
    angles = local * nslab
    first = device * slices
    classes = rows // slices
    planes = nslab // classes
    ups_of = lambda step: [(i, i + step) for i in range(nslab - step)]
    downs_of = lambda step: [(i + step, i) for i in range(nslab - step)]

    routed = local == 1 and classes == ROUTED_CLASSES and slices == LANES and rows & (rows - 1) == 0 and angles <= LANES
    if not routed:
        left = lax.ppermute(volume[slices - 1 :], "slab", ups_of(1))
        right = lax.ppermute(volume[:1], "slab", downs_of(1))
        share = lax.dynamic_slice_in_dim(jnp.pad(fractions, ((0, 0), (1, 1))), first, slices + 2, 1)
        tables = make_tables(share, first, rows, path_weights, bases, slices)
        my_bases = lax.dynamic_slice_in_dim(bases, device * local, local, 0)
        turned = jax.vmap(lambda m, b: jnp.roll(m, b - 1, axis=0))(measured, my_bases)
        by_class = turned.reshape(local, classes, slices, cols).transpose(1, 0, 2, 3)
        outgoing = jnp.tile(by_class, (planes, 1, 1, 1)).reshape(angles, slices, cols)
        seen = lax.all_to_all(outgoing, "slab", split_axis=0, concat_axis=0, tiled=True)
        ends = jnp.roll(by_class[:, :, slices - 1], 1, axis=0)
        ends = jnp.tile(ends, (planes, 1, 1)).reshape(angles, cols // LANES, LANES)
        edge = lax.all_to_all(ends, "slab", split_axis=0, concat_axis=0, tiled=True).reshape(angles, cols)
        return update(volume, left, right, edge, tables, [seen], jnp.zeros((8, LANES), jnp.int32), None, 0, 1, True)[0]

    number = device.astype(jnp.int32)[None]
    *runs, ends = turn(number, bases, measured[0], classes)
    row_of_bases = jnp.pad(bases, (0, LANES - angles), constant_values=1)[None]
    runs, row_of_bases = lax.optimization_barrier((runs, row_of_bases))

    def share_out(part):
        mine = [runs[d * PARTS + part] for d in range(classes)]
        return mine[:1] + [
            lax.ppermute(mine[d], "slab", [(i, i ^ d) for i in range(nslab)]) for d in range(1, classes)
        ]

    own = [share_out(0)]

    most = -(-classes * (planes - 1) // LOAD) + planes - 2
    table = pl.pallas_call(
        functools.partial(plan_kernel, most, planes, classes, angles, slices // PARTS, rows),
        in_specs=[pl.BlockSpec(memory_space=pltpu.SMEM), pl.BlockSpec(memory_space=pltpu.VMEM)],
        out_shape=jax.ShapeDtypeStruct((16, LANES), jnp.int32),
        name="plan_slots",
    )(number, row_of_bases)
    table, ends, low, high = lax.optimization_barrier((table, ends, volume[slices - 1 :], volume[:1]))
    left = lax.ppermute(low, "slab", ups_of(1))
    right = lax.ppermute(high, "slab", downs_of(1))
    ends = jnp.tile(ends.astype(jnp.bfloat16)[None], (planes, 1, 1)).reshape(angles, cols // LANES, LANES)
    edge = lax.all_to_all(ends, "slab", split_axis=0, concat_axis=0, tiled=True).reshape(angles, cols)
    runs, own, table, edge, left, right = lax.optimization_barrier((runs, own, table, edge, left, right))
    own += [share_out(part) for part in range(1, PARTS)]
    slots = table[PARTS * LINES, 0]

    ups, downs = [[] for _ in range(PARTS)], [[] for _ in range(PARTS)]

    def run_slot(slot, part, ups, downs, table, beside=()):
        go_up, go_down = choose(slot, part, table, own[part], ups[part], downs[part])
        if beside:
            go_up, go_down, beside = lax.optimization_barrier((go_up, go_down, beside))
        ups[part].append(lax.ppermute(go_up, "slab", ups_of(classes)))
        downs[part].append(lax.ppermute(go_down, "slab", downs_of(classes)))
        return beside

    run_slot(0, 0, ups, downs, table)
    (late,) = run_slot(0, 1, ups, downs, table, (row_of_bases,))
    tables = [device_tables(number, late, fractions, path_weights, rows, 0)]
    table, tables = lax.optimization_barrier((table, tables))
    run_slot(1, 0, ups, downs, table)
    (late,) = run_slot(1, 1, ups, downs, table, (late,))
    tables.append(device_tables(number, late, fractions, path_weights, rows, 1))
    tables = lax.optimization_barrier(tables)

    def finish(end):
        def branch(ups, downs):
            ups, downs = [list(u) for u in ups], [list(d) for d in downs]
            for slot in range(STEADY, end):
                for part in range(PARTS):
                    run_slot(slot, part, ups, downs, table)
            out, carry = None, edge
            for part in range(PARTS):
                packets = own[part] + ups[part] + downs[part]
                out, carry = update(volume, left, right, carry, tables[part], packets, table, out, part, PARTS, False)
            return out

        return branch

    ends_at = [STEADY + 1, STEADY + 2, most]
    which = jnp.sum(jnp.array([slots > e for e in ends_at[:-1]]).astype(jnp.int32))
    return lax.switch(which, [finish(e) for e in ends_at], ups, downs)


def solution(mesh):
    placed = (P(("groups", "slab"), None, None), P(("groups", "slab"), None, None), P(), P(), P())
    return jax.shard_map(
        on_device,
        mesh=mesh,
        in_specs=placed,
        out_specs=P(("groups", "slab"), None, None),
        check_vma=False,
    )
```

```python
import functools

import jax
import jax.numpy as jnp
from jax import lax
from jax.experimental import pallas as pl
from jax.experimental.pallas import tpu as pltpu
from jax.sharding import PartitionSpec as P

RELAX = 1.0
BLOCK = 16
HALF = 8
LANES = 128
WIDE = 256
PIECES = 4
PARTS = 2
ROUTED_CLASSES = 4
LOAD = 2
STEADY = 2
CODE = 256
LINES = 5
VMEM_LIMIT = 56 * 2**20


def dot(a, b):
    return jnp.dot(a, b, preferred_element_type=jnp.float32)


def widen(coef):
    return jnp.concatenate([coef] * (WIDE // LANES), axis=1)


def spread_out(own, arrived):
    views = list(enumerate(own))
    return views + [(s * LOAD + n, p.at[n]) for s, p in enumerate(arrived) for n in range(p.shape[0])]


def update_kernel(
    dense, part, table_ref, lower_ref, upper_ref, next_ref, left_ref, right_ref, edge_ref, coef_ref, edge_coef_ref,
    image_w_ref, weight_ref, spread_ref, carry_w_ref, *rest,
):
    out_ref, carry_ref, seen_ref, result_ref, sems, out_sems = rest[-6:]
    packets = rest[:-7]
    block = pl.program_id(0)
    blocks = pl.num_programs(0)
    depth, width = lower_ref.shape[1:]
    angles = weight_ref.shape[0]
    first = part * blocks * BLOCK

    def fetch(at_block, act):
        slot = at_block % 2
        rows = pl.ds(pl.multiple_of(at_block * BLOCK, BLOCK), BLOCK)
        if dense:
            act(pltpu.make_async_copy(packets[0].at[:, rows], seen_ref.at[slot], sems.at[slot, 0]))
            return
        middle = (len(packets) - ROUTED_CLASSES) // 2 + ROUTED_CLASSES
        views = [(4, *v) for v in spread_out(packets[:ROUTED_CLASSES], [])]
        views += [(2, *v) for v in spread_out([], packets[ROUTED_CLASSES:middle])]
        views += [(3, *v) for v in spread_out([], packets[middle:])]
        for n, (line, spot, view) in enumerate(views):
            name = table_ref[part * LINES + line, spot]

            @pl.when(name >= 0)
            def _():
                act(pltpu.make_async_copy(view.at[rows], seen_ref.at[slot, name], sems.at[slot, n]))

    def deliver(at_block, act):
        slot = at_block % 2
        size = BLOCK // PIECES
        for n in range(PIECES):
            source = result_ref.at[slot, pl.ds(n * size, size)]
            act(pltpu.make_async_copy(source, out_ref.at[pl.ds(first + at_block * BLOCK + n * size, size)], out_sems.at[slot, n]))

    @pl.when(block == 0)
    def _():
        seen_ref[...] = jnp.zeros_like(seen_ref)
        fetch(block, lambda copy: copy.start())

    @pl.when(block + 1 < blocks)
    def _():
        fetch(block + 1, lambda copy: copy.start())

    @pl.when(block == 0)
    def _():
        if not dense:
            carry_ref[...] = jnp.zeros_like(carry_ref)
            return
        for chunk in range(width // WIDE):
            at = pl.ds(chunk * WIDE, WIDE)
            mine = dot(weight_ref[...], lower_ref[0, :, at])
            before = dot(weight_ref[...], left_ref[0, :, at])
            carry_ref[:, at] = (
                edge_ref[:, at].astype(jnp.float32) * widen(edge_coef_ref[2])
                - mine * widen(edge_coef_ref[0])
                - before * widen(edge_coef_ref[1])
            ).astype(jnp.bfloat16)

    @pl.when(block >= 2)
    def _():
        deliver(block - 2, lambda copy: copy.wait())

    fetch(block, lambda copy: copy.wait())
    slot = block % 2
    final = (block == blocks - 1) & (part == PARTS - 1 or dense)

    def columns(chunk):
        if dense:
            return pl.ds(pl.multiple_of(chunk * WIDE, WIDE), WIDE)
        return slice(chunk * WIDE, (chunk + 1) * WIDE)

    def image(chunk):
        at = columns(chunk)
        images = [dot(image_w_ref[...], r[:, :, at].reshape(HALF * depth, WIDE)) for r in (lower_ref, upper_ref)]
        after = dot(weight_ref[...], jnp.where(final, right_ref[0, :, at], next_ref[0, :, at]))
        return images, after

    def residual(chunk, images, after):
        at = columns(chunk)
        seen = seen_ref[slot, :, :, at].astype(jnp.float32)
        ahead = [pltpu.roll(x.reshape(angles, HALF, WIDE), HALF - 1, 1) for x in images]
        ahead.append(jnp.broadcast_to(after.reshape(angles, 1, WIDE), (angles, HALF, WIDE)))
        tail = lax.broadcasted_iota(jnp.int32, (angles, HALF, WIDE), 1) == HALF - 1
        parts = []
        for half in range(2):
            now = jnp.where(tail, ahead[half + 1], ahead[half]).reshape(angles * HALF, WIDE)
            got = seen[:, half * HALF : (half + 1) * HALF].reshape(angles * HALF, WIDE)
            coef = [widen(coef_ref[0, half, n]) for n in range(3)]
            resid = got * coef[2] - now * coef[0] - images[half] * coef[1]
            parts.append(resid.reshape(angles, HALF, WIDE))
        resid = jnp.concatenate(parts, axis=1)
        return resid.astype(jnp.bfloat16).reshape(angles * BLOCK, WIDE), resid[:, BLOCK - 1].astype(jnp.bfloat16)

    def result(chunk, resid, last):
        at = columns(chunk)
        spread = dot(spread_ref[0], resid).reshape(BLOCK, depth, WIDE)
        extra = dot(carry_w_ref[0], carry_ref[:, at])
        carry_ref[:, at] = last
        for half, r in enumerate((lower_ref, upper_ref)):
            volume = r[:, :, at].astype(jnp.float32)
            here = half * HALF
            if half == 0:
                result_ref[slot, 0, :, at] = volume[0] + spread[0] + extra
                result_ref[slot, 1:HALF, :, at] = volume[1:] + spread[1:HALF]
            else:
                result_ref[slot, here : here + HALF, :, at] = volume + spread[here : here + HALF]

    chunks = width // WIDE
    if dense:
        pl.loop(0, chunks)(lambda chunk: result(chunk, *residual(chunk, *image(chunk))))
    else:
        images, resids = {}, {}
        for n in range(chunks + 2):
            if n < chunks:
                images[n] = image(n)
            if 1 <= n <= chunks:
                resids[n - 1] = residual(n - 1, *images.pop(n - 1))
            if n >= 2:
                result(n - 2, *resids.pop(n - 2))
    deliver(block, lambda copy: copy.start())

    @pl.when(block == blocks - 1)
    def _():
        @pl.when(block >= 1)
        def _():
            deliver(block - 1, lambda copy: copy.wait())

        deliver(block, lambda copy: copy.wait())


def update(volume, left, right, edge, tables, packets, table, before, part, parts, dense):
    slices, depth, cols = volume.shape
    angles = edge.shape[0]
    blocks = slices // BLOCK // parts
    off = part * blocks
    by_block = lambda x: pl.BlockSpec((1,) + x.shape[1:], lambda b, i: (b,) + (0,) * (x.ndim - 1))
    whole = lambda x: pl.BlockSpec(x.shape, lambda b, i: (0,) * x.ndim)
    anywhere = pl.BlockSpec(memory_space=pl.ANY)
    coef, edge_coef, image_w, weights, spread_w, carry_w = tables
    aliases = {} if before is None else {13 + len(packets): 0}
    copies = LOAD * len(packets)
    one = (1, depth, cols)
    return pl.pallas_call(
        functools.partial(update_kernel, dense, part),
        grid_spec=pltpu.PrefetchScalarGridSpec(
            num_scalar_prefetch=1,
            grid=(blocks,),
            in_specs=[
                pl.BlockSpec((HALF, depth, cols), lambda b, i: (2 * (b + off), 0, 0)),
                pl.BlockSpec((HALF, depth, cols), lambda b, i: (2 * (b + off) + 1, 0, 0)),
                pl.BlockSpec(one, lambda b, i: (jnp.minimum((b + off + 1) * BLOCK, slices - 1), 0, 0)),
                pl.BlockSpec(one, lambda b, i: (0, 0, 0)),
                pl.BlockSpec(one, lambda b, i: (0, 0, 0)),
                whole(edge), by_block(coef), whole(edge_coef), whole(image_w), whole(weights),
                by_block(spread_w), by_block(carry_w),
            ]
            + [anywhere] * (len(packets) + 1),
            out_specs=[anywhere, whole(edge)],
            scratch_shapes=[
                pltpu.VMEM((2, angles, BLOCK, cols), jnp.bfloat16),
                pltpu.VMEM((2, BLOCK, depth, cols), jnp.float32),
                pltpu.SemaphoreType.DMA((2, copies)),
                pltpu.SemaphoreType.DMA((2, PIECES)),
            ],
        ),
        out_shape=[jax.ShapeDtypeStruct(volume.shape, jnp.float32), jax.ShapeDtypeStruct(edge.shape, edge.dtype)],
        input_output_aliases=aliases,
        compiler_params=pltpu.CompilerParams(dimension_semantics=("arbitrary",), vmem_limit_bytes=VMEM_LIMIT),
        cost_estimate=pl.CostEstimate(
            flops=4 * slices * depth * cols * angles // parts, bytes_accessed=volume.size * 7 // parts, transcendentals=0
        ),
        name="slab_update",
    )(
        table, volume, volume, volume, left, right, edge, coef, edge_coef, image_w, weights, spread_w, carry_w,
        *packets, edge if before is None else before,
    )


def mend_kernel(weight_ref, first_ref, second_ref, before_ref, out_ref):
    resid = jnp.where(pl.program_id(0) == 0, first_ref[...], second_ref[...])
    out_ref[0] = before_ref[0] + dot(weight_ref[0], resid)


def mend(out, weights, first, second):
    slices, depth, cols = out.shape
    parts = weights.shape[0]
    whole = pl.BlockSpec(first.shape, lambda b: (0, 0))
    slab = pl.BlockSpec((1, depth, cols), lambda b: (b * (slices // parts), 0, 0))
    return pl.pallas_call(
        mend_kernel,
        grid=(parts,),
        in_specs=[pl.BlockSpec((1,) + weights.shape[1:], lambda b: (b, 0, 0)), whole, whole, slab],
        out_specs=slab,
        out_shape=jax.ShapeDtypeStruct(out.shape, out.dtype),
        input_output_aliases={3: 0},
        name="mend_slices",
    )(weights, first, second, out)


def fill_weights(wide_w, turned_w, pick_next, pick_now, pick_carry, spread_ref, carry_w_ref):
    depth, columns = wide_w.shape
    place = lax.broadcasted_iota(jnp.int32, (depth, columns), 1) % BLOCK
    from_next = wide_w * pick_next
    from_now = wide_w * pick_now
    from_carry = turned_w * pick_carry
    for z in range(BLOCK):
        row = jnp.where(place == z, from_next, jnp.where(place == z - 1, from_now, 0.0))
        total = jnp.sum(row, axis=1, keepdims=True)
        if z == 0:
            total = total + jnp.sum(from_carry, axis=1, keepdims=True)
            carry_w_ref[0] = (from_carry * (RELAX / total)).astype(jnp.bfloat16)
        spread_ref[0, z * depth : (z + 1) * depth] = (row * (RELAX / total)).astype(jnp.bfloat16)


def weights_kernel(wide_w_ref, turned_w_ref, pick_ref, pick_carry_ref, spread_ref, carry_w_ref):
    picks = pick_ref[0, 0:1], pick_ref[0, 1:2], pick_carry_ref[0]
    fill_weights(wide_w_ref[...], turned_w_ref[...], *picks, spread_ref, carry_w_ref)


def make_weights(wide_w, turned_w, pick, pick_carry):
    blocks = pick.shape[0]
    depth, angles = turned_w.shape
    by_block = lambda shape: pl.BlockSpec((1,) + shape, lambda b: (b,) + (0,) * len(shape))
    whole = lambda x: pl.BlockSpec(x.shape, lambda b: (0,) * x.ndim)
    spread = (BLOCK * depth, angles * BLOCK)
    carry = (depth, angles)
    return pl.pallas_call(
        weights_kernel,
        grid=(blocks,),
        in_specs=[whole(wide_w), whole(turned_w), by_block(pick.shape[1:]), by_block(pick_carry.shape[1:])],
        out_specs=[by_block(spread), by_block(carry)],
        out_shape=[
            jax.ShapeDtypeStruct((blocks,) + spread, jnp.bfloat16),
            jax.ShapeDtypeStruct((blocks,) + carry, jnp.bfloat16),
        ],
        name="spread_weights",
    )(wide_w, turned_w, pick, pick_carry)


def make_tables(share, first, rows, path_weights, bases, slices):
    angles, depth = path_weights.shape
    blocks = slices // BLOCK
    weights = path_weights.astype(jnp.float32)
    ray_total = jnp.sum(weights, axis=1)[:, None]
    norm = 1.0 / (ray_total * ((1.0 - share[:, 1:]) + share[:, :-1]))
    coefs = jnp.stack([(1.0 - share[:, 1:]) * norm, share[:, :-1] * norm, norm])
    coef = coefs[:, :, 1:].reshape(3, angles, blocks, BLOCK // HALF, HALF).transpose(2, 3, 0, 1, 4)
    coef = coef.reshape(blocks, BLOCK // HALF, 3, angles * HALF, 1)
    coef = jnp.broadcast_to(coef, coef.shape[:4] + (LANES,))
    edge_coef = jnp.broadcast_to(coefs[:, :, :1], (3, angles, LANES))
    share_own = share[:, 1:-1]
    row_now = (first - bases)[:, None] + jnp.arange(slices, dtype=jnp.int32)[None, :]
    w_now = jnp.where((row_now >= 0) & (row_now < rows), 1.0 - share_own, 0.0)
    w_next = jnp.where((row_now + 1 >= 0) & (row_now + 1 < rows), share_own, 0.0)
    pick = jnp.stack([w_next, jnp.pad(w_now[:, 1:], ((0, 0), (0, 1)))]).reshape(2, angles, blocks, BLOCK)
    pick = pick.transpose(2, 0, 1, 3).reshape(blocks, 2, angles * BLOCK)
    pick_carry = w_now[:, ::BLOCK].T[:, None, :]
    eye = jnp.eye(HALF, dtype=jnp.float32)
    image_w = jnp.einsum("ad,yz->ayzd", weights, eye).reshape(angles * HALF, HALF * depth).astype(jnp.bfloat16)
    wide_w = jnp.repeat(weights.T, BLOCK, axis=1)
    return coef, edge_coef, image_w, path_weights, *make_weights(wide_w, weights.T, pick, pick_carry)


def column_of(line, tall):
    sub = lax.broadcasted_iota(jnp.int32, (tall, LANES), 0)
    lane = lax.broadcasted_iota(jnp.int32, (tall, LANES), 1)
    return jnp.max(jnp.where(sub == lane, line, -1), axis=1, keepdims=True)


def tables_kernel(
    rows, off, device_ref, bases_ref, before_ref, own_ref, after_ref, weight_ref,
    coef_ref, edge_coef_ref, image_w_ref, spread_ref, carry_w_ref, wide_ref, turned_ref,
):
    block = pl.program_id(0) + off
    angles, depth = weight_ref.shape
    first = device_ref[0] * LANES
    shape = (angles, LANES)
    lane = lax.broadcasted_iota(jnp.int32, shape, 1)
    sub = lax.broadcasted_iota(jnp.int32, shape, 0)
    weights = weight_ref[...].astype(jnp.float32)
    ray_total = jnp.sum(weights, axis=1, keepdims=True)
    own = own_ref[...]
    ahead = jnp.where(lane == LANES - 1, pltpu.roll(after_ref[...], LANES - 1, 1), pltpu.roll(own, LANES - 1, 1))
    norm = 1.0 / (ray_total * ((1.0 - ahead) + own))
    coefs = ((1.0 - ahead) * norm, own * norm, norm)
    spots = lax.broadcasted_iota(jnp.int32, (angles, HALF, LANES), 2) - lax.broadcasted_iota(jnp.int32, (angles, HALF, LANES), 1)
    for half in range(BLOCK // HALF):
        here = spots == block * BLOCK + half * HALF
        for n, coef in enumerate(coefs):
            tall = jnp.broadcast_to(coef.reshape(angles, 1, LANES), (angles, HALF, LANES))
            tall = jnp.sum(jnp.where(here, tall, 0.0), axis=2, keepdims=True)
            coef_ref[0, half, n] = jnp.broadcast_to(tall, (angles, HALF, LANES)).reshape(angles * HALF, LANES)

    @pl.when(block == off)
    def _():
        edge_own = jnp.sum(jnp.where(lane == 0, own, 0.0), axis=1, keepdims=True)
        edge_before = jnp.sum(jnp.where(lane == LANES - 1, before_ref[...], 0.0), axis=1, keepdims=True)
        edge_norm = 1.0 / (ray_total * ((1.0 - edge_own) + edge_before))
        for n, coef in enumerate(((1.0 - edge_own) * edge_norm, edge_before * edge_norm, edge_norm)):
            edge_coef_ref[n] = jnp.broadcast_to(coef, shape)
        across = (HALF * depth)
        repeat = lax.broadcasted_iota(jnp.int32, (depth, across), 1) % depth
        repeat = jnp.where(repeat == lax.broadcasted_iota(jnp.int32, (depth, across), 0), 1.0, 0.0)
        wide = dot(weight_ref[...], repeat.astype(jnp.bfloat16)).astype(jnp.bfloat16)
        down = angles * HALF
        expand = lax.broadcasted_iota(jnp.int32, (down, angles), 0) // HALF
        expand = jnp.where(expand == lax.broadcasted_iota(jnp.int32, (down, angles), 1), 1.0, 0.0)
        wide = dot(expand.astype(jnp.bfloat16), wide)
        at = lax.broadcasted_iota(jnp.int32, (down, across), 0) % HALF
        same = lax.broadcasted_iota(jnp.int32, (down, across), 1) // depth == at
        image_w_ref[...] = jnp.where(same, wide, 0.0).astype(jnp.bfloat16)

    row_now = first + lane - column_of(bases_ref[...], angles)
    w_now = jnp.where((row_now >= 0) & (row_now < rows), 1.0 - own, 0.0)
    w_next = jnp.where((row_now + 1 >= 0) & (row_now + 1 < rows), own, 0.0)
    columns = angles * BLOCK
    place = lax.broadcasted_iota(jnp.int32, (LANES, columns), 1) % BLOCK
    z = lax.broadcasted_iota(jnp.int32, (LANES, columns), 0) - block * BLOCK
    mine = lax.broadcasted_iota(jnp.int32, (angles, columns), 1) // BLOCK
    mine = mine == lax.broadcasted_iota(jnp.int32, (angles, columns), 0)

    def gather(values, wanted):
        picked = jnp.dot(
            values, jnp.where(wanted, 1.0, 0.0), precision=lax.Precision.HIGHEST, preferred_element_type=jnp.float32
        )
        return jnp.sum(jnp.where(mine, picked, 0.0), axis=0, keepdims=True)

    pick_next = gather(w_next, z == place)
    pick_now = gather(w_now, (z == place + 1) & (place < BLOCK - 1))
    carry = jnp.sum(jnp.where(lane == block * BLOCK, w_now, 0.0), axis=1, keepdims=True)
    square = lax.broadcasted_iota(jnp.int32, (angles, angles), 0) == lax.broadcasted_iota(jnp.int32, (angles, angles), 1)
    pick_carry = jnp.sum(jnp.where(square, carry, 0.0), axis=0, keepdims=True)
    turned = lambda other: lax.dot_general(
        weights, other, (((0,), (0,)), ((), ())), precision=lax.Precision.HIGHEST, preferred_element_type=jnp.float32
    )

    @pl.when(block == off)
    def _():
        wide_ref[...] = turned(jnp.where(mine, 1.0, 0.0))
        turned_ref[...] = turned(jnp.where(square, 1.0, 0.0))

    fill_weights(wide_ref[...], turned_ref[...], pick_next, pick_now, pick_carry, spread_ref, carry_w_ref)


def device_tables(device, row_of_bases, fractions, path_weights, rows, part):
    angles, depth = path_weights.shape
    blocks = LANES // BLOCK // PARTS
    last = fractions.shape[1] // LANES - 1
    column = lambda by: pl.BlockSpec((angles, LANES), lambda b, d: (0, jnp.clip(d[0] + by, 0, last)))
    whole = lambda shape: pl.BlockSpec(shape, lambda b, d: (0,) * len(shape))
    by_block = lambda shape: pl.BlockSpec((1,) + shape, lambda b, d: (b,) + (0,) * len(shape))
    coef = (BLOCK // HALF, 3, angles * HALF, LANES)
    edge_coef = (3, angles, LANES)
    image_w = (angles * HALF, HALF * depth)
    spread = (BLOCK * depth, angles * BLOCK)
    carry = (depth, angles)
    made = pl.pallas_call(
        functools.partial(tables_kernel, rows, part * blocks),
        grid_spec=pltpu.PrefetchScalarGridSpec(
            num_scalar_prefetch=1,
            grid=(blocks,),
            in_specs=[whole((1, LANES)), column(-1), column(0), column(1), whole(path_weights.shape)],
            out_specs=[by_block(coef), whole(edge_coef), whole(image_w), by_block(spread), by_block(carry)],
            scratch_shapes=[
                pltpu.VMEM((depth, angles * BLOCK), jnp.float32),
                pltpu.VMEM((depth, angles), jnp.float32),
            ],
        ),
        out_shape=[
            jax.ShapeDtypeStruct((blocks,) + coef, jnp.float32),
            jax.ShapeDtypeStruct(edge_coef, jnp.float32),
            jax.ShapeDtypeStruct(image_w, jnp.bfloat16),
            jax.ShapeDtypeStruct((blocks,) + spread, jnp.bfloat16),
            jax.ShapeDtypeStruct((blocks,) + carry, jnp.bfloat16),
        ],
        name="make_tables",
    )(device, row_of_bases, fractions, fractions, fractions, path_weights)
    return made[0], made[1], made[2], path_weights, made[3], made[4]


def turn_kernel(classes, count, part, device_ref, bases_ref, seen_ref, *refs):
    outs, twice_ref, sems = refs[:-2], refs[-2], refs[-1]
    rows, cols = seen_ref.shape
    more = twice_ref.shape[0] - rows
    copies = [
        pltpu.make_async_copy(seen_ref, twice_ref.at[pl.ds(0, rows)], sems.at[0]),
        pltpu.make_async_copy(seen_ref.at[pl.ds(0, more)], twice_ref.at[pl.ds(rows, more)], sems.at[1]),
    ]
    for copy in copies:
        copy.start()
    for copy in copies:
        copy.wait()
    device = device_ref[0]
    base = bases_ref[device]
    my_class = device & (classes - 1)
    slices = count * PARTS

    def window(place, size, at):
        start = (place - base + 1 + rows) & (rows - 1)
        begin = pl.multiple_of(start & ~(BLOCK - 1), BLOCK)
        tall = size + BLOCK
        wide = twice_ref[pl.ds(begin, tall), at].astype(jnp.float32)
        return pltpu.roll(wide, (tall - (start - begin)) % tall, 0)

    for d in range(classes):
        place = (my_class ^ d) * slices + part * count

        @pl.loop(0, cols // WIDE)
        def _(chunk):
            at = pl.ds(pl.multiple_of(chunk * WIDE, WIDE), WIDE)
            outs[d][:, at] = window(place, count, at)[:count].astype(jnp.bfloat16)


def turn(device, bases, seen, classes, part):
    rows, cols = seen.shape
    count = rows // classes // PARTS
    return pl.pallas_call(
        functools.partial(turn_kernel, classes, count, part),
        in_specs=[
            pl.BlockSpec(memory_space=pltpu.SMEM),
            pl.BlockSpec(memory_space=pltpu.SMEM),
            pl.BlockSpec(memory_space=pl.ANY),
        ],
        out_specs=[pl.BlockSpec(memory_space=pltpu.VMEM)] * classes,
        out_shape=[jax.ShapeDtypeStruct((count, cols), seen.dtype)] * classes,
        scratch_shapes=[pltpu.VMEM((rows + count + BLOCK, cols), seen.dtype), pltpu.SemaphoreType.DMA((2,))],
        compiler_params=pltpu.CompilerParams(vmem_limit_bytes=32 * 2**20),
        name="turn_rows",
    )(device, bases, seen)


def plan_kernel(slots, planes, classes, angles, count, rows, device_ref, bases_ref, table_ref):
    shape = (2 * PARTS * classes, LANES)
    lane = lax.broadcasted_iota(jnp.int32, shape, 1)
    row = lax.broadcasted_iota(jnp.int32, shape, 0)
    class_shift = classes.bit_length() - 1
    base = jnp.broadcast_to(bases_ref[...], shape) - 1
    low_plane = base >> (rows.bit_length() - 1)
    turned = base & (rows - 1)

    def reach(which):
        lowest = low_plane + jnp.where(which * count + count - 1 < turned, 1, 0)
        highest = low_plane + jnp.where(which * count < turned, 1, 0)
        return lowest, highest

    lowest, highest = reach(row >> 1)
    upward = (row & 1) == 0
    source = lane >> class_shift
    at = jnp.where(upward, source, planes - 1 - source)
    to = jnp.where(lane < angles, jnp.where(upward, highest, planes - 1 - lowest), -1)
    key = to * CODE + (CODE - 1 - lane)
    sent = [jnp.full(shape, -1, jnp.int32) for _ in range(planes - 1)]
    for slot in range(slots):
        begin = at
        for link in range(planes - 1):
            ready = (begin == link) & (to > link)
            for n in range(LOAD):
                best = jnp.max(jnp.where(ready, key, -1), axis=1, keepdims=True)
                taken = ready & (key == best)
                at = jnp.where(taken, link + 1, at)
                ready = ready & (key != best)
                which = jnp.where(best >= 0, CODE - 1 - (best & (CODE - 1)), -1)
                sent[link] = jnp.where(lane == slot * LOAD + n, which, sent[link])

    me = device_ref[0]
    my_class = me & (classes - 1)
    plane = me >> class_shift
    none = jnp.full(shape, -1, jnp.int32)
    used = none
    for link in range(planes - 1):
        used = jnp.maximum(used, sent[link])
    used = jnp.max(used, axis=0, keepdims=True)
    head = lane[:1]
    total = jnp.max(jnp.where(used >= 0, head + 1, 0), axis=1, keepdims=True)

    tall = -(-max(slots * LOAD, angles) // 8) * 8
    sub = lax.broadcasted_iota(jnp.int32, (tall, LANES), 0)
    held = jnp.where(head < classes, plane * classes + (head ^ my_class), -1)
    for part in range(PARTS):
        low_here, high_here = reach(my_class * PARTS + part)
        wanted = (plane >= low_here) & (plane <= high_here) & (lane < angles)
        wanted = column_of(jnp.where(wanted, 1, 0)[:1], tall) > 0
        keep = lambda ids: jnp.max(jnp.where((sub == ids) & wanted, ids, -1), axis=0, keepdims=True)
        for way, spot in ((0, plane), (1, planes - 1 - plane)):
            sends, gets = none, none
            for link in range(planes - 1):
                sends = jnp.where(spot == link, sent[link], sends)
                gets = jnp.where(spot == link + 1, sent[link], gets)
            mine = row == 2 * (my_class * PARTS + part) + way
            sends = jnp.max(jnp.where(mine, sends, -1), axis=0, keepdims=True)
            gets = jnp.max(jnp.where(mine, gets, -1), axis=0, keepdims=True)
            arrived = jnp.max(jnp.where((column_of(gets, tall) == sends) & (sends >= 0), sub, 0), axis=0, keepdims=True)
            own = (sends >> class_shift) == plane
            index = jnp.where(own, (sends & (classes - 1)) ^ my_class, classes + arrived)
            line = part * LINES + way
            table_ref[line : line + 1] = jnp.where(sends >= 0, index, 0)
            table_ref[line + 2 : line + 3] = keep(gets)
        line = part * LINES + 4
        table_ref[line : line + 1] = keep(held)
    table_ref[PARTS * LINES : PARTS * LINES + 1] = jnp.broadcast_to(total, head.shape)


def choose_kernel(slot, part, load, own, ups, table_ref, *refs):
    sources, (*outs, held, sems) = refs[: own + 2 * ups], refs[own + 2 * ups :]
    arrived = sources[own : own + ups], sources[own + ups :]
    views = [spread_out(sources[:own], []) + [(own + n, v) for n, v in spread_out([], side)] for side in arrived]
    spots = [(way, n) for way in range(2) for n in range(load)]
    for way, n in spots:
        for m, view in views[way]:

            @pl.when(table_ref[part * LINES + way, slot * LOAD + n] == m)
            def _():
                pltpu.make_async_copy(view, held.at[way, n], sems.at[0, way, n]).start()

    for way, n in spots:
        pltpu.make_async_copy(sources[0], held.at[way, n], sems.at[0, way, n]).wait()
        pltpu.make_async_copy(held.at[way, n], outs[way].at[n], sems.at[1, way, n]).start()
    for way, n in spots:
        pltpu.make_async_copy(held.at[way, n], outs[way].at[n], sems.at[1, way, n]).wait()


def choose(slot, part, load, table, own, ups, downs):
    anywhere = pl.BlockSpec(memory_space=pl.ANY)
    shape = jax.ShapeDtypeStruct((load,) + own[0].shape, own[0].dtype)
    return pl.pallas_call(
        functools.partial(choose_kernel, slot, part, load, len(own), len(ups)),
        in_specs=[pl.BlockSpec(memory_space=pltpu.SMEM)] + [anywhere] * (len(own) + 2 * len(ups)),
        out_specs=[anywhere, anywhere],
        out_shape=[shape, shape],
        scratch_shapes=[
            pltpu.VMEM((2, load) + own[0].shape, own[0].dtype),
            pltpu.SemaphoreType.DMA((2, 2, load)),
        ],
        cost_estimate=pl.CostEstimate(flops=0, bytes_accessed=4 * load * own[0].size * 2, transcendentals=0),
        name="choose_packet",
    )(table, *own, *ups, *downs)


def on_device(volume, measured, path_weights, fractions, bases):
    slices, depth, cols = volume.shape
    local, rows = measured.shape[:2]
    nslab = lax.axis_size("slab")
    device = lax.axis_index("slab")
    angles = local * nslab
    first = device * slices
    classes = rows // slices
    planes = nslab // classes
    ups_of = lambda step: [(i, i + step) for i in range(nslab - step)]
    downs_of = lambda step: [(i + step, i) for i in range(nslab - step)]

    routed = local == 1 and classes == ROUTED_CLASSES and slices == LANES and rows & (rows - 1) == 0 and angles <= LANES
    if not routed:
        left = lax.ppermute(volume[slices - 1 :], "slab", ups_of(1))
        right = lax.ppermute(volume[:1], "slab", downs_of(1))
        share = lax.dynamic_slice_in_dim(jnp.pad(fractions, ((0, 0), (1, 1))), first, slices + 2, 1)
        tables = make_tables(share, first, rows, path_weights, bases, slices)
        my_bases = lax.dynamic_slice_in_dim(bases, device * local, local, 0)
        turned = jax.vmap(lambda m, b: jnp.roll(m, b - 1, axis=0))(measured, my_bases)
        by_class = turned.reshape(local, classes, slices, cols).transpose(1, 0, 2, 3)
        outgoing = jnp.tile(by_class, (planes, 1, 1, 1)).reshape(angles, slices, cols)
        seen = lax.all_to_all(outgoing, "slab", split_axis=0, concat_axis=0, tiled=True)
        ends = jnp.roll(by_class[:, :, slices - 1], 1, axis=0)
        ends = jnp.tile(ends, (planes, 1, 1)).reshape(angles, cols // LANES, LANES)
        edge = lax.all_to_all(ends, "slab", split_axis=0, concat_axis=0, tiled=True).reshape(angles, cols)
        return update(volume, left, right, edge, tables, [seen], jnp.zeros((8, LANES), jnp.int32), None, 0, 1, True)[0]

    number = device.astype(jnp.int32)[None]
    upper, lower = PARTS - 1, 0
    exchange = lambda runs: [runs[0]] + [
        lax.ppermute(runs[d], "slab", [(i, i ^ d) for i in range(nslab)]) for d in range(1, classes)
    ]
    runs = turn(number, bases, measured[0], classes, upper)
    runs, late_bases, seen = lax.optimization_barrier((runs, bases, measured[0]))
    own = {upper: exchange(runs)}

    row_of_bases = jnp.pad(late_bases, (0, LANES - angles), constant_values=1)[None]
    most = -(-classes * (planes - 1) // LOAD) + planes - 2
    table = pl.pallas_call(
        functools.partial(plan_kernel, most, planes, classes, angles, slices // PARTS, rows),
        in_specs=[pl.BlockSpec(memory_space=pltpu.SMEM), pl.BlockSpec(memory_space=pltpu.VMEM)],
        out_shape=jax.ShapeDtypeStruct((16, LANES), jnp.int32),
        name="plan_slots",
    )(number, row_of_bases)
    runs = turn(number, late_bases, seen, classes, lower)
    tables = {upper: device_tables(number, row_of_bases, fractions, path_weights, rows, upper)}
    own, runs, table, tables = lax.optimization_barrier((own, runs, table, tables))
    own[lower] = exchange(runs)
    need = table[PARTS * LINES, 0]

    def run_slot(slot, part, load, ups, downs, table, beside=()):
        go_up, go_down = choose(slot, part, load, table, own[part], ups[part], downs[part])
        if beside:
            go_up, go_down, beside = lax.optimization_barrier((go_up, go_down, beside))
        ups[part].append(lax.ppermute(go_up, "slab", ups_of(classes)))
        downs[part].append(lax.ppermute(go_down, "slab", downs_of(classes)))
        return beside

    ups, downs = {upper: [], lower: []}, {upper: [], lower: []}
    run_slot(0, upper, LOAD, ups, downs, table)
    high, late = run_slot(0, lower, LOAD, ups, downs, table, (volume[:1], row_of_bases))
    right = lax.ppermute(high, "slab", downs_of(1))
    tables[lower] = device_tables(number, late, fractions, path_weights, rows, lower)
    mends = jnp.concatenate([tables[part][-1][:1] for part in range(PARTS)])
    table, tables, mends = lax.optimization_barrier((table, tables, mends))
    run_slot(1, upper, LOAD, ups, downs, table)
    run_slot(1, lower, LOAD, ups, downs, table)
    right, none = lax.optimization_barrier((right, jnp.zeros((angles, cols), volume.dtype)))

    def finish(end):
        def branch(ups, downs):
            ups, downs = [{part: list(x) for part, x in side.items()} for side in (ups, downs)]
            for slot in range(STEADY, -(-end // LOAD)):
                for part in (upper, lower):
                    run_slot(slot, part, min(LOAD, end - slot * LOAD), ups, downs, table)
            packets = {part: own[part] + ups[part] + downs[part] for part in (upper, lower)}
            args = (volume, right, right, none)
            out, last = update(*args, tables[upper], packets[upper], table, None, upper, PARTS, False)
            first = lax.ppermute(last, "slab", ups_of(1))
            out, second = update(*args, tables[lower], packets[lower], table, out, lower, PARTS, False)
            return mend(out, mends, first, second)

        return branch

    ends = [STEADY * LOAD + n for n in range(1, 5)] + [most * LOAD]
    which = jnp.sum(jnp.array([need > e for e in ends[:-1]]).astype(jnp.int32))
    return lax.switch(which, [finish(e) for e in ends], ups, downs)


def solution(mesh):
    placed = (P(("groups", "slab"), None, None), P(("groups", "slab"), None, None), P(), P(), P())
    return jax.shard_map(
        on_device,
        mesh=mesh,
        in_specs=placed,
        out_specs=P(("groups", "slab"), None, None),
        check_vma=False,
    )
```

```python
import functools

import jax
import jax.numpy as jnp
from jax import lax
from jax.experimental import pallas as pl
from jax.experimental.pallas import tpu as pltpu
from jax.sharding import PartitionSpec as P

RELAX = 1.0
BLOCK = 16
HALF = 8
LANES = 128
WIDE = 256
PIECES = 4
PARTS = 2
ROUTED_CLASSES = 4
LOAD = 2
CODE = 256
LINES = 5
VMEM_LIMIT = 56 * 2**20


def dot(a, b):
    return jnp.dot(a, b, preferred_element_type=jnp.float32)


def widen(coef):
    return jnp.concatenate([coef] * (WIDE // LANES), axis=1)


def spread_out(own, arrived):
    views = list(enumerate(own))
    return views + [(s * LOAD + n, p.at[n]) for s, p in enumerate(arrived) for n in range(p.shape[0])]


def update_kernel(
    dense, part, table_ref, lower_ref, upper_ref, next_ref, left_ref, right_ref, edge_ref, coef_ref, edge_coef_ref,
    image_w_ref, weight_ref, spread_ref, *rest,
):
    out_ref, carry_ref, seen_ref, result_ref, sems, out_sems = rest[-6:]
    packets = rest[:-7]
    block = pl.program_id(0)
    blocks = pl.num_programs(0)
    depth, width = lower_ref.shape[1:]
    angles = weight_ref.shape[0]
    first = part * blocks * BLOCK

    def fetch(at_block, act):
        slot = at_block % 2
        rows = pl.ds(pl.multiple_of(at_block * BLOCK, BLOCK), BLOCK)
        if dense:
            act(pltpu.make_async_copy(packets[0].at[:, rows], seen_ref.at[slot], sems.at[slot, 0]))
            return
        middle = (len(packets) - ROUTED_CLASSES) // 2 + ROUTED_CLASSES
        views = [(4, *v) for v in spread_out(packets[:ROUTED_CLASSES], [])]
        views += [(2, *v) for v in spread_out([], packets[ROUTED_CLASSES:middle])]
        views += [(3, *v) for v in spread_out([], packets[middle:])]
        for n, (line, spot, view) in enumerate(views):
            name = table_ref[part * LINES + line, spot]

            @pl.when(name >= 0)
            def _():
                act(pltpu.make_async_copy(view.at[rows], seen_ref.at[slot, name], sems.at[slot, n]))

    def deliver(at_block, act, pieces=range(PIECES)):
        slot = at_block % 2
        rows = pl.ds(first + at_block * BLOCK, BLOCK)
        for n in pieces:
            at = pl.ds(n * (width // PIECES), width // PIECES)
            act(pltpu.make_async_copy(result_ref.at[slot, :, :, at], out_ref.at[rows, :, at], out_sems.at[slot, n]))

    @pl.when(block == 0)
    def _():
        seen_ref[...] = jnp.zeros_like(seen_ref)
        fetch(block, lambda copy: copy.start())

    @pl.when(block + 1 < blocks)
    def _():
        fetch(block + 1, lambda copy: copy.start())

    @pl.when(block == 0)
    def _():
        if not dense:
            carry_ref[...] = jnp.zeros_like(carry_ref)
            return
        for chunk in range(width // WIDE):
            at = pl.ds(chunk * WIDE, WIDE)
            mine = dot(weight_ref[...], lower_ref[0, :, at])
            before = dot(weight_ref[...], left_ref[0, :, at])
            carry_ref[:, at] = (
                edge_ref[:, at].astype(jnp.float32) * widen(edge_coef_ref[2])
                - mine * widen(edge_coef_ref[0])
                - before * widen(edge_coef_ref[1])
            ).astype(jnp.bfloat16)

    @pl.when(block >= 2)
    def _():
        deliver(block - 2, lambda copy: copy.wait())

    fetch(block, lambda copy: copy.wait())
    slot = block % 2
    final = (block == blocks - 1) & (part == PARTS - 1 or dense)

    def columns(chunk):
        if dense:
            return pl.ds(pl.multiple_of(chunk * WIDE, WIDE), WIDE)
        return slice(chunk * WIDE, (chunk + 1) * WIDE)

    def image(chunk):
        at = columns(chunk)
        images = [dot(image_w_ref[...], r[:, :, at].reshape(HALF * depth, WIDE)) for r in (lower_ref, upper_ref)]
        after = dot(weight_ref[...], jnp.where(final, right_ref[0, :, at], next_ref[0, :, at]))
        return images, after

    def residual(chunk, images, after):
        at = columns(chunk)
        seen = seen_ref[slot, :, :, at].astype(jnp.float32)
        ahead = [pltpu.roll(x.reshape(angles, HALF, WIDE), HALF - 1, 1) for x in images]
        ahead.append(jnp.broadcast_to(after.reshape(angles, 1, WIDE), (angles, HALF, WIDE)))
        tail = lax.broadcasted_iota(jnp.int32, (angles, HALF, WIDE), 1) == HALF - 1
        parts = []
        for half in range(2):
            now = jnp.where(tail, ahead[half + 1], ahead[half]).reshape(angles * HALF, WIDE)
            got = seen[:, half * HALF : (half + 1) * HALF].reshape(angles * HALF, WIDE)
            coef = [widen(coef_ref[0, half, n]) for n in range(3)]
            resid = got * coef[2] - now * coef[0] - images[half] * coef[1]
            parts.append(resid.reshape(angles, HALF, WIDE))
        return parts

    def result(chunk, parts):
        at = columns(chunk)
        carry = carry_ref[:, at]
        for half, (resid, r) in enumerate(zip(parts, (lower_ref, upper_ref))):
            inputs = jnp.concatenate([resid.reshape(angles * HALF, WIDE).astype(jnp.bfloat16), carry])
            spread = dot(spread_ref[half], inputs).reshape(HALF, depth, WIDE)
            carry = resid[:, HALF - 1].astype(jnp.bfloat16)
            result_ref[slot, half * HALF : (half + 1) * HALF, :, at] = r[:, :, at].astype(jnp.float32) + spread
        carry_ref[:, at] = carry

    chunks = width // WIDE
    if dense:
        pl.loop(0, chunks)(lambda chunk: result(chunk, residual(chunk, *image(chunk))))
        deliver(block, lambda copy: copy.start())
    else:
        images, resids = {}, {}
        for n in range(chunks + 2):
            if n < chunks:
                images[n] = image(n)
            if 1 <= n <= chunks:
                resids[n - 1] = residual(n - 1, *images.pop(n - 1))
            if n >= 2:
                result(n - 2, resids.pop(n - 2))
                done = (n - 1) * PIECES
                if done % chunks == 0:
                    deliver(block, lambda copy: copy.start(), [done // chunks - 1])

    @pl.when(block == blocks - 1)
    def _():
        @pl.when(block >= 1)
        def _():
            deliver(block - 1, lambda copy: copy.wait())

        deliver(block, lambda copy: copy.wait())


def update(volume, left, right, edge, tables, packets, table, before, part, parts, dense):
    slices, depth, cols = volume.shape
    angles = edge.shape[0]
    blocks = slices // BLOCK // parts
    off = part * blocks
    by_block = lambda x: pl.BlockSpec((1,) + x.shape[1:], lambda b, i: (b,) + (0,) * (x.ndim - 1))
    whole = lambda x: pl.BlockSpec(x.shape, lambda b, i: (0,) * x.ndim)
    anywhere = pl.BlockSpec(memory_space=pl.ANY)
    coef, edge_coef, image_w, weights, spread_w = tables
    aliases = {} if before is None else {12 + len(packets): 0}
    copies = LOAD * len(packets)
    one = (1, depth, cols)
    return pl.pallas_call(
        functools.partial(update_kernel, dense, part),
        grid_spec=pltpu.PrefetchScalarGridSpec(
            num_scalar_prefetch=1,
            grid=(blocks,),
            in_specs=[
                pl.BlockSpec((HALF, depth, cols), lambda b, i: (2 * (b + off), 0, 0)),
                pl.BlockSpec((HALF, depth, cols), lambda b, i: (2 * (b + off) + 1, 0, 0)),
                pl.BlockSpec(one, lambda b, i: (jnp.minimum((b + off + 1) * BLOCK, slices - 1), 0, 0)),
                pl.BlockSpec(one, lambda b, i: (0, 0, 0)),
                pl.BlockSpec(one, lambda b, i: (0, 0, 0)),
                whole(edge), by_block(coef), whole(edge_coef), whole(image_w), whole(weights),
                pl.BlockSpec((2,) + spread_w.shape[1:], lambda b, i: (b, 0, 0)),
            ]
            + [anywhere] * (len(packets) + 1),
            out_specs=[anywhere, whole(edge)],
            scratch_shapes=[
                pltpu.VMEM((2, angles, BLOCK, cols), jnp.bfloat16),
                pltpu.VMEM((2, BLOCK, depth, cols), jnp.float32),
                pltpu.SemaphoreType.DMA((2, copies)),
                pltpu.SemaphoreType.DMA((2, PIECES)),
            ],
        ),
        out_shape=[jax.ShapeDtypeStruct(volume.shape, jnp.float32), jax.ShapeDtypeStruct(edge.shape, edge.dtype)],
        input_output_aliases=aliases,
        compiler_params=pltpu.CompilerParams(dimension_semantics=("arbitrary",), vmem_limit_bytes=VMEM_LIMIT),
        cost_estimate=pl.CostEstimate(
            flops=4 * slices * depth * cols * angles // parts, bytes_accessed=volume.size * 7 // parts, transcendentals=0
        ),
        name="slab_update",
    )(
        table, volume, volume, volume, left, right, edge, coef, edge_coef, image_w, weights, spread_w,
        *packets, edge if before is None else before,
    )


def mend_kernel(weight_ref, first_ref, second_ref, before_ref, out_ref):
    resid = jnp.where(pl.program_id(0) == 0, first_ref[...], second_ref[...])
    out_ref[0] = before_ref[0] + dot(weight_ref[0], resid)


def mend(out, weights, first, second):
    slices, depth, cols = out.shape
    parts = weights.shape[0]
    whole = pl.BlockSpec(first.shape, lambda b: (0, 0))
    slab = pl.BlockSpec((1, depth, cols), lambda b: (b * (slices // parts), 0, 0))
    return pl.pallas_call(
        mend_kernel,
        grid=(parts,),
        in_specs=[pl.BlockSpec((1,) + weights.shape[1:], lambda b: (b, 0, 0)), whole, whole, slab],
        out_specs=slab,
        out_shape=jax.ShapeDtypeStruct(out.shape, out.dtype),
        input_output_aliases={3: 0},
        name="mend_slices",
    )(weights, first, second, out)


def fill_weights(wide_w, turned_w, pick_next, pick_now, pick_carry, spread_ref, half):
    depth, columns = wide_w.shape
    place = lax.broadcasted_iota(jnp.int32, (depth, columns), 1) % HALF
    from_next = wide_w * pick_next
    from_now = wide_w * pick_now
    from_carry = turned_w * pick_carry
    for z in range(HALF):
        row = jnp.where(place == z, from_next, jnp.where(place == z - 1, from_now, 0.0))
        total = jnp.sum(row, axis=1, keepdims=True)
        carry = jnp.zeros_like(from_carry)
        if z == 0:
            total = total + jnp.sum(from_carry, axis=1, keepdims=True)
            carry = from_carry
        scale = RELAX / total
        spread_ref[half, z * depth : (z + 1) * depth, :columns] = (row * scale).astype(jnp.bfloat16)
        spread_ref[half, z * depth : (z + 1) * depth, columns:] = (carry * scale).astype(jnp.bfloat16)


def weights_kernel(wide_w_ref, turned_w_ref, pick_ref, pick_carry_ref, spread_ref):
    picks = pick_ref[0, 0:1], pick_ref[0, 1:2], pick_carry_ref[0]
    fill_weights(wide_w_ref[...], turned_w_ref[...], *picks, spread_ref, 0)


def make_weights(wide_w, turned_w, pick, pick_carry):
    halves = pick.shape[0]
    depth, angles = turned_w.shape
    by_half = lambda shape: pl.BlockSpec((1,) + shape, lambda b: (b,) + (0,) * len(shape))
    whole = lambda x: pl.BlockSpec(x.shape, lambda b: (0,) * x.ndim)
    spread = (HALF * depth, angles * (HALF + 1))
    return pl.pallas_call(
        weights_kernel,
        grid=(halves,),
        in_specs=[whole(wide_w), whole(turned_w), by_half(pick.shape[1:]), by_half(pick_carry.shape[1:])],
        out_specs=by_half(spread),
        out_shape=jax.ShapeDtypeStruct((halves,) + spread, jnp.bfloat16),
        name="spread_weights",
    )(wide_w, turned_w, pick, pick_carry)


def make_tables(share, first, rows, path_weights, bases, slices):
    angles, depth = path_weights.shape
    blocks = slices // BLOCK
    weights = path_weights.astype(jnp.float32)
    ray_total = jnp.sum(weights, axis=1)[:, None]
    norm = 1.0 / (ray_total * ((1.0 - share[:, 1:]) + share[:, :-1]))
    coefs = jnp.stack([(1.0 - share[:, 1:]) * norm, share[:, :-1] * norm, norm])
    coef = coefs[:, :, 1:].reshape(3, angles, blocks, BLOCK // HALF, HALF).transpose(2, 3, 0, 1, 4)
    coef = coef.reshape(blocks, BLOCK // HALF, 3, angles * HALF, 1)
    coef = jnp.broadcast_to(coef, coef.shape[:4] + (LANES,))
    edge_coef = jnp.broadcast_to(coefs[:, :, :1], (3, angles, LANES))
    share_own = share[:, 1:-1]
    row_now = (first - bases)[:, None] + jnp.arange(slices, dtype=jnp.int32)[None, :]
    w_now = jnp.where((row_now >= 0) & (row_now < rows), 1.0 - share_own, 0.0)
    w_next = jnp.where((row_now + 1 >= 0) & (row_now + 1 < rows), share_own, 0.0)
    halves = slices // HALF
    pick = jnp.stack([w_next, jnp.pad(w_now[:, 1:], ((0, 0), (0, 1)))]).reshape(2, angles, halves, HALF)
    pick = pick.transpose(2, 0, 1, 3).reshape(halves, 2, angles * HALF)
    pick_carry = w_now[:, ::HALF].T[:, None, :]
    eye = jnp.eye(HALF, dtype=jnp.float32)
    image_w = jnp.einsum("ad,yz->ayzd", weights, eye).reshape(angles * HALF, HALF * depth).astype(jnp.bfloat16)
    wide_w = jnp.repeat(weights.T, HALF, axis=1)
    return coef, edge_coef, image_w, path_weights, make_weights(wide_w, weights.T, pick, pick_carry)


def column_of(line, tall):
    sub = lax.broadcasted_iota(jnp.int32, (tall, LANES), 0)
    lane = lax.broadcasted_iota(jnp.int32, (tall, LANES), 1)
    return jnp.max(jnp.where(sub == lane, line, -1), axis=1, keepdims=True)


def tables_kernel(
    rows, off, device_ref, bases_ref, before_ref, own_ref, after_ref, weight_ref,
    coef_ref, edge_coef_ref, image_w_ref, spread_ref, wide_ref, turned_ref,
):
    block = pl.program_id(0) + off
    angles, depth = weight_ref.shape
    first = device_ref[0] * LANES
    shape = (angles, LANES)
    lane = lax.broadcasted_iota(jnp.int32, shape, 1)
    sub = lax.broadcasted_iota(jnp.int32, shape, 0)
    weights = weight_ref[...].astype(jnp.float32)
    ray_total = jnp.sum(weights, axis=1, keepdims=True)
    own = own_ref[...]
    ahead = jnp.where(lane == LANES - 1, pltpu.roll(after_ref[...], LANES - 1, 1), pltpu.roll(own, LANES - 1, 1))
    norm = 1.0 / (ray_total * ((1.0 - ahead) + own))
    coefs = ((1.0 - ahead) * norm, own * norm, norm)
    spots = lax.broadcasted_iota(jnp.int32, (angles, HALF, LANES), 2) - lax.broadcasted_iota(jnp.int32, (angles, HALF, LANES), 1)
    for half in range(BLOCK // HALF):
        here = spots == block * BLOCK + half * HALF
        for n, coef in enumerate(coefs):
            tall = jnp.broadcast_to(coef.reshape(angles, 1, LANES), (angles, HALF, LANES))
            tall = jnp.sum(jnp.where(here, tall, 0.0), axis=2, keepdims=True)
            coef_ref[0, half, n] = jnp.broadcast_to(tall, (angles, HALF, LANES)).reshape(angles * HALF, LANES)

    @pl.when(block == off)
    def _():
        edge_own = jnp.sum(jnp.where(lane == 0, own, 0.0), axis=1, keepdims=True)
        edge_before = jnp.sum(jnp.where(lane == LANES - 1, before_ref[...], 0.0), axis=1, keepdims=True)
        edge_norm = 1.0 / (ray_total * ((1.0 - edge_own) + edge_before))
        for n, coef in enumerate(((1.0 - edge_own) * edge_norm, edge_before * edge_norm, edge_norm)):
            edge_coef_ref[n] = jnp.broadcast_to(coef, shape)
        across = (HALF * depth)
        repeat = lax.broadcasted_iota(jnp.int32, (depth, across), 1) % depth
        repeat = jnp.where(repeat == lax.broadcasted_iota(jnp.int32, (depth, across), 0), 1.0, 0.0)
        wide = dot(weight_ref[...], repeat.astype(jnp.bfloat16)).astype(jnp.bfloat16)
        down = angles * HALF
        expand = lax.broadcasted_iota(jnp.int32, (down, angles), 0) // HALF
        expand = jnp.where(expand == lax.broadcasted_iota(jnp.int32, (down, angles), 1), 1.0, 0.0)
        wide = dot(expand.astype(jnp.bfloat16), wide)
        at = lax.broadcasted_iota(jnp.int32, (down, across), 0) % HALF
        same = lax.broadcasted_iota(jnp.int32, (down, across), 1) // depth == at
        image_w_ref[...] = jnp.where(same, wide, 0.0).astype(jnp.bfloat16)

    row_now = first + lane - column_of(bases_ref[...], angles)
    w_now = jnp.where((row_now >= 0) & (row_now < rows), 1.0 - own, 0.0)
    w_next = jnp.where((row_now + 1 >= 0) & (row_now + 1 < rows), own, 0.0)
    columns = angles * HALF
    place = lax.broadcasted_iota(jnp.int32, (LANES, columns), 1) % HALF
    mine = lax.broadcasted_iota(jnp.int32, (angles, columns), 1) // HALF
    mine = mine == lax.broadcasted_iota(jnp.int32, (angles, columns), 0)
    square = lax.broadcasted_iota(jnp.int32, (angles, angles), 0) == lax.broadcasted_iota(jnp.int32, (angles, angles), 1)

    def gather(values, wanted):
        picked = jnp.dot(
            values, jnp.where(wanted, 1.0, 0.0), precision=lax.Precision.HIGHEST, preferred_element_type=jnp.float32
        )
        return jnp.sum(jnp.where(mine, picked, 0.0), axis=0, keepdims=True)

    turned = lambda other: lax.dot_general(
        weights, other, (((0,), (0,)), ((), ())), precision=lax.Precision.HIGHEST, preferred_element_type=jnp.float32
    )

    @pl.when(block == off)
    def _():
        wide_ref[...] = turned(jnp.where(mine, 1.0, 0.0))
        turned_ref[...] = turned(jnp.where(square, 1.0, 0.0))

    for half in range(BLOCK // HALF):
        start = block * BLOCK + half * HALF
        z = lax.broadcasted_iota(jnp.int32, (LANES, columns), 0) - start
        pick_next = gather(w_next, z == place)
        pick_now = gather(w_now, (z == place + 1) & (place < HALF - 1))
        carry = jnp.sum(jnp.where(lane == start, w_now, 0.0), axis=1, keepdims=True)
        pick_carry = jnp.sum(jnp.where(square, carry, 0.0), axis=0, keepdims=True)
        fill_weights(wide_ref[...], turned_ref[...], pick_next, pick_now, pick_carry, spread_ref, half)


def device_tables(device, row_of_bases, fractions, path_weights, rows, part):
    angles, depth = path_weights.shape
    blocks = LANES // BLOCK // PARTS
    last = fractions.shape[1] // LANES - 1
    column = lambda by: pl.BlockSpec((angles, LANES), lambda b, d: (0, jnp.clip(d[0] + by, 0, last)))
    whole = lambda shape: pl.BlockSpec(shape, lambda b, d: (0,) * len(shape))
    by_block = lambda shape: pl.BlockSpec((1,) + shape, lambda b, d: (b,) + (0,) * len(shape))
    coef = (BLOCK // HALF, 3, angles * HALF, LANES)
    edge_coef = (3, angles, LANES)
    image_w = (angles * HALF, HALF * depth)
    spread = (HALF * depth, angles * (HALF + 1))
    made = pl.pallas_call(
        functools.partial(tables_kernel, rows, part * blocks),
        grid_spec=pltpu.PrefetchScalarGridSpec(
            num_scalar_prefetch=1,
            grid=(blocks,),
            in_specs=[whole((1, LANES)), column(-1), column(0), column(1), whole(path_weights.shape)],
            out_specs=[
                by_block(coef), whole(edge_coef), whole(image_w),
                pl.BlockSpec((2,) + spread, lambda b, d: (b, 0, 0)),
            ],
            scratch_shapes=[
                pltpu.VMEM((depth, angles * HALF), jnp.float32),
                pltpu.VMEM((depth, angles), jnp.float32),
            ],
        ),
        out_shape=[
            jax.ShapeDtypeStruct((blocks,) + coef, jnp.float32),
            jax.ShapeDtypeStruct(edge_coef, jnp.float32),
            jax.ShapeDtypeStruct(image_w, jnp.bfloat16),
            jax.ShapeDtypeStruct((2 * blocks,) + spread, jnp.bfloat16),
        ],
        name="make_tables",
    )(device, row_of_bases, fractions, fractions, fractions, path_weights)
    return made[0], made[1], made[2], path_weights, made[3]


def turn_kernel(classes, count, part, device_ref, bases_ref, seen_ref, *refs):
    outs, twice_ref, sems = refs[:-2], refs[-2], refs[-1]
    rows, cols = seen_ref.shape
    more = twice_ref.shape[0] - rows
    copies = [
        pltpu.make_async_copy(seen_ref, twice_ref.at[pl.ds(0, rows)], sems.at[0]),
        pltpu.make_async_copy(seen_ref.at[pl.ds(0, more)], twice_ref.at[pl.ds(rows, more)], sems.at[1]),
    ]
    for copy in copies:
        copy.start()
    for copy in copies:
        copy.wait()
    device = device_ref[0]
    base = bases_ref[device]
    my_class = device & (classes - 1)
    slices = count * PARTS

    def window(place, size, at):
        start = (place - base + 1 + rows) & (rows - 1)
        begin = pl.multiple_of(start & ~(BLOCK - 1), BLOCK)
        tall = size + BLOCK
        wide = twice_ref[pl.ds(begin, tall), at].astype(jnp.float32)
        return pltpu.roll(wide, (tall - (start - begin)) % tall, 0)

    for d in range(classes):
        place = (my_class ^ d) * slices + part * count

        @pl.loop(0, cols // WIDE)
        def _(chunk):
            at = pl.ds(pl.multiple_of(chunk * WIDE, WIDE), WIDE)
            outs[d][:, at] = window(place, count, at)[:count].astype(jnp.bfloat16)


def turn(device, bases, seen, classes, part):
    rows, cols = seen.shape
    count = rows // classes // PARTS
    return pl.pallas_call(
        functools.partial(turn_kernel, classes, count, part),
        in_specs=[
            pl.BlockSpec(memory_space=pltpu.SMEM),
            pl.BlockSpec(memory_space=pltpu.SMEM),
            pl.BlockSpec(memory_space=pl.ANY),
        ],
        out_specs=[pl.BlockSpec(memory_space=pltpu.VMEM)] * classes,
        out_shape=[jax.ShapeDtypeStruct((count, cols), seen.dtype)] * classes,
        scratch_shapes=[pltpu.VMEM((rows + count + BLOCK, cols), seen.dtype), pltpu.SemaphoreType.DMA((2,))],
        compiler_params=pltpu.CompilerParams(vmem_limit_bytes=32 * 2**20),
        name="turn_rows",
    )(device, bases, seen)


def plan_kernel(slots, planes, classes, angles, count, rows, device_ref, bases_ref, table_ref):
    shape = (2 * PARTS * classes, LANES)
    lane = lax.broadcasted_iota(jnp.int32, shape, 1)
    row = lax.broadcasted_iota(jnp.int32, shape, 0)
    class_shift = classes.bit_length() - 1
    base = jnp.broadcast_to(bases_ref[...], shape) - 1
    low_plane = base >> (rows.bit_length() - 1)
    turned = base & (rows - 1)

    def reach(which):
        lowest = low_plane + jnp.where(which * count + count - 1 < turned, 1, 0)
        highest = low_plane + jnp.where(which * count < turned, 1, 0)
        return lowest, highest

    lowest, highest = reach(row >> 1)
    upward = (row & 1) == 0
    source = lane >> class_shift
    at = jnp.where(upward, source, planes - 1 - source)
    to = jnp.where(lane < angles, jnp.where(upward, highest, planes - 1 - lowest), -1)
    key = to * CODE + (CODE - 1 - lane)
    sent = [jnp.full(shape, -1, jnp.int32) for _ in range(planes - 1)]
    for slot in range(slots):
        begin = at
        for link in range(planes - 1):
            ready = (begin == link) & (to > link)
            for n in range(LOAD):
                best = jnp.max(jnp.where(ready, key, -1), axis=1, keepdims=True)
                taken = ready & (key == best)
                at = jnp.where(taken, link + 1, at)
                ready = ready & (key != best)
                which = jnp.where(best >= 0, CODE - 1 - (best & (CODE - 1)), -1)
                sent[link] = jnp.where(lane == slot * LOAD + n, which, sent[link])

    me = device_ref[0]
    my_class = me & (classes - 1)
    plane = me >> class_shift
    none = jnp.full(shape, -1, jnp.int32)
    used = none
    for link in range(planes - 1):
        used = jnp.maximum(used, sent[link])
    used = jnp.max(used, axis=0, keepdims=True)
    head = lane[:1]
    total = jnp.max(jnp.where(used >= 0, head + 1, 0), axis=1, keepdims=True)

    tall = -(-max(slots * LOAD, angles) // 8) * 8
    sub = lax.broadcasted_iota(jnp.int32, (tall, LANES), 0)
    held = jnp.where(head < classes, plane * classes + (head ^ my_class), -1)
    for part in range(PARTS):
        low_here, high_here = reach(my_class * PARTS + part)
        wanted = (plane >= low_here) & (plane <= high_here) & (lane < angles)
        wanted = column_of(jnp.where(wanted, 1, 0)[:1], tall) > 0
        keep = lambda ids: jnp.max(jnp.where((sub == ids) & wanted, ids, -1), axis=0, keepdims=True)
        for way, spot in ((0, plane), (1, planes - 1 - plane)):
            sends, gets = none, none
            for link in range(planes - 1):
                sends = jnp.where(spot == link, sent[link], sends)
                gets = jnp.where(spot == link + 1, sent[link], gets)
            mine = row == 2 * (my_class * PARTS + part) + way
            sends = jnp.max(jnp.where(mine, sends, -1), axis=0, keepdims=True)
            gets = jnp.max(jnp.where(mine, gets, -1), axis=0, keepdims=True)
            arrived = jnp.max(jnp.where((column_of(gets, tall) == sends) & (sends >= 0), sub, 0), axis=0, keepdims=True)
            own = (sends >> class_shift) == plane
            index = jnp.where(own, (sends & (classes - 1)) ^ my_class, classes + arrived)
            line = part * LINES + way
            table_ref[line : line + 1] = jnp.where(sends >= 0, index, 0)
            table_ref[line + 2 : line + 3] = keep(gets)
        line = part * LINES + 4
        table_ref[line : line + 1] = keep(held)
    table_ref[PARTS * LINES : PARTS * LINES + 1] = jnp.broadcast_to(total, head.shape)


def choose_kernel(slot, part, load, own, ups, table_ref, *refs):
    sources, (*outs, held, sems) = refs[: own + 2 * ups], refs[own + 2 * ups :]
    arrived = sources[own : own + ups], sources[own + ups :]
    views = [spread_out(sources[:own], []) + [(own + n, v) for n, v in spread_out([], side)] for side in arrived]
    spots = [(way, n) for way in range(2) for n in range(load)]
    for way, n in spots:
        for m, view in views[way]:

            @pl.when(table_ref[part * LINES + way, slot * LOAD + n] == m)
            def _():
                pltpu.make_async_copy(view, held.at[way, n], sems.at[0, way, n]).start()

    for way, n in spots:
        pltpu.make_async_copy(sources[0], held.at[way, n], sems.at[0, way, n]).wait()
        pltpu.make_async_copy(held.at[way, n], outs[way].at[n], sems.at[1, way, n]).start()
    for way, n in spots:
        pltpu.make_async_copy(held.at[way, n], outs[way].at[n], sems.at[1, way, n]).wait()


def choose(slot, part, load, table, own, ups, downs):
    anywhere = pl.BlockSpec(memory_space=pl.ANY)
    shape = jax.ShapeDtypeStruct((load,) + own[0].shape, own[0].dtype)
    return pl.pallas_call(
        functools.partial(choose_kernel, slot, part, load, len(own), len(ups)),
        in_specs=[pl.BlockSpec(memory_space=pltpu.SMEM)] + [anywhere] * (len(own) + 2 * len(ups)),
        out_specs=[anywhere, anywhere],
        out_shape=[shape, shape],
        scratch_shapes=[
            pltpu.VMEM((2, load) + own[0].shape, own[0].dtype),
            pltpu.SemaphoreType.DMA((2, 2, load)),
        ],
        cost_estimate=pl.CostEstimate(flops=0, bytes_accessed=4 * load * own[0].size * 2, transcendentals=0),
        name="choose_packet",
    )(table, *own, *ups, *downs)


def on_device(volume, measured, path_weights, fractions, bases):
    slices, depth, cols = volume.shape
    local, rows = measured.shape[:2]
    nslab = lax.axis_size("slab")
    device = lax.axis_index("slab")
    angles = local * nslab
    first = device * slices
    classes = rows // slices
    planes = nslab // classes
    ups_of = lambda step: [(i, i + step) for i in range(nslab - step)]
    downs_of = lambda step: [(i + step, i) for i in range(nslab - step)]

    routed = local == 1 and classes == ROUTED_CLASSES and slices == LANES and rows & (rows - 1) == 0 and angles <= LANES
    if not routed:
        left = lax.ppermute(volume[slices - 1 :], "slab", ups_of(1))
        right = lax.ppermute(volume[:1], "slab", downs_of(1))
        share = lax.dynamic_slice_in_dim(jnp.pad(fractions, ((0, 0), (1, 1))), first, slices + 2, 1)
        tables = make_tables(share, first, rows, path_weights, bases, slices)
        my_bases = lax.dynamic_slice_in_dim(bases, device * local, local, 0)
        turned = jax.vmap(lambda m, b: jnp.roll(m, b - 1, axis=0))(measured, my_bases)
        by_class = turned.reshape(local, classes, slices, cols).transpose(1, 0, 2, 3)
        outgoing = jnp.tile(by_class, (planes, 1, 1, 1)).reshape(angles, slices, cols)
        seen = lax.all_to_all(outgoing, "slab", split_axis=0, concat_axis=0, tiled=True)
        ends = jnp.roll(by_class[:, :, slices - 1], 1, axis=0)
        ends = jnp.tile(ends, (planes, 1, 1)).reshape(angles, cols // LANES, LANES)
        edge = lax.all_to_all(ends, "slab", split_axis=0, concat_axis=0, tiled=True).reshape(angles, cols)
        return update(volume, left, right, edge, tables, [seen], jnp.zeros((8, LANES), jnp.int32), None, 0, 1, True)[0]

    number = device.astype(jnp.int32)[None]
    upper, lower = PARTS - 1, 0
    exchange = lambda runs: [runs[0]] + [
        lax.ppermute(runs[d], "slab", [(i, i ^ d) for i in range(nslab)]) for d in range(1, classes)
    ]
    runs = turn(number, bases, measured[0], classes, upper)
    runs, late_bases, seen = lax.optimization_barrier((runs, bases, measured[0]))
    own = {upper: exchange(runs)}

    row_of_bases = jnp.pad(late_bases, (0, LANES - angles), constant_values=1)[None]
    most = -(-classes * (planes - 1) // LOAD) + planes - 2
    table = pl.pallas_call(
        functools.partial(plan_kernel, most, planes, classes, angles, slices // PARTS, rows),
        in_specs=[pl.BlockSpec(memory_space=pltpu.SMEM), pl.BlockSpec(memory_space=pltpu.VMEM)],
        out_shape=jax.ShapeDtypeStruct((16, LANES), jnp.int32),
        name="plan_slots",
    )(number, row_of_bases)
    runs = turn(number, late_bases, seen, classes, lower)
    tables = {upper: device_tables(number, row_of_bases, fractions, path_weights, rows, upper)}
    arrived, runs, table, tables[upper] = lax.optimization_barrier((own[upper], runs, table, tables[upper]))
    need = table[PARTS * LINES, 0]

    def finish(end):
        def branch(arrived, runs, table, upper_tables, row_of_bases):
            own = {upper: arrived, lower: exchange(runs)}
            ups, downs = {upper: [], lower: []}, {upper: [], lower: []}
            late = (volume[:1], row_of_bases)
            for slot in range(-(-end // LOAD)):
                load = min(LOAD, end - slot * LOAD)
                for part in (upper, lower):
                    go_up, go_down = choose(slot, part, load, table, own[part], ups[part], downs[part])
                    if slot == 0 and part == lower:
                        go_up, go_down, late = lax.optimization_barrier((go_up, go_down, late))
                        right = lax.ppermute(late[0], "slab", downs_of(1))
                        lower_tables = device_tables(number, late[1], fractions, path_weights, rows, lower)
                        mends = jnp.concatenate(
                            [t[-1][:1, :depth, angles * HALF :] for t in (lower_tables, upper_tables)]
                        )
                        table, lower_tables, mends = lax.optimization_barrier((table, lower_tables, mends))
                    ups[part].append(lax.ppermute(go_up, "slab", ups_of(classes)))
                    downs[part].append(lax.ppermute(go_down, "slab", downs_of(classes)))
            packets = {part: own[part] + ups[part] + downs[part] for part in (upper, lower)}
            args = (volume, right, right, jnp.zeros((angles, cols), volume.dtype))
            out, last = update(*args, upper_tables, packets[upper], table, None, upper, PARTS, False)
            first = lax.ppermute(last, "slab", ups_of(1))
            out, second = update(*args, lower_tables, packets[lower], table, out, lower, PARTS, False)
            return mend(out, mends, first, second)

        return branch

    ends = [5, 6, 7, 8, most * LOAD]
    which = jnp.sum(jnp.array([need > e for e in ends[:-1]]).astype(jnp.int32))
    return lax.switch(which, [finish(e) for e in ends], arrived, runs, table, tables[upper], row_of_bases)


def solution(mesh):
    placed = (P(("groups", "slab"), None, None), P(("groups", "slab"), None, None), P(), P(), P())
    return jax.shard_map(
        on_device,
        mesh=mesh,
        in_specs=placed,
        out_specs=P(("groups", "slab"), None, None),
        check_vma=False,
    )
```

```python
import functools

import jax
import jax.numpy as jnp
from jax import lax
from jax.experimental import pallas as pl
from jax.experimental.pallas import tpu as pltpu
from jax.sharding import PartitionSpec as P

RELAX = 1.0
BLOCK = 16
HALF = 8
LANES = 128
WIDE = 256
PIECES = 4
PARTS = 2
ROUTED_CLASSES = 4
LOAD = 2
CODE = 256
LINES = 5
VMEM_LIMIT = 56 * 2**20


def dot(a, b):
    return jnp.dot(a, b, preferred_element_type=jnp.float32)


def widen(coef):
    return jnp.concatenate([coef] * (WIDE // LANES), axis=1)


def spread_out(own, arrived):
    views = list(enumerate(own))
    return views + [(s * LOAD + n, p.at[n]) for s, p in enumerate(arrived) for n in range(p.shape[0])]


def update_kernel(
    dense, part, table_ref, lower_ref, upper_ref, next_ref, left_ref, right_ref, edge_ref, coef_ref, edge_coef_ref,
    image_w_ref, weight_ref, spread_ref, *rest,
):
    out_ref, carry_ref, seen_ref, result_ref, sems, out_sems = rest[-6:]
    packets = rest[:-7]
    block = pl.program_id(0)
    blocks = pl.num_programs(0)
    depth, width = lower_ref.shape[1:]
    angles = weight_ref.shape[0]
    first = part * blocks * BLOCK

    def fetch(at_block, act):
        slot = at_block % 2
        rows = pl.ds(pl.multiple_of(at_block * BLOCK, BLOCK), BLOCK)
        if dense:
            act(pltpu.make_async_copy(packets[0].at[:, rows], seen_ref.at[slot], sems.at[slot, 0]))
            return
        middle = (len(packets) - ROUTED_CLASSES) // 2 + ROUTED_CLASSES
        views = [(4, *v) for v in spread_out(packets[:ROUTED_CLASSES], [])]
        views += [(2, *v) for v in spread_out([], packets[ROUTED_CLASSES:middle])]
        views += [(3, *v) for v in spread_out([], packets[middle:])]
        for n, (line, spot, view) in enumerate(views):
            name = table_ref[part * LINES + line, spot]

            @pl.when(name >= 0)
            def _():
                act(pltpu.make_async_copy(view.at[rows], seen_ref.at[slot, name], sems.at[slot, n]))

    def deliver(at_block, act, pieces=range(PIECES)):
        slot = at_block % 2
        rows = pl.ds(first + at_block * BLOCK, BLOCK)
        for n in pieces:
            at = pl.ds(n * (width // PIECES), width // PIECES)
            act(pltpu.make_async_copy(result_ref.at[slot, :, :, at], out_ref.at[rows, :, at], out_sems.at[slot, n]))

    @pl.when(block == 0)
    def _():
        seen_ref[...] = jnp.zeros_like(seen_ref)
        fetch(block, lambda copy: copy.start())

    @pl.when(block + 1 < blocks)
    def _():
        fetch(block + 1, lambda copy: copy.start())

    @pl.when(block == 0)
    def _():
        if not dense:
            carry_ref[...] = jnp.zeros_like(carry_ref)
            return
        for chunk in range(width // WIDE):
            at = pl.ds(chunk * WIDE, WIDE)
            mine = dot(weight_ref[...], lower_ref[0, :, at])
            before = dot(weight_ref[...], left_ref[0, :, at])
            carry_ref[:, at] = (
                edge_ref[:, at].astype(jnp.float32) * widen(edge_coef_ref[2])
                - mine * widen(edge_coef_ref[0])
                - before * widen(edge_coef_ref[1])
            ).astype(jnp.bfloat16)

    @pl.when(block >= 2)
    def _():
        deliver(block - 2, lambda copy: copy.wait())

    fetch(block, lambda copy: copy.wait())
    slot = block % 2
    final = (block == blocks - 1) & (part == PARTS - 1 or dense)

    def columns(chunk):
        if dense:
            return pl.ds(pl.multiple_of(chunk * WIDE, WIDE), WIDE)
        return slice(chunk * WIDE, (chunk + 1) * WIDE)

    def image(chunk):
        at = columns(chunk)
        images = [dot(image_w_ref[...], r[:, :, at].reshape(HALF * depth, WIDE)) for r in (lower_ref, upper_ref)]
        after = dot(weight_ref[...], jnp.where(final, right_ref[0, :, at], next_ref[0, :, at]))
        return images, after

    def residual(chunk, images, after):
        at = columns(chunk)
        seen = seen_ref[slot, :, :, at].astype(jnp.float32)
        ahead = [pltpu.roll(x.reshape(angles, HALF, WIDE), HALF - 1, 1) for x in images]
        ahead.append(jnp.broadcast_to(after.reshape(angles, 1, WIDE), (angles, HALF, WIDE)))
        tail = lax.broadcasted_iota(jnp.int32, (angles, HALF, WIDE), 1) == HALF - 1
        parts = []
        for half in range(2):
            now = jnp.where(tail, ahead[half + 1], ahead[half]).reshape(angles * HALF, WIDE)
            got = seen[:, half * HALF : (half + 1) * HALF].reshape(angles * HALF, WIDE)
            coef = [widen(coef_ref[0, half, n]) for n in range(3)]
            resid = got * coef[2] - now * coef[0] - images[half] * coef[1]
            parts.append(resid.reshape(angles, HALF, WIDE))
        return parts

    def result(chunk, parts):
        at = columns(chunk)
        carry = carry_ref[:, at]
        for half, (resid, r) in enumerate(zip(parts, (lower_ref, upper_ref))):
            inputs = jnp.concatenate([resid.reshape(angles * HALF, WIDE).astype(jnp.bfloat16), carry])
            spread = dot(spread_ref[half], inputs).reshape(HALF, depth, WIDE)
            carry = resid[:, HALF - 1].astype(jnp.bfloat16)
            result_ref[slot, half * HALF : (half + 1) * HALF, :, at] = r[:, :, at].astype(jnp.float32) + spread
        carry_ref[:, at] = carry

    chunks = width // WIDE
    if dense:
        pl.loop(0, chunks)(lambda chunk: result(chunk, residual(chunk, *image(chunk))))
        deliver(block, lambda copy: copy.start())
    else:
        images, resids = {}, {}
        for n in range(chunks + 2):
            if n < chunks:
                images[n] = image(n)
            if 1 <= n <= chunks:
                resids[n - 1] = residual(n - 1, *images.pop(n - 1))
            if n >= 2:
                result(n - 2, resids.pop(n - 2))
                done = (n - 1) * PIECES
                if done % chunks == 0:
                    deliver(block, lambda copy: copy.start(), [done // chunks - 1])

    @pl.when(block == blocks - 1)
    def _():
        @pl.when(block >= 1)
        def _():
            deliver(block - 1, lambda copy: copy.wait())

        deliver(block, lambda copy: copy.wait())


def update(volume, left, right, edge, tables, packets, table, before, part, parts, dense):
    slices, depth, cols = volume.shape
    angles = edge.shape[0]
    blocks = slices // BLOCK // parts
    off = part * blocks
    by_block = lambda x: pl.BlockSpec((1,) + x.shape[1:], lambda b, i: (b,) + (0,) * (x.ndim - 1))
    whole = lambda x: pl.BlockSpec(x.shape, lambda b, i: (0,) * x.ndim)
    anywhere = pl.BlockSpec(memory_space=pl.ANY)
    coef, edge_coef, image_w, weights, spread_w = tables
    aliases = {} if before is None else {12 + len(packets): 0}
    copies = LOAD * len(packets)
    one = (1, depth, cols)
    return pl.pallas_call(
        functools.partial(update_kernel, dense, part),
        grid_spec=pltpu.PrefetchScalarGridSpec(
            num_scalar_prefetch=1,
            grid=(blocks,),
            in_specs=[
                pl.BlockSpec((HALF, depth, cols), lambda b, i: (2 * (b + off), 0, 0)),
                pl.BlockSpec((HALF, depth, cols), lambda b, i: (2 * (b + off) + 1, 0, 0)),
                pl.BlockSpec(one, lambda b, i: (jnp.minimum((b + off + 1) * BLOCK, slices - 1), 0, 0)),
                pl.BlockSpec(one, lambda b, i: (0, 0, 0)),
                pl.BlockSpec(one, lambda b, i: (0, 0, 0)),
                whole(edge), by_block(coef), whole(edge_coef), whole(image_w), whole(weights),
                pl.BlockSpec((2,) + spread_w.shape[1:], lambda b, i: (b, 0, 0)),
            ]
            + [anywhere] * (len(packets) + 1),
            out_specs=[anywhere, whole(edge)],
            scratch_shapes=[
                pltpu.VMEM((2, angles, BLOCK, cols), jnp.bfloat16),
                pltpu.VMEM((2, BLOCK, depth, cols), jnp.float32),
                pltpu.SemaphoreType.DMA((2, copies)),
                pltpu.SemaphoreType.DMA((2, PIECES)),
            ],
        ),
        out_shape=[jax.ShapeDtypeStruct(volume.shape, jnp.float32), jax.ShapeDtypeStruct(edge.shape, edge.dtype)],
        input_output_aliases=aliases,
        compiler_params=pltpu.CompilerParams(dimension_semantics=("arbitrary",), vmem_limit_bytes=VMEM_LIMIT),
        cost_estimate=pl.CostEstimate(
            flops=4 * slices * depth * cols * angles // parts, bytes_accessed=volume.size * 7 // parts, transcendentals=0
        ),
        name="slab_update",
    )(
        table, volume, volume, volume, left, right, edge, coef, edge_coef, image_w, weights, spread_w,
        *packets, edge if before is None else before,
    )


def mend_kernel(weight_ref, first_ref, second_ref, before_ref, out_ref):
    resid = jnp.where(pl.program_id(0) == 0, first_ref[...], second_ref[...])
    out_ref[0] = before_ref[0] + dot(weight_ref[0], resid)


def mend(out, weights, first, second):
    slices, depth, cols = out.shape
    parts = weights.shape[0]
    whole = pl.BlockSpec(first.shape, lambda b: (0, 0))
    slab = pl.BlockSpec((1, depth, cols), lambda b: (b * (slices // parts), 0, 0))
    return pl.pallas_call(
        mend_kernel,
        grid=(parts,),
        in_specs=[pl.BlockSpec((1,) + weights.shape[1:], lambda b: (b, 0, 0)), whole, whole, slab],
        out_specs=slab,
        out_shape=jax.ShapeDtypeStruct(out.shape, out.dtype),
        input_output_aliases={3: 0},
        name="mend_slices",
    )(weights, first, second, out)


def fill_weights(wide_w, turned_w, pick_next, pick_now, pick_carry, spread_ref, half):
    depth, columns = wide_w.shape
    place = lax.broadcasted_iota(jnp.int32, (depth, columns), 1) % HALF
    from_next = wide_w * pick_next
    from_now = wide_w * pick_now
    from_carry = turned_w * pick_carry
    for z in range(HALF):
        row = jnp.where(place == z, from_next, jnp.where(place == z - 1, from_now, 0.0))
        total = jnp.sum(row, axis=1, keepdims=True)
        carry = jnp.zeros_like(from_carry)
        if z == 0:
            total = total + jnp.sum(from_carry, axis=1, keepdims=True)
            carry = from_carry
        scale = RELAX / total
        spread_ref[half, z * depth : (z + 1) * depth, :columns] = (row * scale).astype(jnp.bfloat16)
        spread_ref[half, z * depth : (z + 1) * depth, columns:] = (carry * scale).astype(jnp.bfloat16)


def weights_kernel(wide_w_ref, turned_w_ref, pick_ref, pick_carry_ref, spread_ref):
    picks = pick_ref[0, 0:1], pick_ref[0, 1:2], pick_carry_ref[0]
    fill_weights(wide_w_ref[...], turned_w_ref[...], *picks, spread_ref, 0)


def make_weights(wide_w, turned_w, pick, pick_carry):
    halves = pick.shape[0]
    depth, angles = turned_w.shape
    by_half = lambda shape: pl.BlockSpec((1,) + shape, lambda b: (b,) + (0,) * len(shape))
    whole = lambda x: pl.BlockSpec(x.shape, lambda b: (0,) * x.ndim)
    spread = (HALF * depth, angles * (HALF + 1))
    return pl.pallas_call(
        weights_kernel,
        grid=(halves,),
        in_specs=[whole(wide_w), whole(turned_w), by_half(pick.shape[1:]), by_half(pick_carry.shape[1:])],
        out_specs=by_half(spread),
        out_shape=jax.ShapeDtypeStruct((halves,) + spread, jnp.bfloat16),
        name="spread_weights",
    )(wide_w, turned_w, pick, pick_carry)


def make_tables(share, first, rows, path_weights, bases, slices):
    angles, depth = path_weights.shape
    blocks = slices // BLOCK
    weights = path_weights.astype(jnp.float32)
    ray_total = jnp.sum(weights, axis=1)[:, None]
    norm = 1.0 / (ray_total * ((1.0 - share[:, 1:]) + share[:, :-1]))
    coefs = jnp.stack([(1.0 - share[:, 1:]) * norm, share[:, :-1] * norm, norm])
    coef = coefs[:, :, 1:].reshape(3, angles, blocks, BLOCK // HALF, HALF).transpose(2, 3, 0, 1, 4)
    coef = coef.reshape(blocks, BLOCK // HALF, 3, angles * HALF, 1)
    coef = jnp.broadcast_to(coef, coef.shape[:4] + (LANES,))
    edge_coef = jnp.broadcast_to(coefs[:, :, :1], (3, angles, LANES))
    share_own = share[:, 1:-1]
    row_now = (first - bases)[:, None] + jnp.arange(slices, dtype=jnp.int32)[None, :]
    w_now = jnp.where((row_now >= 0) & (row_now < rows), 1.0 - share_own, 0.0)
    w_next = jnp.where((row_now + 1 >= 0) & (row_now + 1 < rows), share_own, 0.0)
    halves = slices // HALF
    pick = jnp.stack([w_next, jnp.pad(w_now[:, 1:], ((0, 0), (0, 1)))]).reshape(2, angles, halves, HALF)
    pick = pick.transpose(2, 0, 1, 3).reshape(halves, 2, angles * HALF)
    pick_carry = w_now[:, ::HALF].T[:, None, :]
    eye = jnp.eye(HALF, dtype=jnp.float32)
    image_w = jnp.einsum("ad,yz->ayzd", weights, eye).reshape(angles * HALF, HALF * depth).astype(jnp.bfloat16)
    wide_w = jnp.repeat(weights.T, HALF, axis=1)
    return coef, edge_coef, image_w, path_weights, make_weights(wide_w, weights.T, pick, pick_carry)


def column_of(line, tall):
    sub = lax.broadcasted_iota(jnp.int32, (tall, LANES), 0)
    lane = lax.broadcasted_iota(jnp.int32, (tall, LANES), 1)
    return jnp.max(jnp.where(sub == lane, line, -1), axis=1, keepdims=True)


def tables_kernel(
    rows, off, device_ref, bases_ref, before_ref, own_ref, after_ref, weight_ref,
    coef_ref, edge_coef_ref, image_w_ref, spread_ref, wide_ref, turned_ref,
):
    block = pl.program_id(0) + off
    angles, depth = weight_ref.shape
    first = device_ref[0] * LANES
    shape = (angles, LANES)
    lane = lax.broadcasted_iota(jnp.int32, shape, 1)
    sub = lax.broadcasted_iota(jnp.int32, shape, 0)
    weights = weight_ref[...].astype(jnp.float32)
    ray_total = jnp.sum(weights, axis=1, keepdims=True)
    own = own_ref[...]
    ahead = jnp.where(lane == LANES - 1, pltpu.roll(after_ref[...], LANES - 1, 1), pltpu.roll(own, LANES - 1, 1))
    norm = 1.0 / (ray_total * ((1.0 - ahead) + own))
    coefs = ((1.0 - ahead) * norm, own * norm, norm)
    spots = lax.broadcasted_iota(jnp.int32, (angles, HALF, LANES), 2) - lax.broadcasted_iota(jnp.int32, (angles, HALF, LANES), 1)
    for half in range(BLOCK // HALF):
        here = spots == block * BLOCK + half * HALF
        for n, coef in enumerate(coefs):
            tall = jnp.broadcast_to(coef.reshape(angles, 1, LANES), (angles, HALF, LANES))
            tall = jnp.sum(jnp.where(here, tall, 0.0), axis=2, keepdims=True)
            coef_ref[0, half, n] = jnp.broadcast_to(tall, (angles, HALF, LANES)).reshape(angles * HALF, LANES)

    @pl.when(block == off)
    def _():
        edge_own = jnp.sum(jnp.where(lane == 0, own, 0.0), axis=1, keepdims=True)
        edge_before = jnp.sum(jnp.where(lane == LANES - 1, before_ref[...], 0.0), axis=1, keepdims=True)
        edge_norm = 1.0 / (ray_total * ((1.0 - edge_own) + edge_before))
        for n, coef in enumerate(((1.0 - edge_own) * edge_norm, edge_before * edge_norm, edge_norm)):
            edge_coef_ref[n] = jnp.broadcast_to(coef, shape)
        across = (HALF * depth)
        repeat = lax.broadcasted_iota(jnp.int32, (depth, across), 1) % depth
        repeat = jnp.where(repeat == lax.broadcasted_iota(jnp.int32, (depth, across), 0), 1.0, 0.0)
        wide = dot(weight_ref[...], repeat.astype(jnp.bfloat16)).astype(jnp.bfloat16)
        down = angles * HALF
        expand = lax.broadcasted_iota(jnp.int32, (down, angles), 0) // HALF
        expand = jnp.where(expand == lax.broadcasted_iota(jnp.int32, (down, angles), 1), 1.0, 0.0)
        wide = dot(expand.astype(jnp.bfloat16), wide)
        at = lax.broadcasted_iota(jnp.int32, (down, across), 0) % HALF
        same = lax.broadcasted_iota(jnp.int32, (down, across), 1) // depth == at
        image_w_ref[...] = jnp.where(same, wide, 0.0).astype(jnp.bfloat16)

    row_now = first + lane - column_of(bases_ref[...], angles)
    w_now = jnp.where((row_now >= 0) & (row_now < rows), 1.0 - own, 0.0)
    w_next = jnp.where((row_now + 1 >= 0) & (row_now + 1 < rows), own, 0.0)
    columns = angles * HALF
    mine = lax.broadcasted_iota(jnp.int32, (angles, columns), 1) // HALF
    mine = mine == lax.broadcasted_iota(jnp.int32, (angles, columns), 0)
    square = lax.broadcasted_iota(jnp.int32, (angles, angles), 0) == lax.broadcasted_iota(jnp.int32, (angles, angles), 1)

    def gather(values, start, count):
        near = jnp.where(lane < count, pltpu.roll(values, (2 * LANES - start) % LANES, 1), 0.0)
        step = HALF
        while step < LANES:
            near = near + pltpu.roll(near, step, 1)
            step *= 2
        return jnp.sum(jnp.where(mine, near, 0.0), axis=0, keepdims=True)

    turned = lambda other: lax.dot_general(
        weights, other, (((0,), (0,)), ((), ())), precision=lax.Precision.HIGHEST, preferred_element_type=jnp.float32
    )

    @pl.when(block == off)
    def _():
        wide_ref[...] = turned(jnp.where(mine, 1.0, 0.0))
        turned_ref[...] = turned(jnp.where(square, 1.0, 0.0))

    for half in range(BLOCK // HALF):
        start = block * BLOCK + half * HALF
        pick_next = gather(w_next, start, HALF)
        pick_now = gather(w_now, start + 1, HALF - 1)
        carry = jnp.sum(jnp.where(lane == start, w_now, 0.0), axis=1, keepdims=True)
        pick_carry = jnp.sum(jnp.where(square, carry, 0.0), axis=0, keepdims=True)
        fill_weights(wide_ref[...], turned_ref[...], pick_next, pick_now, pick_carry, spread_ref, half)


def device_tables(device, row_of_bases, fractions, path_weights, rows, part):
    angles, depth = path_weights.shape
    blocks = LANES // BLOCK // PARTS
    last = fractions.shape[1] // LANES - 1
    column = lambda by: pl.BlockSpec((angles, LANES), lambda b, d: (0, jnp.clip(d[0] + by, 0, last)))
    whole = lambda shape: pl.BlockSpec(shape, lambda b, d: (0,) * len(shape))
    by_block = lambda shape: pl.BlockSpec((1,) + shape, lambda b, d: (b,) + (0,) * len(shape))
    coef = (BLOCK // HALF, 3, angles * HALF, LANES)
    edge_coef = (3, angles, LANES)
    image_w = (angles * HALF, HALF * depth)
    spread = (HALF * depth, angles * (HALF + 1))
    made = pl.pallas_call(
        functools.partial(tables_kernel, rows, part * blocks),
        grid_spec=pltpu.PrefetchScalarGridSpec(
            num_scalar_prefetch=1,
            grid=(blocks,),
            in_specs=[whole((1, LANES)), column(-1), column(0), column(1), whole(path_weights.shape)],
            out_specs=[
                by_block(coef), whole(edge_coef), whole(image_w),
                pl.BlockSpec((2,) + spread, lambda b, d: (b, 0, 0)),
            ],
            scratch_shapes=[
                pltpu.VMEM((depth, angles * HALF), jnp.float32),
                pltpu.VMEM((depth, angles), jnp.float32),
            ],
        ),
        out_shape=[
            jax.ShapeDtypeStruct((blocks,) + coef, jnp.float32),
            jax.ShapeDtypeStruct(edge_coef, jnp.float32),
            jax.ShapeDtypeStruct(image_w, jnp.bfloat16),
            jax.ShapeDtypeStruct((2 * blocks,) + spread, jnp.bfloat16),
        ],
        name="make_tables",
    )(device, row_of_bases, fractions, fractions, fractions, path_weights)
    return made[0], made[1], made[2], path_weights, made[3]


def turn_kernel(classes, count, part, device_ref, bases_ref, seen_ref, *refs):
    outs, twice_ref, sems = refs[:-2], refs[-2], refs[-1]
    rows, cols = seen_ref.shape
    more = twice_ref.shape[0] - rows
    copies = [
        pltpu.make_async_copy(seen_ref, twice_ref.at[pl.ds(0, rows)], sems.at[0]),
        pltpu.make_async_copy(seen_ref.at[pl.ds(0, more)], twice_ref.at[pl.ds(rows, more)], sems.at[1]),
    ]
    for copy in copies:
        copy.start()
    for copy in copies:
        copy.wait()
    device = device_ref[0]
    base = bases_ref[device]
    my_class = device & (classes - 1)
    slices = count * PARTS

    def window(place, size, at):
        start = (place - base + 1 + rows) & (rows - 1)
        begin = pl.multiple_of(start & ~(BLOCK - 1), BLOCK)
        tall = size + BLOCK
        wide = twice_ref[pl.ds(begin, tall), at].astype(jnp.float32)
        return pltpu.roll(wide, (tall - (start - begin)) % tall, 0)

    for d in range(classes):
        place = (my_class ^ d) * slices + part * count

        @pl.loop(0, cols // WIDE)
        def _(chunk):
            at = pl.ds(pl.multiple_of(chunk * WIDE, WIDE), WIDE)
            outs[d][:, at] = window(place, count, at)[:count].astype(jnp.bfloat16)


def turn(device, bases, seen, classes, part):
    rows, cols = seen.shape
    count = rows // classes // PARTS
    return pl.pallas_call(
        functools.partial(turn_kernel, classes, count, part),
        in_specs=[
            pl.BlockSpec(memory_space=pltpu.SMEM),
            pl.BlockSpec(memory_space=pltpu.SMEM),
            pl.BlockSpec(memory_space=pl.ANY),
        ],
        out_specs=[pl.BlockSpec(memory_space=pltpu.VMEM)] * classes,
        out_shape=[jax.ShapeDtypeStruct((count, cols), seen.dtype)] * classes,
        scratch_shapes=[pltpu.VMEM((rows + count + BLOCK, cols), seen.dtype), pltpu.SemaphoreType.DMA((2,))],
        compiler_params=pltpu.CompilerParams(vmem_limit_bytes=32 * 2**20),
        name="turn_rows",
    )(device, bases, seen)


def plan_kernel(slots, planes, classes, angles, count, rows, device_ref, bases_ref, table_ref):
    shape = (2 * PARTS * classes, LANES)
    lane = lax.broadcasted_iota(jnp.int32, shape, 1)
    row = lax.broadcasted_iota(jnp.int32, shape, 0)
    class_shift = classes.bit_length() - 1
    base = jnp.broadcast_to(bases_ref[...], shape) - 1
    low_plane = base >> (rows.bit_length() - 1)
    turned = base & (rows - 1)

    def reach(which):
        lowest = low_plane + jnp.where(which * count + count - 1 < turned, 1, 0)
        highest = low_plane + jnp.where(which * count < turned, 1, 0)
        return lowest, highest

    lowest, highest = reach(row >> 1)
    upward = (row & 1) == 0
    source = lane >> class_shift
    at = jnp.where(upward, source, planes - 1 - source)
    to = jnp.where(lane < angles, jnp.where(upward, highest, planes - 1 - lowest), -1)
    key = to * CODE + (CODE - 1 - lane)
    sent = [jnp.full(shape, -1, jnp.int32) for _ in range(planes - 1)]
    for slot in range(slots):
        begin = at
        for link in range(planes - 1):
            ready = (begin == link) & (to > link)
            for n in range(LOAD):
                best = jnp.max(jnp.where(ready, key, -1), axis=1, keepdims=True)
                taken = ready & (key == best)
                at = jnp.where(taken, link + 1, at)
                ready = ready & (key != best)
                which = jnp.where(best >= 0, CODE - 1 - (best & (CODE - 1)), -1)
                sent[link] = jnp.where(lane == slot * LOAD + n, which, sent[link])

    me = device_ref[0]
    my_class = me & (classes - 1)
    plane = me >> class_shift
    none = jnp.full(shape, -1, jnp.int32)
    used = none
    for link in range(planes - 1):
        used = jnp.maximum(used, sent[link])
    used = jnp.max(used, axis=0, keepdims=True)
    head = lane[:1]
    total = jnp.max(jnp.where(used >= 0, head + 1, 0), axis=1, keepdims=True)

    tall = -(-max(slots * LOAD, angles) // 8) * 8
    sub = lax.broadcasted_iota(jnp.int32, (tall, LANES), 0)
    held = jnp.where(head < classes, plane * classes + (head ^ my_class), -1)
    for part in range(PARTS):
        low_here, high_here = reach(my_class * PARTS + part)
        wanted = (plane >= low_here) & (plane <= high_here) & (lane < angles)
        wanted = column_of(jnp.where(wanted, 1, 0)[:1], tall) > 0
        keep = lambda ids: jnp.max(jnp.where((sub == ids) & wanted, ids, -1), axis=0, keepdims=True)
        for way, spot in ((0, plane), (1, planes - 1 - plane)):
            sends, gets = none, none
            for link in range(planes - 1):
                sends = jnp.where(spot == link, sent[link], sends)
                gets = jnp.where(spot == link + 1, sent[link], gets)
            mine = row == 2 * (my_class * PARTS + part) + way
            sends = jnp.max(jnp.where(mine, sends, -1), axis=0, keepdims=True)
            gets = jnp.max(jnp.where(mine, gets, -1), axis=0, keepdims=True)
            arrived = jnp.max(jnp.where((column_of(gets, tall) == sends) & (sends >= 0), sub, 0), axis=0, keepdims=True)
            own = (sends >> class_shift) == plane
            index = jnp.where(own, (sends & (classes - 1)) ^ my_class, classes + arrived)
            line = part * LINES + way
            table_ref[line : line + 1] = jnp.where(sends >= 0, index, 0)
            table_ref[line + 2 : line + 3] = keep(gets)
        line = part * LINES + 4
        table_ref[line : line + 1] = keep(held)
    table_ref[PARTS * LINES : PARTS * LINES + 1] = jnp.broadcast_to(total, head.shape)


def choose_kernel(slot, part, load, own, ups, table_ref, *refs):
    sources, (*outs, sems) = refs[: own + 2 * ups], refs[own + 2 * ups :]
    arrived = sources[own : own + ups], sources[own + ups :]
    views = [spread_out(sources[:own], []) + [(own + n, v) for n, v in spread_out([], side)] for side in arrived]
    spots = [(way, n) for way in range(2) for n in range(load)]
    for way, n in spots:
        for m, view in views[way]:

            @pl.when(table_ref[part * LINES + way, slot * LOAD + n] == m)
            def _():
                pltpu.make_async_copy(view, outs[way].at[n], sems.at[way, n]).start()

    for way, n in spots:
        pltpu.make_async_copy(sources[0], outs[way].at[n], sems.at[way, n]).wait()


def choose(slot, part, load, table, own, ups, downs):
    anywhere = pl.BlockSpec(memory_space=pl.ANY)
    shape = jax.ShapeDtypeStruct((load,) + own[0].shape, own[0].dtype)
    return pl.pallas_call(
        functools.partial(choose_kernel, slot, part, load, len(own), len(ups)),
        in_specs=[pl.BlockSpec(memory_space=pltpu.SMEM)] + [anywhere] * (len(own) + 2 * len(ups)),
        out_specs=[pl.BlockSpec(memory_space=pltpu.VMEM)] * 2,
        out_shape=[shape, shape],
        scratch_shapes=[pltpu.SemaphoreType.DMA((2, load))],
        cost_estimate=pl.CostEstimate(flops=0, bytes_accessed=4 * load * own[0].size * 2, transcendentals=0),
        name="choose_packet",
    )(table, *own, *ups, *downs)


def on_device(volume, measured, path_weights, fractions, bases):
    slices, depth, cols = volume.shape
    local, rows = measured.shape[:2]
    nslab = lax.axis_size("slab")
    device = lax.axis_index("slab")
    angles = local * nslab
    first = device * slices
    classes = rows // slices
    planes = nslab // classes
    ups_of = lambda step: [(i, i + step) for i in range(nslab - step)]
    downs_of = lambda step: [(i + step, i) for i in range(nslab - step)]

    routed = local == 1 and classes == ROUTED_CLASSES and slices == LANES and rows & (rows - 1) == 0 and angles * HALF == LANES

    def dense(volume, measured, path_weights, fractions, bases):
        left = lax.ppermute(volume[slices - 1 :], "slab", ups_of(1))
        right = lax.ppermute(volume[:1], "slab", downs_of(1))
        share = lax.dynamic_slice_in_dim(jnp.pad(fractions, ((0, 0), (1, 1))), first, slices + 2, 1)
        tables = make_tables(share, first, rows, path_weights, bases, slices)
        my_bases = lax.dynamic_slice_in_dim(bases, device * local, local, 0)
        turned = jax.vmap(lambda m, b: jnp.roll(m, b - 1, axis=0))(measured, my_bases)
        by_class = turned.reshape(local, classes, slices, cols).transpose(1, 0, 2, 3)
        outgoing = jnp.tile(by_class, (planes, 1, 1, 1)).reshape(angles, slices, cols)
        seen = lax.all_to_all(outgoing, "slab", split_axis=0, concat_axis=0, tiled=True)
        ends = jnp.roll(by_class[:, :, slices - 1], 1, axis=0)
        ends = jnp.tile(ends, (planes, 1, 1)).reshape(angles, cols // LANES, LANES)
        edge = lax.all_to_all(ends, "slab", split_axis=0, concat_axis=0, tiled=True).reshape(angles, cols)
        return update(volume, left, right, edge, tables, [seen], jnp.zeros((8, LANES), jnp.int32), None, 0, 1, True)[0]

    if not routed:
        return dense(volume, measured, path_weights, fractions, bases)

    number = device.astype(jnp.int32)[None]
    upper, lower = PARTS - 1, 0
    exchange = lambda runs: [runs[0]] + [
        lax.ppermute(runs[d], "slab", [(i, i ^ d) for i in range(nslab)]) for d in range(1, classes)
    ]
    runs = turn(number, bases, measured[0], classes, upper)
    runs, late_bases, seen = lax.optimization_barrier((runs, bases, measured[0]))
    own = {upper: exchange(runs)}

    row_of_bases = jnp.pad(late_bases, (0, LANES - angles), constant_values=1)[None]
    most = -(-classes * (planes - 1) // LOAD) + planes - 2
    table = pl.pallas_call(
        functools.partial(plan_kernel, most, planes, classes, angles, slices // PARTS, rows),
        in_specs=[pl.BlockSpec(memory_space=pltpu.SMEM), pl.BlockSpec(memory_space=pltpu.VMEM)],
        out_shape=jax.ShapeDtypeStruct((16, LANES), jnp.int32),
        name="plan_slots",
    )(number, row_of_bases)
    need = table[PARTS * LINES, 0]
    ends = [5, 6, 7]
    which = jnp.sum(jnp.array([need > e for e in ends]).astype(jnp.int32))
    table, which, high = lax.optimization_barrier((table, which, volume[:1]))
    right = lax.ppermute(high, "slab", downs_of(1))
    runs = turn(number, bases, seen, classes, lower)
    tables = device_tables(number, row_of_bases, fractions, path_weights, rows, upper)
    arrived, runs, table, tables, right = lax.optimization_barrier((own[upper], runs, table, tables, right))

    def finish(end):
        def branch(arrived, runs, table, upper_tables, right):
            own = {upper: arrived, lower: exchange(runs)}
            ups, downs = {upper: [], lower: []}, {upper: [], lower: []}
            late = row_of_bases
            for slot in range(-(-end // LOAD)):
                load = min(LOAD, end - slot * LOAD)
                for part in (upper, lower):
                    go_up, go_down = choose(slot, part, load, table, own[part], ups[part], downs[part])
                    if slot == 0 and part == lower:
                        go_up, go_down, late = lax.optimization_barrier((go_up, go_down, late))
                        lower_tables = device_tables(number, late, fractions, path_weights, rows, lower)
                        mends = jnp.concatenate(
                            [t[-1][:1, :depth, angles * HALF :] for t in (lower_tables, upper_tables)]
                        )
                        table, lower_tables, mends = lax.optimization_barrier((table, lower_tables, mends))
                    ups[part].append(lax.ppermute(go_up, "slab", ups_of(classes)))
                    downs[part].append(lax.ppermute(go_down, "slab", downs_of(classes)))
            packets = {part: own[part] + ups[part] + downs[part] for part in (upper, lower)}
            args = (volume, right, right, jnp.zeros((angles, cols), volume.dtype))
            out, last = update(*args, upper_tables, packets[upper], table, None, upper, PARTS, False)
            first = lax.ppermute(last, "slab", ups_of(1))
            out, second = update(*args, lower_tables, packets[lower], table, out, lower, PARTS, False)
            return mend(out, mends, first, second)

        return branch

    others = lambda *_: dense(volume, measured, path_weights, fractions, bases)
    return lax.switch(which, [finish(e) for e in ends] + [others], arrived, runs, table, tables, right)


def solution(mesh):
    placed = (P(("groups", "slab"), None, None), P(("groups", "slab"), None, None), P(), P(), P())
    return jax.shard_map(
        on_device,
        mesh=mesh,
        in_specs=placed,
        out_specs=P(("groups", "slab"), None, None),
        check_vma=False,
    )
```

```python
import functools

import jax
import jax.numpy as jnp
from jax import lax
from jax.experimental import pallas as pl
from jax.experimental.pallas import tpu as pltpu
from jax.sharding import PartitionSpec as P

RELAX = 1.0
BLOCK = 16
HALF = 8
LANES = 128
WIDE = 256
PIECES = 4
PARTS = 2
ROUTED_CLASSES = 4
LOAD = 2
CODE = 256
LINES = 5
VMEM_LIMIT = 56 * 2**20


def dot(a, b):
    return jnp.dot(a, b, preferred_element_type=jnp.float32)


def widen(coef):
    return jnp.concatenate([coef] * (WIDE // LANES), axis=1)


def spread_out(own, arrived):
    views = list(enumerate(own))
    return views + [(s * LOAD + n, p.at[n]) for s, p in enumerate(arrived) for n in range(p.shape[0])]


def update_kernel(
    dense, part, table_ref, lower_ref, upper_ref, next_ref, right_ref, coef_ref, image_w_ref, weight_ref, spread_ref, *rest
):
    if dense:
        left_ref, edge_ref, edge_coef_ref, *rest = rest
    out_ref, carry_ref, seen_ref, result_ref, sems, out_sems = rest[-6:]
    packets = rest[:-7]
    block = pl.program_id(0)
    blocks = pl.num_programs(0)
    depth, width = lower_ref.shape[1:]
    angles = weight_ref.shape[0]
    first = part * blocks * BLOCK

    def fetch(at_block, act):
        slot = at_block % 2
        rows = pl.ds(pl.multiple_of(at_block * BLOCK, BLOCK), BLOCK)
        if dense:
            act(pltpu.make_async_copy(packets[0].at[:, rows], seen_ref.at[slot], sems.at[slot, 0]))
            return
        middle = (len(packets) - ROUTED_CLASSES) // 2 + ROUTED_CLASSES
        views = [(4, *v) for v in spread_out(packets[:ROUTED_CLASSES], [])]
        views += [(2, *v) for v in spread_out([], packets[ROUTED_CLASSES:middle])]
        views += [(3, *v) for v in spread_out([], packets[middle:])]
        for n, (line, spot, view) in enumerate(views):
            name = table_ref[part * LINES + line, spot]

            @pl.when(name >= 0)
            def _():
                act(pltpu.make_async_copy(view.at[rows], seen_ref.at[slot, name], sems.at[slot, n]))

    def deliver(at_block, act, pieces=range(PIECES)):
        slot = at_block % 2
        rows = pl.ds(first + at_block * BLOCK, BLOCK)
        for n in pieces:
            at = pl.ds(n * (width // PIECES), width // PIECES)
            act(pltpu.make_async_copy(result_ref.at[slot, :, :, at], out_ref.at[rows, :, at], out_sems.at[slot, n]))

    @pl.when(block == 0)
    def _():
        seen_ref[...] = jnp.zeros_like(seen_ref)
        fetch(block, lambda copy: copy.start())

    @pl.when(block + 1 < blocks)
    def _():
        fetch(block + 1, lambda copy: copy.start())

    @pl.when(block == 0)
    def _():
        if not dense:
            carry_ref[...] = jnp.zeros_like(carry_ref)
            return
        for chunk in range(width // WIDE):
            at = pl.ds(chunk * WIDE, WIDE)
            mine = dot(weight_ref[...], lower_ref[0, :, at])
            before = dot(weight_ref[...], left_ref[0, :, at])
            carry_ref[:, at] = (
                edge_ref[:, at].astype(jnp.float32) * widen(edge_coef_ref[2])
                - mine * widen(edge_coef_ref[0])
                - before * widen(edge_coef_ref[1])
            ).astype(jnp.bfloat16)

    @pl.when(block >= 2)
    def _():
        deliver(block - 2, lambda copy: copy.wait())

    fetch(block, lambda copy: copy.wait())
    slot = block % 2
    final = (block == blocks - 1) & (part == PARTS - 1 or dense)

    def columns(chunk):
        if dense:
            return pl.ds(pl.multiple_of(chunk * WIDE, WIDE), WIDE)
        return slice(chunk * WIDE, (chunk + 1) * WIDE)

    def image(chunk):
        at = columns(chunk)
        images = [dot(image_w_ref[...], r[:, :, at].reshape(HALF * depth, WIDE)) for r in (lower_ref, upper_ref)]
        after = dot(weight_ref[...], jnp.where(final, right_ref[0, :, at], next_ref[0, :, at]))
        return images, after

    def residual(chunk, images, after):
        at = columns(chunk)
        seen = seen_ref[slot, :, :, at].astype(jnp.float32)
        ahead = [pltpu.roll(x.reshape(angles, HALF, WIDE), HALF - 1, 1) for x in images]
        ahead.append(jnp.broadcast_to(after.reshape(angles, 1, WIDE), (angles, HALF, WIDE)))
        tail = lax.broadcasted_iota(jnp.int32, (angles, HALF, WIDE), 1) == HALF - 1
        parts = []
        for half in range(2):
            now = jnp.where(tail, ahead[half + 1], ahead[half]).reshape(angles * HALF, WIDE)
            got = seen[:, half * HALF : (half + 1) * HALF].reshape(angles * HALF, WIDE)
            coef = [widen(coef_ref[0, half, n]) for n in range(3)]
            resid = got * coef[2] - now * coef[0] - images[half] * coef[1]
            parts.append(resid.reshape(angles, HALF, WIDE))
        return parts

    def result(chunk, parts):
        at = columns(chunk)
        carry = carry_ref[:, at]
        for half, (resid, r) in enumerate(zip(parts, (lower_ref, upper_ref))):
            inputs = jnp.concatenate([resid.reshape(angles * HALF, WIDE).astype(jnp.bfloat16), carry])
            spread = dot(spread_ref[half], inputs).reshape(HALF, depth, WIDE)
            carry = resid[:, HALF - 1].astype(jnp.bfloat16)
            result_ref[slot, half * HALF : (half + 1) * HALF, :, at] = r[:, :, at].astype(jnp.float32) + spread
        carry_ref[:, at] = carry

    chunks = width // WIDE
    if dense:
        pl.loop(0, chunks)(lambda chunk: result(chunk, residual(chunk, *image(chunk))))
        deliver(block, lambda copy: copy.start())
    else:
        images, resids = {}, {}
        for n in range(chunks + 2):
            if n < chunks:
                images[n] = image(n)
            if 1 <= n <= chunks:
                resids[n - 1] = residual(n - 1, *images.pop(n - 1))
            if n >= 2:
                result(n - 2, resids.pop(n - 2))
                done = (n - 1) * PIECES
                if done % chunks == 0:
                    deliver(block, lambda copy: copy.start(), [done // chunks - 1])

    @pl.when(block == blocks - 1)
    def _():
        @pl.when(block >= 1)
        def _():
            deliver(block - 1, lambda copy: copy.wait())

        deliver(block, lambda copy: copy.wait())


def update(volume, right, tables, packets, table, before, part, parts, ahead=None):
    slices, depth, cols = volume.shape
    dense = ahead is not None
    blocks = slices // BLOCK // parts
    off = part * blocks
    by_block = lambda x: pl.BlockSpec((1,) + x.shape[1:], lambda b, i: (b,) + (0,) * (x.ndim - 1))
    whole = lambda x: pl.BlockSpec(x.shape, lambda b, i: (0,) * x.ndim)
    anywhere = pl.BlockSpec(memory_space=pl.ANY)
    coef, edge_coef, image_w, weights, spread_w = tables
    angles = weights.shape[0]
    ahead = [*ahead, edge_coef] if dense else []
    held = jax.ShapeDtypeStruct((angles, cols), volume.dtype)
    if before is None:
        before = coef
    aliases = {9 + len(ahead) + len(packets): 0} if before.shape == volume.shape else {}
    copies = LOAD * len(packets)
    one = (1, depth, cols)
    return pl.pallas_call(
        functools.partial(update_kernel, dense, part),
        grid_spec=pltpu.PrefetchScalarGridSpec(
            num_scalar_prefetch=1,
            grid=(blocks,),
            in_specs=[
                pl.BlockSpec((HALF, depth, cols), lambda b, i: (2 * (b + off), 0, 0)),
                pl.BlockSpec((HALF, depth, cols), lambda b, i: (2 * (b + off) + 1, 0, 0)),
                pl.BlockSpec(one, lambda b, i: (jnp.minimum((b + off + 1) * BLOCK, slices - 1), 0, 0)),
                whole(right), by_block(coef), whole(image_w), whole(weights),
                pl.BlockSpec((2,) + spread_w.shape[1:], lambda b, i: (b, 0, 0)),
            ]
            + [whole(x) for x in ahead]
            + [anywhere] * (len(packets) + 1),
            out_specs=[anywhere, whole(held)],
            scratch_shapes=[
                pltpu.VMEM((2, angles, BLOCK, cols), jnp.bfloat16),
                pltpu.VMEM((2, BLOCK, depth, cols), jnp.float32),
                pltpu.SemaphoreType.DMA((2, copies)),
                pltpu.SemaphoreType.DMA((2, PIECES)),
            ],
        ),
        out_shape=[jax.ShapeDtypeStruct(volume.shape, jnp.float32), held],
        input_output_aliases=aliases,
        compiler_params=pltpu.CompilerParams(dimension_semantics=("arbitrary",), vmem_limit_bytes=VMEM_LIMIT),
        cost_estimate=pl.CostEstimate(
            flops=4 * slices * depth * cols * angles // parts, bytes_accessed=volume.size * 7 // parts, transcendentals=0
        ),
        name="slab_update",
    )(
        table, volume, volume, volume, right, coef, image_w, weights, spread_w, *ahead, *packets, before
    )


def mend_kernel(lower_ref, upper_ref, first_ref, second_ref, before_ref, out_ref):
    columns = lower_ref.shape[2] - first_ref.shape[0]

    @pl.when(pl.program_id(0) == 0)
    def _():
        out_ref[0] = before_ref[0] + dot(lower_ref[0, :, columns:], first_ref[...])

    @pl.when(pl.program_id(0) == 1)
    def _():
        out_ref[0] = before_ref[0] + dot(upper_ref[0, :, columns:], second_ref[...])


def mend(out, lower, upper, first, second):
    slices, depth, cols = out.shape
    whole = pl.BlockSpec(first.shape, lambda b: (0, 0))
    weights = pl.BlockSpec((1, depth, lower.shape[2]), lambda b: (0, 0, 0))
    slab = pl.BlockSpec((1, depth, cols), lambda b: (b * (slices // 2), 0, 0))
    return pl.pallas_call(
        mend_kernel,
        grid=(2,),
        in_specs=[weights, weights, whole, whole, slab],
        out_specs=slab,
        out_shape=jax.ShapeDtypeStruct(out.shape, out.dtype),
        input_output_aliases={4: 0},
        name="mend_slices",
    )(lower, upper, first, second, out)


def fill_weights(wide_w, turned_w, pick_next, pick_now, pick_carry, spread_ref, half):
    depth, columns = wide_w.shape
    place = lax.broadcasted_iota(jnp.int32, (depth, columns), 1) % HALF
    from_next = wide_w * pick_next
    from_now = wide_w * pick_now
    from_carry = turned_w * pick_carry
    for z in range(HALF):
        row = jnp.where(place == z, from_next, jnp.where(place == z - 1, from_now, 0.0))
        total = jnp.sum(row, axis=1, keepdims=True)
        carry = jnp.zeros_like(from_carry)
        if z == 0:
            total = total + jnp.sum(from_carry, axis=1, keepdims=True)
            carry = from_carry
        scale = RELAX / total
        spread_ref[half, z * depth : (z + 1) * depth, :columns] = (row * scale).astype(jnp.bfloat16)
        spread_ref[half, z * depth : (z + 1) * depth, columns:] = (carry * scale).astype(jnp.bfloat16)


def weights_kernel(wide_w_ref, turned_w_ref, pick_ref, pick_carry_ref, spread_ref):
    picks = pick_ref[0, 0:1], pick_ref[0, 1:2], pick_carry_ref[0]
    fill_weights(wide_w_ref[...], turned_w_ref[...], *picks, spread_ref, 0)


def make_weights(wide_w, turned_w, pick, pick_carry):
    halves = pick.shape[0]
    depth, angles = turned_w.shape
    by_half = lambda shape: pl.BlockSpec((1,) + shape, lambda b: (b,) + (0,) * len(shape))
    whole = lambda x: pl.BlockSpec(x.shape, lambda b: (0,) * x.ndim)
    spread = (HALF * depth, angles * (HALF + 1))
    return pl.pallas_call(
        weights_kernel,
        grid=(halves,),
        in_specs=[whole(wide_w), whole(turned_w), by_half(pick.shape[1:]), by_half(pick_carry.shape[1:])],
        out_specs=by_half(spread),
        out_shape=jax.ShapeDtypeStruct((halves,) + spread, jnp.bfloat16),
        name="spread_weights",
    )(wide_w, turned_w, pick, pick_carry)


def make_tables(share, first, rows, path_weights, bases, slices):
    angles, depth = path_weights.shape
    blocks = slices // BLOCK
    weights = path_weights.astype(jnp.float32)
    ray_total = jnp.sum(weights, axis=1)[:, None]
    norm = 1.0 / (ray_total * ((1.0 - share[:, 1:]) + share[:, :-1]))
    coefs = jnp.stack([(1.0 - share[:, 1:]) * norm, share[:, :-1] * norm, norm])
    coef = coefs[:, :, 1:].reshape(3, angles, blocks, BLOCK // HALF, HALF).transpose(2, 3, 0, 1, 4)
    coef = coef.reshape(blocks, BLOCK // HALF, 3, angles * HALF, 1)
    coef = jnp.broadcast_to(coef, coef.shape[:4] + (LANES,))
    edge_coef = jnp.broadcast_to(coefs[:, :, :1], (3, angles, LANES))
    share_own = share[:, 1:-1]
    row_now = (first - bases)[:, None] + jnp.arange(slices, dtype=jnp.int32)[None, :]
    w_now = jnp.where((row_now >= 0) & (row_now < rows), 1.0 - share_own, 0.0)
    w_next = jnp.where((row_now + 1 >= 0) & (row_now + 1 < rows), share_own, 0.0)
    halves = slices // HALF
    pick = jnp.stack([w_next, jnp.pad(w_now[:, 1:], ((0, 0), (0, 1)))]).reshape(2, angles, halves, HALF)
    pick = pick.transpose(2, 0, 1, 3).reshape(halves, 2, angles * HALF)
    pick_carry = w_now[:, ::HALF].T[:, None, :]
    eye = jnp.eye(HALF, dtype=jnp.float32)
    image_w = jnp.einsum("ad,yz->ayzd", weights, eye).reshape(angles * HALF, HALF * depth).astype(jnp.bfloat16)
    wide_w = jnp.repeat(weights.T, HALF, axis=1)
    return coef, edge_coef, image_w, path_weights, make_weights(wide_w, weights.T, pick, pick_carry)


def column_of(line, tall):
    sub = lax.broadcasted_iota(jnp.int32, (tall, LANES), 0)
    lane = lax.broadcasted_iota(jnp.int32, (tall, LANES), 1)
    return jnp.max(jnp.where(sub == lane, line, -1), axis=1, keepdims=True)


def tables_kernel(
    rows, off, device_ref, bases_ref, before_ref, own_ref, after_ref, weight_ref,
    coef_ref, edge_coef_ref, image_w_ref, spread_ref, wide_ref, turned_ref,
):
    block = pl.program_id(0) + off
    angles, depth = weight_ref.shape
    first = device_ref[0] * LANES
    shape = (angles, LANES)
    lane = lax.broadcasted_iota(jnp.int32, shape, 1)
    sub = lax.broadcasted_iota(jnp.int32, shape, 0)
    weights = weight_ref[...].astype(jnp.float32)
    ray_total = jnp.sum(weights, axis=1, keepdims=True)
    own = own_ref[...]
    ahead = jnp.where(lane == LANES - 1, pltpu.roll(after_ref[...], LANES - 1, 1), pltpu.roll(own, LANES - 1, 1))
    norm = 1.0 / (ray_total * ((1.0 - ahead) + own))
    coefs = ((1.0 - ahead) * norm, own * norm, norm)
    spots = lax.broadcasted_iota(jnp.int32, (angles, HALF, LANES), 2) - lax.broadcasted_iota(jnp.int32, (angles, HALF, LANES), 1)
    for half in range(BLOCK // HALF):
        here = spots == block * BLOCK + half * HALF
        for n, coef in enumerate(coefs):
            tall = jnp.broadcast_to(coef.reshape(angles, 1, LANES), (angles, HALF, LANES))
            tall = jnp.sum(jnp.where(here, tall, 0.0), axis=2, keepdims=True)
            coef_ref[0, half, n] = jnp.broadcast_to(tall, (angles, HALF, LANES)).reshape(angles * HALF, LANES)

    @pl.when(block == off)
    def _():
        edge_own = jnp.sum(jnp.where(lane == 0, own, 0.0), axis=1, keepdims=True)
        edge_before = jnp.sum(jnp.where(lane == LANES - 1, before_ref[...], 0.0), axis=1, keepdims=True)
        edge_norm = 1.0 / (ray_total * ((1.0 - edge_own) + edge_before))
        for n, coef in enumerate(((1.0 - edge_own) * edge_norm, edge_before * edge_norm, edge_norm)):
            edge_coef_ref[n] = jnp.broadcast_to(coef, shape)
        across = (HALF * depth)
        repeat = lax.broadcasted_iota(jnp.int32, (depth, across), 1) % depth
        repeat = jnp.where(repeat == lax.broadcasted_iota(jnp.int32, (depth, across), 0), 1.0, 0.0)
        wide = dot(weight_ref[...], repeat.astype(jnp.bfloat16)).astype(jnp.bfloat16)
        down = angles * HALF
        expand = lax.broadcasted_iota(jnp.int32, (down, angles), 0) // HALF
        expand = jnp.where(expand == lax.broadcasted_iota(jnp.int32, (down, angles), 1), 1.0, 0.0)
        wide = dot(expand.astype(jnp.bfloat16), wide)
        at = lax.broadcasted_iota(jnp.int32, (down, across), 0) % HALF
        same = lax.broadcasted_iota(jnp.int32, (down, across), 1) // depth == at
        image_w_ref[...] = jnp.where(same, wide, 0.0).astype(jnp.bfloat16)

    row_now = first + lane - column_of(bases_ref[...], angles)
    w_now = jnp.where((row_now >= 0) & (row_now < rows), 1.0 - own, 0.0)
    w_next = jnp.where((row_now + 1 >= 0) & (row_now + 1 < rows), own, 0.0)
    columns = angles * HALF
    mine = lax.broadcasted_iota(jnp.int32, (angles, columns), 1) // HALF
    mine = mine == lax.broadcasted_iota(jnp.int32, (angles, columns), 0)
    square = lax.broadcasted_iota(jnp.int32, (angles, angles), 0) == lax.broadcasted_iota(jnp.int32, (angles, angles), 1)

    def gather(values, start, count):
        near = jnp.where(lane < count, pltpu.roll(values, (2 * LANES - start) % LANES, 1), 0.0)
        step = HALF
        while step < LANES:
            near = near + pltpu.roll(near, step, 1)
            step *= 2
        return jnp.sum(jnp.where(mine, near, 0.0), axis=0, keepdims=True)

    turned = lambda other: lax.dot_general(
        weights, other, (((0,), (0,)), ((), ())), precision=lax.Precision.HIGHEST, preferred_element_type=jnp.float32
    )

    @pl.when(block == off)
    def _():
        wide_ref[...] = turned(jnp.where(mine, 1.0, 0.0))
        turned_ref[...] = turned(jnp.where(square, 1.0, 0.0))

    for half in range(BLOCK // HALF):
        start = block * BLOCK + half * HALF
        pick_next = gather(w_next, start, HALF)
        pick_now = gather(w_now, start + 1, HALF - 1)
        carry = jnp.sum(jnp.where(lane == start, w_now, 0.0), axis=1, keepdims=True)
        pick_carry = jnp.sum(jnp.where(square, carry, 0.0), axis=0, keepdims=True)
        fill_weights(wide_ref[...], turned_ref[...], pick_next, pick_now, pick_carry, spread_ref, half)


def device_tables(device, row_of_bases, fractions, path_weights, rows, part):
    angles, depth = path_weights.shape
    blocks = LANES // BLOCK // PARTS
    last = fractions.shape[1] // LANES - 1
    column = lambda by: pl.BlockSpec((angles, LANES), lambda b, d: (0, jnp.clip(d[0] + by, 0, last)))
    whole = lambda shape: pl.BlockSpec(shape, lambda b, d: (0,) * len(shape))
    by_block = lambda shape: pl.BlockSpec((1,) + shape, lambda b, d: (b,) + (0,) * len(shape))
    coef = (BLOCK // HALF, 3, angles * HALF, LANES)
    edge_coef = (3, angles, LANES)
    image_w = (angles * HALF, HALF * depth)
    spread = (HALF * depth, angles * (HALF + 1))
    made = pl.pallas_call(
        functools.partial(tables_kernel, rows, part * blocks),
        grid_spec=pltpu.PrefetchScalarGridSpec(
            num_scalar_prefetch=1,
            grid=(blocks,),
            in_specs=[whole((1, LANES)), column(-1), column(0), column(1), whole(path_weights.shape)],
            out_specs=[
                by_block(coef), whole(edge_coef), whole(image_w),
                pl.BlockSpec((2,) + spread, lambda b, d: (b, 0, 0)),
            ],
            scratch_shapes=[
                pltpu.VMEM((depth, angles * HALF), jnp.float32),
                pltpu.VMEM((depth, angles), jnp.float32),
            ],
        ),
        out_shape=[
            jax.ShapeDtypeStruct((blocks,) + coef, jnp.float32),
            jax.ShapeDtypeStruct(edge_coef, jnp.float32),
            jax.ShapeDtypeStruct(image_w, jnp.bfloat16),
            jax.ShapeDtypeStruct((2 * blocks,) + spread, jnp.bfloat16),
        ],
        name="make_tables",
    )(device, row_of_bases, fractions, fractions, fractions, path_weights)
    return made[0], made[1], made[2], path_weights, made[3]


def turn_kernel(classes, count, device_ref, bases_ref, seen_ref, *refs):
    outs, twice_ref, sems = refs[:-2], refs[-2], refs[-1]
    rows, cols = seen_ref.shape
    more = twice_ref.shape[0] - rows
    copies = [
        pltpu.make_async_copy(seen_ref, twice_ref.at[pl.ds(0, rows)], sems.at[0]),
        pltpu.make_async_copy(seen_ref.at[pl.ds(0, more)], twice_ref.at[pl.ds(rows, more)], sems.at[1]),
    ]
    for copy in copies:
        copy.start()
    for copy in copies:
        copy.wait()
    device = device_ref[0]
    base = bases_ref[device]
    my_class = device & (classes - 1)
    slices = count * PARTS

    def window(place, size, at):
        start = (place - base + 1 + rows) & (rows - 1)
        begin = pl.multiple_of(start & ~(BLOCK - 1), BLOCK)
        tall = size + BLOCK
        wide = twice_ref[pl.ds(begin, tall), at].astype(jnp.float32)
        return pltpu.roll(wide, (tall - (start - begin)) % tall, 0)

    for n, out in enumerate(outs):
        place = (my_class ^ (n // PARTS)) * slices + n % PARTS * count

        @pl.loop(0, cols // WIDE)
        def _(chunk):
            at = pl.ds(pl.multiple_of(chunk * WIDE, WIDE), WIDE)
            out[:, at] = window(place, count, at)[:count].astype(jnp.bfloat16)


def turn(device, bases, seen, classes):
    rows, cols = seen.shape
    count = rows // classes // PARTS
    return pl.pallas_call(
        functools.partial(turn_kernel, classes, count),
        in_specs=[
            pl.BlockSpec(memory_space=pltpu.SMEM),
            pl.BlockSpec(memory_space=pltpu.SMEM),
            pl.BlockSpec(memory_space=pl.ANY),
        ],
        out_specs=[pl.BlockSpec(memory_space=pltpu.VMEM)] * (classes * PARTS),
        out_shape=[jax.ShapeDtypeStruct((count, cols), seen.dtype)] * (classes * PARTS),
        scratch_shapes=[pltpu.VMEM((rows + count + BLOCK, cols), seen.dtype), pltpu.SemaphoreType.DMA((2,))],
        compiler_params=pltpu.CompilerParams(vmem_limit_bytes=32 * 2**20),
        name="turn_rows",
    )(device, bases, seen)


def plan_kernel(slots, planes, classes, angles, count, rows, ends, device_ref, bases_ref, table_ref, which_ref):
    shape = (2 * PARTS * classes, LANES)
    lane = lax.broadcasted_iota(jnp.int32, shape, 1)
    row = lax.broadcasted_iota(jnp.int32, shape, 0)
    class_shift = classes.bit_length() - 1
    base = jnp.broadcast_to(bases_ref[...], shape) - 1
    low_plane = base >> (rows.bit_length() - 1)
    turned = base & (rows - 1)

    def reach(which):
        lowest = low_plane + jnp.where(which * count + count - 1 < turned, 1, 0)
        highest = low_plane + jnp.where(which * count < turned, 1, 0)
        return lowest, highest

    lowest, highest = reach(row >> 1)
    upward = (row & 1) == 0
    source = lane >> class_shift
    at = jnp.where(upward, source, planes - 1 - source)
    to = jnp.where(lane < angles, jnp.where(upward, highest, planes - 1 - lowest), -1)
    key = to * CODE + (CODE - 1 - lane)
    sent = [jnp.full(shape, -1, jnp.int32) for _ in range(planes - 1)]
    for slot in range(slots):
        begin = at
        for link in range(planes - 1):
            ready = (begin == link) & (to > link)
            for n in range(LOAD):
                best = jnp.max(jnp.where(ready, key, -1), axis=1, keepdims=True)
                taken = ready & (key == best)
                at = jnp.where(taken, link + 1, at)
                ready = ready & (key != best)
                which = jnp.where(best >= 0, CODE - 1 - (best & (CODE - 1)), -1)
                sent[link] = jnp.where(lane == slot * LOAD + n, which, sent[link])

    me = device_ref[0]
    my_class = me & (classes - 1)
    plane = me >> class_shift
    none = jnp.full(shape, -1, jnp.int32)
    used = none
    for link in range(planes - 1):
        used = jnp.maximum(used, sent[link])
    used = jnp.max(used, axis=0, keepdims=True)
    head = lane[:1]
    need = jnp.max(jnp.where(used >= 0, head + 1, 0))
    which_ref[0] = sum(jnp.where(need > end, 1, 0) for end in ends)

    tall = -(-max(slots * LOAD, angles) // 8) * 8
    sub = lax.broadcasted_iota(jnp.int32, (tall, LANES), 0)
    held = jnp.where(head < classes, plane * classes + (head ^ my_class), -1)
    for part in range(PARTS):
        low_here, high_here = reach(my_class * PARTS + part)
        wanted = (plane >= low_here) & (plane <= high_here) & (lane < angles)
        wanted = column_of(jnp.where(wanted, 1, 0)[:1], tall) > 0
        keep = lambda ids: jnp.max(jnp.where((sub == ids) & wanted, ids, -1), axis=0, keepdims=True)
        for way, spot in ((0, plane), (1, planes - 1 - plane)):
            sends, gets = none, none
            for link in range(planes - 1):
                sends = jnp.where(spot == link, sent[link], sends)
                gets = jnp.where(spot == link + 1, sent[link], gets)
            mine = row == 2 * (my_class * PARTS + part) + way
            sends = jnp.max(jnp.where(mine, sends, -1), axis=0, keepdims=True)
            gets = jnp.max(jnp.where(mine, gets, -1), axis=0, keepdims=True)
            arrived = jnp.max(jnp.where((column_of(gets, tall) == sends) & (sends >= 0), sub, 0), axis=0, keepdims=True)
            own = (sends >> class_shift) == plane
            index = jnp.where(own, (sends & (classes - 1)) ^ my_class, classes + arrived)
            line = part * LINES + way
            table_ref[line : line + 1] = jnp.where(sends >= 0, index, 0)
            table_ref[line + 2 : line + 3] = keep(gets)
        line = part * LINES + 4
        table_ref[line : line + 1] = keep(held)


def choose_kernel(slot, part, load, own, ups, table_ref, *refs):
    sources, (*outs, sems) = refs[: own + 2 * ups], refs[own + 2 * ups :]
    arrived = sources[own : own + ups], sources[own + ups :]
    views = [spread_out(sources[:own], []) + [(own + n, v) for n, v in spread_out([], side)] for side in arrived]
    spots = [(way, n) for way in range(2) for n in range(load)]
    for way, n in spots:
        for m, view in views[way]:

            @pl.when(table_ref[part * LINES + way, slot * LOAD + n] == m)
            def _():
                pltpu.make_async_copy(view, outs[way].at[n], sems.at[way, n]).start()

    for way, n in spots:
        pltpu.make_async_copy(sources[0], outs[way].at[n], sems.at[way, n]).wait()


def choose(slot, part, load, table, own, ups, downs):
    anywhere = pl.BlockSpec(memory_space=pl.ANY)
    shape = jax.ShapeDtypeStruct((load,) + own[0].shape, own[0].dtype)
    return pl.pallas_call(
        functools.partial(choose_kernel, slot, part, load, len(own), len(ups)),
        in_specs=[pl.BlockSpec(memory_space=pltpu.SMEM)] + [anywhere] * (len(own) + 2 * len(ups)),
        out_specs=[pl.BlockSpec(memory_space=pltpu.VMEM)] * 2,
        out_shape=[shape, shape],
        scratch_shapes=[pltpu.SemaphoreType.DMA((2, load))],
        cost_estimate=pl.CostEstimate(flops=0, bytes_accessed=4 * load * own[0].size * 2, transcendentals=0),
        name="choose_packet",
    )(table, *own, *ups, *downs)


def on_device(volume, measured, path_weights, fractions, bases):
    slices, depth, cols = volume.shape
    local, rows = measured.shape[:2]
    nslab = lax.axis_size("slab")
    device = lax.axis_index("slab")
    angles = local * nslab
    first = device * slices
    classes = rows // slices
    planes = nslab // classes
    ups_of = lambda step: [(i, i + step) for i in range(nslab - step)]
    downs_of = lambda step: [(i + step, i) for i in range(nslab - step)]

    routed = local == 1 and classes == ROUTED_CLASSES and slices == LANES and rows & (rows - 1) == 0 and angles * HALF == LANES

    def dense(volume, measured, path_weights, fractions, bases):
        left = lax.ppermute(volume[slices - 1 :], "slab", ups_of(1))
        right = lax.ppermute(volume[:1], "slab", downs_of(1))
        share = lax.dynamic_slice_in_dim(jnp.pad(fractions, ((0, 0), (1, 1))), first, slices + 2, 1)
        tables = make_tables(share, first, rows, path_weights, bases, slices)
        my_bases = lax.dynamic_slice_in_dim(bases, device * local, local, 0)
        turned = jax.vmap(lambda m, b: jnp.roll(m, b - 1, axis=0))(measured, my_bases)
        by_class = turned.reshape(local, classes, slices, cols).transpose(1, 0, 2, 3)
        outgoing = jnp.tile(by_class, (planes, 1, 1, 1)).reshape(angles, slices, cols)
        seen = lax.all_to_all(outgoing, "slab", split_axis=0, concat_axis=0, tiled=True)
        ends = jnp.roll(by_class[:, :, slices - 1], 1, axis=0)
        ends = jnp.tile(ends, (planes, 1, 1)).reshape(angles, cols // LANES, LANES)
        edge = lax.all_to_all(ends, "slab", split_axis=0, concat_axis=0, tiled=True).reshape(angles, cols)
        return update(volume, right, tables, [seen], jnp.zeros((8, LANES), jnp.int32), None, 0, 1, (left, edge))[0]

    if not routed:
        return dense(volume, measured, path_weights, fractions, bases)

    number = device.astype(jnp.int32)[None]
    upper, lower = PARTS - 1, 0
    exchange = lambda runs: [runs[0]] + [
        lax.ppermute(runs[d], "slab", [(i, i ^ d) for i in range(nslab)]) for d in range(1, classes)
    ]
    runs = turn(number, bases, measured[0], classes)
    runs, late_bases = lax.optimization_barrier((runs, bases))
    own = {upper: exchange(runs[upper::PARTS])}

    row_of_bases = jnp.pad(late_bases, (0, LANES - angles), constant_values=1)[None]
    most = -(-classes * (planes - 1) // LOAD) + planes - 2
    ends = [5, 6, 7]
    table, which = pl.pallas_call(
        functools.partial(plan_kernel, most, planes, classes, angles, slices // PARTS, rows, ends),
        in_specs=[pl.BlockSpec(memory_space=pltpu.SMEM), pl.BlockSpec(memory_space=pltpu.VMEM)],
        out_specs=[pl.BlockSpec(memory_space=pltpu.VMEM), pl.BlockSpec(memory_space=pltpu.SMEM)],
        out_shape=[jax.ShapeDtypeStruct((16, LANES), jnp.int32), jax.ShapeDtypeStruct((1,), jnp.int32)],
        name="plan_slots",
    )(number, row_of_bases)
    table, which, high = lax.optimization_barrier((table, which, volume[:1]))
    right = lax.ppermute(high, "slab", downs_of(1))
    tables = device_tables(number, row_of_bases, fractions, path_weights, rows, upper)
    arrived, runs, table, tables, right = lax.optimization_barrier((own[upper], runs[lower::PARTS], table, tables, right))

    def finish(end):
        def branch(arrived, runs, table, upper_tables, right):
            own = {upper: arrived, lower: exchange(runs)}
            ups, downs = {upper: [], lower: []}, {upper: [], lower: []}
            late = row_of_bases
            for slot in range(-(-end // LOAD)):
                load = min(LOAD, end - slot * LOAD)
                for part in (upper, lower):
                    go_up, go_down = choose(slot, part, load, table, own[part], ups[part], downs[part])
                    if slot == 1 and part == lower:
                        go_up, go_down, late = lax.optimization_barrier((go_up, go_down, late))
                        lower_tables = device_tables(number, late, fractions, path_weights, rows, lower)
                        table, lower_tables = lax.optimization_barrier((table, lower_tables))
                    ups[part].append(lax.ppermute(go_up, "slab", ups_of(classes)))
                    downs[part].append(lax.ppermute(go_down, "slab", downs_of(classes)))
            packets = {part: own[part] + ups[part] + downs[part] for part in (upper, lower)}
            out, last = update(volume, right, upper_tables, packets[upper], table, None, upper, PARTS)
            first = lax.ppermute(last, "slab", ups_of(1))
            out, second = update(volume, right, lower_tables, packets[lower], table, out, lower, PARTS)
            return mend(out, lower_tables[-1], upper_tables[-1], first, second)

        return branch

    others = lambda *_: dense(volume, measured, path_weights, fractions, bases)
    return lax.switch(which[0], [finish(e) for e in ends] + [others], arrived, runs, table, tables, right)


def solution(mesh):
    placed = (P(("groups", "slab"), None, None), P(("groups", "slab"), None, None), P(), P(), P())
    return jax.shard_map(
        on_device,
        mesh=mesh,
        in_specs=placed,
        out_specs=P(("groups", "slab"), None, None),
        check_vma=False,
    )
```

```python
import functools

import jax
import jax.numpy as jnp
from jax import lax
from jax.experimental import pallas as pl
from jax.experimental.pallas import tpu as pltpu
from jax.sharding import PartitionSpec as P

RELAX = 1.0
BLOCK = 16
HALF = 8
LANES = 128
WIDE = 256
PIECES = 4
PARTS = 2
ROUTED_CLASSES = 4
LOAD = 2
CODE = 256
LINES = 5
VMEM_LIMIT = 56 * 2**20


def dot(a, b):
    return jnp.dot(a, b, preferred_element_type=jnp.float32)


def widen(coef):
    return jnp.concatenate([coef] * (WIDE // LANES), axis=1)


def spread_out(own, arrived):
    views = list(enumerate(own))
    return views + [(s * LOAD + n, p.at[n]) for s, p in enumerate(arrived) for n in range(p.shape[0])]


def update_kernel(
    dense, part, table_ref, lower_ref, upper_ref, next_ref, right_ref, coef_ref, image_w_ref, weight_ref, spread_ref, *rest
):
    if dense:
        left_ref, edge_ref, edge_coef_ref, *rest = rest
    out_ref, carry_ref, seen_ref, result_ref, sems, out_sems = rest[-6:]
    packets = rest[:-7]
    block = pl.program_id(0)
    blocks = pl.num_programs(0)
    depth, width = lower_ref.shape[1:]
    angles = weight_ref.shape[0]
    first = part * blocks * BLOCK

    def fetch(at_block, act):
        slot = at_block % 2
        rows = pl.ds(pl.multiple_of(at_block * BLOCK, BLOCK), BLOCK)
        if dense:
            act(pltpu.make_async_copy(packets[0].at[:, rows], seen_ref.at[slot], sems.at[slot, 0]))
            return
        middle = (len(packets) - ROUTED_CLASSES) // 2 + ROUTED_CLASSES
        views = [(4, *v) for v in spread_out(packets[:ROUTED_CLASSES], [])]
        views += [(2, *v) for v in spread_out([], packets[ROUTED_CLASSES:middle])]
        views += [(3, *v) for v in spread_out([], packets[middle:])]
        for n, (line, spot, view) in enumerate(views):
            name = table_ref[part * LINES + line, spot]

            @pl.when(name >= 0)
            def _():
                act(pltpu.make_async_copy(view.at[rows], seen_ref.at[slot, name], sems.at[slot, n]))

    def deliver(at_block, act, pieces=range(PIECES)):
        slot = at_block % 2
        rows = pl.ds(first + at_block * BLOCK, BLOCK)
        for n in pieces:
            at = pl.ds(n * (width // PIECES), width // PIECES)
            act(pltpu.make_async_copy(result_ref.at[slot, :, :, at], out_ref.at[rows, :, at], out_sems.at[slot, n]))

    @pl.when(block == 0)
    def _():
        seen_ref[...] = jnp.zeros_like(seen_ref)
        fetch(block, lambda copy: copy.start())

    @pl.when(block + 1 < blocks)
    def _():
        fetch(block + 1, lambda copy: copy.start())

    @pl.when(block == 0)
    def _():
        if not dense:
            carry_ref[...] = jnp.zeros_like(carry_ref)
            return
        for chunk in range(width // WIDE):
            at = pl.ds(chunk * WIDE, WIDE)
            mine = dot(weight_ref[...], lower_ref[0, :, at])
            before = dot(weight_ref[...], left_ref[0, :, at])
            carry_ref[:, at] = (
                edge_ref[:, at].astype(jnp.float32) * widen(edge_coef_ref[2])
                - mine * widen(edge_coef_ref[0])
                - before * widen(edge_coef_ref[1])
            ).astype(jnp.bfloat16)

    @pl.when(block >= 2)
    def _():
        deliver(block - 2, lambda copy: copy.wait())

    fetch(block, lambda copy: copy.wait())
    slot = block % 2
    final = (block == blocks - 1) & (part == PARTS - 1 or dense)

    def columns(chunk):
        if dense:
            return pl.ds(pl.multiple_of(chunk * WIDE, WIDE), WIDE)
        return slice(chunk * WIDE, (chunk + 1) * WIDE)

    def image(chunk):
        at = columns(chunk)
        images = [dot(image_w_ref[...], r[:, :, at].reshape(HALF * depth, WIDE)) for r in (lower_ref, upper_ref)]
        after = dot(weight_ref[...], jnp.where(final, right_ref[0, :, at], next_ref[0, :, at]))
        return images, after

    def residual(chunk, images, after):
        at = columns(chunk)
        seen = seen_ref[slot, :, :, at].astype(jnp.float32)
        ahead = [pltpu.roll(x.reshape(angles, HALF, WIDE), HALF - 1, 1) for x in images]
        ahead.append(jnp.broadcast_to(after.reshape(angles, 1, WIDE), (angles, HALF, WIDE)))
        tail = lax.broadcasted_iota(jnp.int32, (angles, HALF, WIDE), 1) == HALF - 1
        parts = []
        for half in range(2):
            now = jnp.where(tail, ahead[half + 1], ahead[half]).reshape(angles * HALF, WIDE)
            got = seen[:, half * HALF : (half + 1) * HALF].reshape(angles * HALF, WIDE)
            coef = [widen(coef_ref[0, half, n]) for n in range(3)]
            resid = got * coef[2] - now * coef[0] - images[half] * coef[1]
            parts.append(resid.reshape(angles, HALF, WIDE))
        return parts

    def result(chunk, parts):
        at = columns(chunk)
        carry = carry_ref[:, at]
        for half, (resid, r) in enumerate(zip(parts, (lower_ref, upper_ref))):
            inputs = jnp.concatenate([resid.reshape(angles * HALF, WIDE).astype(jnp.bfloat16), carry])
            spread = dot(spread_ref[half], inputs).reshape(HALF, depth, WIDE)
            carry = resid[:, HALF - 1].astype(jnp.bfloat16)
            result_ref[slot, half * HALF : (half + 1) * HALF, :, at] = r[:, :, at].astype(jnp.float32) + spread
        carry_ref[:, at] = carry

    chunks = width // WIDE
    if dense:
        pl.loop(0, chunks)(lambda chunk: result(chunk, residual(chunk, *image(chunk))))
        deliver(block, lambda copy: copy.start())
    else:
        images, resids = {}, {}
        for n in range(chunks + 2):
            if n < chunks:
                images[n] = image(n)
            if 1 <= n <= chunks:
                resids[n - 1] = residual(n - 1, *images.pop(n - 1))
            if n >= 2:
                result(n - 2, resids.pop(n - 2))
                done = (n - 1) * PIECES
                if done % chunks == 0:
                    deliver(block, lambda copy: copy.start(), [done // chunks - 1])

    @pl.when(block == blocks - 1)
    def _():
        @pl.when(block >= 1)
        def _():
            deliver(block - 1, lambda copy: copy.wait())

        deliver(block, lambda copy: copy.wait())


def update(volume, right, tables, packets, table, before, part, parts, ahead=None):
    slices, depth, cols = volume.shape
    dense = ahead is not None
    blocks = slices // BLOCK // parts
    off = part * blocks
    by_block = lambda x: pl.BlockSpec((1,) + x.shape[1:], lambda b, i: (b,) + (0,) * (x.ndim - 1))
    whole = lambda x: pl.BlockSpec(x.shape, lambda b, i: (0,) * x.ndim)
    anywhere = pl.BlockSpec(memory_space=pl.ANY)
    coef, edge_coef, image_w, weights, spread_w = tables
    angles = weights.shape[0]
    ahead = [*ahead, edge_coef] if dense else []
    held = jax.ShapeDtypeStruct((angles, cols), volume.dtype)
    if before is None:
        before = coef
    aliases = {9 + len(ahead) + len(packets): 0} if before.shape == volume.shape else {}
    copies = LOAD * len(packets)
    one = (1, depth, cols)
    return pl.pallas_call(
        functools.partial(update_kernel, dense, part),
        grid_spec=pltpu.PrefetchScalarGridSpec(
            num_scalar_prefetch=1,
            grid=(blocks,),
            in_specs=[
                pl.BlockSpec((HALF, depth, cols), lambda b, i: (2 * (b + off), 0, 0)),
                pl.BlockSpec((HALF, depth, cols), lambda b, i: (2 * (b + off) + 1, 0, 0)),
                pl.BlockSpec(one, lambda b, i: (jnp.minimum((b + off + 1) * BLOCK, slices - 1), 0, 0)),
                whole(right), by_block(coef), whole(image_w), whole(weights),
                pl.BlockSpec((2,) + spread_w.shape[1:], lambda b, i: (b, 0, 0)),
            ]
            + [whole(x) for x in ahead]
            + [anywhere] * (len(packets) + 1),
            out_specs=[anywhere, whole(held)],
            scratch_shapes=[
                pltpu.VMEM((2, angles, BLOCK, cols), jnp.bfloat16),
                pltpu.VMEM((2, BLOCK, depth, cols), jnp.float32),
                pltpu.SemaphoreType.DMA((2, copies)),
                pltpu.SemaphoreType.DMA((2, PIECES)),
            ],
        ),
        out_shape=[jax.ShapeDtypeStruct(volume.shape, jnp.float32), held],
        input_output_aliases=aliases,
        compiler_params=pltpu.CompilerParams(dimension_semantics=("arbitrary",), vmem_limit_bytes=VMEM_LIMIT),
        cost_estimate=pl.CostEstimate(
            flops=4 * slices * depth * cols * angles // parts, bytes_accessed=volume.size * 7 // parts, transcendentals=0
        ),
        name="slab_update",
    )(
        table, volume, volume, volume, right, coef, image_w, weights, spread_w, *ahead, *packets, before
    )


def mend_kernel(lower_ref, upper_ref, first_ref, second_ref, before_ref, out_ref):
    columns = lower_ref.shape[2] - first_ref.shape[0]

    @pl.when(pl.program_id(0) == 0)
    def _():
        out_ref[0] = before_ref[0] + dot(lower_ref[0, :, columns:], first_ref[...])

    @pl.when(pl.program_id(0) == 1)
    def _():
        out_ref[0] = before_ref[0] + dot(upper_ref[0, :, columns:], second_ref[...])


def mend(out, lower, upper, first, second):
    slices, depth, cols = out.shape
    whole = pl.BlockSpec(first.shape, lambda b: (0, 0))
    weights = pl.BlockSpec((1, depth, lower.shape[2]), lambda b: (0, 0, 0))
    slab = pl.BlockSpec((1, depth, cols), lambda b: (b * (slices // 2), 0, 0))
    return pl.pallas_call(
        mend_kernel,
        grid=(2,),
        in_specs=[weights, weights, whole, whole, slab],
        out_specs=slab,
        out_shape=jax.ShapeDtypeStruct(out.shape, out.dtype),
        input_output_aliases={4: 0},
        name="mend_slices",
    )(lower, upper, first, second, out)


def fill_weights(wide_w, turned_w, pick_next, pick_now, pick_carry, spread_ref, half):
    depth, columns = wide_w.shape
    place = lax.broadcasted_iota(jnp.int32, (depth, columns), 1) % HALF
    from_next = wide_w * pick_next
    from_now = wide_w * pick_now
    from_carry = turned_w * pick_carry
    for z in range(HALF):
        row = jnp.where(place == z, from_next, jnp.where(place == z - 1, from_now, 0.0))
        total = jnp.sum(row, axis=1, keepdims=True)
        carry = jnp.zeros_like(from_carry)
        if z == 0:
            total = total + jnp.sum(from_carry, axis=1, keepdims=True)
            carry = from_carry
        scale = RELAX / total
        spread_ref[half, z * depth : (z + 1) * depth, :columns] = (row * scale).astype(jnp.bfloat16)
        spread_ref[half, z * depth : (z + 1) * depth, columns:] = (carry * scale).astype(jnp.bfloat16)


def weights_kernel(wide_w_ref, turned_w_ref, pick_ref, pick_carry_ref, spread_ref):
    picks = pick_ref[0, 0:1], pick_ref[0, 1:2], pick_carry_ref[0]
    fill_weights(wide_w_ref[...], turned_w_ref[...], *picks, spread_ref, 0)


def make_weights(wide_w, turned_w, pick, pick_carry):
    halves = pick.shape[0]
    depth, angles = turned_w.shape
    by_half = lambda shape: pl.BlockSpec((1,) + shape, lambda b: (b,) + (0,) * len(shape))
    whole = lambda x: pl.BlockSpec(x.shape, lambda b: (0,) * x.ndim)
    spread = (HALF * depth, angles * (HALF + 1))
    return pl.pallas_call(
        weights_kernel,
        grid=(halves,),
        in_specs=[whole(wide_w), whole(turned_w), by_half(pick.shape[1:]), by_half(pick_carry.shape[1:])],
        out_specs=by_half(spread),
        out_shape=jax.ShapeDtypeStruct((halves,) + spread, jnp.bfloat16),
        name="spread_weights",
    )(wide_w, turned_w, pick, pick_carry)


def make_tables(share, first, rows, path_weights, bases, slices):
    angles, depth = path_weights.shape
    blocks = slices // BLOCK
    weights = path_weights.astype(jnp.float32)
    ray_total = jnp.sum(weights, axis=1)[:, None]
    norm = 1.0 / (ray_total * ((1.0 - share[:, 1:]) + share[:, :-1]))
    coefs = jnp.stack([(1.0 - share[:, 1:]) * norm, share[:, :-1] * norm, norm])
    coef = coefs[:, :, 1:].reshape(3, angles, blocks, BLOCK // HALF, HALF).transpose(2, 3, 0, 1, 4)
    coef = coef.reshape(blocks, BLOCK // HALF, 3, angles * HALF, 1)
    coef = jnp.broadcast_to(coef, coef.shape[:4] + (LANES,))
    edge_coef = jnp.broadcast_to(coefs[:, :, :1], (3, angles, LANES))
    share_own = share[:, 1:-1]
    row_now = (first - bases)[:, None] + jnp.arange(slices, dtype=jnp.int32)[None, :]
    w_now = jnp.where((row_now >= 0) & (row_now < rows), 1.0 - share_own, 0.0)
    w_next = jnp.where((row_now + 1 >= 0) & (row_now + 1 < rows), share_own, 0.0)
    halves = slices // HALF
    pick = jnp.stack([w_next, jnp.pad(w_now[:, 1:], ((0, 0), (0, 1)))]).reshape(2, angles, halves, HALF)
    pick = pick.transpose(2, 0, 1, 3).reshape(halves, 2, angles * HALF)
    pick_carry = w_now[:, ::HALF].T[:, None, :]
    eye = jnp.eye(HALF, dtype=jnp.float32)
    image_w = jnp.einsum("ad,yz->ayzd", weights, eye).reshape(angles * HALF, HALF * depth).astype(jnp.bfloat16)
    wide_w = jnp.repeat(weights.T, HALF, axis=1)
    return coef, edge_coef, image_w, path_weights, make_weights(wide_w, weights.T, pick, pick_carry)


def column_of(line, tall):
    sub = lax.broadcasted_iota(jnp.int32, (tall, LANES), 0)
    lane = lax.broadcasted_iota(jnp.int32, (tall, LANES), 1)
    return jnp.max(jnp.where(sub == lane, line, -1), axis=1, keepdims=True)


def tables_kernel(rows, off, base_piece, device_ref, bases_ref, own_ref, after_ref, weight_ref, *rest):
    if base_piece:
        coef_ref, spread_ref, image_w_ref, wide_ref, turned_ref = rest
    else:
        coef_ref, spread_ref, wide_ref, turned_ref = rest[2:]
    block = pl.program_id(0) + off
    angles, depth = weight_ref.shape
    first = device_ref[0] * LANES
    shape = (angles, LANES)
    lane = lax.broadcasted_iota(jnp.int32, shape, 1)
    sub = lax.broadcasted_iota(jnp.int32, shape, 0)
    weights = weight_ref[...].astype(jnp.float32)
    ray_total = jnp.sum(weights, axis=1, keepdims=True)
    own = own_ref[...]
    ahead = jnp.where(lane == LANES - 1, pltpu.roll(after_ref[...], LANES - 1, 1), pltpu.roll(own, LANES - 1, 1))
    norm = 1.0 / (ray_total * ((1.0 - ahead) + own))
    coefs = ((1.0 - ahead) * norm, own * norm, norm)
    spots = lax.broadcasted_iota(jnp.int32, (angles, HALF, LANES), 2) - lax.broadcasted_iota(jnp.int32, (angles, HALF, LANES), 1)
    for half in range(BLOCK // HALF):
        here = spots == block * BLOCK + half * HALF
        for n, coef in enumerate(coefs):
            tall = jnp.broadcast_to(coef.reshape(angles, 1, LANES), (angles, HALF, LANES))
            tall = jnp.sum(jnp.where(here, tall, 0.0), axis=2, keepdims=True)
            coef_ref[0, half, n] = jnp.broadcast_to(tall, (angles, HALF, LANES)).reshape(angles * HALF, LANES)

    def fill_image_weights():
        across = (HALF * depth)
        repeat = lax.broadcasted_iota(jnp.int32, (depth, across), 1) % depth
        repeat = jnp.where(repeat == lax.broadcasted_iota(jnp.int32, (depth, across), 0), 1.0, 0.0)
        wide = dot(weight_ref[...], repeat.astype(jnp.bfloat16)).astype(jnp.bfloat16)
        down = angles * HALF
        expand = lax.broadcasted_iota(jnp.int32, (down, angles), 0) // HALF
        expand = jnp.where(expand == lax.broadcasted_iota(jnp.int32, (down, angles), 1), 1.0, 0.0)
        wide = dot(expand.astype(jnp.bfloat16), wide)
        at = lax.broadcasted_iota(jnp.int32, (down, across), 0) % HALF
        same = lax.broadcasted_iota(jnp.int32, (down, across), 1) // depth == at
        image_w_ref[...] = jnp.where(same, wide, 0.0).astype(jnp.bfloat16)

    if base_piece:
        pl.when(block == off)(fill_image_weights)
    row_now = first + lane - column_of(bases_ref[...], angles)
    w_now = jnp.where((row_now >= 0) & (row_now < rows), 1.0 - own, 0.0)
    w_next = jnp.where((row_now + 1 >= 0) & (row_now + 1 < rows), own, 0.0)
    columns = angles * HALF
    mine = lax.broadcasted_iota(jnp.int32, (angles, columns), 1) // HALF
    mine = mine == lax.broadcasted_iota(jnp.int32, (angles, columns), 0)
    square = lax.broadcasted_iota(jnp.int32, (angles, angles), 0) == lax.broadcasted_iota(jnp.int32, (angles, angles), 1)

    def gather(values, start, count):
        near = jnp.where(lane < count, pltpu.roll(values, (2 * LANES - start) % LANES, 1), 0.0)
        step = HALF
        while step < LANES:
            near = near + pltpu.roll(near, step, 1)
            step *= 2
        return jnp.sum(jnp.where(mine, near, 0.0), axis=0, keepdims=True)

    turned = lambda other: lax.dot_general(
        weights, other, (((0,), (0,)), ((), ())), precision=lax.Precision.HIGHEST, preferred_element_type=jnp.float32
    )

    @pl.when(block == off)
    def _():
        wide_ref[...] = turned(jnp.where(mine, 1.0, 0.0))
        turned_ref[...] = turned(jnp.where(square, 1.0, 0.0))

    for half in range(BLOCK // HALF):
        start = block * BLOCK + half * HALF
        pick_next = gather(w_next, start, HALF)
        pick_now = gather(w_now, start + 1, HALF - 1)
        carry = jnp.sum(jnp.where(lane == start, w_now, 0.0), axis=1, keepdims=True)
        pick_carry = jnp.sum(jnp.where(square, carry, 0.0), axis=0, keepdims=True)
        fill_weights(wide_ref[...], turned_ref[...], pick_next, pick_now, pick_carry, spread_ref, half)


def device_tables(device, row_of_bases, fractions, path_weights, rows, part, piece, made=None):
    angles, depth = path_weights.shape
    blocks = LANES // BLOCK // PARTS
    steps = blocks // 2
    here = piece * steps
    last = fractions.shape[1] // LANES - 1
    column = lambda by: pl.BlockSpec((angles, LANES), lambda b, d: (0, jnp.clip(d[0] + by, 0, last)))
    whole = lambda shape: pl.BlockSpec(shape, lambda b, d: (0,) * len(shape))
    coef = (BLOCK // HALF, 3, angles * HALF, LANES)
    image_w = (angles * HALF, HALF * depth)
    spread = (HALF * depth, angles * (HALF + 1))
    out_specs = [
        pl.BlockSpec((1,) + coef, lambda b, d: (b + here, 0, 0, 0, 0)),
        pl.BlockSpec((2,) + spread, lambda b, d: (b + here, 0, 0)),
    ]
    out_shape = [
        jax.ShapeDtypeStruct((blocks,) + coef, jnp.float32),
        jax.ShapeDtypeStruct((2 * blocks,) + spread, jnp.bfloat16),
    ]
    if made is None:
        out_specs.append(whole(image_w))
        out_shape.append(jax.ShapeDtypeStruct(image_w, jnp.bfloat16))
    filled = [] if made is None else [made[0], made[4]]
    done = pl.pallas_call(
        functools.partial(tables_kernel, rows, part * blocks + here, made is None),
        grid_spec=pltpu.PrefetchScalarGridSpec(
            num_scalar_prefetch=1,
            grid=(steps,),
            in_specs=[whole((1, LANES)), column(0), column(1), whole(path_weights.shape)]
            + [pl.BlockSpec(memory_space=pl.ANY)] * len(filled),
            out_specs=out_specs,
            scratch_shapes=[
                pltpu.VMEM((depth, angles * HALF), jnp.float32),
                pltpu.VMEM((depth, angles), jnp.float32),
            ],
        ),
        out_shape=out_shape,
        input_output_aliases={5 + n: n for n in range(len(filled))},
        name="make_tables",
    )(device, row_of_bases, fractions, fractions, path_weights, *filled)
    return done[0], None, done[2] if made is None else made[2], path_weights, done[1]


def turn_kernel(classes, count, part, device_ref, bases_ref, seen_ref, *refs):
    outs, twice_ref, sems = refs[:-2], refs[-2], refs[-1]
    rows, cols = seen_ref.shape
    more = twice_ref.shape[0] - rows
    copies = [
        pltpu.make_async_copy(seen_ref, twice_ref.at[pl.ds(0, rows)], sems.at[0]),
        pltpu.make_async_copy(seen_ref.at[pl.ds(0, more)], twice_ref.at[pl.ds(rows, more)], sems.at[1]),
    ]
    for copy in copies:
        copy.start()
    for copy in copies:
        copy.wait()
    device = device_ref[0]
    base = bases_ref[device]
    my_class = device & (classes - 1)
    slices = count * PARTS

    def window(place, size, at):
        start = (place - base + 1 + rows) & (rows - 1)
        begin = pl.multiple_of(start & ~(BLOCK - 1), BLOCK)
        tall = size + BLOCK
        wide = twice_ref[pl.ds(begin, tall), at].astype(jnp.float32)
        return pltpu.roll(wide, (tall - (start - begin)) % tall, 0)

    for n, out in enumerate(outs):
        place = (my_class ^ n) * slices + part * count

        @pl.loop(0, cols // WIDE)
        def _(chunk):
            at = pl.ds(pl.multiple_of(chunk * WIDE, WIDE), WIDE)
            out[:, at] = window(place, count, at)[:count].astype(jnp.bfloat16)


def turn(device, bases, seen, classes, part):
    rows, cols = seen.shape
    count = rows // classes // PARTS
    return pl.pallas_call(
        functools.partial(turn_kernel, classes, count, part),
        in_specs=[
            pl.BlockSpec(memory_space=pltpu.SMEM),
            pl.BlockSpec(memory_space=pltpu.SMEM),
            pl.BlockSpec(memory_space=pl.ANY),
        ],
        out_specs=[pl.BlockSpec(memory_space=pltpu.VMEM)] * classes,
        out_shape=[jax.ShapeDtypeStruct((count, cols), seen.dtype)] * classes,
        scratch_shapes=[pltpu.VMEM((rows + count + BLOCK, cols), seen.dtype), pltpu.SemaphoreType.DMA((2,))],
        compiler_params=pltpu.CompilerParams(vmem_limit_bytes=32 * 2**20),
        name="turn_rows",
    )(device, bases, seen)


def plan_kernel(slots, planes, classes, angles, count, rows, ends, device_ref, bases_ref, table_ref, which_ref):
    shape = (2 * PARTS * classes, LANES)
    lane = lax.broadcasted_iota(jnp.int32, shape, 1)
    row = lax.broadcasted_iota(jnp.int32, shape, 0)
    class_shift = classes.bit_length() - 1
    base = jnp.broadcast_to(bases_ref[...], shape) - 1
    low_plane = base >> (rows.bit_length() - 1)
    turned = base & (rows - 1)

    def reach(which):
        lowest = low_plane + jnp.where(which * count + count - 1 < turned, 1, 0)
        highest = low_plane + jnp.where(which * count < turned, 1, 0)
        return lowest, highest

    lowest, highest = reach(row >> 1)
    upward = (row & 1) == 0
    source = lane >> class_shift
    at = jnp.where(upward, source, planes - 1 - source)
    to = jnp.where(lane < angles, jnp.where(upward, highest, planes - 1 - lowest), -1)
    key = to * CODE + (CODE - 1 - lane)
    sent = [jnp.full(shape, -1, jnp.int32) for _ in range(planes - 1)]
    for slot in range(slots):
        begin = at
        for link in range(planes - 1):
            ready = (begin == link) & (to > link)
            for n in range(LOAD):
                best = jnp.max(jnp.where(ready, key, -1), axis=1, keepdims=True)
                taken = ready & (key == best)
                at = jnp.where(taken, link + 1, at)
                ready = ready & (key != best)
                which = jnp.where(best >= 0, CODE - 1 - (best & (CODE - 1)), -1)
                sent[link] = jnp.where(lane == slot * LOAD + n, which, sent[link])

    me = device_ref[0]
    my_class = me & (classes - 1)
    plane = me >> class_shift
    none = jnp.full(shape, -1, jnp.int32)
    used = none
    for link in range(planes - 1):
        used = jnp.maximum(used, sent[link])
    used = jnp.max(used, axis=0, keepdims=True)
    head = lane[:1]
    need = jnp.max(jnp.where(used >= 0, head + 1, 0))
    which_ref[0] = sum(jnp.where(need > end, 1, 0) for end in ends)

    tall = -(-max(slots * LOAD, angles) // 8) * 8
    sub = lax.broadcasted_iota(jnp.int32, (tall, LANES), 0)
    held = jnp.where(head < classes, plane * classes + (head ^ my_class), -1)
    for part in range(PARTS):
        low_here, high_here = reach(my_class * PARTS + part)
        wanted = (plane >= low_here) & (plane <= high_here) & (lane < angles)
        wanted = column_of(jnp.where(wanted, 1, 0)[:1], tall) > 0
        keep = lambda ids: jnp.max(jnp.where((sub == ids) & wanted, ids, -1), axis=0, keepdims=True)
        for way, spot in ((0, plane), (1, planes - 1 - plane)):
            sends, gets = none, none
            for link in range(planes - 1):
                sends = jnp.where(spot == link, sent[link], sends)
                gets = jnp.where(spot == link + 1, sent[link], gets)
            mine = row == 2 * (my_class * PARTS + part) + way
            sends = jnp.max(jnp.where(mine, sends, -1), axis=0, keepdims=True)
            gets = jnp.max(jnp.where(mine, gets, -1), axis=0, keepdims=True)
            arrived = jnp.max(jnp.where((column_of(gets, tall) == sends) & (sends >= 0), sub, 0), axis=0, keepdims=True)
            own = (sends >> class_shift) == plane
            index = jnp.where(own, (sends & (classes - 1)) ^ my_class, classes + arrived)
            line = part * LINES + way
            table_ref[line : line + 1] = jnp.where(sends >= 0, index, 0)
            table_ref[line + 2 : line + 3] = keep(gets)
        line = part * LINES + 4
        table_ref[line : line + 1] = keep(held)


def choose_kernel(slot, part, load, own, ups, table_ref, *refs):
    sources, (*outs, sems) = refs[: own + 2 * ups], refs[own + 2 * ups :]
    arrived = sources[own : own + ups], sources[own + ups :]
    views = [spread_out(sources[:own], []) + [(own + n, v) for n, v in spread_out([], side)] for side in arrived]
    spots = [(way, n) for way in range(2) for n in range(load)]
    for way, n in spots:
        for m, view in views[way]:

            @pl.when(table_ref[part * LINES + way, slot * LOAD + n] == m)
            def _():
                pltpu.make_async_copy(view, outs[way].at[n], sems.at[way, n]).start()

    for way, n in spots:
        pltpu.make_async_copy(sources[0], outs[way].at[n], sems.at[way, n]).wait()


def choose(slot, part, load, table, own, ups, downs):
    anywhere = pl.BlockSpec(memory_space=pl.ANY)
    shape = jax.ShapeDtypeStruct((load,) + own[0].shape, own[0].dtype)
    return pl.pallas_call(
        functools.partial(choose_kernel, slot, part, load, len(own), len(ups)),
        in_specs=[pl.BlockSpec(memory_space=pltpu.SMEM)] + [anywhere] * (len(own) + 2 * len(ups)),
        out_specs=[pl.BlockSpec(memory_space=pltpu.VMEM)] * 2,
        out_shape=[shape, shape],
        scratch_shapes=[pltpu.SemaphoreType.DMA((2, load))],
        cost_estimate=pl.CostEstimate(flops=0, bytes_accessed=4 * load * own[0].size * 2, transcendentals=0),
        name="choose_packet",
    )(table, *own, *ups, *downs)


def on_device(volume, measured, path_weights, fractions, bases):
    slices, depth, cols = volume.shape
    local, rows = measured.shape[:2]
    nslab = lax.axis_size("slab")
    device = lax.axis_index("slab")
    angles = local * nslab
    first = device * slices
    classes = rows // slices
    planes = nslab // classes
    ups_of = lambda step: [(i, i + step) for i in range(nslab - step)]
    downs_of = lambda step: [(i + step, i) for i in range(nslab - step)]

    routed = local == 1 and classes == ROUTED_CLASSES and slices == LANES and rows & (rows - 1) == 0 and angles * HALF == LANES

    def dense(volume, measured, path_weights, fractions, bases):
        left = lax.ppermute(volume[slices - 1 :], "slab", ups_of(1))
        right = lax.ppermute(volume[:1], "slab", downs_of(1))
        share = lax.dynamic_slice_in_dim(jnp.pad(fractions, ((0, 0), (1, 1))), first, slices + 2, 1)
        tables = make_tables(share, first, rows, path_weights, bases, slices)
        my_bases = lax.dynamic_slice_in_dim(bases, device * local, local, 0)
        turned = jax.vmap(lambda m, b: jnp.roll(m, b - 1, axis=0))(measured, my_bases)
        by_class = turned.reshape(local, classes, slices, cols).transpose(1, 0, 2, 3)
        outgoing = jnp.tile(by_class, (planes, 1, 1, 1)).reshape(angles, slices, cols)
        seen = lax.all_to_all(outgoing, "slab", split_axis=0, concat_axis=0, tiled=True)
        ends = jnp.roll(by_class[:, :, slices - 1], 1, axis=0)
        ends = jnp.tile(ends, (planes, 1, 1)).reshape(angles, cols // LANES, LANES)
        edge = lax.all_to_all(ends, "slab", split_axis=0, concat_axis=0, tiled=True).reshape(angles, cols)
        return update(volume, right, tables, [seen], jnp.zeros((8, LANES), jnp.int32), None, 0, 1, (left, edge))[0]

    if not routed:
        return dense(volume, measured, path_weights, fractions, bases)

    number = device.astype(jnp.int32)[None]
    upper, lower = PARTS - 1, 0
    exchange = lambda runs: [runs[0]] + [
        lax.ppermute(runs[d], "slab", [(i, i ^ d) for i in range(nslab)]) for d in range(1, classes)
    ]
    runs = turn(number, bases, measured[0], classes, upper)
    runs, late_bases, seen = lax.optimization_barrier((runs, bases, measured[0]))
    own = {upper: exchange(runs)}

    row_of_bases = jnp.pad(late_bases, (0, LANES - angles), constant_values=1)[None]
    most = -(-classes * (planes - 1) // LOAD) + planes - 2
    ends = [5, 6, 7]
    table, which = pl.pallas_call(
        functools.partial(plan_kernel, most, planes, classes, angles, slices // PARTS, rows, ends),
        in_specs=[pl.BlockSpec(memory_space=pltpu.SMEM), pl.BlockSpec(memory_space=pltpu.VMEM)],
        out_specs=[pl.BlockSpec(memory_space=pltpu.VMEM), pl.BlockSpec(memory_space=pltpu.SMEM)],
        out_shape=[jax.ShapeDtypeStruct((16, LANES), jnp.int32), jax.ShapeDtypeStruct((1,), jnp.int32)],
        name="plan_slots",
    )(number, row_of_bases)
    table, which, high = lax.optimization_barrier((table, which, volume[:1]))
    right = lax.ppermute(high, "slab", downs_of(1))
    runs = turn(number, bases, seen, classes, lower)
    tables = device_tables(number, row_of_bases, fractions, path_weights, rows, upper, 0)
    tables = [tables[0], *tables[2:]]
    arrived, runs, table, tables, right = lax.optimization_barrier((own[upper], runs, table, tables, right))

    def finish(end):
        def branch(arrived, runs, table, upper_tables, right):
            own = {upper: arrived, lower: exchange(runs)}
            ups, downs = {upper: [], lower: []}, {upper: [], lower: []}
            late = row_of_bases
            tables = {upper: (upper_tables[0], None, *upper_tables[1:]), lower: None}
            beside = {(0, upper): (upper, 1), (1, upper): (lower, 0), (1, lower): (lower, 1)}
            for slot in range(-(-end // LOAD)):
                load = min(LOAD, end - slot * LOAD)
                for part in (upper, lower):
                    go_up, go_down = choose(slot, part, load, table, own[part], ups[part], downs[part])
                    if (slot, part) in beside:
                        go_up, go_down, late = lax.optimization_barrier((go_up, go_down, late))
                        where, piece = beside[slot, part]
                        made = device_tables(number, late, fractions, path_weights, rows, where, piece, tables[where])
                        table, made = lax.optimization_barrier((table, made))
                        tables[where] = made
                    ups[part].append(lax.ppermute(go_up, "slab", ups_of(classes)))
                    downs[part].append(lax.ppermute(go_down, "slab", downs_of(classes)))
            packets = {part: own[part] + ups[part] + downs[part] for part in (upper, lower)}
            out, last = update(volume, right, tables[upper], packets[upper], table, None, upper, PARTS)
            first = lax.ppermute(last, "slab", ups_of(1))
            out, second = update(volume, right, tables[lower], packets[lower], table, out, lower, PARTS)
            return mend(out, tables[lower][-1], tables[upper][-1], first, second)

        return branch

    others = lambda *_: dense(volume, measured, path_weights, fractions, bases)
    return lax.switch(which[0], [finish(e) for e in ends] + [others], arrived, runs, table, tables, right)


def solution(mesh):
    placed = (P(("groups", "slab"), None, None), P(("groups", "slab"), None, None), P(), P(), P())
    return jax.shard_map(
        on_device,
        mesh=mesh,
        in_specs=placed,
        out_specs=P(("groups", "slab"), None, None),
        check_vma=False,
    )
```

```python
import functools

import jax
import jax.numpy as jnp
from jax import lax
from jax.experimental import pallas as pl
from jax.experimental.pallas import tpu as pltpu
from jax.sharding import PartitionSpec as P

RELAX = 1.0
BLOCK = 16
HALF = 8
LANES = 128
WIDE = 256
PIECES = 4
PARTS = 2
ROUTED_CLASSES = 4
LOAD = 2
CODE = 256
LINES = 5
VMEM_LIMIT = 56 * 2**20


def dot(a, b):
    return jnp.dot(a, b, preferred_element_type=jnp.float32)


def widen(coef):
    return jnp.concatenate([coef] * (WIDE // LANES), axis=1)


def spread_out(own, arrived):
    views = list(enumerate(own))
    return views + [(s * LOAD + n, p.at[n]) for s, p in enumerate(arrived) for n in range(p.shape[0])]


def update_kernel(
    dense, part, table_ref, lower_ref, upper_ref, next_ref, right_ref, coef_ref, image_w_ref, weight_ref, spread_ref, *rest
):
    if dense:
        left_ref, edge_ref, edge_coef_ref, *rest = rest
    out_ref, carry_ref, seen_ref, result_ref, sems, out_sems = rest[-6:]
    packets = rest[:-7]
    block = pl.program_id(0)
    blocks = pl.num_programs(0)
    depth, width = lower_ref.shape[1:]
    angles = weight_ref.shape[0]
    first = part * blocks * BLOCK

    def fetch(at_block, act):
        slot = at_block % 2
        rows = pl.ds(pl.multiple_of(at_block * BLOCK, BLOCK), BLOCK)
        if dense:
            act(pltpu.make_async_copy(packets[0].at[:, rows], seen_ref.at[slot], sems.at[slot, 0]))
            return
        middle = (len(packets) - ROUTED_CLASSES) // 2 + ROUTED_CLASSES
        views = [(4, *v) for v in spread_out(packets[:ROUTED_CLASSES], [])]
        views += [(2, *v) for v in spread_out([], packets[ROUTED_CLASSES:middle])]
        views += [(3, *v) for v in spread_out([], packets[middle:])]
        for n, (line, spot, view) in enumerate(views):
            name = table_ref[part * LINES + line, spot]

            @pl.when(name >= 0)
            def _():
                act(pltpu.make_async_copy(view.at[rows], seen_ref.at[slot, name], sems.at[slot, n]))

    def deliver(at_block, act, pieces=range(PIECES)):
        slot = at_block % 2
        rows = pl.ds(first + at_block * BLOCK, BLOCK)
        for n in pieces:
            at = pl.ds(n * (width // PIECES), width // PIECES)
            act(pltpu.make_async_copy(result_ref.at[slot, :, :, at], out_ref.at[rows, :, at], out_sems.at[slot, n]))

    @pl.when(block == 0)
    def _():
        seen_ref[...] = jnp.zeros_like(seen_ref)
        fetch(block, lambda copy: copy.start())

    @pl.when(block + 1 < blocks)
    def _():
        fetch(block + 1, lambda copy: copy.start())

    @pl.when(block == 0)
    def _():
        if not dense:
            carry_ref[...] = jnp.zeros_like(carry_ref)
            return
        for chunk in range(width // WIDE):
            at = pl.ds(chunk * WIDE, WIDE)
            mine = dot(weight_ref[...], lower_ref[0, :, at])
            before = dot(weight_ref[...], left_ref[0, :, at])
            carry_ref[:, at] = (
                edge_ref[:, at].astype(jnp.float32) * widen(edge_coef_ref[2])
                - mine * widen(edge_coef_ref[0])
                - before * widen(edge_coef_ref[1])
            ).astype(jnp.bfloat16)

    @pl.when(block >= 2)
    def _():
        deliver(block - 2, lambda copy: copy.wait())

    fetch(block, lambda copy: copy.wait())
    slot = block % 2
    final = (block == blocks - 1) & (part == PARTS - 1 or dense)

    def columns(chunk):
        if dense:
            return pl.ds(pl.multiple_of(chunk * WIDE, WIDE), WIDE)
        return slice(chunk * WIDE, (chunk + 1) * WIDE)

    def image(chunk):
        at = columns(chunk)
        images = [dot(image_w_ref[...], r[:, :, at].reshape(HALF * depth, WIDE)) for r in (lower_ref, upper_ref)]
        after = dot(weight_ref[...], jnp.where(final, right_ref[0, :, at], next_ref[0, :, at]))
        return images, after

    def residual(chunk, images, after):
        at = columns(chunk)
        seen = seen_ref[slot, :, :, at].astype(jnp.float32)
        ahead = [pltpu.roll(x.reshape(angles, HALF, WIDE), HALF - 1, 1) for x in images]
        ahead.append(jnp.broadcast_to(after.reshape(angles, 1, WIDE), (angles, HALF, WIDE)))
        tail = lax.broadcasted_iota(jnp.int32, (angles, HALF, WIDE), 1) == HALF - 1
        parts = []
        for half in range(2):
            now = jnp.where(tail, ahead[half + 1], ahead[half]).reshape(angles * HALF, WIDE)
            got = seen[:, half * HALF : (half + 1) * HALF].reshape(angles * HALF, WIDE)
            coef = [widen(coef_ref[0, half, n]) for n in range(3)]
            resid = got * coef[2] - now * coef[0] - images[half] * coef[1]
            parts.append(resid.reshape(angles, HALF, WIDE))
        return parts

    def result(chunk, parts):
        at = columns(chunk)
        carry = carry_ref[:, at]
        for half, (resid, r) in enumerate(zip(parts, (lower_ref, upper_ref))):
            inputs = jnp.concatenate([resid.reshape(angles * HALF, WIDE).astype(jnp.bfloat16), carry])
            spread = dot(spread_ref[half], inputs).reshape(HALF, depth, WIDE)
            carry = resid[:, HALF - 1].astype(jnp.bfloat16)
            result_ref[slot, half * HALF : (half + 1) * HALF, :, at] = r[:, :, at].astype(jnp.float32) + spread
        carry_ref[:, at] = carry

    chunks = width // WIDE
    if dense:
        pl.loop(0, chunks)(lambda chunk: result(chunk, residual(chunk, *image(chunk))))
        deliver(block, lambda copy: copy.start())
    else:
        images, resids = {}, {}
        for n in range(chunks + 2):
            if n < chunks:
                images[n] = image(n)
            if 1 <= n <= chunks:
                resids[n - 1] = residual(n - 1, *images.pop(n - 1))
            if n >= 2:
                result(n - 2, resids.pop(n - 2))
                done = (n - 1) * PIECES
                if done % chunks == 0:
                    deliver(block, lambda copy: copy.start(), [done // chunks - 1])

    @pl.when(block == blocks - 1)
    def _():
        @pl.when(block >= 1)
        def _():
            deliver(block - 1, lambda copy: copy.wait())

        deliver(block, lambda copy: copy.wait())


def update(volume, right, tables, packets, table, before, part, parts, ahead=None):
    slices, depth, cols = volume.shape
    dense = ahead is not None
    blocks = slices // BLOCK // parts
    off = part * blocks
    by_block = lambda x: pl.BlockSpec((1,) + x.shape[1:], lambda b, i: (b,) + (0,) * (x.ndim - 1))
    whole = lambda x: pl.BlockSpec(x.shape, lambda b, i: (0,) * x.ndim)
    anywhere = pl.BlockSpec(memory_space=pl.ANY)
    coef, edge_coef, image_w, weights, spread_w = tables
    angles = weights.shape[0]
    ahead = [*ahead, edge_coef] if dense else []
    held = jax.ShapeDtypeStruct((angles, cols), volume.dtype)
    if before is None:
        before = coef
    aliases = {9 + len(ahead) + len(packets): 0} if before.shape == volume.shape else {}
    copies = LOAD * len(packets)
    one = (1, depth, cols)
    return pl.pallas_call(
        functools.partial(update_kernel, dense, part),
        grid_spec=pltpu.PrefetchScalarGridSpec(
            num_scalar_prefetch=1,
            grid=(blocks,),
            in_specs=[
                pl.BlockSpec((HALF, depth, cols), lambda b, i: (2 * (b + off), 0, 0)),
                pl.BlockSpec((HALF, depth, cols), lambda b, i: (2 * (b + off) + 1, 0, 0)),
                pl.BlockSpec(one, lambda b, i: (jnp.minimum((b + off + 1) * BLOCK, slices - 1), 0, 0)),
                whole(right), by_block(coef), whole(image_w), whole(weights),
                pl.BlockSpec((2,) + spread_w.shape[1:], lambda b, i: (b, 0, 0)),
            ]
            + [whole(x) for x in ahead]
            + [anywhere] * (len(packets) + 1),
            out_specs=[anywhere, whole(held)],
            scratch_shapes=[
                pltpu.VMEM((2, angles, BLOCK, cols), jnp.bfloat16),
                pltpu.VMEM((2, BLOCK, depth, cols), jnp.float32),
                pltpu.SemaphoreType.DMA((2, copies)),
                pltpu.SemaphoreType.DMA((2, PIECES)),
            ],
        ),
        out_shape=[jax.ShapeDtypeStruct(volume.shape, jnp.float32), held],
        input_output_aliases=aliases,
        compiler_params=pltpu.CompilerParams(dimension_semantics=("arbitrary",), vmem_limit_bytes=VMEM_LIMIT),
        cost_estimate=pl.CostEstimate(
            flops=4 * slices * depth * cols * angles // parts, bytes_accessed=volume.size * 7 // parts, transcendentals=0
        ),
        name="slab_update",
    )(
        table, volume, volume, volume, right, coef, image_w, weights, spread_w, *ahead, *packets, before
    )


def mend_kernel(lower_ref, upper_ref, first_ref, second_ref, before_ref, out_ref):
    columns = lower_ref.shape[2] - first_ref.shape[0]

    @pl.when(pl.program_id(0) == 0)
    def _():
        out_ref[0] = before_ref[0] + dot(lower_ref[0, :, columns:], first_ref[...])

    @pl.when(pl.program_id(0) == 1)
    def _():
        out_ref[0] = before_ref[0] + dot(upper_ref[0, :, columns:], second_ref[...])


def mend(out, lower, upper, first, second):
    slices, depth, cols = out.shape
    whole = pl.BlockSpec(first.shape, lambda b: (0, 0))
    weights = pl.BlockSpec((1, depth, lower.shape[2]), lambda b: (0, 0, 0))
    slab = pl.BlockSpec((1, depth, cols), lambda b: (b * (slices // 2), 0, 0))
    return pl.pallas_call(
        mend_kernel,
        grid=(2,),
        in_specs=[weights, weights, whole, whole, slab],
        out_specs=slab,
        out_shape=jax.ShapeDtypeStruct(out.shape, out.dtype),
        input_output_aliases={4: 0},
        name="mend_slices",
    )(lower, upper, first, second, out)


def fill_weights(wide_w, turned_w, pick_next, pick_now, pick_carry, spread_ref, half):
    depth, columns = wide_w.shape
    place = lax.broadcasted_iota(jnp.int32, (depth, columns), 1) % HALF
    from_next = wide_w * pick_next
    from_now = wide_w * pick_now
    from_carry = turned_w * pick_carry
    for z in range(HALF):
        row = jnp.where(place == z, from_next, jnp.where(place == z - 1, from_now, 0.0))
        total = jnp.sum(row, axis=1, keepdims=True)
        carry = jnp.zeros_like(from_carry)
        if z == 0:
            total = total + jnp.sum(from_carry, axis=1, keepdims=True)
            carry = from_carry
        scale = RELAX / total
        spread_ref[half, z * depth : (z + 1) * depth, :columns] = (row * scale).astype(jnp.bfloat16)
        spread_ref[half, z * depth : (z + 1) * depth, columns:] = (carry * scale).astype(jnp.bfloat16)


def weights_kernel(wide_w_ref, turned_w_ref, pick_ref, pick_carry_ref, spread_ref):
    picks = pick_ref[0, 0:1], pick_ref[0, 1:2], pick_carry_ref[0]
    fill_weights(wide_w_ref[...], turned_w_ref[...], *picks, spread_ref, 0)


def make_weights(wide_w, turned_w, pick, pick_carry):
    halves = pick.shape[0]
    depth, angles = turned_w.shape
    by_half = lambda shape: pl.BlockSpec((1,) + shape, lambda b: (b,) + (0,) * len(shape))
    whole = lambda x: pl.BlockSpec(x.shape, lambda b: (0,) * x.ndim)
    spread = (HALF * depth, angles * (HALF + 1))
    return pl.pallas_call(
        weights_kernel,
        grid=(halves,),
        in_specs=[whole(wide_w), whole(turned_w), by_half(pick.shape[1:]), by_half(pick_carry.shape[1:])],
        out_specs=by_half(spread),
        out_shape=jax.ShapeDtypeStruct((halves,) + spread, jnp.bfloat16),
        name="spread_weights",
    )(wide_w, turned_w, pick, pick_carry)


def make_tables(share, first, rows, path_weights, bases, slices):
    angles, depth = path_weights.shape
    blocks = slices // BLOCK
    weights = path_weights.astype(jnp.float32)
    ray_total = jnp.sum(weights, axis=1)[:, None]
    norm = 1.0 / (ray_total * ((1.0 - share[:, 1:]) + share[:, :-1]))
    coefs = jnp.stack([(1.0 - share[:, 1:]) * norm, share[:, :-1] * norm, norm])
    coef = coefs[:, :, 1:].reshape(3, angles, blocks, BLOCK // HALF, HALF).transpose(2, 3, 0, 1, 4)
    coef = coef.reshape(blocks, BLOCK // HALF, 3, angles * HALF, 1)
    coef = jnp.broadcast_to(coef, coef.shape[:4] + (LANES,))
    edge_coef = jnp.broadcast_to(coefs[:, :, :1], (3, angles, LANES))
    share_own = share[:, 1:-1]
    row_now = (first - bases)[:, None] + jnp.arange(slices, dtype=jnp.int32)[None, :]
    w_now = jnp.where((row_now >= 0) & (row_now < rows), 1.0 - share_own, 0.0)
    w_next = jnp.where((row_now + 1 >= 0) & (row_now + 1 < rows), share_own, 0.0)
    halves = slices // HALF
    pick = jnp.stack([w_next, jnp.pad(w_now[:, 1:], ((0, 0), (0, 1)))]).reshape(2, angles, halves, HALF)
    pick = pick.transpose(2, 0, 1, 3).reshape(halves, 2, angles * HALF)
    pick_carry = w_now[:, ::HALF].T[:, None, :]
    eye = jnp.eye(HALF, dtype=jnp.float32)
    image_w = jnp.einsum("ad,yz->ayzd", weights, eye).reshape(angles * HALF, HALF * depth).astype(jnp.bfloat16)
    wide_w = jnp.repeat(weights.T, HALF, axis=1)
    return coef, edge_coef, image_w, path_weights, make_weights(wide_w, weights.T, pick, pick_carry)


def column_of(line, tall):
    sub = lax.broadcasted_iota(jnp.int32, (tall, LANES), 0)
    lane = lax.broadcasted_iota(jnp.int32, (tall, LANES), 1)
    return jnp.max(jnp.where(sub == lane, line, -1), axis=1, keepdims=True)


def tables_kernel(rows, off, base_piece, device_ref, bases_ref, own_ref, after_ref, weight_ref, *rest):
    if base_piece:
        coef_ref, spread_ref, image_w_ref, wide_ref, turned_ref = rest
    else:
        coef_ref, spread_ref, wide_ref, turned_ref = rest[2:]
    block = pl.program_id(0) + off
    angles, depth = weight_ref.shape
    first = device_ref[0] * LANES
    shape = (angles, LANES)
    lane = lax.broadcasted_iota(jnp.int32, shape, 1)
    sub = lax.broadcasted_iota(jnp.int32, shape, 0)
    weights = weight_ref[...].astype(jnp.float32)
    ray_total = jnp.sum(weights, axis=1, keepdims=True)
    own = own_ref[...]
    ahead = jnp.where(lane == LANES - 1, pltpu.roll(after_ref[...], LANES - 1, 1), pltpu.roll(own, LANES - 1, 1))
    norm = 1.0 / (ray_total * ((1.0 - ahead) + own))
    coefs = ((1.0 - ahead) * norm, own * norm, norm)
    spots = lax.broadcasted_iota(jnp.int32, (angles, HALF, LANES), 2) - lax.broadcasted_iota(jnp.int32, (angles, HALF, LANES), 1)
    for half in range(BLOCK // HALF):
        here = spots == block * BLOCK + half * HALF
        for n, coef in enumerate(coefs):
            tall = jnp.broadcast_to(coef.reshape(angles, 1, LANES), (angles, HALF, LANES))
            tall = jnp.sum(jnp.where(here, tall, 0.0), axis=2, keepdims=True)
            coef_ref[0, half, n] = jnp.broadcast_to(tall, (angles, HALF, LANES)).reshape(angles * HALF, LANES)

    def fill_image_weights():
        across = (HALF * depth)
        repeat = lax.broadcasted_iota(jnp.int32, (depth, across), 1) % depth
        repeat = jnp.where(repeat == lax.broadcasted_iota(jnp.int32, (depth, across), 0), 1.0, 0.0)
        wide = dot(weight_ref[...], repeat.astype(jnp.bfloat16)).astype(jnp.bfloat16)
        down = angles * HALF
        expand = lax.broadcasted_iota(jnp.int32, (down, angles), 0) // HALF
        expand = jnp.where(expand == lax.broadcasted_iota(jnp.int32, (down, angles), 1), 1.0, 0.0)
        wide = dot(expand.astype(jnp.bfloat16), wide)
        at = lax.broadcasted_iota(jnp.int32, (down, across), 0) % HALF
        same = lax.broadcasted_iota(jnp.int32, (down, across), 1) // depth == at
        image_w_ref[...] = jnp.where(same, wide, 0.0).astype(jnp.bfloat16)

    if base_piece:
        pl.when(block == off)(fill_image_weights)
    row_now = first + lane - column_of(bases_ref[...], angles)
    w_now = jnp.where((row_now >= 0) & (row_now < rows), 1.0 - own, 0.0)
    w_next = jnp.where((row_now + 1 >= 0) & (row_now + 1 < rows), own, 0.0)
    columns = angles * HALF
    mine = lax.broadcasted_iota(jnp.int32, (angles, columns), 1) // HALF
    mine = mine == lax.broadcasted_iota(jnp.int32, (angles, columns), 0)
    square = lax.broadcasted_iota(jnp.int32, (angles, angles), 0) == lax.broadcasted_iota(jnp.int32, (angles, angles), 1)

    def gather(values, start, count):
        near = jnp.where(lane < count, pltpu.roll(values, (2 * LANES - start) % LANES, 1), 0.0)
        step = HALF
        while step < LANES:
            near = near + pltpu.roll(near, step, 1)
            step *= 2
        return jnp.sum(jnp.where(mine, near, 0.0), axis=0, keepdims=True)

    turned = lambda other: lax.dot_general(
        weights, other, (((0,), (0,)), ((), ())), precision=lax.Precision.HIGHEST, preferred_element_type=jnp.float32
    )

    @pl.when(block == off)
    def _():
        wide_ref[...] = turned(jnp.where(mine, 1.0, 0.0))
        turned_ref[...] = turned(jnp.where(square, 1.0, 0.0))

    for half in range(BLOCK // HALF):
        start = block * BLOCK + half * HALF
        pick_next = gather(w_next, start, HALF)
        pick_now = gather(w_now, start + 1, HALF - 1)
        carry = jnp.sum(jnp.where(lane == start, w_now, 0.0), axis=1, keepdims=True)
        pick_carry = jnp.sum(jnp.where(square, carry, 0.0), axis=0, keepdims=True)
        fill_weights(wide_ref[...], turned_ref[...], pick_next, pick_now, pick_carry, spread_ref, half)


def device_tables(device, row_of_bases, fractions, path_weights, rows, part, piece, made=None):
    angles, depth = path_weights.shape
    blocks = LANES // BLOCK // PARTS
    steps = blocks // 2
    here = piece * steps
    last = fractions.shape[1] // LANES - 1
    column = lambda by: pl.BlockSpec((angles, LANES), lambda b, d: (0, jnp.clip(d[0] + by, 0, last)))
    whole = lambda shape: pl.BlockSpec(shape, lambda b, d: (0,) * len(shape))
    coef = (BLOCK // HALF, 3, angles * HALF, LANES)
    image_w = (angles * HALF, HALF * depth)
    spread = (HALF * depth, angles * (HALF + 1))
    out_specs = [
        pl.BlockSpec((1,) + coef, lambda b, d: (b + here, 0, 0, 0, 0)),
        pl.BlockSpec((2,) + spread, lambda b, d: (b + here, 0, 0)),
    ]
    out_shape = [
        jax.ShapeDtypeStruct((blocks,) + coef, jnp.float32),
        jax.ShapeDtypeStruct((2 * blocks,) + spread, jnp.bfloat16),
    ]
    if made is None:
        out_specs.append(whole(image_w))
        out_shape.append(jax.ShapeDtypeStruct(image_w, jnp.bfloat16))
    filled = [] if made is None else [made[0], made[4]]
    done = pl.pallas_call(
        functools.partial(tables_kernel, rows, part * blocks + here, made is None),
        grid_spec=pltpu.PrefetchScalarGridSpec(
            num_scalar_prefetch=1,
            grid=(steps,),
            in_specs=[whole((1, LANES)), column(0), column(1), whole(path_weights.shape)]
            + [pl.BlockSpec(memory_space=pl.ANY)] * len(filled),
            out_specs=out_specs,
            scratch_shapes=[
                pltpu.VMEM((depth, angles * HALF), jnp.float32),
                pltpu.VMEM((depth, angles), jnp.float32),
            ],
        ),
        out_shape=out_shape,
        input_output_aliases={5 + n: n for n in range(len(filled))},
        name="make_tables",
    )(device, row_of_bases, fractions, fractions, path_weights, *filled)
    return done[0], None, done[2] if made is None else made[2], path_weights, done[1]


def turn_kernel(classes, count, part, device_ref, bases_ref, seen_ref, *refs):
    outs, twice_ref, sems = refs[:-2], refs[-2], refs[-1]
    rows, cols = seen_ref.shape
    more = twice_ref.shape[0] - rows
    copies = [
        pltpu.make_async_copy(seen_ref, twice_ref.at[pl.ds(0, rows)], sems.at[0]),
        pltpu.make_async_copy(seen_ref.at[pl.ds(0, more)], twice_ref.at[pl.ds(rows, more)], sems.at[1]),
    ]
    for copy in copies:
        copy.start()
    for copy in copies:
        copy.wait()
    device = device_ref[0]
    base = bases_ref[device]
    my_class = device & (classes - 1)
    slices = count * PARTS

    def window(place, size, at):
        start = (place - base + 1 + rows) & (rows - 1)
        begin = pl.multiple_of(start & ~(BLOCK - 1), BLOCK)
        tall = size + BLOCK
        wide = twice_ref[pl.ds(begin, tall), at].astype(jnp.float32)
        return pltpu.roll(wide, (tall - (start - begin)) % tall, 0)

    for n, out in enumerate(outs):
        place = (my_class ^ n) * slices + part * count

        @pl.loop(0, cols // WIDE)
        def _(chunk):
            at = pl.ds(pl.multiple_of(chunk * WIDE, WIDE), WIDE)
            out[:, at] = window(place, count, at)[:count].astype(jnp.bfloat16)


def turn(device, bases, seen, classes, part):
    rows, cols = seen.shape
    count = rows // classes // PARTS
    return pl.pallas_call(
        functools.partial(turn_kernel, classes, count, part),
        in_specs=[
            pl.BlockSpec(memory_space=pltpu.SMEM),
            pl.BlockSpec(memory_space=pltpu.SMEM),
            pl.BlockSpec(memory_space=pl.ANY),
        ],
        out_specs=[pl.BlockSpec(memory_space=pltpu.VMEM)] * classes,
        out_shape=[jax.ShapeDtypeStruct((count, cols), seen.dtype)] * classes,
        scratch_shapes=[pltpu.VMEM((rows + count + BLOCK, cols), seen.dtype), pltpu.SemaphoreType.DMA((2,))],
        compiler_params=pltpu.CompilerParams(vmem_limit_bytes=32 * 2**20),
        name="turn_rows",
    )(device, bases, seen)


def plan_kernel(slots, planes, classes, angles, count, rows, ends, device_ref, bases_ref, table_ref, which_ref):
    shape = (2 * PARTS * classes, LANES)
    lane = lax.broadcasted_iota(jnp.int32, shape, 1)
    row = lax.broadcasted_iota(jnp.int32, shape, 0)
    class_shift = classes.bit_length() - 1
    base = jnp.broadcast_to(bases_ref[...], shape) - 1
    low_plane = base >> (rows.bit_length() - 1)
    turned = base & (rows - 1)

    def reach(which):
        lowest = low_plane + jnp.where(which * count + count - 1 < turned, 1, 0)
        highest = low_plane + jnp.where(which * count < turned, 1, 0)
        return lowest, highest

    lowest, highest = reach(row >> 1)
    upward = (row & 1) == 0
    source = lane >> class_shift
    at = jnp.where(upward, source, planes - 1 - source)
    to = jnp.where(lane < angles, jnp.where(upward, highest, planes - 1 - lowest), -1)
    key = to * CODE + (CODE - 1 - lane)
    sent = [jnp.full(shape, -1, jnp.int32) for _ in range(planes - 1)]
    for slot in range(slots):
        begin = at
        for link in range(planes - 1):
            ready = (begin == link) & (to > link)
            for n in range(LOAD):
                best = jnp.max(jnp.where(ready, key, -1), axis=1, keepdims=True)
                taken = ready & (key == best)
                at = jnp.where(taken, link + 1, at)
                ready = ready & (key != best)
                which = jnp.where(best >= 0, CODE - 1 - (best & (CODE - 1)), -1)
                sent[link] = jnp.where(lane == slot * LOAD + n, which, sent[link])

    me = device_ref[0]
    my_class = me & (classes - 1)
    plane = me >> class_shift
    none = jnp.full(shape, -1, jnp.int32)
    used = none
    for link in range(planes - 1):
        used = jnp.maximum(used, sent[link])
    used = jnp.max(used, axis=0, keepdims=True)
    head = lane[:1]
    need = jnp.max(jnp.where(used >= 0, head + 1, 0))
    which_ref[0] = sum(jnp.where(need > end, 1, 0) for end in ends)

    tall = -(-max(slots * LOAD, angles) // 8) * 8
    sub = lax.broadcasted_iota(jnp.int32, (tall, LANES), 0)
    held = jnp.where(head < classes, plane * classes + (head ^ my_class), -1)
    for part in range(PARTS):
        low_here, high_here = reach(my_class * PARTS + part)
        wanted = (plane >= low_here) & (plane <= high_here) & (lane < angles)
        wanted = column_of(jnp.where(wanted, 1, 0)[:1], tall) > 0
        keep = lambda ids: jnp.max(jnp.where((sub == ids) & wanted, ids, -1), axis=0, keepdims=True)
        moves = []
        for way, spot in ((0, plane), (1, planes - 1 - plane)):
            sends, gets = none, none
            for link in range(planes - 1):
                sends = jnp.where(spot == link, sent[link], sends)
                gets = jnp.where(spot == link + 1, sent[link], gets)
            mine = row == 2 * (my_class * PARTS + part) + way
            sends = jnp.max(jnp.where(mine, sends, -1), axis=0, keepdims=True)
            gets = jnp.max(jnp.where(mine, gets, -1), axis=0, keepdims=True)
            arrived = jnp.max(jnp.where((column_of(gets, tall) == sends) & (sends >= 0), sub, 0), axis=0, keepdims=True)
            own = (sends >> class_shift) == plane
            index = jnp.where(own, (sends & (classes - 1)) ^ my_class, classes + arrived)
            moves.append((jnp.where(sends >= 0, index, 0), keep(gets)))
        for exchange in range(2):
            upward = ((plane + exchange) & 1) == 0
            line = part * LINES + exchange
            table_ref[line : line + 1] = jnp.where(upward, moves[0][0], moves[1][0])
            table_ref[line + 2 : line + 3] = jnp.where(upward, moves[1][1], moves[0][1])
        line = part * LINES + 4
        table_ref[line : line + 1] = keep(held)


def choose_kernel(slot, part, load, own, ups, table_ref, *refs):
    sources, (*outs, sems) = refs[: own + 2 * ups], refs[own + 2 * ups :]
    arrived = sources[own + ups :], sources[own : own + ups]
    views = [spread_out(sources[:own], []) + [(own + n, v) for n, v in spread_out([], side)] for side in arrived]
    spots = [(way, n) for way in range(2) for n in range(load)]
    for way, n in spots:
        for m, view in views[way]:

            @pl.when(table_ref[part * LINES + way, slot * LOAD + n] == m)
            def _():
                pltpu.make_async_copy(view, outs[way].at[n], sems.at[way, n]).start()

    for way, n in spots:
        pltpu.make_async_copy(sources[0], outs[way].at[n], sems.at[way, n]).wait()


def choose(slot, part, load, table, own, ups, downs):
    anywhere = pl.BlockSpec(memory_space=pl.ANY)
    shape = jax.ShapeDtypeStruct((load,) + own[0].shape, own[0].dtype)
    return pl.pallas_call(
        functools.partial(choose_kernel, slot, part, load, len(own), len(ups)),
        in_specs=[pl.BlockSpec(memory_space=pltpu.SMEM)] + [anywhere] * (len(own) + 2 * len(ups)),
        out_specs=[pl.BlockSpec(memory_space=pltpu.VMEM)] * 2,
        out_shape=[shape, shape],
        scratch_shapes=[pltpu.SemaphoreType.DMA((2, load))],
        cost_estimate=pl.CostEstimate(flops=0, bytes_accessed=4 * load * own[0].size * 2, transcendentals=0),
        name="choose_packet",
    )(table, *own, *ups, *downs)


def on_device(volume, measured, path_weights, fractions, bases):
    slices, depth, cols = volume.shape
    local, rows = measured.shape[:2]
    nslab = lax.axis_size("slab")
    device = lax.axis_index("slab")
    angles = local * nslab
    first = device * slices
    classes = rows // slices
    planes = nslab // classes
    pairs = [(i, i + classes) for i in range(nslab - classes)]
    pairs = [[p for p in pairs if p[0] // classes % 2 == odd] for odd in range(2)]
    pairs = [p + [(j, i) for i, j in p] for p in pairs]
    ups_of = lambda step: [(i, i + step) for i in range(nslab - step)]
    downs_of = lambda step: [(i + step, i) for i in range(nslab - step)]

    routed = local == 1 and classes == ROUTED_CLASSES and slices == LANES and rows & (rows - 1) == 0 and angles * HALF == LANES

    def dense(volume, measured, path_weights, fractions, bases):
        left = lax.ppermute(volume[slices - 1 :], "slab", ups_of(1))
        right = lax.ppermute(volume[:1], "slab", downs_of(1))
        share = lax.dynamic_slice_in_dim(jnp.pad(fractions, ((0, 0), (1, 1))), first, slices + 2, 1)
        tables = make_tables(share, first, rows, path_weights, bases, slices)
        my_bases = lax.dynamic_slice_in_dim(bases, device * local, local, 0)
        turned = jax.vmap(lambda m, b: jnp.roll(m, b - 1, axis=0))(measured, my_bases)
        by_class = turned.reshape(local, classes, slices, cols).transpose(1, 0, 2, 3)
        outgoing = jnp.tile(by_class, (planes, 1, 1, 1)).reshape(angles, slices, cols)
        seen = lax.all_to_all(outgoing, "slab", split_axis=0, concat_axis=0, tiled=True)
        ends = jnp.roll(by_class[:, :, slices - 1], 1, axis=0)
        ends = jnp.tile(ends, (planes, 1, 1)).reshape(angles, cols // LANES, LANES)
        edge = lax.all_to_all(ends, "slab", split_axis=0, concat_axis=0, tiled=True).reshape(angles, cols)
        return update(volume, right, tables, [seen], jnp.zeros((8, LANES), jnp.int32), None, 0, 1, (left, edge))[0]

    if not routed:
        return dense(volume, measured, path_weights, fractions, bases)

    number = device.astype(jnp.int32)[None]
    upper, lower = PARTS - 1, 0
    exchange = lambda runs: [runs[0]] + [
        lax.ppermute(runs[d], "slab", [(i, i ^ d) for i in range(nslab)]) for d in range(1, classes)
    ]
    runs = turn(number, bases, measured[0], classes, upper)
    runs, late_bases, seen = lax.optimization_barrier((runs, bases, measured[0]))
    own = {upper: exchange(runs)}

    row_of_bases = jnp.pad(late_bases, (0, LANES - angles), constant_values=1)[None]
    most = -(-classes * (planes - 1) // LOAD) + planes - 2
    ends = [5, 6, 7]
    table, which = pl.pallas_call(
        functools.partial(plan_kernel, most, planes, classes, angles, slices // PARTS, rows, ends),
        in_specs=[pl.BlockSpec(memory_space=pltpu.SMEM), pl.BlockSpec(memory_space=pltpu.VMEM)],
        out_specs=[pl.BlockSpec(memory_space=pltpu.VMEM), pl.BlockSpec(memory_space=pltpu.SMEM)],
        out_shape=[jax.ShapeDtypeStruct((16, LANES), jnp.int32), jax.ShapeDtypeStruct((1,), jnp.int32)],
        name="plan_slots",
    )(number, row_of_bases)
    table, which, high = lax.optimization_barrier((table, which, volume[:1]))
    right = lax.ppermute(high, "slab", downs_of(1))
    runs = turn(number, bases, seen, classes, lower)
    tables = device_tables(number, row_of_bases, fractions, path_weights, rows, upper, 0)
    tables = [tables[0], *tables[2:]]
    arrived, runs, table, tables, right = lax.optimization_barrier((own[upper], runs, table, tables, right))

    def finish(end):
        def branch(arrived, runs, table, upper_tables, right):
            own = {upper: arrived, lower: exchange(runs)}
            first, other = {upper: [], lower: []}, {upper: [], lower: []}
            late = row_of_bases
            tables = {upper: (upper_tables[0], None, *upper_tables[1:]), lower: None}
            beside = {(0, upper): (upper, 1), (1, upper): (lower, 0), (1, lower): (lower, 1)}
            for slot in range(-(-end // LOAD)):
                load = min(LOAD, end - slot * LOAD)
                for part in (upper, lower):
                    go_first, go_other = choose(slot, part, load, table, own[part], first[part], other[part])
                    if (slot, part) in beside:
                        go_first, go_other, late = lax.optimization_barrier((go_first, go_other, late))
                        where, piece = beside[slot, part]
                        made = device_tables(number, late, fractions, path_weights, rows, where, piece, tables[where])
                        table, made = lax.optimization_barrier((table, made))
                        tables[where] = made
                    first[part].append(lax.ppermute(go_first, "slab", pairs[0]))
                    other[part].append(lax.ppermute(go_other, "slab", pairs[1]))
            packets = {part: own[part] + first[part] + other[part] for part in (upper, lower)}
            out, last = update(volume, right, tables[upper], packets[upper], table, None, upper, PARTS)
            ahead = lax.ppermute(last, "slab", ups_of(1))
            out, second = update(volume, right, tables[lower], packets[lower], table, out, lower, PARTS)
            return mend(out, tables[lower][-1], tables[upper][-1], ahead, second)

        return branch

    others = lambda *_: dense(volume, measured, path_weights, fractions, bases)
    return lax.switch(which[0], [finish(e) for e in ends] + [others], arrived, runs, table, tables, right)


def solution(mesh):
    placed = (P(("groups", "slab"), None, None), P(("groups", "slab"), None, None), P(), P(), P())
    return jax.shard_map(
        on_device,
        mesh=mesh,
        in_specs=placed,
        out_specs=P(("groups", "slab"), None, None),
        check_vma=False,
    )
```

```python
import functools

import jax
import jax.numpy as jnp
from jax import lax
from jax.experimental import pallas as pl
from jax.experimental.pallas import tpu as pltpu
from jax.sharding import PartitionSpec as P

RELAX = 1.0
BLOCK = 16
HALF = 8
LANES = 128
WIDE = 512
PIECES = 4
PARTS = 2
ROUTED_CLASSES = 4
LOAD = 2
CODE = 256
LINES = 5
VMEM_LIMIT = 56 * 2**20


def dot(a, b):
    return jnp.dot(a, b, preferred_element_type=jnp.float32)


def widen(coef):
    return jnp.concatenate([coef] * (WIDE // LANES), axis=1)


def spread_out(own, arrived):
    views = list(enumerate(own))
    return views + [(s * LOAD + n, p.at[n]) for s, p in enumerate(arrived) for n in range(p.shape[0])]


def update_kernel(
    dense, part, table_ref, lower_ref, upper_ref, next_ref, right_ref, coef_ref, image_w_ref, weight_ref, spread_ref, *rest
):
    if dense:
        left_ref, edge_ref, edge_coef_ref, *rest = rest
    out_ref, carry_ref, seen_ref, result_ref, sems, out_sems = rest[-6:]
    packets = rest[:-7]
    block = pl.program_id(0)
    blocks = pl.num_programs(0)
    depth, width = lower_ref.shape[1:]
    angles = weight_ref.shape[0]
    first = part * blocks * BLOCK

    def fetch(at_block, act):
        slot = at_block % 2
        rows = pl.ds(pl.multiple_of(at_block * BLOCK, BLOCK), BLOCK)
        if dense:
            act(pltpu.make_async_copy(packets[0].at[:, rows], seen_ref.at[slot], sems.at[slot, 0]))
            return
        middle = (len(packets) - ROUTED_CLASSES) // 2 + ROUTED_CLASSES
        views = [(4, *v) for v in spread_out(packets[:ROUTED_CLASSES], [])]
        views += [(2, *v) for v in spread_out([], packets[ROUTED_CLASSES:middle])]
        views += [(3, *v) for v in spread_out([], packets[middle:])]
        for n, (line, spot, view) in enumerate(views):
            name = table_ref[part * LINES + line, spot]

            @pl.when(name >= 0)
            def _():
                act(pltpu.make_async_copy(view.at[rows], seen_ref.at[slot, name], sems.at[slot, n]))

    def deliver(at_block, act, pieces=range(PIECES)):
        slot = at_block % 2
        rows = pl.ds(first + at_block * BLOCK, BLOCK)
        for n in pieces:
            at = pl.ds(n * (width // PIECES), width // PIECES)
            act(pltpu.make_async_copy(result_ref.at[slot, :, :, at], out_ref.at[rows, :, at], out_sems.at[slot, n]))

    @pl.when(block == 0)
    def _():
        seen_ref[...] = jnp.zeros_like(seen_ref)
        fetch(block, lambda copy: copy.start())

    @pl.when(block + 1 < blocks)
    def _():
        fetch(block + 1, lambda copy: copy.start())

    @pl.when(block == 0)
    def _():
        if not dense:
            carry_ref[...] = jnp.zeros_like(carry_ref)
            return
        for chunk in range(width // WIDE):
            at = pl.ds(chunk * WIDE, WIDE)
            mine = dot(weight_ref[...], lower_ref[0, :, at])
            before = dot(weight_ref[...], left_ref[0, :, at])
            carry_ref[:, at] = (
                edge_ref[:, at].astype(jnp.float32) * widen(edge_coef_ref[2])
                - mine * widen(edge_coef_ref[0])
                - before * widen(edge_coef_ref[1])
            ).astype(jnp.bfloat16)

    @pl.when(block >= 2)
    def _():
        deliver(block - 2, lambda copy: copy.wait())

    fetch(block, lambda copy: copy.wait())
    slot = block % 2
    final = (block == blocks - 1) & (part == PARTS - 1 or dense)

    def columns(chunk):
        if dense:
            return pl.ds(pl.multiple_of(chunk * WIDE, WIDE), WIDE)
        return slice(chunk * WIDE, (chunk + 1) * WIDE)

    def image(chunk):
        at = columns(chunk)
        images = [dot(image_w_ref[...], r[:, :, at].reshape(HALF * depth, WIDE)) for r in (lower_ref, upper_ref)]
        after = dot(weight_ref[...], jnp.where(final, right_ref[0, :, at], next_ref[0, :, at]))
        return images, after

    def residual(chunk, images, after):
        at = columns(chunk)
        seen = seen_ref[slot, :, :, at].astype(jnp.float32)
        ahead = [pltpu.roll(x.reshape(angles, HALF, WIDE), HALF - 1, 1) for x in images]
        ahead.append(jnp.broadcast_to(after.reshape(angles, 1, WIDE), (angles, HALF, WIDE)))
        tail = lax.broadcasted_iota(jnp.int32, (angles, HALF, WIDE), 1) == HALF - 1
        parts = []
        for half in range(2):
            now = jnp.where(tail, ahead[half + 1], ahead[half]).reshape(angles * HALF, WIDE)
            got = seen[:, half * HALF : (half + 1) * HALF].reshape(angles * HALF, WIDE)
            coef = [widen(coef_ref[0, half, n]) for n in range(3)]
            resid = got * coef[2] - now * coef[0] - images[half] * coef[1]
            parts.append(resid.reshape(angles, HALF, WIDE))
        return parts

    def result(chunk, parts):
        at = columns(chunk)
        carry = carry_ref[:, at]
        for half, (resid, r) in enumerate(zip(parts, (lower_ref, upper_ref))):
            inputs = jnp.concatenate([resid.reshape(angles * HALF, WIDE).astype(jnp.bfloat16), carry])
            spread = dot(spread_ref[half], inputs).reshape(HALF, depth, WIDE)
            carry = resid[:, HALF - 1].astype(jnp.bfloat16)
            result_ref[slot, half * HALF : (half + 1) * HALF, :, at] = r[:, :, at].astype(jnp.float32) + spread
        carry_ref[:, at] = carry

    chunks = width // WIDE
    if dense:
        pl.loop(0, chunks)(lambda chunk: result(chunk, residual(chunk, *image(chunk))))
        deliver(block, lambda copy: copy.start())
    else:
        images, resids = {}, {}
        for n in range(chunks + 2):
            if n < chunks:
                images[n] = image(n)
            if 1 <= n <= chunks:
                resids[n - 1] = residual(n - 1, *images.pop(n - 1))
            if n >= 2:
                result(n - 2, resids.pop(n - 2))
                done = (n - 1) * PIECES
                if done % chunks == 0:
                    deliver(block, lambda copy: copy.start(), [done // chunks - 1])

    @pl.when(block == blocks - 1)
    def _():
        @pl.when(block >= 1)
        def _():
            deliver(block - 1, lambda copy: copy.wait())

        deliver(block, lambda copy: copy.wait())


def update(volume, right, tables, packets, table, before, part, parts, ahead=None):
    slices, depth, cols = volume.shape
    dense = ahead is not None
    blocks = slices // BLOCK // parts
    off = part * blocks
    by_block = lambda x: pl.BlockSpec((1,) + x.shape[1:], lambda b, i: (b,) + (0,) * (x.ndim - 1))
    whole = lambda x: pl.BlockSpec(x.shape, lambda b, i: (0,) * x.ndim)
    anywhere = pl.BlockSpec(memory_space=pl.ANY)
    coef, edge_coef, image_w, weights, spread_w = tables
    angles = weights.shape[0]
    ahead = [*ahead, edge_coef] if dense else []
    held = jax.ShapeDtypeStruct((angles, cols), volume.dtype)
    if before is None:
        before = coef
    aliases = {9 + len(ahead) + len(packets): 0} if before.shape == volume.shape else {}
    copies = LOAD * len(packets)
    one = (1, depth, cols)
    return pl.pallas_call(
        functools.partial(update_kernel, dense, part),
        grid_spec=pltpu.PrefetchScalarGridSpec(
            num_scalar_prefetch=1,
            grid=(blocks,),
            in_specs=[
                pl.BlockSpec((HALF, depth, cols), lambda b, i: (2 * (b + off), 0, 0)),
                pl.BlockSpec((HALF, depth, cols), lambda b, i: (2 * (b + off) + 1, 0, 0)),
                pl.BlockSpec(one, lambda b, i: (jnp.minimum((b + off + 1) * BLOCK, slices - 1), 0, 0)),
                whole(right), by_block(coef), whole(image_w), whole(weights),
                pl.BlockSpec((2,) + spread_w.shape[1:], lambda b, i: (b, 0, 0)),
            ]
            + [whole(x) for x in ahead]
            + [anywhere] * (len(packets) + 1),
            out_specs=[anywhere, whole(held)],
            scratch_shapes=[
                pltpu.VMEM((2, angles, BLOCK, cols), jnp.bfloat16),
                pltpu.VMEM((2, BLOCK, depth, cols), jnp.float32),
                pltpu.SemaphoreType.DMA((2, copies)),
                pltpu.SemaphoreType.DMA((2, PIECES)),
            ],
        ),
        out_shape=[jax.ShapeDtypeStruct(volume.shape, jnp.float32), held],
        input_output_aliases=aliases,
        compiler_params=pltpu.CompilerParams(dimension_semantics=("arbitrary",), vmem_limit_bytes=VMEM_LIMIT),
        cost_estimate=pl.CostEstimate(
            flops=4 * slices * depth * cols * angles // parts, bytes_accessed=volume.size * 7 // parts, transcendentals=0
        ),
        name="slab_update",
    )(
        table, volume, volume, volume, right, coef, image_w, weights, spread_w, *ahead, *packets, before
    )


def mend_kernel(lower_ref, upper_ref, first_ref, second_ref, before_ref, out_ref):
    columns = lower_ref.shape[2] - first_ref.shape[0]

    @pl.when(pl.program_id(0) == 0)
    def _():
        out_ref[0] = before_ref[0] + dot(lower_ref[0, :, columns:], first_ref[...])

    @pl.when(pl.program_id(0) == 1)
    def _():
        out_ref[0] = before_ref[0] + dot(upper_ref[0, :, columns:], second_ref[...])


def mend(out, lower, upper, first, second):
    slices, depth, cols = out.shape
    whole = pl.BlockSpec(first.shape, lambda b: (0, 0))
    weights = pl.BlockSpec((1, depth, lower.shape[2]), lambda b: (0, 0, 0))
    slab = pl.BlockSpec((1, depth, cols), lambda b: (b * (slices // 2), 0, 0))
    return pl.pallas_call(
        mend_kernel,
        grid=(2,),
        in_specs=[weights, weights, whole, whole, slab],
        out_specs=slab,
        out_shape=jax.ShapeDtypeStruct(out.shape, out.dtype),
        input_output_aliases={4: 0},
        name="mend_slices",
    )(lower, upper, first, second, out)


def fill_weights(wide_w, turned_w, pick_next, pick_now, pick_carry, spread_ref, half):
    depth, columns = wide_w.shape
    place = lax.broadcasted_iota(jnp.int32, (depth, columns), 1) % HALF
    from_next = wide_w * pick_next
    from_now = wide_w * pick_now
    from_carry = turned_w * pick_carry
    for z in range(HALF):
        row = jnp.where(place == z, from_next, jnp.where(place == z - 1, from_now, 0.0))
        total = jnp.sum(row, axis=1, keepdims=True)
        carry = jnp.zeros_like(from_carry)
        if z == 0:
            total = total + jnp.sum(from_carry, axis=1, keepdims=True)
            carry = from_carry
        scale = RELAX / total
        spread_ref[half, z * depth : (z + 1) * depth, :columns] = (row * scale).astype(jnp.bfloat16)
        spread_ref[half, z * depth : (z + 1) * depth, columns:] = (carry * scale).astype(jnp.bfloat16)


def weights_kernel(wide_w_ref, turned_w_ref, pick_ref, pick_carry_ref, spread_ref):
    picks = pick_ref[0, 0:1], pick_ref[0, 1:2], pick_carry_ref[0]
    fill_weights(wide_w_ref[...], turned_w_ref[...], *picks, spread_ref, 0)


def make_weights(wide_w, turned_w, pick, pick_carry):
    halves = pick.shape[0]
    depth, angles = turned_w.shape
    by_half = lambda shape: pl.BlockSpec((1,) + shape, lambda b: (b,) + (0,) * len(shape))
    whole = lambda x: pl.BlockSpec(x.shape, lambda b: (0,) * x.ndim)
    spread = (HALF * depth, angles * (HALF + 1))
    return pl.pallas_call(
        weights_kernel,
        grid=(halves,),
        in_specs=[whole(wide_w), whole(turned_w), by_half(pick.shape[1:]), by_half(pick_carry.shape[1:])],
        out_specs=by_half(spread),
        out_shape=jax.ShapeDtypeStruct((halves,) + spread, jnp.bfloat16),
        name="spread_weights",
    )(wide_w, turned_w, pick, pick_carry)


def make_tables(share, first, rows, path_weights, bases, slices):
    angles, depth = path_weights.shape
    blocks = slices // BLOCK
    weights = path_weights.astype(jnp.float32)
    ray_total = jnp.sum(weights, axis=1)[:, None]
    norm = 1.0 / (ray_total * ((1.0 - share[:, 1:]) + share[:, :-1]))
    coefs = jnp.stack([(1.0 - share[:, 1:]) * norm, share[:, :-1] * norm, norm])
    coef = coefs[:, :, 1:].reshape(3, angles, blocks, BLOCK // HALF, HALF).transpose(2, 3, 0, 1, 4)
    coef = coef.reshape(blocks, BLOCK // HALF, 3, angles * HALF, 1)
    coef = jnp.broadcast_to(coef, coef.shape[:4] + (LANES,))
    edge_coef = jnp.broadcast_to(coefs[:, :, :1], (3, angles, LANES))
    share_own = share[:, 1:-1]
    row_now = (first - bases)[:, None] + jnp.arange(slices, dtype=jnp.int32)[None, :]
    w_now = jnp.where((row_now >= 0) & (row_now < rows), 1.0 - share_own, 0.0)
    w_next = jnp.where((row_now + 1 >= 0) & (row_now + 1 < rows), share_own, 0.0)
    halves = slices // HALF
    pick = jnp.stack([w_next, jnp.pad(w_now[:, 1:], ((0, 0), (0, 1)))]).reshape(2, angles, halves, HALF)
    pick = pick.transpose(2, 0, 1, 3).reshape(halves, 2, angles * HALF)
    pick_carry = w_now[:, ::HALF].T[:, None, :]
    eye = jnp.eye(HALF, dtype=jnp.float32)
    image_w = jnp.einsum("ad,yz->ayzd", weights, eye).reshape(angles * HALF, HALF * depth).astype(jnp.bfloat16)
    wide_w = jnp.repeat(weights.T, HALF, axis=1)
    return coef, edge_coef, image_w, path_weights, make_weights(wide_w, weights.T, pick, pick_carry)


def column_of(line, tall):
    sub = lax.broadcasted_iota(jnp.int32, (tall, LANES), 0)
    lane = lax.broadcasted_iota(jnp.int32, (tall, LANES), 1)
    return jnp.max(jnp.where(sub == lane, line, -1), axis=1, keepdims=True)


def tables_kernel(rows, off, base_piece, device_ref, bases_ref, own_ref, after_ref, weight_ref, *rest):
    if base_piece:
        coef_ref, spread_ref, image_w_ref, wide_ref, turned_ref = rest
    else:
        coef_ref, spread_ref, wide_ref, turned_ref = rest[2:]
    block = pl.program_id(0) + off
    angles, depth = weight_ref.shape
    first = device_ref[0] * LANES
    shape = (angles, LANES)
    lane = lax.broadcasted_iota(jnp.int32, shape, 1)
    sub = lax.broadcasted_iota(jnp.int32, shape, 0)
    weights = weight_ref[...].astype(jnp.float32)
    ray_total = jnp.sum(weights, axis=1, keepdims=True)
    own = own_ref[...]
    ahead = jnp.where(lane == LANES - 1, pltpu.roll(after_ref[...], LANES - 1, 1), pltpu.roll(own, LANES - 1, 1))
    norm = 1.0 / (ray_total * ((1.0 - ahead) + own))
    coefs = ((1.0 - ahead) * norm, own * norm, norm)
    spots = lax.broadcasted_iota(jnp.int32, (angles, HALF, LANES), 2) - lax.broadcasted_iota(jnp.int32, (angles, HALF, LANES), 1)
    for half in range(BLOCK // HALF):
        here = spots == block * BLOCK + half * HALF
        for n, coef in enumerate(coefs):
            tall = jnp.broadcast_to(coef.reshape(angles, 1, LANES), (angles, HALF, LANES))
            tall = jnp.sum(jnp.where(here, tall, 0.0), axis=2, keepdims=True)
            coef_ref[0, half, n] = jnp.broadcast_to(tall, (angles, HALF, LANES)).reshape(angles * HALF, LANES)

    def fill_image_weights():
        across = (HALF * depth)
        repeat = lax.broadcasted_iota(jnp.int32, (depth, across), 1) % depth
        repeat = jnp.where(repeat == lax.broadcasted_iota(jnp.int32, (depth, across), 0), 1.0, 0.0)
        wide = dot(weight_ref[...], repeat.astype(jnp.bfloat16)).astype(jnp.bfloat16)
        down = angles * HALF
        expand = lax.broadcasted_iota(jnp.int32, (down, angles), 0) // HALF
        expand = jnp.where(expand == lax.broadcasted_iota(jnp.int32, (down, angles), 1), 1.0, 0.0)
        wide = dot(expand.astype(jnp.bfloat16), wide)
        at = lax.broadcasted_iota(jnp.int32, (down, across), 0) % HALF
        same = lax.broadcasted_iota(jnp.int32, (down, across), 1) // depth == at
        image_w_ref[...] = jnp.where(same, wide, 0.0).astype(jnp.bfloat16)

    if base_piece:
        pl.when(block == off)(fill_image_weights)
    row_now = first + lane - column_of(bases_ref[...], angles)
    w_now = jnp.where((row_now >= 0) & (row_now < rows), 1.0 - own, 0.0)
    w_next = jnp.where((row_now + 1 >= 0) & (row_now + 1 < rows), own, 0.0)
    columns = angles * HALF
    mine = lax.broadcasted_iota(jnp.int32, (angles, columns), 1) // HALF
    mine = mine == lax.broadcasted_iota(jnp.int32, (angles, columns), 0)
    square = lax.broadcasted_iota(jnp.int32, (angles, angles), 0) == lax.broadcasted_iota(jnp.int32, (angles, angles), 1)

    def gather(values, start, count):
        near = jnp.where(lane < count, pltpu.roll(values, (2 * LANES - start) % LANES, 1), 0.0)
        step = HALF
        while step < LANES:
            near = near + pltpu.roll(near, step, 1)
            step *= 2
        return jnp.sum(jnp.where(mine, near, 0.0), axis=0, keepdims=True)

    turned = lambda other: lax.dot_general(
        weights, other, (((0,), (0,)), ((), ())), precision=lax.Precision.HIGHEST, preferred_element_type=jnp.float32
    )

    @pl.when(block == off)
    def _():
        wide_ref[...] = turned(jnp.where(mine, 1.0, 0.0))
        turned_ref[...] = turned(jnp.where(square, 1.0, 0.0))

    for half in range(BLOCK // HALF):
        start = block * BLOCK + half * HALF
        pick_next = gather(w_next, start, HALF)
        pick_now = gather(w_now, start + 1, HALF - 1)
        carry = jnp.sum(jnp.where(lane == start, w_now, 0.0), axis=1, keepdims=True)
        pick_carry = jnp.sum(jnp.where(square, carry, 0.0), axis=0, keepdims=True)
        fill_weights(wide_ref[...], turned_ref[...], pick_next, pick_now, pick_carry, spread_ref, half)


def device_tables(device, row_of_bases, fractions, path_weights, rows, part, piece, made=None):
    angles, depth = path_weights.shape
    blocks = LANES // BLOCK // PARTS
    steps = blocks // 2
    here = piece * steps
    last = fractions.shape[1] // LANES - 1
    column = lambda by: pl.BlockSpec((angles, LANES), lambda b, d: (0, jnp.clip(d[0] + by, 0, last)))
    whole = lambda shape: pl.BlockSpec(shape, lambda b, d: (0,) * len(shape))
    coef = (BLOCK // HALF, 3, angles * HALF, LANES)
    image_w = (angles * HALF, HALF * depth)
    spread = (HALF * depth, angles * (HALF + 1))
    out_specs = [
        pl.BlockSpec((1,) + coef, lambda b, d: (b + here, 0, 0, 0, 0)),
        pl.BlockSpec((2,) + spread, lambda b, d: (b + here, 0, 0)),
    ]
    out_shape = [
        jax.ShapeDtypeStruct((blocks,) + coef, jnp.float32),
        jax.ShapeDtypeStruct((2 * blocks,) + spread, jnp.bfloat16),
    ]
    if made is None:
        out_specs.append(whole(image_w))
        out_shape.append(jax.ShapeDtypeStruct(image_w, jnp.bfloat16))
    filled = [] if made is None else [made[0], made[4]]
    done = pl.pallas_call(
        functools.partial(tables_kernel, rows, part * blocks + here, made is None),
        grid_spec=pltpu.PrefetchScalarGridSpec(
            num_scalar_prefetch=1,
            grid=(steps,),
            in_specs=[whole((1, LANES)), column(0), column(1), whole(path_weights.shape)]
            + [pl.BlockSpec(memory_space=pl.ANY)] * len(filled),
            out_specs=out_specs,
            scratch_shapes=[
                pltpu.VMEM((depth, angles * HALF), jnp.float32),
                pltpu.VMEM((depth, angles), jnp.float32),
            ],
        ),
        out_shape=out_shape,
        input_output_aliases={5 + n: n for n in range(len(filled))},
        name="make_tables",
    )(device, row_of_bases, fractions, fractions, path_weights, *filled)
    return done[0], None, done[2] if made is None else made[2], path_weights, done[1]


def turn_kernel(classes, count, part, device_ref, bases_ref, seen_ref, *refs):
    outs, twice_ref, sems = refs[:-2], refs[-2], refs[-1]
    rows, cols = seen_ref.shape
    more = twice_ref.shape[0] - rows
    copies = [
        pltpu.make_async_copy(seen_ref, twice_ref.at[pl.ds(0, rows)], sems.at[0]),
        pltpu.make_async_copy(seen_ref.at[pl.ds(0, more)], twice_ref.at[pl.ds(rows, more)], sems.at[1]),
    ]
    for copy in copies:
        copy.start()
    for copy in copies:
        copy.wait()
    device = device_ref[0]
    base = bases_ref[device]
    my_class = device & (classes - 1)
    slices = count * PARTS

    def window(place, size, at):
        start = (place - base + 1 + rows) & (rows - 1)
        begin = pl.multiple_of(start & ~(BLOCK - 1), BLOCK)
        tall = size + BLOCK
        wide = twice_ref[pl.ds(begin, tall), at].astype(jnp.float32)
        return pltpu.roll(wide, (tall - (start - begin)) % tall, 0)

    for n, out in enumerate(outs):
        place = (my_class ^ n) * slices + part * count

        @pl.loop(0, cols // WIDE)
        def _(chunk):
            at = pl.ds(pl.multiple_of(chunk * WIDE, WIDE), WIDE)
            out[:, at] = window(place, count, at)[:count].astype(jnp.bfloat16)


def turn(device, bases, seen, classes, part):
    rows, cols = seen.shape
    count = rows // classes // PARTS
    return pl.pallas_call(
        functools.partial(turn_kernel, classes, count, part),
        in_specs=[
            pl.BlockSpec(memory_space=pltpu.SMEM),
            pl.BlockSpec(memory_space=pltpu.SMEM),
            pl.BlockSpec(memory_space=pl.ANY),
        ],
        out_specs=[pl.BlockSpec(memory_space=pltpu.VMEM)] * classes,
        out_shape=[jax.ShapeDtypeStruct((count, cols), seen.dtype)] * classes,
        scratch_shapes=[pltpu.VMEM((rows + count + BLOCK, cols), seen.dtype), pltpu.SemaphoreType.DMA((2,))],
        compiler_params=pltpu.CompilerParams(vmem_limit_bytes=32 * 2**20),
        name="turn_rows",
    )(device, bases, seen)


def plan_kernel(slots, planes, classes, angles, count, rows, ends, device_ref, bases_ref, table_ref, which_ref):
    shape = (2 * PARTS * classes, LANES)
    lane = lax.broadcasted_iota(jnp.int32, shape, 1)
    row = lax.broadcasted_iota(jnp.int32, shape, 0)
    class_shift = classes.bit_length() - 1
    base = jnp.broadcast_to(bases_ref[...], shape) - 1
    low_plane = base >> (rows.bit_length() - 1)
    turned = base & (rows - 1)

    def reach(which):
        lowest = low_plane + jnp.where(which * count + count - 1 < turned, 1, 0)
        highest = low_plane + jnp.where(which * count < turned, 1, 0)
        return lowest, highest

    lowest, highest = reach(row >> 1)
    upward = (row & 1) == 0
    source = lane >> class_shift
    at = jnp.where(upward, source, planes - 1 - source)
    to = jnp.where(lane < angles, jnp.where(upward, highest, planes - 1 - lowest), -1)
    key = to * CODE + (CODE - 1 - lane)
    sent = [jnp.full(shape, -1, jnp.int32) for _ in range(planes - 1)]
    for slot in range(slots):
        begin = at
        for link in range(planes - 1):
            ready = (begin == link) & (to > link)
            for n in range(LOAD):
                best = jnp.max(jnp.where(ready, key, -1), axis=1, keepdims=True)
                taken = ready & (key == best)
                at = jnp.where(taken, link + 1, at)
                ready = ready & (key != best)
                which = jnp.where(best >= 0, CODE - 1 - (best & (CODE - 1)), -1)
                sent[link] = jnp.where(lane == slot * LOAD + n, which, sent[link])

    me = device_ref[0]
    my_class = me & (classes - 1)
    plane = me >> class_shift
    none = jnp.full(shape, -1, jnp.int32)
    used = none
    for link in range(planes - 1):
        used = jnp.maximum(used, sent[link])
    used = jnp.max(used, axis=0, keepdims=True)
    head = lane[:1]
    need = jnp.max(jnp.where(used >= 0, head + 1, 0))
    which_ref[0] = sum(jnp.where(need > end, 1, 0) for end in ends)

    tall = -(-max(slots * LOAD, angles) // 8) * 8
    sub = lax.broadcasted_iota(jnp.int32, (tall, LANES), 0)
    held = jnp.where(head < classes, plane * classes + (head ^ my_class), -1)
    for part in range(PARTS):
        low_here, high_here = reach(my_class * PARTS + part)
        wanted = (plane >= low_here) & (plane <= high_here) & (lane < angles)
        wanted = column_of(jnp.where(wanted, 1, 0)[:1], tall) > 0
        keep = lambda ids: jnp.max(jnp.where((sub == ids) & wanted, ids, -1), axis=0, keepdims=True)
        moves = []
        for way, spot in ((0, plane), (1, planes - 1 - plane)):
            sends, gets = none, none
            for link in range(planes - 1):
                sends = jnp.where(spot == link, sent[link], sends)
                gets = jnp.where(spot == link + 1, sent[link], gets)
            mine = row == 2 * (my_class * PARTS + part) + way
            sends = jnp.max(jnp.where(mine, sends, -1), axis=0, keepdims=True)
            gets = jnp.max(jnp.where(mine, gets, -1), axis=0, keepdims=True)
            arrived = jnp.max(jnp.where((column_of(gets, tall) == sends) & (sends >= 0), sub, 0), axis=0, keepdims=True)
            own = (sends >> class_shift) == plane
            index = jnp.where(own, (sends & (classes - 1)) ^ my_class, classes + arrived)
            moves.append((jnp.where(sends >= 0, index, 0), keep(gets)))
        for exchange in range(2):
            upward = ((plane + exchange) & 1) == 0
            line = part * LINES + exchange
            table_ref[line : line + 1] = jnp.where(upward, moves[0][0], moves[1][0])
            table_ref[line + 2 : line + 3] = jnp.where(upward, moves[1][1], moves[0][1])
        line = part * LINES + 4
        table_ref[line : line + 1] = keep(held)


def choose_kernel(slot, part, load, own, ups, table_ref, *refs):
    sources, (*outs, sems) = refs[: own + 2 * ups], refs[own + 2 * ups :]
    arrived = sources[own + ups :], sources[own : own + ups]
    views = [spread_out(sources[:own], []) + [(own + n, v) for n, v in spread_out([], side)] for side in arrived]
    spots = [(way, n) for way in range(2) for n in range(load)]
    for way, n in spots:
        for m, view in views[way]:

            @pl.when(table_ref[part * LINES + way, slot * LOAD + n] == m)
            def _():
                pltpu.make_async_copy(view, outs[way].at[n], sems.at[way, n]).start()

    for way, n in spots:
        pltpu.make_async_copy(sources[0], outs[way].at[n], sems.at[way, n]).wait()


def choose(slot, part, load, table, own, ups, downs):
    anywhere = pl.BlockSpec(memory_space=pl.ANY)
    shape = jax.ShapeDtypeStruct((load,) + own[0].shape, own[0].dtype)
    return pl.pallas_call(
        functools.partial(choose_kernel, slot, part, load, len(own), len(ups)),
        in_specs=[pl.BlockSpec(memory_space=pltpu.SMEM)] + [anywhere] * (len(own) + 2 * len(ups)),
        out_specs=[pl.BlockSpec(memory_space=pltpu.VMEM)] * 2,
        out_shape=[shape, shape],
        scratch_shapes=[pltpu.SemaphoreType.DMA((2, load))],
        cost_estimate=pl.CostEstimate(flops=0, bytes_accessed=4 * load * own[0].size * 2, transcendentals=0),
        name="choose_packet",
    )(table, *own, *ups, *downs)


def on_device(volume, measured, path_weights, fractions, bases):
    slices, depth, cols = volume.shape
    local, rows = measured.shape[:2]
    nslab = lax.axis_size("slab")
    device = lax.axis_index("slab")
    angles = local * nslab
    first = device * slices
    classes = rows // slices
    planes = nslab // classes
    pairs = [(i, i + classes) for i in range(nslab - classes)]
    pairs = [[p for p in pairs if p[0] // classes % 2 == odd] for odd in range(2)]
    pairs = [p + [(j, i) for i, j in p] for p in pairs]
    ups_of = lambda step: [(i, i + step) for i in range(nslab - step)]
    downs_of = lambda step: [(i + step, i) for i in range(nslab - step)]

    routed = local == 1 and classes == ROUTED_CLASSES and slices == LANES and rows & (rows - 1) == 0 and angles * HALF == LANES

    def dense(volume, measured, path_weights, fractions, bases):
        left = lax.ppermute(volume[slices - 1 :], "slab", ups_of(1))
        right = lax.ppermute(volume[:1], "slab", downs_of(1))
        share = lax.dynamic_slice_in_dim(jnp.pad(fractions, ((0, 0), (1, 1))), first, slices + 2, 1)
        tables = make_tables(share, first, rows, path_weights, bases, slices)
        my_bases = lax.dynamic_slice_in_dim(bases, device * local, local, 0)
        turned = jax.vmap(lambda m, b: jnp.roll(m, b - 1, axis=0))(measured, my_bases)
        by_class = turned.reshape(local, classes, slices, cols).transpose(1, 0, 2, 3)
        outgoing = jnp.tile(by_class, (planes, 1, 1, 1)).reshape(angles, slices, cols)
        seen = lax.all_to_all(outgoing, "slab", split_axis=0, concat_axis=0, tiled=True)
        ends = jnp.roll(by_class[:, :, slices - 1], 1, axis=0)
        ends = jnp.tile(ends, (planes, 1, 1)).reshape(angles, cols // LANES, LANES)
        edge = lax.all_to_all(ends, "slab", split_axis=0, concat_axis=0, tiled=True).reshape(angles, cols)
        return update(volume, right, tables, [seen], jnp.zeros((8, LANES), jnp.int32), None, 0, 1, (left, edge))[0]

    if not routed:
        return dense(volume, measured, path_weights, fractions, bases)

    number = device.astype(jnp.int32)[None]
    upper, lower = PARTS - 1, 0
    exchange = lambda runs: [runs[0]] + [
        lax.ppermute(runs[d], "slab", [(i, i ^ d) for i in range(nslab)]) for d in range(1, classes)
    ]
    runs = turn(number, bases, measured[0], classes, upper)
    runs, late_bases, seen = lax.optimization_barrier((runs, bases, measured[0]))
    own = {upper: exchange(runs)}

    row_of_bases = jnp.pad(late_bases, (0, LANES - angles), constant_values=1)[None]
    most = -(-classes * (planes - 1) // LOAD) + planes - 2
    ends = [5, 6, 7]
    table, which = pl.pallas_call(
        functools.partial(plan_kernel, most, planes, classes, angles, slices // PARTS, rows, ends),
        in_specs=[pl.BlockSpec(memory_space=pltpu.SMEM), pl.BlockSpec(memory_space=pltpu.VMEM)],
        out_specs=[pl.BlockSpec(memory_space=pltpu.VMEM), pl.BlockSpec(memory_space=pltpu.SMEM)],
        out_shape=[jax.ShapeDtypeStruct((16, LANES), jnp.int32), jax.ShapeDtypeStruct((1,), jnp.int32)],
        name="plan_slots",
    )(number, row_of_bases)
    table, which, high = lax.optimization_barrier((table, which, volume[:1]))
    right = lax.ppermute(high, "slab", downs_of(1))
    runs = turn(number, bases, seen, classes, lower)
    tables = device_tables(number, row_of_bases, fractions, path_weights, rows, upper, 0)
    tables = [tables[0], *tables[2:]]
    arrived, runs, table, tables, right = lax.optimization_barrier((own[upper], runs, table, tables, right))

    def finish(end):
        def branch(arrived, runs, table, upper_tables, right):
            own = {upper: arrived, lower: exchange(runs)}
            first, other = {upper: [], lower: []}, {upper: [], lower: []}
            late = row_of_bases
            tables = {upper: (upper_tables[0], None, *upper_tables[1:]), lower: None}
            beside = {(0, upper): (upper, 1), (1, upper): (lower, 0), (1, lower): (lower, 1)}
            for slot in range(-(-end // LOAD)):
                load = min(LOAD, end - slot * LOAD)
                for part in (upper, lower):
                    go_first, go_other = choose(slot, part, load, table, own[part], first[part], other[part])
                    if (slot, part) in beside:
                        go_first, go_other, late = lax.optimization_barrier((go_first, go_other, late))
                        where, piece = beside[slot, part]
                        made = device_tables(number, late, fractions, path_weights, rows, where, piece, tables[where])
                        table, made = lax.optimization_barrier((table, made))
                        tables[where] = made
                    first[part].append(lax.ppermute(go_first, "slab", pairs[0]))
                    other[part].append(lax.ppermute(go_other, "slab", pairs[1]))
            packets = {part: own[part] + first[part] + other[part] for part in (upper, lower)}
            out, last = update(volume, right, tables[upper], packets[upper], table, None, upper, PARTS)
            ahead = lax.ppermute(last, "slab", ups_of(1))
            out, second = update(volume, right, tables[lower], packets[lower], table, out, lower, PARTS)
            return mend(out, tables[lower][-1], tables[upper][-1], ahead, second)

        return branch

    others = lambda *_: dense(volume, measured, path_weights, fractions, bases)
    return lax.switch(which[0], [finish(e) for e in ends] + [others], arrived, runs, table, tables, right)


def solution(mesh):
    placed = (P(("groups", "slab"), None, None), P(("groups", "slab"), None, None), P(), P(), P())
    return jax.shard_map(
        on_device,
        mesh=mesh,
        in_specs=placed,
        out_specs=P(("groups", "slab"), None, None),
        check_vma=False,
    )
```

```python
import functools

import jax
import jax.numpy as jnp
from jax import lax
from jax.experimental import pallas as pl
from jax.experimental.pallas import tpu as pltpu
from jax.sharding import PartitionSpec as P

RELAX = 1.0
BLOCK = 16
HALF = 8
LANES = 128
WIDE = 256
PIECES = 4
PARTS = 2
ROUTED_CLASSES = 4
LOAD = 2
CODE = 256
LINES = 5
VMEM_LIMIT = 56 * 2**20


def dot(a, b):
    return jnp.dot(a, b, preferred_element_type=jnp.float32)


def widen(coef):
    return jnp.concatenate([coef] * (WIDE // LANES), axis=1)


def spread_out(own, arrived):
    views = list(enumerate(own))
    return views + [(s * LOAD + n, p.at[n]) for s, p in enumerate(arrived) for n in range(p.shape[0])]


def update_kernel(
    dense, part, table_ref, lower_ref, upper_ref, next_ref, right_ref, coef_ref, image_w_ref, weight_ref, spread_ref, *rest
):
    if dense:
        left_ref, edge_ref, edge_coef_ref, *rest = rest
    out_ref, carry_ref, seen_ref, result_ref, sems, out_sems = rest[-6:]
    packets = rest[:-7]
    block = pl.program_id(0)
    blocks = pl.num_programs(0)
    depth, width = lower_ref.shape[1:]
    angles = weight_ref.shape[0]
    first = part * blocks * BLOCK

    def fetch(at_block, act):
        slot = at_block % 2
        rows = pl.ds(pl.multiple_of(at_block * BLOCK, BLOCK), BLOCK)
        if dense:
            act(pltpu.make_async_copy(packets[0].at[:, rows], seen_ref.at[slot], sems.at[slot, 0]))
            return
        middle = (len(packets) - ROUTED_CLASSES) // 2 + ROUTED_CLASSES
        views = [(4, *v) for v in spread_out(packets[:ROUTED_CLASSES], [])]
        views += [(2, *v) for v in spread_out([], packets[ROUTED_CLASSES:middle])]
        views += [(3, *v) for v in spread_out([], packets[middle:])]
        for n, (line, spot, view) in enumerate(views):
            name = table_ref[part * LINES + line, spot]

            @pl.when(name >= 0)
            def _():
                act(pltpu.make_async_copy(view.at[rows], seen_ref.at[slot, name], sems.at[slot, n]))

    def deliver(at_block, act, pieces=range(PIECES)):
        slot = at_block % 2
        rows = pl.ds(first + at_block * BLOCK, BLOCK)
        for n in pieces:
            at = pl.ds(n * (width // PIECES), width // PIECES)
            act(pltpu.make_async_copy(result_ref.at[slot, :, :, at], out_ref.at[rows, :, at], out_sems.at[slot, n]))

    @pl.when(block == 0)
    def _():
        seen_ref[...] = jnp.zeros_like(seen_ref)
        fetch(block, lambda copy: copy.start())

    @pl.when(block + 1 < blocks)
    def _():
        fetch(block + 1, lambda copy: copy.start())

    @pl.when(block == 0)
    def _():
        if not dense:
            carry_ref[...] = jnp.zeros_like(carry_ref)
            return
        for chunk in range(width // WIDE):
            at = pl.ds(chunk * WIDE, WIDE)
            mine = dot(weight_ref[...], lower_ref[0, :, at])
            before = dot(weight_ref[...], left_ref[0, :, at])
            carry_ref[:, at] = (
                edge_ref[:, at].astype(jnp.float32) * widen(edge_coef_ref[2])
                - mine * widen(edge_coef_ref[0])
                - before * widen(edge_coef_ref[1])
            ).astype(jnp.bfloat16)

    @pl.when(block >= 2)
    def _():
        deliver(block - 2, lambda copy: copy.wait())

    fetch(block, lambda copy: copy.wait())
    slot = block % 2
    final = (block == blocks - 1) & (part == PARTS - 1 or dense)

    def columns(chunk):
        if dense:
            return pl.ds(pl.multiple_of(chunk * WIDE, WIDE), WIDE)
        return slice(chunk * WIDE, (chunk + 1) * WIDE)

    def image(chunk):
        at = columns(chunk)
        images = [dot(image_w_ref[...], r[:, :, at].reshape(HALF * depth, WIDE)) for r in (lower_ref, upper_ref)]
        after = dot(weight_ref[...], jnp.where(final, right_ref[0, :, at], next_ref[0, :, at]))
        return images, after

    def residual(chunk, images, after):
        at = columns(chunk)
        seen = seen_ref[slot, :, :, at].astype(jnp.float32)
        ahead = [pltpu.roll(x.reshape(angles, HALF, WIDE), HALF - 1, 1) for x in images]
        ahead.append(jnp.broadcast_to(after.reshape(angles, 1, WIDE), (angles, HALF, WIDE)))
        tail = lax.broadcasted_iota(jnp.int32, (angles, HALF, WIDE), 1) == HALF - 1
        parts = []
        for half in range(2):
            now = jnp.where(tail, ahead[half + 1], ahead[half]).reshape(angles * HALF, WIDE)
            got = seen[:, half * HALF : (half + 1) * HALF].reshape(angles * HALF, WIDE)
            coef = [widen(coef_ref[0, half, n]) for n in range(3)]
            resid = got * coef[2] - now * coef[0] - images[half] * coef[1]
            parts.append(resid.reshape(angles, HALF, WIDE))
        return parts

    def result(chunk, parts):
        at = columns(chunk)
        carry = carry_ref[:, at]
        for half, (resid, r) in enumerate(zip(parts, (lower_ref, upper_ref))):
            inputs = jnp.concatenate([resid.reshape(angles * HALF, WIDE).astype(jnp.bfloat16), carry])
            spread = dot(spread_ref[half], inputs).reshape(HALF, depth, WIDE)
            carry = resid[:, HALF - 1].astype(jnp.bfloat16)
            result_ref[slot, half * HALF : (half + 1) * HALF, :, at] = r[:, :, at].astype(jnp.float32) + spread
        carry_ref[:, at] = carry

    chunks = width // WIDE
    if dense:
        pl.loop(0, chunks)(lambda chunk: result(chunk, residual(chunk, *image(chunk))))
        deliver(block, lambda copy: copy.start())
    else:
        images, resids = {}, {}
        for n in range(chunks + 2):
            if n < chunks:
                images[n] = image(n)
            if 1 <= n <= chunks:
                resids[n - 1] = residual(n - 1, *images.pop(n - 1))
            if n >= 2:
                result(n - 2, resids.pop(n - 2))
                done = (n - 1) * PIECES
                if done % chunks == 0:
                    deliver(block, lambda copy: copy.start(), [done // chunks - 1])

    @pl.when(block == blocks - 1)
    def _():
        @pl.when(block >= 1)
        def _():
            deliver(block - 1, lambda copy: copy.wait())

        deliver(block, lambda copy: copy.wait())


def update(volume, right, tables, packets, table, before, part, parts, ahead=None):
    slices, depth, cols = volume.shape
    dense = ahead is not None
    blocks = slices // BLOCK // parts
    off = part * blocks
    by_block = lambda x: pl.BlockSpec((1,) + x.shape[1:], lambda b, i: (b,) + (0,) * (x.ndim - 1))
    whole = lambda x: pl.BlockSpec(x.shape, lambda b, i: (0,) * x.ndim)
    anywhere = pl.BlockSpec(memory_space=pl.ANY)
    coef, edge_coef, image_w, weights, spread_w = tables
    angles = weights.shape[0]
    ahead = [*ahead, edge_coef] if dense else []
    held = jax.ShapeDtypeStruct((angles, cols), volume.dtype)
    if before is None:
        before = coef
    aliases = {9 + len(ahead) + len(packets): 0} if before.shape == volume.shape else {}
    copies = LOAD * len(packets)
    one = (1, depth, cols)
    return pl.pallas_call(
        functools.partial(update_kernel, dense, part),
        grid_spec=pltpu.PrefetchScalarGridSpec(
            num_scalar_prefetch=1,
            grid=(blocks,),
            in_specs=[
                pl.BlockSpec((HALF, depth, cols), lambda b, i: (2 * (b + off), 0, 0)),
                pl.BlockSpec((HALF, depth, cols), lambda b, i: (2 * (b + off) + 1, 0, 0)),
                pl.BlockSpec(one, lambda b, i: (jnp.minimum((b + off + 1) * BLOCK, slices - 1), 0, 0)),
                whole(right), by_block(coef), whole(image_w), whole(weights),
                pl.BlockSpec((2,) + spread_w.shape[1:], lambda b, i: (b, 0, 0)),
            ]
            + [whole(x) for x in ahead]
            + [anywhere] * (len(packets) + 1),
            out_specs=[anywhere, whole(held)],
            scratch_shapes=[
                pltpu.VMEM((2, angles, BLOCK, cols), jnp.bfloat16),
                pltpu.VMEM((2, BLOCK, depth, cols), jnp.float32),
                pltpu.SemaphoreType.DMA((2, copies)),
                pltpu.SemaphoreType.DMA((2, PIECES)),
            ],
        ),
        out_shape=[jax.ShapeDtypeStruct(volume.shape, jnp.float32), held],
        input_output_aliases=aliases,
        compiler_params=pltpu.CompilerParams(dimension_semantics=("arbitrary",), vmem_limit_bytes=VMEM_LIMIT),
        cost_estimate=pl.CostEstimate(
            flops=4 * slices * depth * cols * angles // parts, bytes_accessed=volume.size * 7 // parts, transcendentals=0
        ),
        name="slab_update",
    )(
        table, volume, volume, volume, right, coef, image_w, weights, spread_w, *ahead, *packets, before
    )


def mend_kernel(lower_ref, upper_ref, first_ref, second_ref, before_ref, out_ref):
    columns = lower_ref.shape[2] - first_ref.shape[0]

    @pl.when(pl.program_id(0) == 0)
    def _():
        out_ref[0] = before_ref[0] + dot(lower_ref[0, :, columns:], first_ref[...])

    @pl.when(pl.program_id(0) == 1)
    def _():
        out_ref[0] = before_ref[0] + dot(upper_ref[0, :, columns:], second_ref[...])


def mend(out, lower, upper, first, second):
    slices, depth, cols = out.shape
    whole = pl.BlockSpec(first.shape, lambda b: (0, 0))
    weights = pl.BlockSpec((1, depth, lower.shape[2]), lambda b: (0, 0, 0))
    slab = pl.BlockSpec((1, depth, cols), lambda b: (b * (slices // 2), 0, 0))
    return pl.pallas_call(
        mend_kernel,
        grid=(2,),
        in_specs=[weights, weights, whole, whole, slab],
        out_specs=slab,
        out_shape=jax.ShapeDtypeStruct(out.shape, out.dtype),
        input_output_aliases={4: 0},
        name="mend_slices",
    )(lower, upper, first, second, out)


def fill_weights(wide_w, turned_w, pick_next, pick_now, pick_carry, spread_ref, half):
    depth, columns = wide_w.shape
    place = lax.broadcasted_iota(jnp.int32, (depth, columns), 1) % HALF
    from_next = wide_w * pick_next
    from_now = wide_w * pick_now
    from_carry = turned_w * pick_carry
    for z in range(HALF):
        row = jnp.where(place == z, from_next, jnp.where(place == z - 1, from_now, 0.0))
        total = jnp.sum(row, axis=1, keepdims=True)
        carry = jnp.zeros_like(from_carry)
        if z == 0:
            total = total + jnp.sum(from_carry, axis=1, keepdims=True)
            carry = from_carry
        scale = RELAX / total
        spread_ref[half, z * depth : (z + 1) * depth, :columns] = (row * scale).astype(jnp.bfloat16)
        spread_ref[half, z * depth : (z + 1) * depth, columns:] = (carry * scale).astype(jnp.bfloat16)


def weights_kernel(wide_w_ref, turned_w_ref, pick_ref, pick_carry_ref, spread_ref):
    picks = pick_ref[0, 0:1], pick_ref[0, 1:2], pick_carry_ref[0]
    fill_weights(wide_w_ref[...], turned_w_ref[...], *picks, spread_ref, 0)


def make_weights(wide_w, turned_w, pick, pick_carry):
    halves = pick.shape[0]
    depth, angles = turned_w.shape
    by_half = lambda shape: pl.BlockSpec((1,) + shape, lambda b: (b,) + (0,) * len(shape))
    whole = lambda x: pl.BlockSpec(x.shape, lambda b: (0,) * x.ndim)
    spread = (HALF * depth, angles * (HALF + 1))
    return pl.pallas_call(
        weights_kernel,
        grid=(halves,),
        in_specs=[whole(wide_w), whole(turned_w), by_half(pick.shape[1:]), by_half(pick_carry.shape[1:])],
        out_specs=by_half(spread),
        out_shape=jax.ShapeDtypeStruct((halves,) + spread, jnp.bfloat16),
        name="spread_weights",
    )(wide_w, turned_w, pick, pick_carry)


def make_tables(share, first, rows, path_weights, bases, slices):
    angles, depth = path_weights.shape
    blocks = slices // BLOCK
    weights = path_weights.astype(jnp.float32)
    ray_total = jnp.sum(weights, axis=1)[:, None]
    norm = 1.0 / (ray_total * ((1.0 - share[:, 1:]) + share[:, :-1]))
    coefs = jnp.stack([(1.0 - share[:, 1:]) * norm, share[:, :-1] * norm, norm])
    coef = coefs[:, :, 1:].reshape(3, angles, blocks, BLOCK // HALF, HALF).transpose(2, 3, 0, 1, 4)
    coef = coef.reshape(blocks, BLOCK // HALF, 3, angles * HALF, 1)
    coef = jnp.broadcast_to(coef, coef.shape[:4] + (LANES,))
    edge_coef = jnp.broadcast_to(coefs[:, :, :1], (3, angles, LANES))
    share_own = share[:, 1:-1]
    row_now = (first - bases)[:, None] + jnp.arange(slices, dtype=jnp.int32)[None, :]
    w_now = jnp.where((row_now >= 0) & (row_now < rows), 1.0 - share_own, 0.0)
    w_next = jnp.where((row_now + 1 >= 0) & (row_now + 1 < rows), share_own, 0.0)
    halves = slices // HALF
    pick = jnp.stack([w_next, jnp.pad(w_now[:, 1:], ((0, 0), (0, 1)))]).reshape(2, angles, halves, HALF)
    pick = pick.transpose(2, 0, 1, 3).reshape(halves, 2, angles * HALF)
    pick_carry = w_now[:, ::HALF].T[:, None, :]
    eye = jnp.eye(HALF, dtype=jnp.float32)
    image_w = jnp.einsum("ad,yz->ayzd", weights, eye).reshape(angles * HALF, HALF * depth).astype(jnp.bfloat16)
    wide_w = jnp.repeat(weights.T, HALF, axis=1)
    return coef, edge_coef, image_w, path_weights, make_weights(wide_w, weights.T, pick, pick_carry)


def column_of(line, tall):
    sub = lax.broadcasted_iota(jnp.int32, (tall, LANES), 0)
    lane = lax.broadcasted_iota(jnp.int32, (tall, LANES), 1)
    return jnp.max(jnp.where(sub == lane, line, -1), axis=1, keepdims=True)


def tables_kernel(rows, off, base_piece, device_ref, bases_ref, own_ref, after_ref, weight_ref, *rest):
    if base_piece:
        coef_ref, spread_ref, image_w_ref, wide_ref, turned_ref = rest
    else:
        coef_ref, spread_ref, wide_ref, turned_ref = rest[2:]
    block = pl.program_id(0) + off
    angles, depth = weight_ref.shape
    first = device_ref[0] * LANES
    shape = (angles, LANES)
    lane = lax.broadcasted_iota(jnp.int32, shape, 1)
    sub = lax.broadcasted_iota(jnp.int32, shape, 0)
    weights = weight_ref[...].astype(jnp.float32)
    ray_total = jnp.sum(weights, axis=1, keepdims=True)
    own = own_ref[...]
    ahead = jnp.where(lane == LANES - 1, pltpu.roll(after_ref[...], LANES - 1, 1), pltpu.roll(own, LANES - 1, 1))
    norm = 1.0 / (ray_total * ((1.0 - ahead) + own))
    coefs = ((1.0 - ahead) * norm, own * norm, norm)
    spots = lax.broadcasted_iota(jnp.int32, (angles, HALF, LANES), 2) - lax.broadcasted_iota(jnp.int32, (angles, HALF, LANES), 1)
    for half in range(BLOCK // HALF):
        here = spots == block * BLOCK + half * HALF
        for n, coef in enumerate(coefs):
            tall = jnp.broadcast_to(coef.reshape(angles, 1, LANES), (angles, HALF, LANES))
            tall = jnp.sum(jnp.where(here, tall, 0.0), axis=2, keepdims=True)
            coef_ref[0, half, n] = jnp.broadcast_to(tall, (angles, HALF, LANES)).reshape(angles * HALF, LANES)

    def fill_image_weights():
        across = (HALF * depth)
        repeat = lax.broadcasted_iota(jnp.int32, (depth, across), 1) % depth
        repeat = jnp.where(repeat == lax.broadcasted_iota(jnp.int32, (depth, across), 0), 1.0, 0.0)
        wide = dot(weight_ref[...], repeat.astype(jnp.bfloat16)).astype(jnp.bfloat16)
        down = angles * HALF
        expand = lax.broadcasted_iota(jnp.int32, (down, angles), 0) // HALF
        expand = jnp.where(expand == lax.broadcasted_iota(jnp.int32, (down, angles), 1), 1.0, 0.0)
        wide = dot(expand.astype(jnp.bfloat16), wide)
        at = lax.broadcasted_iota(jnp.int32, (down, across), 0) % HALF
        same = lax.broadcasted_iota(jnp.int32, (down, across), 1) // depth == at
        image_w_ref[...] = jnp.where(same, wide, 0.0).astype(jnp.bfloat16)

    if base_piece:
        pl.when(block == off)(fill_image_weights)
    row_now = first + lane - column_of(bases_ref[...], angles)
    w_now = jnp.where((row_now >= 0) & (row_now < rows), 1.0 - own, 0.0)
    w_next = jnp.where((row_now + 1 >= 0) & (row_now + 1 < rows), own, 0.0)
    columns = angles * HALF
    mine = lax.broadcasted_iota(jnp.int32, (angles, columns), 1) // HALF
    mine = mine == lax.broadcasted_iota(jnp.int32, (angles, columns), 0)
    square = lax.broadcasted_iota(jnp.int32, (angles, angles), 0) == lax.broadcasted_iota(jnp.int32, (angles, angles), 1)

    def gather(values, start, count):
        near = jnp.where(lane < count, pltpu.roll(values, (2 * LANES - start) % LANES, 1), 0.0)
        step = HALF
        while step < LANES:
            near = near + pltpu.roll(near, step, 1)
            step *= 2
        return jnp.sum(jnp.where(mine, near, 0.0), axis=0, keepdims=True)

    turned = lambda other: lax.dot_general(
        weights, other, (((0,), (0,)), ((), ())), precision=lax.Precision.HIGHEST, preferred_element_type=jnp.float32
    )

    @pl.when(block == off)
    def _():
        wide_ref[...] = turned(jnp.where(mine, 1.0, 0.0))
        turned_ref[...] = turned(jnp.where(square, 1.0, 0.0))

    for half in range(BLOCK // HALF):
        start = block * BLOCK + half * HALF
        pick_next = gather(w_next, start, HALF)
        pick_now = gather(w_now, start + 1, HALF - 1)
        carry = jnp.sum(jnp.where(lane == start, w_now, 0.0), axis=1, keepdims=True)
        pick_carry = jnp.sum(jnp.where(square, carry, 0.0), axis=0, keepdims=True)
        fill_weights(wide_ref[...], turned_ref[...], pick_next, pick_now, pick_carry, spread_ref, half)


def device_tables(device, row_of_bases, fractions, path_weights, rows, part, piece, made=None):
    angles, depth = path_weights.shape
    blocks = LANES // BLOCK // PARTS
    steps = blocks // 2
    here = piece * steps
    last = fractions.shape[1] // LANES - 1
    column = lambda by: pl.BlockSpec((angles, LANES), lambda b, d: (0, jnp.clip(d[0] + by, 0, last)))
    whole = lambda shape: pl.BlockSpec(shape, lambda b, d: (0,) * len(shape))
    coef = (BLOCK // HALF, 3, angles * HALF, LANES)
    image_w = (angles * HALF, HALF * depth)
    spread = (HALF * depth, angles * (HALF + 1))
    out_specs = [
        pl.BlockSpec((1,) + coef, lambda b, d: (b + here, 0, 0, 0, 0)),
        pl.BlockSpec((2,) + spread, lambda b, d: (b + here, 0, 0)),
    ]
    out_shape = [
        jax.ShapeDtypeStruct((blocks,) + coef, jnp.float32),
        jax.ShapeDtypeStruct((2 * blocks,) + spread, jnp.bfloat16),
    ]
    if made is None:
        out_specs.append(whole(image_w))
        out_shape.append(jax.ShapeDtypeStruct(image_w, jnp.bfloat16))
    filled = [] if made is None else [made[0], made[4]]
    done = pl.pallas_call(
        functools.partial(tables_kernel, rows, part * blocks + here, made is None),
        grid_spec=pltpu.PrefetchScalarGridSpec(
            num_scalar_prefetch=1,
            grid=(steps,),
            in_specs=[whole((1, LANES)), column(0), column(1), whole(path_weights.shape)]
            + [pl.BlockSpec(memory_space=pl.ANY)] * len(filled),
            out_specs=out_specs,
            scratch_shapes=[
                pltpu.VMEM((depth, angles * HALF), jnp.float32),
                pltpu.VMEM((depth, angles), jnp.float32),
            ],
        ),
        out_shape=out_shape,
        input_output_aliases={5 + n: n for n in range(len(filled))},
        name="make_tables",
    )(device, row_of_bases, fractions, fractions, path_weights, *filled)
    return done[0], None, done[2] if made is None else made[2], path_weights, done[1]


def turn_kernel(classes, count, part, device_ref, bases_ref, seen_ref, volume_ref, *refs):
    *outs, slice_ref, twice_ref, sems = refs
    pltpu.make_async_copy(volume_ref.at[pl.ds(0, 1)], slice_ref, sems.at[2]).start()
    rows, cols = seen_ref.shape
    more = twice_ref.shape[0] - rows
    copies = [
        pltpu.make_async_copy(seen_ref, twice_ref.at[pl.ds(0, rows)], sems.at[0]),
        pltpu.make_async_copy(seen_ref.at[pl.ds(0, more)], twice_ref.at[pl.ds(rows, more)], sems.at[1]),
    ]
    for copy in copies:
        copy.start()
    for copy in copies:
        copy.wait()
    device = device_ref[0]
    base = bases_ref[device]
    my_class = device & (classes - 1)
    slices = count * PARTS

    def window(place, size, at):
        start = (place - base + 1 + rows) & (rows - 1)
        begin = pl.multiple_of(start & ~(BLOCK - 1), BLOCK)
        tall = size + BLOCK
        wide = twice_ref[pl.ds(begin, tall), at].astype(jnp.float32)
        return pltpu.roll(wide, (tall - (start - begin)) % tall, 0)

    for n, out in enumerate(outs):
        place = (my_class ^ n) * slices + part * count

        @pl.loop(0, cols // WIDE)
        def _(chunk):
            at = pl.ds(pl.multiple_of(chunk * WIDE, WIDE), WIDE)
            out[:, at] = window(place, count, at)[:count].astype(jnp.bfloat16)

    pltpu.make_async_copy(volume_ref.at[pl.ds(0, 1)], slice_ref, sems.at[2]).wait()


def turn(device, bases, seen, volume, classes, part):
    rows, cols = seen.shape
    count = rows // classes // PARTS
    return pl.pallas_call(
        functools.partial(turn_kernel, classes, count, part),
        in_specs=[
            pl.BlockSpec(memory_space=pltpu.SMEM),
            pl.BlockSpec(memory_space=pltpu.SMEM),
            pl.BlockSpec(memory_space=pl.ANY),
            pl.BlockSpec(memory_space=pl.ANY),
        ],
        out_specs=[pl.BlockSpec(memory_space=pltpu.VMEM)] * (classes + 1),
        out_shape=[jax.ShapeDtypeStruct((count, cols), seen.dtype)] * classes
        + [jax.ShapeDtypeStruct((1,) + volume.shape[1:], volume.dtype)],
        scratch_shapes=[pltpu.VMEM((rows + count + BLOCK, cols), seen.dtype), pltpu.SemaphoreType.DMA((3,))],
        compiler_params=pltpu.CompilerParams(vmem_limit_bytes=32 * 2**20),
        name="turn_rows",
    )(device, bases, seen, volume)


def plan_kernel(slots, planes, classes, angles, count, rows, ends, device_ref, bases_ref, table_ref, which_ref):
    shape = (2 * PARTS * classes, LANES)
    lane = lax.broadcasted_iota(jnp.int32, shape, 1)
    row = lax.broadcasted_iota(jnp.int32, shape, 0)
    class_shift = classes.bit_length() - 1
    base = jnp.broadcast_to(bases_ref[...], shape) - 1
    low_plane = base >> (rows.bit_length() - 1)
    turned = base & (rows - 1)

    def reach(which):
        lowest = low_plane + jnp.where(which * count + count - 1 < turned, 1, 0)
        highest = low_plane + jnp.where(which * count < turned, 1, 0)
        return lowest, highest

    lowest, highest = reach(row >> 1)
    upward = (row & 1) == 0
    source = lane >> class_shift
    at = jnp.where(upward, source, planes - 1 - source)
    to = jnp.where(lane < angles, jnp.where(upward, highest, planes - 1 - lowest), -1)
    key = to * CODE + (CODE - 1 - lane)
    sent = [jnp.full(shape, -1, jnp.int32) for _ in range(planes - 1)]
    for slot in range(slots):
        begin = at
        for link in range(planes - 1):
            ready = (begin == link) & (to > link)
            for n in range(LOAD):
                best = jnp.max(jnp.where(ready, key, -1), axis=1, keepdims=True)
                taken = ready & (key == best)
                at = jnp.where(taken, link + 1, at)
                ready = ready & (key != best)
                which = jnp.where(best >= 0, CODE - 1 - (best & (CODE - 1)), -1)
                sent[link] = jnp.where(lane == slot * LOAD + n, which, sent[link])

    me = device_ref[0]
    my_class = me & (classes - 1)
    plane = me >> class_shift
    none = jnp.full(shape, -1, jnp.int32)
    used = none
    for link in range(planes - 1):
        used = jnp.maximum(used, sent[link])
    used = jnp.max(used, axis=0, keepdims=True)
    head = lane[:1]
    need = jnp.max(jnp.where(used >= 0, head + 1, 0))
    need = jnp.where(jnp.max(to - at) > 0, slots * LOAD + 1, need)
    which_ref[0] = sum(jnp.where(need > end, 1, 0) for end in ends)

    tall = -(-max(slots * LOAD, angles) // 8) * 8
    sub = lax.broadcasted_iota(jnp.int32, (tall, LANES), 0)
    held = jnp.where(head < classes, plane * classes + (head ^ my_class), -1)
    for part in range(PARTS):
        low_here, high_here = reach(my_class * PARTS + part)
        wanted = (plane >= low_here) & (plane <= high_here) & (lane < angles)
        wanted = column_of(jnp.where(wanted, 1, 0)[:1], tall) > 0
        keep = lambda ids: jnp.max(jnp.where((sub == ids) & wanted, ids, -1), axis=0, keepdims=True)
        moves = []
        for way, spot in ((0, plane), (1, planes - 1 - plane)):
            sends, gets = none, none
            for link in range(planes - 1):
                sends = jnp.where(spot == link, sent[link], sends)
                gets = jnp.where(spot == link + 1, sent[link], gets)
            mine = row == 2 * (my_class * PARTS + part) + way
            sends = jnp.max(jnp.where(mine, sends, -1), axis=0, keepdims=True)
            gets = jnp.max(jnp.where(mine, gets, -1), axis=0, keepdims=True)
            arrived = jnp.max(jnp.where((column_of(gets, tall) == sends) & (sends >= 0), sub, 0), axis=0, keepdims=True)
            own = (sends >> class_shift) == plane
            index = jnp.where(own, (sends & (classes - 1)) ^ my_class, classes + arrived)
            moves.append((jnp.where(sends >= 0, index, 0), keep(gets)))
        for exchange in range(2):
            upward = ((plane + exchange) & 1) == 0
            line = part * LINES + exchange
            table_ref[line : line + 1] = jnp.where(upward, moves[0][0], moves[1][0])
            table_ref[line + 2 : line + 3] = jnp.where(upward, moves[1][1], moves[0][1])
        line = part * LINES + 4
        table_ref[line : line + 1] = keep(held)


def choose_kernel(slot, part, load, own, ups, table_ref, *refs):
    sources, (*outs, sems) = refs[: own + 2 * ups], refs[own + 2 * ups :]
    arrived = sources[own + ups :], sources[own : own + ups]
    views = [spread_out(sources[:own], []) + [(own + n, v) for n, v in spread_out([], side)] for side in arrived]
    spots = [(way, n) for way in range(2) for n in range(load)]
    for way, n in spots:
        for m, view in views[way]:

            @pl.when(table_ref[part * LINES + way, slot * LOAD + n] == m)
            def _():
                pltpu.make_async_copy(view, outs[way].at[n], sems.at[way, n]).start()

    for way, n in spots:
        pltpu.make_async_copy(sources[0], outs[way].at[n], sems.at[way, n]).wait()


def choose(slot, part, load, table, own, ups, downs):
    anywhere = pl.BlockSpec(memory_space=pl.ANY)
    shape = jax.ShapeDtypeStruct((load,) + own[0].shape, own[0].dtype)
    return pl.pallas_call(
        functools.partial(choose_kernel, slot, part, load, len(own), len(ups)),
        in_specs=[pl.BlockSpec(memory_space=pltpu.SMEM)] + [anywhere] * (len(own) + 2 * len(ups)),
        out_specs=[pl.BlockSpec(memory_space=pltpu.VMEM)] * 2,
        out_shape=[shape, shape],
        scratch_shapes=[pltpu.SemaphoreType.DMA((2, load))],
        cost_estimate=pl.CostEstimate(flops=0, bytes_accessed=4 * load * own[0].size * 2, transcendentals=0),
        name="choose_packet",
    )(table, *own, *ups, *downs)


def on_device(volume, measured, path_weights, fractions, bases):
    slices, depth, cols = volume.shape
    local, rows = measured.shape[:2]
    nslab = lax.axis_size("slab")
    device = lax.axis_index("slab")
    angles = local * nslab
    first = device * slices
    classes = rows // slices
    planes = nslab // classes
    pairs = [(i, i + classes) for i in range(nslab - classes)]
    pairs = [[p for p in pairs if p[0] // classes % 2 == odd] for odd in range(2)]
    pairs = [p + [(j, i) for i, j in p] for p in pairs]
    ups_of = lambda step: [(i, i + step) for i in range(nslab - step)]
    downs_of = lambda step: [(i + step, i) for i in range(nslab - step)]

    routed = local == 1 and classes == ROUTED_CLASSES and slices == LANES and rows & (rows - 1) == 0 and angles * HALF == LANES

    def dense(volume, measured, path_weights, fractions, bases):
        left = lax.ppermute(volume[slices - 1 :], "slab", ups_of(1))
        right = lax.ppermute(volume[:1], "slab", downs_of(1))
        share = lax.dynamic_slice_in_dim(jnp.pad(fractions, ((0, 0), (1, 1))), first, slices + 2, 1)
        tables = make_tables(share, first, rows, path_weights, bases, slices)
        my_bases = lax.dynamic_slice_in_dim(bases, device * local, local, 0)
        turned = jax.vmap(lambda m, b: jnp.roll(m, b - 1, axis=0))(measured, my_bases)
        by_class = turned.reshape(local, classes, slices, cols).transpose(1, 0, 2, 3)
        outgoing = jnp.tile(by_class, (planes, 1, 1, 1)).reshape(angles, slices, cols)
        seen = lax.all_to_all(outgoing, "slab", split_axis=0, concat_axis=0, tiled=True)
        ends = jnp.roll(by_class[:, :, slices - 1], 1, axis=0)
        ends = jnp.tile(ends, (planes, 1, 1)).reshape(angles, cols // LANES, LANES)
        edge = lax.all_to_all(ends, "slab", split_axis=0, concat_axis=0, tiled=True).reshape(angles, cols)
        return update(volume, right, tables, [seen], jnp.zeros((8, LANES), jnp.int32), None, 0, 1, (left, edge))[0]

    if not routed:
        return dense(volume, measured, path_weights, fractions, bases)

    number = device.astype(jnp.int32)[None]
    upper, lower = PARTS - 1, 0
    exchange = lambda runs: [runs[0]] + [
        lax.ppermute(runs[d], "slab", [(i, i ^ d) for i in range(nslab)]) for d in range(1, classes)
    ]
    *runs, high = turn(number, bases, measured[0], volume, classes, upper)
    runs, late_bases, seen = lax.optimization_barrier((runs, bases, measured[0]))
    own = {upper: exchange(runs)}

    row_of_bases = jnp.pad(late_bases, (0, LANES - angles), constant_values=1)[None]
    ends = [5, 6, 7]
    most = -(-ends[-1] // LOAD)
    table, which = pl.pallas_call(
        functools.partial(plan_kernel, most, planes, classes, angles, slices // PARTS, rows, ends),
        in_specs=[pl.BlockSpec(memory_space=pltpu.SMEM), pl.BlockSpec(memory_space=pltpu.VMEM)],
        out_specs=[pl.BlockSpec(memory_space=pltpu.VMEM), pl.BlockSpec(memory_space=pltpu.SMEM)],
        out_shape=[jax.ShapeDtypeStruct((16, LANES), jnp.int32), jax.ShapeDtypeStruct((1,), jnp.int32)],
        name="plan_slots",
    )(number, row_of_bases)
    table, which, high = lax.optimization_barrier((table, which, high))
    right = lax.ppermute(high, "slab", downs_of(1))
    *runs, _ = turn(number, bases, seen, volume, classes, lower)
    tables = device_tables(number, row_of_bases, fractions, path_weights, rows, upper, 0)
    tables = [tables[0], *tables[2:]]
    arrived, runs, table, tables, right = lax.optimization_barrier((own[upper], runs, table, tables, right))

    def finish(end):
        def branch(arrived, runs, table, upper_tables, right):
            own = {upper: arrived, lower: exchange(runs)}
            first, other = {upper: [], lower: []}, {upper: [], lower: []}
            late = row_of_bases
            tables = {upper: (upper_tables[0], None, *upper_tables[1:]), lower: None}
            beside = {(0, upper): (upper, 1), (1, upper): (lower, 0), (1, lower): (lower, 1)}
            for slot in range(-(-end // LOAD)):
                load = min(LOAD, end - slot * LOAD)
                for part in (upper, lower):
                    go_first, go_other = choose(slot, part, load, table, own[part], first[part], other[part])
                    if (slot, part) in beside:
                        go_first, go_other, late = lax.optimization_barrier((go_first, go_other, late))
                        where, piece = beside[slot, part]
                        made = device_tables(number, late, fractions, path_weights, rows, where, piece, tables[where])
                        table, made = lax.optimization_barrier((table, made))
                        tables[where] = made
                    first[part].append(lax.ppermute(go_first, "slab", pairs[0]))
                    other[part].append(lax.ppermute(go_other, "slab", pairs[1]))
            packets = {part: own[part] + first[part] + other[part] for part in (upper, lower)}
            out, last = update(volume, right, tables[upper], packets[upper], table, None, upper, PARTS)
            ahead = lax.ppermute(last, "slab", ups_of(1))
            out, second = update(volume, right, tables[lower], packets[lower], table, out, lower, PARTS)
            return mend(out, tables[lower][-1], tables[upper][-1], ahead, second)

        return branch

    others = lambda *_: dense(volume, measured, path_weights, fractions, bases)
    return lax.switch(which[0], [finish(e) for e in ends] + [others], arrived, runs, table, tables, right)


def solution(mesh):
    placed = (P(("groups", "slab"), None, None), P(("groups", "slab"), None, None), P(), P(), P())
    return jax.shard_map(
        on_device,
        mesh=mesh,
        in_specs=placed,
        out_specs=P(("groups", "slab"), None, None),
        check_vma=False,
    )
```

```python
import functools

import jax
import jax.numpy as jnp
from jax import lax
from jax.experimental import pallas as pl
from jax.experimental.pallas import tpu as pltpu
from jax.sharding import PartitionSpec as P

RELAX = 1.0
BLOCK = 16
HALF = 8
LANES = 128
WIDE = 256
PIECES = 4
PARTS = 2
ROUTED_CLASSES = 4
LOAD = 2
CODE = 256
LINES = 5
VMEM_LIMIT = 56 * 2**20


def dot(a, b):
    return jnp.dot(a, b, preferred_element_type=jnp.float32)


def widen(coef):
    return jnp.concatenate([coef] * (WIDE // LANES), axis=1)


def spread_out(own, arrived):
    views = list(enumerate(own))
    return views + [(s * LOAD + n, p.at[n]) for s, p in enumerate(arrived) for n in range(p.shape[0])]


def update_kernel(
    dense, part, table_ref, lower_ref, upper_ref, next_ref, right_ref, coef_ref, image_w_ref, weight_ref, spread_ref, *rest
):
    if dense:
        left_ref, edge_ref, edge_coef_ref, *rest = rest
    out_ref, carry_ref, seen_ref, result_ref, sems, out_sems = rest[-6:]
    packets = rest[:-7]
    block = pl.program_id(0)
    blocks = pl.num_programs(0)
    depth, width = lower_ref.shape[1:]
    angles = weight_ref.shape[0]
    first = part * blocks * BLOCK

    def fetch(at_block, act):
        slot = at_block % 2
        rows = pl.ds(pl.multiple_of(at_block * BLOCK, BLOCK), BLOCK)
        if dense:
            act(pltpu.make_async_copy(packets[0].at[:, rows], seen_ref.at[slot], sems.at[slot, 0]))
            return
        middle = (len(packets) - ROUTED_CLASSES) // 2 + ROUTED_CLASSES
        views = [(4, *v) for v in spread_out(packets[:ROUTED_CLASSES], [])]
        views += [(2, *v) for v in spread_out([], packets[ROUTED_CLASSES:middle])]
        views += [(3, *v) for v in spread_out([], packets[middle:])]
        for n, (line, spot, view) in enumerate(views):
            name = table_ref[part * LINES + line, spot]

            @pl.when(name >= 0)
            def _():
                act(pltpu.make_async_copy(view.at[rows], seen_ref.at[slot, name], sems.at[slot, n]))

    def deliver(at_block, act, pieces=range(PIECES)):
        slot = at_block % 2
        rows = pl.ds(first + at_block * BLOCK, BLOCK)
        for n in pieces:
            at = pl.ds(n * (width // PIECES), width // PIECES)
            act(pltpu.make_async_copy(result_ref.at[slot, :, :, at], out_ref.at[rows, :, at], out_sems.at[slot, n]))

    @pl.when(block == 0)
    def _():
        seen_ref[...] = jnp.zeros_like(seen_ref)
        fetch(block, lambda copy: copy.start())

    @pl.when(block + 1 < blocks)
    def _():
        fetch(block + 1, lambda copy: copy.start())

    @pl.when(block == 0)
    def _():
        if not dense:
            carry_ref[...] = jnp.zeros_like(carry_ref)
            return
        for chunk in range(width // WIDE):
            at = pl.ds(chunk * WIDE, WIDE)
            mine = dot(weight_ref[...], lower_ref[0, :, at])
            before = dot(weight_ref[...], left_ref[0, :, at])
            carry_ref[:, at] = (
                edge_ref[:, at].astype(jnp.float32) * widen(edge_coef_ref[2])
                - mine * widen(edge_coef_ref[0])
                - before * widen(edge_coef_ref[1])
            ).astype(jnp.bfloat16)

    @pl.when(block >= 2)
    def _():
        deliver(block - 2, lambda copy: copy.wait())

    fetch(block, lambda copy: copy.wait())
    slot = block % 2
    final = (block == blocks - 1) & (part == PARTS - 1 or dense)

    def columns(chunk):
        if dense:
            return pl.ds(pl.multiple_of(chunk * WIDE, WIDE), WIDE)
        return slice(chunk * WIDE, (chunk + 1) * WIDE)

    def image(chunk):
        at = columns(chunk)
        images = [dot(image_w_ref[...], r[:, :, at].reshape(HALF * depth, WIDE)) for r in (lower_ref, upper_ref)]
        after = dot(weight_ref[...], jnp.where(final, right_ref[0, :, at], next_ref[0, :, at]))
        return images, after

    def residual(chunk, images, after):
        at = columns(chunk)
        seen = seen_ref[slot, :, :, at].astype(jnp.float32)
        ahead = [pltpu.roll(x.reshape(angles, HALF, WIDE), HALF - 1, 1) for x in images]
        ahead.append(jnp.broadcast_to(after.reshape(angles, 1, WIDE), (angles, HALF, WIDE)))
        tail = lax.broadcasted_iota(jnp.int32, (angles, HALF, WIDE), 1) == HALF - 1
        parts = []
        for half in range(2):
            now = jnp.where(tail, ahead[half + 1], ahead[half]).reshape(angles * HALF, WIDE)
            got = seen[:, half * HALF : (half + 1) * HALF].reshape(angles * HALF, WIDE)
            coef = [widen(coef_ref[0, half, n]) for n in range(3)]
            resid = got * coef[2] - now * coef[0] - images[half] * coef[1]
            parts.append(resid.reshape(angles, HALF, WIDE))
        return parts

    def result(chunk, parts):
        at = columns(chunk)
        carry = carry_ref[:, at]
        for half, (resid, r) in enumerate(zip(parts, (lower_ref, upper_ref))):
            inputs = jnp.concatenate([resid.reshape(angles * HALF, WIDE).astype(jnp.bfloat16), carry])
            spread = dot(spread_ref[half], inputs).reshape(HALF, depth, WIDE)
            carry = resid[:, HALF - 1].astype(jnp.bfloat16)
            result_ref[slot, half * HALF : (half + 1) * HALF, :, at] = r[:, :, at].astype(jnp.float32) + spread
        carry_ref[:, at] = carry

    chunks = width // WIDE
    if dense:
        pl.loop(0, chunks)(lambda chunk: result(chunk, residual(chunk, *image(chunk))))
        deliver(block, lambda copy: copy.start())
    else:
        images, resids = {}, {}
        for n in range(chunks + 2):
            if n < chunks:
                images[n] = image(n)
            if 1 <= n <= chunks:
                resids[n - 1] = residual(n - 1, *images.pop(n - 1))
            if n >= 2:
                result(n - 2, resids.pop(n - 2))
                done = (n - 1) * PIECES
                if done % chunks == 0:
                    deliver(block, lambda copy: copy.start(), [done // chunks - 1])

    @pl.when(block == blocks - 1)
    def _():
        @pl.when(block >= 1)
        def _():
            deliver(block - 1, lambda copy: copy.wait())

        deliver(block, lambda copy: copy.wait())


def update(volume, right, tables, packets, table, before, part, parts, ahead=None):
    slices, depth, cols = volume.shape
    dense = ahead is not None
    blocks = slices // BLOCK // parts
    off = part * blocks
    by_block = lambda x: pl.BlockSpec((1,) + x.shape[1:], lambda b, i: (b,) + (0,) * (x.ndim - 1))
    whole = lambda x: pl.BlockSpec(x.shape, lambda b, i: (0,) * x.ndim)
    anywhere = pl.BlockSpec(memory_space=pl.ANY)
    coef, edge_coef, image_w, weights, spread_w = tables
    angles = weights.shape[0]
    ahead = [*ahead, edge_coef] if dense else []
    held = jax.ShapeDtypeStruct((angles, cols), volume.dtype)
    if before is None:
        before = coef
    aliases = {9 + len(ahead) + len(packets): 0} if before.shape == volume.shape else {}
    copies = LOAD * len(packets)
    one = (1, depth, cols)
    return pl.pallas_call(
        functools.partial(update_kernel, dense, part),
        grid_spec=pltpu.PrefetchScalarGridSpec(
            num_scalar_prefetch=1,
            grid=(blocks,),
            in_specs=[
                pl.BlockSpec((HALF, depth, cols), lambda b, i: (2 * (b + off), 0, 0)),
                pl.BlockSpec((HALF, depth, cols), lambda b, i: (2 * (b + off) + 1, 0, 0)),
                pl.BlockSpec(one, lambda b, i: (jnp.minimum((b + off + 1) * BLOCK, slices - 1), 0, 0)),
                whole(right), by_block(coef), whole(image_w), whole(weights),
                pl.BlockSpec((2,) + spread_w.shape[1:], lambda b, i: (b, 0, 0)),
            ]
            + [whole(x) for x in ahead]
            + [anywhere] * (len(packets) + 1),
            out_specs=[anywhere, whole(held)],
            scratch_shapes=[
                pltpu.VMEM((2, angles, BLOCK, cols), jnp.bfloat16),
                pltpu.VMEM((2, BLOCK, depth, cols), jnp.float32),
                pltpu.SemaphoreType.DMA((2, copies)),
                pltpu.SemaphoreType.DMA((2, PIECES)),
            ],
        ),
        out_shape=[jax.ShapeDtypeStruct(volume.shape, jnp.float32), held],
        input_output_aliases=aliases,
        compiler_params=pltpu.CompilerParams(dimension_semantics=("arbitrary",), vmem_limit_bytes=VMEM_LIMIT),
        cost_estimate=pl.CostEstimate(
            flops=4 * slices * depth * cols * angles // parts, bytes_accessed=volume.size * 7 // parts, transcendentals=0
        ),
        name="slab_update",
    )(
        table, volume, volume, volume, right, coef, image_w, weights, spread_w, *ahead, *packets, before
    )


def mend_kernel(lower_ref, upper_ref, first_ref, second_ref, before_ref, out_ref):
    columns = lower_ref.shape[2] - first_ref.shape[0]

    @pl.when(pl.program_id(0) == 0)
    def _():
        out_ref[0] = before_ref[0] + dot(lower_ref[0, :, columns:], first_ref[...])

    @pl.when(pl.program_id(0) == 1)
    def _():
        out_ref[0] = before_ref[0] + dot(upper_ref[0, :, columns:], second_ref[...])


def mend(out, lower, upper, first, second):
    slices, depth, cols = out.shape
    whole = pl.BlockSpec(first.shape, lambda b: (0, 0))
    weights = pl.BlockSpec((1, depth, lower.shape[2]), lambda b: (0, 0, 0))
    slab = pl.BlockSpec((1, depth, cols), lambda b: (b * (slices // 2), 0, 0))
    return pl.pallas_call(
        mend_kernel,
        grid=(2,),
        in_specs=[weights, weights, whole, whole, slab],
        out_specs=slab,
        out_shape=jax.ShapeDtypeStruct(out.shape, out.dtype),
        input_output_aliases={4: 0},
        name="mend_slices",
    )(lower, upper, first, second, out)


def fill_weights(wide_w, turned_w, pick_next, pick_now, pick_carry, spread_ref, half):
    depth, columns = wide_w.shape
    place = lax.broadcasted_iota(jnp.int32, (depth, columns), 1) % HALF
    from_next = wide_w * pick_next
    from_now = wide_w * pick_now
    from_carry = turned_w * pick_carry
    for z in range(HALF):
        row = jnp.where(place == z, from_next, jnp.where(place == z - 1, from_now, 0.0))
        total = jnp.sum(row, axis=1, keepdims=True)
        carry = jnp.zeros_like(from_carry)
        if z == 0:
            total = total + jnp.sum(from_carry, axis=1, keepdims=True)
            carry = from_carry
        scale = RELAX / total
        spread_ref[half, z * depth : (z + 1) * depth, :columns] = (row * scale).astype(jnp.bfloat16)
        spread_ref[half, z * depth : (z + 1) * depth, columns:] = (carry * scale).astype(jnp.bfloat16)


def weights_kernel(wide_w_ref, turned_w_ref, pick_ref, pick_carry_ref, spread_ref):
    picks = pick_ref[0, 0:1], pick_ref[0, 1:2], pick_carry_ref[0]
    fill_weights(wide_w_ref[...], turned_w_ref[...], *picks, spread_ref, 0)


def make_weights(wide_w, turned_w, pick, pick_carry):
    halves = pick.shape[0]
    depth, angles = turned_w.shape
    by_half = lambda shape: pl.BlockSpec((1,) + shape, lambda b: (b,) + (0,) * len(shape))
    whole = lambda x: pl.BlockSpec(x.shape, lambda b: (0,) * x.ndim)
    spread = (HALF * depth, angles * (HALF + 1))
    return pl.pallas_call(
        weights_kernel,
        grid=(halves,),
        in_specs=[whole(wide_w), whole(turned_w), by_half(pick.shape[1:]), by_half(pick_carry.shape[1:])],
        out_specs=by_half(spread),
        out_shape=jax.ShapeDtypeStruct((halves,) + spread, jnp.bfloat16),
        name="spread_weights",
    )(wide_w, turned_w, pick, pick_carry)


def make_tables(share, first, rows, path_weights, bases, slices):
    angles, depth = path_weights.shape
    blocks = slices // BLOCK
    weights = path_weights.astype(jnp.float32)
    ray_total = jnp.sum(weights, axis=1)[:, None]
    norm = 1.0 / (ray_total * ((1.0 - share[:, 1:]) + share[:, :-1]))
    coefs = jnp.stack([(1.0 - share[:, 1:]) * norm, share[:, :-1] * norm, norm])
    coef = coefs[:, :, 1:].reshape(3, angles, blocks, BLOCK // HALF, HALF).transpose(2, 3, 0, 1, 4)
    coef = coef.reshape(blocks, BLOCK // HALF, 3, angles * HALF, 1)
    coef = jnp.broadcast_to(coef, coef.shape[:4] + (LANES,))
    edge_coef = jnp.broadcast_to(coefs[:, :, :1], (3, angles, LANES))
    share_own = share[:, 1:-1]
    row_now = (first - bases)[:, None] + jnp.arange(slices, dtype=jnp.int32)[None, :]
    w_now = jnp.where((row_now >= 0) & (row_now < rows), 1.0 - share_own, 0.0)
    w_next = jnp.where((row_now + 1 >= 0) & (row_now + 1 < rows), share_own, 0.0)
    halves = slices // HALF
    pick = jnp.stack([w_next, jnp.pad(w_now[:, 1:], ((0, 0), (0, 1)))]).reshape(2, angles, halves, HALF)
    pick = pick.transpose(2, 0, 1, 3).reshape(halves, 2, angles * HALF)
    pick_carry = w_now[:, ::HALF].T[:, None, :]
    eye = jnp.eye(HALF, dtype=jnp.float32)
    image_w = jnp.einsum("ad,yz->ayzd", weights, eye).reshape(angles * HALF, HALF * depth).astype(jnp.bfloat16)
    wide_w = jnp.repeat(weights.T, HALF, axis=1)
    return coef, edge_coef, image_w, path_weights, make_weights(wide_w, weights.T, pick, pick_carry)


def column_of(line, tall):
    sub = lax.broadcasted_iota(jnp.int32, (tall, LANES), 0)
    lane = lax.broadcasted_iota(jnp.int32, (tall, LANES), 1)
    return jnp.max(jnp.where(sub == lane, line, -1), axis=1, keepdims=True)


def tables_kernel(rows, off, base_piece, device_ref, bases_ref, own_ref, after_ref, weight_ref, *rest):
    if base_piece:
        coef_ref, spread_ref, image_w_ref, wide_ref, turned_ref = rest
    else:
        coef_ref, spread_ref, wide_ref, turned_ref = rest[2:]
    block = pl.program_id(0) + off
    angles, depth = weight_ref.shape
    first = device_ref[0] * LANES
    shape = (angles, LANES)
    lane = lax.broadcasted_iota(jnp.int32, shape, 1)
    sub = lax.broadcasted_iota(jnp.int32, shape, 0)
    weights = weight_ref[...].astype(jnp.float32)
    ray_total = jnp.sum(weights, axis=1, keepdims=True)
    own = own_ref[...]
    ahead = jnp.where(lane == LANES - 1, pltpu.roll(after_ref[...], LANES - 1, 1), pltpu.roll(own, LANES - 1, 1))
    norm = 1.0 / (ray_total * ((1.0 - ahead) + own))
    coefs = ((1.0 - ahead) * norm, own * norm, norm)
    spots = lax.broadcasted_iota(jnp.int32, (angles, HALF, LANES), 2) - lax.broadcasted_iota(jnp.int32, (angles, HALF, LANES), 1)
    for half in range(BLOCK // HALF):
        here = spots == block * BLOCK + half * HALF
        for n, coef in enumerate(coefs):
            tall = jnp.broadcast_to(coef.reshape(angles, 1, LANES), (angles, HALF, LANES))
            tall = jnp.sum(jnp.where(here, tall, 0.0), axis=2, keepdims=True)
            coef_ref[0, half, n] = jnp.broadcast_to(tall, (angles, HALF, LANES)).reshape(angles * HALF, LANES)

    def fill_image_weights():
        across = (HALF * depth)
        repeat = lax.broadcasted_iota(jnp.int32, (depth, across), 1) % depth
        repeat = jnp.where(repeat == lax.broadcasted_iota(jnp.int32, (depth, across), 0), 1.0, 0.0)
        wide = dot(weight_ref[...], repeat.astype(jnp.bfloat16)).astype(jnp.bfloat16)
        down = angles * HALF
        expand = lax.broadcasted_iota(jnp.int32, (down, angles), 0) // HALF
        expand = jnp.where(expand == lax.broadcasted_iota(jnp.int32, (down, angles), 1), 1.0, 0.0)
        wide = dot(expand.astype(jnp.bfloat16), wide)
        at = lax.broadcasted_iota(jnp.int32, (down, across), 0) % HALF
        same = lax.broadcasted_iota(jnp.int32, (down, across), 1) // depth == at
        image_w_ref[...] = jnp.where(same, wide, 0.0).astype(jnp.bfloat16)

    if base_piece:
        pl.when(block == off)(fill_image_weights)
    row_now = first + lane - column_of(bases_ref[...], angles)
    w_now = jnp.where((row_now >= 0) & (row_now < rows), 1.0 - own, 0.0)
    w_next = jnp.where((row_now + 1 >= 0) & (row_now + 1 < rows), own, 0.0)
    columns = angles * HALF
    mine = lax.broadcasted_iota(jnp.int32, (angles, columns), 1) // HALF
    mine = mine == lax.broadcasted_iota(jnp.int32, (angles, columns), 0)
    square = lax.broadcasted_iota(jnp.int32, (angles, angles), 0) == lax.broadcasted_iota(jnp.int32, (angles, angles), 1)

    def gather(values, start, count):
        near = jnp.where(lane < count, pltpu.roll(values, (2 * LANES - start) % LANES, 1), 0.0)
        step = HALF
        while step < LANES:
            near = near + pltpu.roll(near, step, 1)
            step *= 2
        return jnp.sum(jnp.where(mine, near, 0.0), axis=0, keepdims=True)

    turned = lambda other: lax.dot_general(
        weights, other, (((0,), (0,)), ((), ())), precision=lax.Precision.HIGHEST, preferred_element_type=jnp.float32
    )

    @pl.when(block == off)
    def _():
        wide_ref[...] = turned(jnp.where(mine, 1.0, 0.0))
        turned_ref[...] = turned(jnp.where(square, 1.0, 0.0))

    for half in range(BLOCK // HALF):
        start = block * BLOCK + half * HALF
        pick_next = gather(w_next, start, HALF)
        pick_now = gather(w_now, start + 1, HALF - 1)
        carry = jnp.sum(jnp.where(lane == start, w_now, 0.0), axis=1, keepdims=True)
        pick_carry = jnp.sum(jnp.where(square, carry, 0.0), axis=0, keepdims=True)
        fill_weights(wide_ref[...], turned_ref[...], pick_next, pick_now, pick_carry, spread_ref, half)


def device_tables(device, row_of_bases, fractions, path_weights, rows, part, piece, made=None):
    angles, depth = path_weights.shape
    blocks = LANES // BLOCK // PARTS
    steps = blocks // 2
    here = piece * steps
    last = fractions.shape[1] // LANES - 1
    column = lambda by: pl.BlockSpec((angles, LANES), lambda b, d: (0, jnp.clip(d[0] + by, 0, last)))
    whole = lambda shape: pl.BlockSpec(shape, lambda b, d: (0,) * len(shape))
    coef = (BLOCK // HALF, 3, angles * HALF, LANES)
    image_w = (angles * HALF, HALF * depth)
    spread = (HALF * depth, angles * (HALF + 1))
    out_specs = [
        pl.BlockSpec((1,) + coef, lambda b, d: (b + here, 0, 0, 0, 0)),
        pl.BlockSpec((2,) + spread, lambda b, d: (b + here, 0, 0)),
    ]
    out_shape = [
        jax.ShapeDtypeStruct((blocks,) + coef, jnp.float32),
        jax.ShapeDtypeStruct((2 * blocks,) + spread, jnp.bfloat16),
    ]
    if made is None:
        out_specs.append(whole(image_w))
        out_shape.append(jax.ShapeDtypeStruct(image_w, jnp.bfloat16))
    filled = [] if made is None else [made[0], made[4]]
    done = pl.pallas_call(
        functools.partial(tables_kernel, rows, part * blocks + here, made is None),
        grid_spec=pltpu.PrefetchScalarGridSpec(
            num_scalar_prefetch=1,
            grid=(steps,),
            in_specs=[whole((1, LANES)), column(0), column(1), whole(path_weights.shape)]
            + [pl.BlockSpec(memory_space=pl.ANY)] * len(filled),
            out_specs=out_specs,
            scratch_shapes=[
                pltpu.VMEM((depth, angles * HALF), jnp.float32),
                pltpu.VMEM((depth, angles), jnp.float32),
            ],
        ),
        out_shape=out_shape,
        input_output_aliases={5 + n: n for n in range(len(filled))},
        name="make_tables",
    )(device, row_of_bases, fractions, fractions, path_weights, *filled)
    return done[0], None, done[2] if made is None else made[2], path_weights, done[1]


def turn_kernel(classes, count, part, device_ref, bases_ref, seen_ref, volume_ref, *refs):
    *outs, slice_ref, twice_ref, sems = refs
    pltpu.make_async_copy(volume_ref.at[pl.ds(0, 1)], slice_ref, sems.at[2]).start()
    rows, cols = seen_ref.shape
    more = twice_ref.shape[0] - rows
    copies = [
        pltpu.make_async_copy(seen_ref, twice_ref.at[pl.ds(0, rows)], sems.at[0]),
        pltpu.make_async_copy(seen_ref.at[pl.ds(0, more)], twice_ref.at[pl.ds(rows, more)], sems.at[1]),
    ]
    for copy in copies:
        copy.start()
    for copy in copies:
        copy.wait()
    device = device_ref[0]
    base = bases_ref[device]
    my_class = device & (classes - 1)
    slices = count * PARTS

    def window(place, size, at):
        start = (place - base + 1 + rows) & (rows - 1)
        begin = pl.multiple_of(start & ~(BLOCK - 1), BLOCK)
        tall = size + BLOCK
        wide = twice_ref[pl.ds(begin, tall), at].astype(jnp.float32)
        return pltpu.roll(wide, (tall - (start - begin)) % tall, 0)

    for n, out in enumerate(outs):
        place = (my_class ^ n) * slices + part * count

        @pl.loop(0, cols // WIDE)
        def _(chunk):
            at = pl.ds(pl.multiple_of(chunk * WIDE, WIDE), WIDE)
            out[:, at] = window(place, count, at)[:count].astype(jnp.bfloat16)

    pltpu.make_async_copy(volume_ref.at[pl.ds(0, 1)], slice_ref, sems.at[2]).wait()


def turn(device, bases, seen, volume, classes, part):
    rows, cols = seen.shape
    count = rows // classes // PARTS
    return pl.pallas_call(
        functools.partial(turn_kernel, classes, count, part),
        in_specs=[
            pl.BlockSpec(memory_space=pltpu.SMEM),
            pl.BlockSpec(memory_space=pltpu.SMEM),
            pl.BlockSpec(memory_space=pl.ANY),
            pl.BlockSpec(memory_space=pl.ANY),
        ],
        out_specs=[pl.BlockSpec(memory_space=pltpu.VMEM)] * (classes + 1),
        out_shape=[jax.ShapeDtypeStruct((count, cols), seen.dtype)] * classes
        + [jax.ShapeDtypeStruct((1,) + volume.shape[1:], volume.dtype)],
        scratch_shapes=[pltpu.VMEM((rows + count + BLOCK, cols), seen.dtype), pltpu.SemaphoreType.DMA((3,))],
        compiler_params=pltpu.CompilerParams(vmem_limit_bytes=32 * 2**20),
        name="turn_rows",
    )(device, bases, seen, volume)


def plan_kernel(slots, planes, classes, angles, count, rows, ends, device_ref, bases_ref, table_ref, which_ref):
    shape = (2 * PARTS * classes, LANES)
    lane = lax.broadcasted_iota(jnp.int32, shape, 1)
    row = lax.broadcasted_iota(jnp.int32, shape, 0)
    class_shift = classes.bit_length() - 1
    base = jnp.broadcast_to(bases_ref[...], shape) - 1
    low_plane = base >> (rows.bit_length() - 1)
    turned = base & (rows - 1)

    def reach(which):
        lowest = low_plane + jnp.where(which * count + count - 1 < turned, 1, 0)
        highest = low_plane + jnp.where(which * count < turned, 1, 0)
        return lowest, highest

    lowest, highest = reach(row >> 1)
    upward = (row & 1) == 0
    source = lane >> class_shift
    at = jnp.where(upward, source, planes - 1 - source)
    to = jnp.where(lane < angles, jnp.where(upward, highest, planes - 1 - lowest), -1)
    key = to * CODE + (CODE - 1 - lane)
    sent = [jnp.full(shape, -1, jnp.int32) for _ in range(planes - 1)]
    for slot in range(slots):
        begin = at
        for link in range(planes - 1):
            ready = (begin == link) & (to > link)
            for n in range(LOAD):
                best = jnp.max(jnp.where(ready, key, -1), axis=1, keepdims=True)
                taken = ready & (key == best)
                at = jnp.where(taken, link + 1, at)
                ready = ready & (key != best)
                which = jnp.where(best >= 0, CODE - 1 - (best & (CODE - 1)), -1)
                sent[link] = jnp.where(lane == slot * LOAD + n, which, sent[link])

    me = device_ref[0]
    my_class = me & (classes - 1)
    plane = me >> class_shift
    none = jnp.full(shape, -1, jnp.int32)
    used = none
    for link in range(planes - 1):
        used = jnp.maximum(used, sent[link])
    used = jnp.max(used, axis=0, keepdims=True)
    head = lane[:1]
    need = jnp.max(jnp.where(used >= 0, head + 1, 0))
    left = jnp.max(jnp.where(lane < angles, to - at, 0))
    need = jnp.where(left > 0, slots * LOAD + 1, need)
    which_ref[0] = sum(jnp.where(need > end, 1, 0) for end in ends)

    tall = -(-max(slots * LOAD, angles) // 8) * 8
    sub = lax.broadcasted_iota(jnp.int32, (tall, LANES), 0)
    held = jnp.where(head < classes, plane * classes + (head ^ my_class), -1)
    for part in range(PARTS):
        low_here, high_here = reach(my_class * PARTS + part)
        wanted = (plane >= low_here) & (plane <= high_here) & (lane < angles)
        wanted = column_of(jnp.where(wanted, 1, 0)[:1], tall) > 0
        keep = lambda ids: jnp.max(jnp.where((sub == ids) & wanted, ids, -1), axis=0, keepdims=True)
        moves = []
        for way, spot in ((0, plane), (1, planes - 1 - plane)):
            sends, gets = none, none
            for link in range(planes - 1):
                sends = jnp.where(spot == link, sent[link], sends)
                gets = jnp.where(spot == link + 1, sent[link], gets)
            mine = row == 2 * (my_class * PARTS + part) + way
            sends = jnp.max(jnp.where(mine, sends, -1), axis=0, keepdims=True)
            gets = jnp.max(jnp.where(mine, gets, -1), axis=0, keepdims=True)
            arrived = jnp.max(jnp.where((column_of(gets, tall) == sends) & (sends >= 0), sub, 0), axis=0, keepdims=True)
            own = (sends >> class_shift) == plane
            index = jnp.where(own, (sends & (classes - 1)) ^ my_class, classes + arrived)
            moves.append((jnp.where(sends >= 0, index, 0), keep(gets)))
        for exchange in range(2):
            upward = ((plane + exchange) & 1) == 0
            line = part * LINES + exchange
            table_ref[line : line + 1] = jnp.where(upward, moves[0][0], moves[1][0])
            table_ref[line + 2 : line + 3] = jnp.where(upward, moves[1][1], moves[0][1])
        line = part * LINES + 4
        table_ref[line : line + 1] = keep(held)


def choose_kernel(slot, part, load, own, ups, table_ref, *refs):
    sources, (*outs, sems) = refs[: own + 2 * ups], refs[own + 2 * ups :]
    arrived = sources[own + ups :], sources[own : own + ups]
    views = [spread_out(sources[:own], []) + [(own + n, v) for n, v in spread_out([], side)] for side in arrived]
    spots = [(way, n) for way in range(2) for n in range(load)]
    for way, n in spots:
        for m, view in views[way]:

            @pl.when(table_ref[part * LINES + way, slot * LOAD + n] == m)
            def _():
                pltpu.make_async_copy(view, outs[way].at[n], sems.at[way, n]).start()

    for way, n in spots:
        pltpu.make_async_copy(sources[0], outs[way].at[n], sems.at[way, n]).wait()


def choose(slot, part, load, table, own, ups, downs):
    anywhere = pl.BlockSpec(memory_space=pl.ANY)
    shape = jax.ShapeDtypeStruct((load,) + own[0].shape, own[0].dtype)
    return pl.pallas_call(
        functools.partial(choose_kernel, slot, part, load, len(own), len(ups)),
        in_specs=[pl.BlockSpec(memory_space=pltpu.SMEM)] + [anywhere] * (len(own) + 2 * len(ups)),
        out_specs=[pl.BlockSpec(memory_space=pltpu.VMEM)] * 2,
        out_shape=[shape, shape],
        scratch_shapes=[pltpu.SemaphoreType.DMA((2, load))],
        cost_estimate=pl.CostEstimate(flops=0, bytes_accessed=4 * load * own[0].size * 2, transcendentals=0),
        name="choose_packet",
    )(table, *own, *ups, *downs)


def on_device(volume, measured, path_weights, fractions, bases):
    slices, depth, cols = volume.shape
    local, rows = measured.shape[:2]
    nslab = lax.axis_size("slab")
    device = lax.axis_index("slab")
    angles = local * nslab
    first = device * slices
    classes = rows // slices
    planes = nslab // classes
    pairs = [(i, i + classes) for i in range(nslab - classes)]
    pairs = [[p for p in pairs if p[0] // classes % 2 == odd] for odd in range(2)]
    pairs = [p + [(j, i) for i, j in p] for p in pairs]
    ups_of = lambda step: [(i, i + step) for i in range(nslab - step)]
    downs_of = lambda step: [(i + step, i) for i in range(nslab - step)]

    routed = local == 1 and classes == ROUTED_CLASSES and slices == LANES and rows & (rows - 1) == 0 and angles * HALF == LANES

    def dense(volume, measured, path_weights, fractions, bases):
        left = lax.ppermute(volume[slices - 1 :], "slab", ups_of(1))
        right = lax.ppermute(volume[:1], "slab", downs_of(1))
        share = lax.dynamic_slice_in_dim(jnp.pad(fractions, ((0, 0), (1, 1))), first, slices + 2, 1)
        tables = make_tables(share, first, rows, path_weights, bases, slices)
        my_bases = lax.dynamic_slice_in_dim(bases, device * local, local, 0)
        turned = jax.vmap(lambda m, b: jnp.roll(m, b - 1, axis=0))(measured, my_bases)
        by_class = turned.reshape(local, classes, slices, cols).transpose(1, 0, 2, 3)
        outgoing = jnp.tile(by_class, (planes, 1, 1, 1)).reshape(angles, slices, cols)
        seen = lax.all_to_all(outgoing, "slab", split_axis=0, concat_axis=0, tiled=True)
        ends = jnp.roll(by_class[:, :, slices - 1], 1, axis=0)
        ends = jnp.tile(ends, (planes, 1, 1)).reshape(angles, cols // LANES, LANES)
        edge = lax.all_to_all(ends, "slab", split_axis=0, concat_axis=0, tiled=True).reshape(angles, cols)
        return update(volume, right, tables, [seen], jnp.zeros((8, LANES), jnp.int32), None, 0, 1, (left, edge))[0]

    if not routed:
        return dense(volume, measured, path_weights, fractions, bases)

    number = device.astype(jnp.int32)[None]
    upper, lower = PARTS - 1, 0
    exchange = lambda runs: [runs[0]] + [
        lax.ppermute(runs[d], "slab", [(i, i ^ d) for i in range(nslab)]) for d in range(1, classes)
    ]
    *runs, high = turn(number, bases, measured[0], volume, classes, upper)
    runs, late_bases, seen = lax.optimization_barrier((runs, bases, measured[0]))
    own = {upper: exchange(runs)}

    row_of_bases = jnp.pad(late_bases, (0, LANES - angles), constant_values=1)[None]
    ends = [5, 6, 7]
    most = -(-ends[-1] // LOAD)
    table, which = pl.pallas_call(
        functools.partial(plan_kernel, most, planes, classes, angles, slices // PARTS, rows, ends),
        in_specs=[pl.BlockSpec(memory_space=pltpu.SMEM), pl.BlockSpec(memory_space=pltpu.VMEM)],
        out_specs=[pl.BlockSpec(memory_space=pltpu.VMEM), pl.BlockSpec(memory_space=pltpu.SMEM)],
        out_shape=[jax.ShapeDtypeStruct((16, LANES), jnp.int32), jax.ShapeDtypeStruct((1,), jnp.int32)],
        name="plan_slots",
    )(number, row_of_bases)
    table, which, high = lax.optimization_barrier((table, which, high))
    right = lax.ppermute(high, "slab", downs_of(1))
    *runs, _ = turn(number, bases, seen, volume, classes, lower)
    tables = device_tables(number, row_of_bases, fractions, path_weights, rows, upper, 0)
    tables = [tables[0], *tables[2:]]
    arrived, runs, table, tables, right = lax.optimization_barrier((own[upper], runs, table, tables, right))

    def finish(end):
        def branch(arrived, runs, table, upper_tables, right):
            own = {upper: arrived, lower: exchange(runs)}
            first, other = {upper: [], lower: []}, {upper: [], lower: []}
            late = row_of_bases
            tables = {upper: (upper_tables[0], None, *upper_tables[1:]), lower: None}
            beside = {(0, upper): (upper, 1), (1, upper): (lower, 0), (1, lower): (lower, 1)}
            for slot in range(-(-end // LOAD)):
                load = min(LOAD, end - slot * LOAD)
                for part in (upper, lower):
                    go_first, go_other = choose(slot, part, load, table, own[part], first[part], other[part])
                    if (slot, part) in beside:
                        go_first, go_other, late = lax.optimization_barrier((go_first, go_other, late))
                        where, piece = beside[slot, part]
                        made = device_tables(number, late, fractions, path_weights, rows, where, piece, tables[where])
                        table, made = lax.optimization_barrier((table, made))
                        tables[where] = made
                    first[part].append(lax.ppermute(go_first, "slab", pairs[0]))
                    other[part].append(lax.ppermute(go_other, "slab", pairs[1]))
            packets = {part: own[part] + first[part] + other[part] for part in (upper, lower)}
            out, last = update(volume, right, tables[upper], packets[upper], table, None, upper, PARTS)
            ahead = lax.ppermute(last, "slab", ups_of(1))
            out, second = update(volume, right, tables[lower], packets[lower], table, out, lower, PARTS)
            return mend(out, tables[lower][-1], tables[upper][-1], ahead, second)

        return branch

    others = lambda *_: dense(volume, measured, path_weights, fractions, bases)
    return lax.switch(which[0], [finish(e) for e in ends] + [others], arrived, runs, table, tables, right)


def solution(mesh):
    placed = (P(("groups", "slab"), None, None), P(("groups", "slab"), None, None), P(), P(), P())
    return jax.shard_map(
        on_device,
        mesh=mesh,
        in_specs=placed,
        out_specs=P(("groups", "slab"), None, None),
        check_vma=False,
    )
```

```python
import functools

import jax
import jax.numpy as jnp
from jax import lax
from jax.experimental import pallas as pl
from jax.experimental.pallas import tpu as pltpu
from jax.sharding import PartitionSpec as P

RELAX = 1.0
BLOCK = 16
HALF = 8
LANES = 128
WIDE = 256
PIECES = 4
PARTS = 2
ROUTED_CLASSES = 4
LOAD = 2
CODE = 256
LINES = 5
VMEM_LIMIT = 56 * 2**20


def dot(a, b):
    return jnp.dot(a, b, preferred_element_type=jnp.float32)


def widen(coef):
    return jnp.concatenate([coef] * (WIDE // LANES), axis=1)


def spread_out(own, arrived):
    views = list(enumerate(own))
    return views + [(s * LOAD + n, p.at[n]) for s, p in enumerate(arrived) for n in range(p.shape[0])]


def update_kernel(
    dense, part, table_ref, lower_ref, upper_ref, next_ref, right_ref, coef_ref, image_w_ref, weight_ref, spread_ref, *rest
):
    if dense:
        left_ref, edge_ref, edge_coef_ref, *rest = rest
    out_ref, carry_ref, seen_ref, result_ref, sems, out_sems = rest[-6:]
    packets = rest[:-7]
    block = pl.program_id(0)
    blocks = pl.num_programs(0)
    depth, width = lower_ref.shape[1:]
    angles = weight_ref.shape[0]
    first = part * blocks * BLOCK

    def fetch(at_block, act):
        slot = at_block % 2
        rows = pl.ds(pl.multiple_of(at_block * BLOCK, BLOCK), BLOCK)
        if dense:
            act(pltpu.make_async_copy(packets[0].at[:, rows], seen_ref.at[slot], sems.at[slot, 0]))
            return
        middle = (len(packets) - ROUTED_CLASSES) // 2 + ROUTED_CLASSES
        views = [(4, *v) for v in spread_out(packets[:ROUTED_CLASSES], [])]
        views += [(2, *v) for v in spread_out([], packets[ROUTED_CLASSES:middle])]
        views += [(3, *v) for v in spread_out([], packets[middle:])]
        for n, (line, spot, view) in enumerate(views):
            name = table_ref[part * LINES + line, spot]

            @pl.when(name >= 0)
            def _():
                act(pltpu.make_async_copy(view.at[rows], seen_ref.at[slot, name], sems.at[slot, n]))

    def deliver(at_block, act, pieces=range(PIECES)):
        slot = at_block % 2
        rows = pl.ds(first + at_block * BLOCK, BLOCK)
        for n in pieces:
            at = pl.ds(n * (width // PIECES), width // PIECES)
            act(pltpu.make_async_copy(result_ref.at[slot, :, :, at], out_ref.at[rows, :, at], out_sems.at[slot, n]))

    @pl.when(block == 0)
    def _():
        seen_ref[...] = jnp.zeros_like(seen_ref)
        fetch(block, lambda copy: copy.start())

    @pl.when(block + 1 < blocks)
    def _():
        fetch(block + 1, lambda copy: copy.start())

    @pl.when(block == 0)
    def _():
        if not dense:
            carry_ref[...] = jnp.zeros_like(carry_ref)
            return
        for chunk in range(width // WIDE):
            at = pl.ds(chunk * WIDE, WIDE)
            mine = dot(weight_ref[...], lower_ref[0, :, at])
            before = dot(weight_ref[...], left_ref[0, :, at])
            carry_ref[:, at] = (
                edge_ref[:, at].astype(jnp.float32) * widen(edge_coef_ref[2])
                - mine * widen(edge_coef_ref[0])
                - before * widen(edge_coef_ref[1])
            ).astype(jnp.bfloat16)

    @pl.when(block >= 2)
    def _():
        deliver(block - 2, lambda copy: copy.wait())

    fetch(block, lambda copy: copy.wait())
    slot = block % 2
    final = (block == blocks - 1) & (part == PARTS - 1 or dense)

    def columns(chunk):
        if dense:
            return pl.ds(pl.multiple_of(chunk * WIDE, WIDE), WIDE)
        return slice(chunk * WIDE, (chunk + 1) * WIDE)

    def image(chunk):
        at = columns(chunk)
        images = [dot(image_w_ref[...], r[:, :, at].reshape(HALF * depth, WIDE)) for r in (lower_ref, upper_ref)]
        after = dot(weight_ref[...], jnp.where(final, right_ref[0, :, at], next_ref[0, :, at]))
        return images, after

    def residual(chunk, images, after):
        at = columns(chunk)
        seen = seen_ref[slot, :, :, at].astype(jnp.float32)
        ahead = [pltpu.roll(x.reshape(angles, HALF, WIDE), HALF - 1, 1) for x in images]
        ahead.append(jnp.broadcast_to(after.reshape(angles, 1, WIDE), (angles, HALF, WIDE)))
        tail = lax.broadcasted_iota(jnp.int32, (angles, HALF, WIDE), 1) == HALF - 1
        parts = []
        for half in range(2):
            now = jnp.where(tail, ahead[half + 1], ahead[half]).reshape(angles * HALF, WIDE)
            got = seen[:, half * HALF : (half + 1) * HALF].reshape(angles * HALF, WIDE)
            coef = [widen(coef_ref[0, half, n]) for n in range(3)]
            resid = got * coef[2] - now * coef[0] - images[half] * coef[1]
            parts.append(resid.reshape(angles, HALF, WIDE))
        return parts

    def result(chunk, parts):
        at = columns(chunk)
        carry = carry_ref[:, at]
        for half, (resid, r) in enumerate(zip(parts, (lower_ref, upper_ref))):
            inputs = jnp.concatenate([resid.reshape(angles * HALF, WIDE).astype(jnp.bfloat16), carry])
            spread = dot(spread_ref[half], inputs).reshape(HALF, depth, WIDE)
            carry = resid[:, HALF - 1].astype(jnp.bfloat16)
            result_ref[slot, half * HALF : (half + 1) * HALF, :, at] = r[:, :, at].astype(jnp.float32) + spread
        carry_ref[:, at] = carry

    chunks = width // WIDE
    if dense:
        pl.loop(0, chunks)(lambda chunk: result(chunk, residual(chunk, *image(chunk))))
        deliver(block, lambda copy: copy.start())
    else:
        images, resids = {}, {}
        for n in range(chunks + 2):
            if n < chunks:
                images[n] = image(n)
            if 1 <= n <= chunks:
                resids[n - 1] = residual(n - 1, *images.pop(n - 1))
            if n >= 2:
                result(n - 2, resids.pop(n - 2))
                done = (n - 1) * PIECES
                if done % chunks == 0:
                    deliver(block, lambda copy: copy.start(), [done // chunks - 1])

    @pl.when(block == blocks - 1)
    def _():
        @pl.when(block >= 1)
        def _():
            deliver(block - 1, lambda copy: copy.wait())

        deliver(block, lambda copy: copy.wait())


def update(volume, right, tables, packets, table, before, part, parts, ahead=None):
    slices, depth, cols = volume.shape
    dense = ahead is not None
    blocks = slices // BLOCK // parts
    off = part * blocks
    by_block = lambda x: pl.BlockSpec((1,) + x.shape[1:], lambda b, i: (b,) + (0,) * (x.ndim - 1))
    whole = lambda x: pl.BlockSpec(x.shape, lambda b, i: (0,) * x.ndim)
    anywhere = pl.BlockSpec(memory_space=pl.ANY)
    coef, edge_coef, image_w, weights, spread_w = tables
    angles = weights.shape[0]
    ahead = [*ahead, edge_coef] if dense else []
    held = jax.ShapeDtypeStruct((angles, cols), volume.dtype)
    if before is None:
        before = coef
    aliases = {9 + len(ahead) + len(packets): 0} if before.shape == volume.shape else {}
    copies = LOAD * len(packets)
    one = (1, depth, cols)
    return pl.pallas_call(
        functools.partial(update_kernel, dense, part),
        grid_spec=pltpu.PrefetchScalarGridSpec(
            num_scalar_prefetch=1,
            grid=(blocks,),
            in_specs=[
                pl.BlockSpec((HALF, depth, cols), lambda b, i: (2 * (b + off), 0, 0)),
                pl.BlockSpec((HALF, depth, cols), lambda b, i: (2 * (b + off) + 1, 0, 0)),
                pl.BlockSpec(one, lambda b, i: (jnp.minimum((b + off + 1) * BLOCK, slices - 1), 0, 0)),
                whole(right), by_block(coef), whole(image_w), whole(weights),
                pl.BlockSpec((2,) + spread_w.shape[1:], lambda b, i: (b, 0, 0)),
            ]
            + [whole(x) for x in ahead]
            + [anywhere] * (len(packets) + 1),
            out_specs=[anywhere, whole(held)],
            scratch_shapes=[
                pltpu.VMEM((2, angles, BLOCK, cols), jnp.bfloat16),
                pltpu.VMEM((2, BLOCK, depth, cols), jnp.float32),
                pltpu.SemaphoreType.DMA((2, copies)),
                pltpu.SemaphoreType.DMA((2, PIECES)),
            ],
        ),
        out_shape=[jax.ShapeDtypeStruct(volume.shape, jnp.float32), held],
        input_output_aliases=aliases,
        compiler_params=pltpu.CompilerParams(dimension_semantics=("arbitrary",), vmem_limit_bytes=VMEM_LIMIT),
        cost_estimate=pl.CostEstimate(
            flops=4 * slices * depth * cols * angles // parts, bytes_accessed=volume.size * 7 // parts, transcendentals=0
        ),
        name="slab_update",
    )(
        table, volume, volume, volume, right, coef, image_w, weights, spread_w, *ahead, *packets, before
    )


def mend_kernel(lower_ref, upper_ref, first_ref, second_ref, before_ref, out_ref):
    columns = lower_ref.shape[2] - first_ref.shape[0]

    @pl.when(pl.program_id(0) == 0)
    def _():
        out_ref[0] = before_ref[0] + dot(lower_ref[0, :, columns:], first_ref[...])

    @pl.when(pl.program_id(0) == 1)
    def _():
        out_ref[0] = before_ref[0] + dot(upper_ref[0, :, columns:], second_ref[...])


def mend(out, lower, upper, first, second):
    slices, depth, cols = out.shape
    whole = pl.BlockSpec(first.shape, lambda b: (0, 0))
    weights = pl.BlockSpec((1, depth, lower.shape[2]), lambda b: (0, 0, 0))
    slab = pl.BlockSpec((1, depth, cols), lambda b: (b * (slices // 2), 0, 0))
    return pl.pallas_call(
        mend_kernel,
        grid=(2,),
        in_specs=[weights, weights, whole, whole, slab],
        out_specs=slab,
        out_shape=jax.ShapeDtypeStruct(out.shape, out.dtype),
        input_output_aliases={4: 0},
        name="mend_slices",
    )(lower, upper, first, second, out)


def fill_weights(wide_w, turned_w, pick_next, pick_now, pick_carry, spread_ref, half):
    depth, columns = wide_w.shape
    place = lax.broadcasted_iota(jnp.int32, (depth, columns), 1) % HALF
    from_next = wide_w * pick_next
    from_now = wide_w * pick_now
    from_carry = turned_w * pick_carry
    for z in range(HALF):
        row = jnp.where(place == z, from_next, jnp.where(place == z - 1, from_now, 0.0))
        total = jnp.sum(row, axis=1, keepdims=True)
        carry = jnp.zeros_like(from_carry)
        if z == 0:
            total = total + jnp.sum(from_carry, axis=1, keepdims=True)
            carry = from_carry
        scale = RELAX / total
        spread_ref[half, z * depth : (z + 1) * depth, :columns] = (row * scale).astype(jnp.bfloat16)
        spread_ref[half, z * depth : (z + 1) * depth, columns:] = (carry * scale).astype(jnp.bfloat16)


def weights_kernel(wide_w_ref, turned_w_ref, pick_ref, pick_carry_ref, spread_ref):
    picks = pick_ref[0, 0:1], pick_ref[0, 1:2], pick_carry_ref[0]
    fill_weights(wide_w_ref[...], turned_w_ref[...], *picks, spread_ref, 0)


def make_weights(wide_w, turned_w, pick, pick_carry):
    halves = pick.shape[0]
    depth, angles = turned_w.shape
    by_half = lambda shape: pl.BlockSpec((1,) + shape, lambda b: (b,) + (0,) * len(shape))
    whole = lambda x: pl.BlockSpec(x.shape, lambda b: (0,) * x.ndim)
    spread = (HALF * depth, angles * (HALF + 1))
    return pl.pallas_call(
        weights_kernel,
        grid=(halves,),
        in_specs=[whole(wide_w), whole(turned_w), by_half(pick.shape[1:]), by_half(pick_carry.shape[1:])],
        out_specs=by_half(spread),
        out_shape=jax.ShapeDtypeStruct((halves,) + spread, jnp.bfloat16),
        name="spread_weights",
    )(wide_w, turned_w, pick, pick_carry)


def make_tables(share, first, rows, path_weights, bases, slices):
    angles, depth = path_weights.shape
    blocks = slices // BLOCK
    weights = path_weights.astype(jnp.float32)
    ray_total = jnp.sum(weights, axis=1)[:, None]
    norm = 1.0 / (ray_total * ((1.0 - share[:, 1:]) + share[:, :-1]))
    coefs = jnp.stack([(1.0 - share[:, 1:]) * norm, share[:, :-1] * norm, norm])
    coef = coefs[:, :, 1:].reshape(3, angles, blocks, BLOCK // HALF, HALF).transpose(2, 3, 0, 1, 4)
    coef = coef.reshape(blocks, BLOCK // HALF, 3, angles * HALF, 1)
    coef = jnp.broadcast_to(coef, coef.shape[:4] + (LANES,))
    edge_coef = jnp.broadcast_to(coefs[:, :, :1], (3, angles, LANES))
    share_own = share[:, 1:-1]
    row_now = (first - bases)[:, None] + jnp.arange(slices, dtype=jnp.int32)[None, :]
    w_now = jnp.where((row_now >= 0) & (row_now < rows), 1.0 - share_own, 0.0)
    w_next = jnp.where((row_now + 1 >= 0) & (row_now + 1 < rows), share_own, 0.0)
    halves = slices // HALF
    pick = jnp.stack([w_next, jnp.pad(w_now[:, 1:], ((0, 0), (0, 1)))]).reshape(2, angles, halves, HALF)
    pick = pick.transpose(2, 0, 1, 3).reshape(halves, 2, angles * HALF)
    pick_carry = w_now[:, ::HALF].T[:, None, :]
    eye = jnp.eye(HALF, dtype=jnp.float32)
    image_w = jnp.einsum("ad,yz->ayzd", weights, eye).reshape(angles * HALF, HALF * depth).astype(jnp.bfloat16)
    wide_w = jnp.repeat(weights.T, HALF, axis=1)
    return coef, edge_coef, image_w, path_weights, make_weights(wide_w, weights.T, pick, pick_carry)


def column_of(line, tall):
    sub = lax.broadcasted_iota(jnp.int32, (tall, LANES), 0)
    lane = lax.broadcasted_iota(jnp.int32, (tall, LANES), 1)
    return jnp.max(jnp.where(sub == lane, line, -1), axis=1, keepdims=True)


def tables_kernel(rows, off, base_piece, device_ref, bases_ref, own_ref, after_ref, weight_ref, *rest):
    if base_piece:
        coef_ref, spread_ref, image_w_ref, wide_ref, turned_ref = rest
    else:
        coef_ref, spread_ref, wide_ref, turned_ref = rest[2:]
    block = pl.program_id(0) + off
    angles, depth = weight_ref.shape
    first = device_ref[0] * LANES
    shape = (angles, LANES)
    lane = lax.broadcasted_iota(jnp.int32, shape, 1)
    sub = lax.broadcasted_iota(jnp.int32, shape, 0)
    weights = weight_ref[...].astype(jnp.float32)
    ray_total = jnp.sum(weights, axis=1, keepdims=True)
    own = own_ref[...]
    ahead = jnp.where(lane == LANES - 1, pltpu.roll(after_ref[...], LANES - 1, 1), pltpu.roll(own, LANES - 1, 1))
    norm = 1.0 / (ray_total * ((1.0 - ahead) + own))
    coefs = ((1.0 - ahead) * norm, own * norm, norm)
    spots = lax.broadcasted_iota(jnp.int32, (angles, HALF, LANES), 2) - lax.broadcasted_iota(jnp.int32, (angles, HALF, LANES), 1)
    for half in range(BLOCK // HALF):
        here = spots == block * BLOCK + half * HALF
        for n, coef in enumerate(coefs):
            tall = jnp.broadcast_to(coef.reshape(angles, 1, LANES), (angles, HALF, LANES))
            tall = jnp.sum(jnp.where(here, tall, 0.0), axis=2, keepdims=True)
            coef_ref[0, half, n] = jnp.broadcast_to(tall, (angles, HALF, LANES)).reshape(angles * HALF, LANES)

    def fill_image_weights():
        across = (HALF * depth)
        repeat = lax.broadcasted_iota(jnp.int32, (depth, across), 1) % depth
        repeat = jnp.where(repeat == lax.broadcasted_iota(jnp.int32, (depth, across), 0), 1.0, 0.0)
        wide = dot(weight_ref[...], repeat.astype(jnp.bfloat16)).astype(jnp.bfloat16)
        down = angles * HALF
        expand = lax.broadcasted_iota(jnp.int32, (down, angles), 0) // HALF
        expand = jnp.where(expand == lax.broadcasted_iota(jnp.int32, (down, angles), 1), 1.0, 0.0)
        wide = dot(expand.astype(jnp.bfloat16), wide)
        at = lax.broadcasted_iota(jnp.int32, (down, across), 0) % HALF
        same = lax.broadcasted_iota(jnp.int32, (down, across), 1) // depth == at
        image_w_ref[...] = jnp.where(same, wide, 0.0).astype(jnp.bfloat16)

    if base_piece:
        pl.when(block == off)(fill_image_weights)
    row_now = first + lane - column_of(bases_ref[...], angles)
    w_now = jnp.where((row_now >= 0) & (row_now < rows), 1.0 - own, 0.0)
    w_next = jnp.where((row_now + 1 >= 0) & (row_now + 1 < rows), own, 0.0)
    columns = angles * HALF
    mine = lax.broadcasted_iota(jnp.int32, (angles, columns), 1) // HALF
    mine = mine == lax.broadcasted_iota(jnp.int32, (angles, columns), 0)
    square = lax.broadcasted_iota(jnp.int32, (angles, angles), 0) == lax.broadcasted_iota(jnp.int32, (angles, angles), 1)

    def gather(values, start, count):
        near = jnp.where(lane < count, pltpu.roll(values, (2 * LANES - start) % LANES, 1), 0.0)
        step = HALF
        while step < LANES:
            near = near + pltpu.roll(near, step, 1)
            step *= 2
        return jnp.sum(jnp.where(mine, near, 0.0), axis=0, keepdims=True)

    turned = lambda other: lax.dot_general(
        weights, other, (((0,), (0,)), ((), ())), precision=lax.Precision.HIGHEST, preferred_element_type=jnp.float32
    )

    @pl.when(block == off)
    def _():
        wide_ref[...] = turned(jnp.where(mine, 1.0, 0.0))
        turned_ref[...] = turned(jnp.where(square, 1.0, 0.0))

    for half in range(BLOCK // HALF):
        start = block * BLOCK + half * HALF
        pick_next = gather(w_next, start, HALF)
        pick_now = gather(w_now, start + 1, HALF - 1)
        carry = jnp.sum(jnp.where(lane == start, w_now, 0.0), axis=1, keepdims=True)
        pick_carry = jnp.sum(jnp.where(square, carry, 0.0), axis=0, keepdims=True)
        fill_weights(wide_ref[...], turned_ref[...], pick_next, pick_now, pick_carry, spread_ref, half)


def device_tables(device, row_of_bases, fractions, path_weights, rows, part, piece, made=None):
    angles, depth = path_weights.shape
    blocks = LANES // BLOCK // PARTS
    steps = blocks // 2
    here = piece * steps
    last = fractions.shape[1] // LANES - 1
    column = lambda by: pl.BlockSpec((angles, LANES), lambda b, d: (0, jnp.clip(d[0] + by, 0, last)))
    whole = lambda shape: pl.BlockSpec(shape, lambda b, d: (0,) * len(shape))
    coef = (BLOCK // HALF, 3, angles * HALF, LANES)
    image_w = (angles * HALF, HALF * depth)
    spread = (HALF * depth, angles * (HALF + 1))
    out_specs = [
        pl.BlockSpec((1,) + coef, lambda b, d: (b + here, 0, 0, 0, 0)),
        pl.BlockSpec((2,) + spread, lambda b, d: (b + here, 0, 0)),
    ]
    out_shape = [
        jax.ShapeDtypeStruct((blocks,) + coef, jnp.float32),
        jax.ShapeDtypeStruct((2 * blocks,) + spread, jnp.bfloat16),
    ]
    if made is None:
        out_specs.append(whole(image_w))
        out_shape.append(jax.ShapeDtypeStruct(image_w, jnp.bfloat16))
    filled = [] if made is None else [made[0], made[4]]
    done = pl.pallas_call(
        functools.partial(tables_kernel, rows, part * blocks + here, made is None),
        grid_spec=pltpu.PrefetchScalarGridSpec(
            num_scalar_prefetch=1,
            grid=(steps,),
            in_specs=[whole((1, LANES)), column(0), column(1), whole(path_weights.shape)]
            + [pl.BlockSpec(memory_space=pl.ANY)] * len(filled),
            out_specs=out_specs,
            scratch_shapes=[
                pltpu.VMEM((depth, angles * HALF), jnp.float32),
                pltpu.VMEM((depth, angles), jnp.float32),
            ],
        ),
        out_shape=out_shape,
        input_output_aliases={5 + n: n for n in range(len(filled))},
        name="make_tables",
    )(device, row_of_bases, fractions, fractions, path_weights, *filled)
    return done[0], None, done[2] if made is None else made[2], path_weights, done[1]


def turn_kernel(classes, count, part, device_ref, bases_ref, seen_ref, volume_ref, *refs):
    *outs, slice_ref, twice_ref, sems = refs
    pltpu.make_async_copy(volume_ref.at[pl.ds(0, 1)], slice_ref, sems.at[2]).start()
    rows, cols = seen_ref.shape
    more = twice_ref.shape[0] - rows
    copies = [
        pltpu.make_async_copy(seen_ref, twice_ref.at[pl.ds(0, rows)], sems.at[0]),
        pltpu.make_async_copy(seen_ref.at[pl.ds(0, more)], twice_ref.at[pl.ds(rows, more)], sems.at[1]),
    ]
    for copy in copies:
        copy.start()
    for copy in copies:
        copy.wait()
    device = device_ref[0]
    base = bases_ref[device]
    my_class = device & (classes - 1)
    slices = count * PARTS

    def window(place, size, at):
        start = (place - base + 1 + rows) & (rows - 1)
        begin = pl.multiple_of(start & ~(BLOCK - 1), BLOCK)
        tall = size + BLOCK
        wide = twice_ref[pl.ds(begin, tall), at].astype(jnp.float32)
        return pltpu.roll(wide, (tall - (start - begin)) % tall, 0)

    for n, out in enumerate(outs):
        place = (my_class ^ n) * slices + part * count

        @pl.loop(0, cols // WIDE)
        def _(chunk):
            at = pl.ds(pl.multiple_of(chunk * WIDE, WIDE), WIDE)
            out[:, at] = window(place, count, at)[:count].astype(jnp.bfloat16)

    pltpu.make_async_copy(volume_ref.at[pl.ds(0, 1)], slice_ref, sems.at[2]).wait()


def turn(device, bases, seen, volume, classes, part):
    rows, cols = seen.shape
    count = rows // classes // PARTS
    return pl.pallas_call(
        functools.partial(turn_kernel, classes, count, part),
        in_specs=[
            pl.BlockSpec(memory_space=pltpu.SMEM),
            pl.BlockSpec(memory_space=pltpu.SMEM),
            pl.BlockSpec(memory_space=pl.ANY),
            pl.BlockSpec(memory_space=pl.ANY),
        ],
        out_specs=[pl.BlockSpec(memory_space=pltpu.VMEM)] * (classes + 1),
        out_shape=[jax.ShapeDtypeStruct((count, cols), seen.dtype)] * classes
        + [jax.ShapeDtypeStruct((1,) + volume.shape[1:], volume.dtype)],
        scratch_shapes=[pltpu.VMEM((rows + count + BLOCK, cols), seen.dtype), pltpu.SemaphoreType.DMA((3,))],
        compiler_params=pltpu.CompilerParams(vmem_limit_bytes=32 * 2**20),
        name="turn_rows",
    )(device, bases, seen, volume)


def plan_kernel(slots, planes, classes, angles, count, rows, ends, device_ref, bases_ref, table_ref, which_ref):
    shape = (2 * PARTS * classes, LANES)
    lane = lax.broadcasted_iota(jnp.int32, shape, 1)
    row = lax.broadcasted_iota(jnp.int32, shape, 0)
    class_shift = classes.bit_length() - 1
    base = jnp.broadcast_to(bases_ref[...], shape) - 1
    low_plane = base >> (rows.bit_length() - 1)
    turned = base & (rows - 1)

    def reach(which):
        lowest = low_plane + jnp.where(which * count + count - 1 < turned, 1, 0)
        highest = low_plane + jnp.where(which * count < turned, 1, 0)
        return lowest, highest

    lowest, highest = reach(row >> 1)
    upward = (row & 1) == 0
    source = lane >> class_shift
    at = jnp.where(upward, source, planes - 1 - source)
    to = jnp.where(lane < angles, jnp.where(upward, highest, planes - 1 - lowest), -1)
    key = to * CODE + (CODE - 1 - lane)
    sent = [jnp.full(shape, -1, jnp.int32) for _ in range(planes - 1)]
    for slot in range(slots):
        begin = at
        for link in range(planes - 1):
            ready = (begin == link) & (to > link)
            for n in range(LOAD):
                best = jnp.max(jnp.where(ready, key, -1), axis=1, keepdims=True)
                taken = ready & (key == best)
                at = jnp.where(taken, link + 1, at)
                ready = ready & (key != best)
                which = jnp.where(best >= 0, CODE - 1 - (best & (CODE - 1)), -1)
                sent[link] = jnp.where(lane == slot * LOAD + n, which, sent[link])

    me = device_ref[0]
    my_class = me & (classes - 1)
    plane = me >> class_shift
    none = jnp.full(shape, -1, jnp.int32)
    used = none
    for link in range(planes - 1):
        used = jnp.maximum(used, sent[link])
    used = jnp.max(used, axis=0, keepdims=True)
    head = lane[:1]
    need = jnp.max(jnp.where(used >= 0, head + 1, 0))
    left = jnp.max(jnp.where(lane < angles, to - at, 0))
    need = jnp.where(left > 0, slots * LOAD + 1, need)
    which_ref[0] = sum(jnp.where(need > end, 1, 0) for end in ends)

    tall = -(-max(slots * LOAD, angles) // 8) * 8
    sub = lax.broadcasted_iota(jnp.int32, (tall, LANES), 0)
    held = jnp.where(head < classes, plane * classes + (head ^ my_class), -1)
    for part in range(PARTS):
        low_here, high_here = reach(my_class * PARTS + part)
        wanted = (plane >= low_here) & (plane <= high_here) & (lane < angles)
        wanted = column_of(jnp.where(wanted, 1, 0)[:1], tall) > 0
        keep = lambda ids: jnp.max(jnp.where((sub == ids) & wanted, ids, -1), axis=0, keepdims=True)
        moves = []
        for way, spot in ((0, plane), (1, planes - 1 - plane)):
            sends, gets = none, none
            for link in range(planes - 1):
                sends = jnp.where(spot == link, sent[link], sends)
                gets = jnp.where(spot == link + 1, sent[link], gets)
            mine = row == 2 * (my_class * PARTS + part) + way
            sends = jnp.max(jnp.where(mine, sends, -1), axis=0, keepdims=True)
            gets = jnp.max(jnp.where(mine, gets, -1), axis=0, keepdims=True)
            arrived = jnp.max(jnp.where((column_of(gets, tall) == sends) & (sends >= 0), sub, 0), axis=0, keepdims=True)
            own = (sends >> class_shift) == plane
            index = jnp.where(own, (sends & (classes - 1)) ^ my_class, classes + arrived)
            moves.append((jnp.where(sends >= 0, index, 0), keep(gets)))
        for exchange in range(2):
            upward = ((plane + exchange) & 1) == 0
            line = part * LINES + exchange
            table_ref[line : line + 1] = jnp.where(upward, moves[0][0], moves[1][0])
            table_ref[line + 2 : line + 3] = jnp.where(upward, moves[1][1], moves[0][1])
        line = part * LINES + 4
        table_ref[line : line + 1] = keep(held)


def choose_kernel(slot, part, load, own, ups, table_ref, *refs):
    sources, (*outs, sems) = refs[: own + 2 * ups], refs[own + 2 * ups :]
    arrived = sources[own + ups :], sources[own : own + ups]
    views = [spread_out(sources[:own], []) + [(own + n, v) for n, v in spread_out([], side)] for side in arrived]
    spots = [(way, n) for way in range(2) for n in range(load)]
    for way, n in spots:
        for m, view in views[way]:

            @pl.when(table_ref[part * LINES + way, slot * LOAD + n] == m)
            def _():
                pltpu.make_async_copy(view, outs[way].at[n], sems.at[way, n]).start()

    for way, n in spots:
        pltpu.make_async_copy(sources[0], outs[way].at[n], sems.at[way, n]).wait()


def choose(slot, part, load, table, own, ups, downs):
    anywhere = pl.BlockSpec(memory_space=pl.ANY)
    shape = jax.ShapeDtypeStruct((load,) + own[0].shape, own[0].dtype)
    return pl.pallas_call(
        functools.partial(choose_kernel, slot, part, load, len(own), len(ups)),
        in_specs=[pl.BlockSpec(memory_space=pltpu.SMEM)] + [anywhere] * (len(own) + 2 * len(ups)),
        out_specs=[pl.BlockSpec(memory_space=pltpu.VMEM)] * 2,
        out_shape=[shape, shape],
        scratch_shapes=[pltpu.SemaphoreType.DMA((2, load))],
        cost_estimate=pl.CostEstimate(flops=0, bytes_accessed=4 * load * own[0].size * 2, transcendentals=0),
        name="choose_packet",
    )(table, *own, *ups, *downs)


def on_device(volume, measured, path_weights, fractions, bases):
    slices, depth, cols = volume.shape
    local, rows = measured.shape[:2]
    nslab = lax.axis_size("slab")
    device = lax.axis_index("slab")
    angles = local * nslab
    first = device * slices
    classes = rows // slices
    planes = nslab // classes
    pairs = [(i, i + classes) for i in range(nslab - classes)]
    pairs = [[p for p in pairs if p[0] // classes % 2 == odd] for odd in range(2)]
    pairs = [p + [(j, i) for i, j in p] for p in pairs]
    ups_of = lambda step: [(i, i + step) for i in range(nslab - step)]
    downs_of = lambda step: [(i + step, i) for i in range(nslab - step)]

    routed = local == 1 and classes == ROUTED_CLASSES and slices == LANES and rows & (rows - 1) == 0 and angles * HALF == LANES

    def dense(volume, measured, path_weights, fractions, bases):
        left = lax.ppermute(volume[slices - 1 :], "slab", ups_of(1))
        right = lax.ppermute(volume[:1], "slab", downs_of(1))
        share = lax.dynamic_slice_in_dim(jnp.pad(fractions, ((0, 0), (1, 1))), first, slices + 2, 1)
        tables = make_tables(share, first, rows, path_weights, bases, slices)
        my_bases = lax.dynamic_slice_in_dim(bases, device * local, local, 0)
        turned = jax.vmap(lambda m, b: jnp.roll(m, b - 1, axis=0))(measured, my_bases)
        by_class = turned.reshape(local, classes, slices, cols).transpose(1, 0, 2, 3)
        outgoing = jnp.tile(by_class, (planes, 1, 1, 1)).reshape(angles, slices, cols)
        seen = lax.all_to_all(outgoing, "slab", split_axis=0, concat_axis=0, tiled=True)
        ends = jnp.roll(by_class[:, :, slices - 1], 1, axis=0)
        ends = jnp.tile(ends, (planes, 1, 1)).reshape(angles, cols // LANES, LANES)
        edge = lax.all_to_all(ends, "slab", split_axis=0, concat_axis=0, tiled=True).reshape(angles, cols)
        return update(volume, right, tables, [seen], jnp.zeros((8, LANES), jnp.int32), None, 0, 1, (left, edge))[0]

    if not routed:
        return dense(volume, measured, path_weights, fractions, bases)

    number = device.astype(jnp.int32)[None]
    upper, lower = PARTS - 1, 0
    exchange = lambda runs: [runs[0]] + [
        lax.ppermute(runs[d], "slab", [(i, i ^ d) for i in range(nslab)]) for d in range(1, classes)
    ]
    *runs, high = turn(number, bases, measured[0], volume, classes, upper)
    runs, late_bases, seen = lax.optimization_barrier((runs, bases, measured[0]))
    own = {upper: exchange(runs)}

    row_of_bases = jnp.pad(late_bases, (0, LANES - angles), constant_values=1)[None]
    ends = [5, 6, 7, 8]
    most = -(-ends[-1] // LOAD)
    table, which = pl.pallas_call(
        functools.partial(plan_kernel, most, planes, classes, angles, slices // PARTS, rows, ends),
        in_specs=[pl.BlockSpec(memory_space=pltpu.SMEM), pl.BlockSpec(memory_space=pltpu.VMEM)],
        out_specs=[pl.BlockSpec(memory_space=pltpu.VMEM), pl.BlockSpec(memory_space=pltpu.SMEM)],
        out_shape=[jax.ShapeDtypeStruct((16, LANES), jnp.int32), jax.ShapeDtypeStruct((1,), jnp.int32)],
        name="plan_slots",
    )(number, row_of_bases)
    table, which, high = lax.optimization_barrier((table, which, high))
    right = lax.ppermute(high, "slab", downs_of(1))
    *runs, _ = turn(number, bases, seen, volume, classes, lower)
    tables = device_tables(number, row_of_bases, fractions, path_weights, rows, upper, 0)
    tables = [tables[0], *tables[2:]]
    arrived, runs, table, tables, right = lax.optimization_barrier((own[upper], runs, table, tables, right))

    def finish(end):
        def branch(arrived, runs, table, upper_tables, right):
            own = {upper: arrived, lower: exchange(runs)}
            first, other = {upper: [], lower: []}, {upper: [], lower: []}
            late = row_of_bases
            tables = {upper: (upper_tables[0], None, *upper_tables[1:]), lower: None}
            beside = {(0, upper): (upper, 1), (1, upper): (lower, 0), (1, lower): (lower, 1)}
            for slot in range(-(-end // LOAD)):
                load = min(LOAD, end - slot * LOAD)
                for part in (upper, lower):
                    go_first, go_other = choose(slot, part, load, table, own[part], first[part], other[part])
                    if (slot, part) in beside:
                        go_first, go_other, late = lax.optimization_barrier((go_first, go_other, late))
                        where, piece = beside[slot, part]
                        made = device_tables(number, late, fractions, path_weights, rows, where, piece, tables[where])
                        table, made = lax.optimization_barrier((table, made))
                        tables[where] = made
                    first[part].append(lax.ppermute(go_first, "slab", pairs[0]))
                    other[part].append(lax.ppermute(go_other, "slab", pairs[1]))
            packets = {part: own[part] + first[part] + other[part] for part in (upper, lower)}
            out, last = update(volume, right, tables[upper], packets[upper], table, None, upper, PARTS)
            ahead = lax.ppermute(last, "slab", ups_of(1))
            out, second = update(volume, right, tables[lower], packets[lower], table, out, lower, PARTS)
            return mend(out, tables[lower][-1], tables[upper][-1], ahead, second)

        return branch

    others = lambda *_: dense(volume, measured, path_weights, fractions, bases)
    return lax.switch(which[0], [finish(e) for e in ends] + [others], arrived, runs, table, tables, right)


def solution(mesh):
    placed = (P(("groups", "slab"), None, None), P(("groups", "slab"), None, None), P(), P(), P())
    return jax.shard_map(
        on_device,
        mesh=mesh,
        in_specs=placed,
        out_specs=P(("groups", "slab"), None, None),
        check_vma=False,
    )
```
